32 devices in a mesh: src: 8 (over y, x, core), tgt: 4 (over z).
Axes of the slice: x: 2, y: 2, z: 4, core: 2. Of those that a mesh axis runs over, the one named last changes fastest.
Arguments:
- src_points: bfloat16 [8192, 1024], P(('src', 'tgt')), may hold values from -6 to 6
- tgt_points: bfloat16 [8192, 1024], P(('src', 'tgt')), may hold values from -24 to 24
- src_factor: bfloat16 [8192, 256], P(('src', 'tgt')), may hold values from 0.25 to 4
- tgt_factor: bfloat16 [8192, 256], P(('src', 'tgt')), may hold values from 0.25 to 4
- inner_marginal: float32 [256], replicated, may hold values from 0.3 to 3
- src_cluster: int32 [8192], P(('src', 'tgt')), may hold values from 0 to 63, as said below
- tgt_cluster: int32 [8192], P(('src', 'tgt')), may hold values from 0 to 63, as said below
Outputs:
- src_update: bfloat16 [8192, 256], P(('src', 'tgt'))
- tgt_update: bfloat16 [8192, 256], P(('src', 'tgt'))
- mapped: bfloat16 [8192, 1024], P(('src', 'tgt'))
The draws below stay inside these ranges and needn't reach their ends.
Inputs may be any that keep to these rules, and one draw needn't show every extreme that they name: `src_cluster`: Co-cluster c belongs to the owner c // 2 (devices in the order of src+tgt). Over the 256 source points of one device, the points whose co-cluster belongs to one owner number at most 16, and at least one for every owner; some owner receives exactly 16 from every device. `tgt_cluster`: Co-cluster c belongs to the owner c // 2. Over the 256 target points of one device, the points whose co-cluster belongs to one owner number at most 16, and at least one for every owner; some owner receives exactly 16 from every device. Every co-cluster holds at least one target point.
All inputs are finite; a program needn't handle non-finite values. Where the reference program divides by a largest or mean magnitude, that divisor is 1e-20 or more.
Results may differ from the reference program's by a relative error of at most 0.0049.
Values may be sent and summed in bfloat16 or wider, within the bound.
No kernel may reach another device: no remote copies, remote signals or barrier semaphores. Data moves between devices by JAX's collectives and lax.ppermute only.
A program may use at most 64 MiB of HBM per device.

```python
import math
import jax
import jax.numpy as jnp
from jax import lax

D = 1024
R = 256
ROWS = 256
CL_DEV = 2
CAP = 16
POINTS = 8192
DEVICES = 32


def cluster_draw(key, salt):
    salted = jax.random.fold_in(key, salt)
    heavy = jax.random.randint(jax.random.fold_in(salted, 1), (), 0, DEVICES)
    slot_count = DEVICES * CAP
    slot_ids = jnp.arange(slot_count, dtype=jnp.int32)
    forced = jnp.logical_or(slot_ids // CAP == heavy, slot_ids % CAP == 0)

    def one_block(block_id):
        block_key = jax.random.fold_in(salted, 100 + block_id)
        ordering = jax.random.permutation(jax.random.fold_in(block_key, 1), slot_count).astype(jnp.int32)
        priority = jnp.where(forced, slot_count, 0) + ordering
        chosen = jnp.argsort(-priority)[:ROWS].astype(jnp.int32)
        mixing = jax.random.permutation(jax.random.fold_in(block_key, 2), ROWS)
        chosen = chosen[mixing]
        owners = chosen // CAP
        picks = jax.random.randint(jax.random.fold_in(block_key, 3), (ROWS,), 0, CL_DEV)
        picks = jnp.where(chosen % CAP == 0, block_id % CL_DEV, picks)
        return owners * CL_DEV + picks
    blocks = lax.map(one_block, jnp.arange(DEVICES, dtype=jnp.int32))
    return blocks.reshape(-1).astype(jnp.int32)


def draw_src_cluster(key, part):
    return cluster_draw(key, 5)


def draw_tgt_cluster(key, part):
    return cluster_draw(key, 6)


def block_scale(stream_key, dims, cuts, low, top_value):
    def one(position, blocks):
        draws = jax.random.uniform(jax.random.fold_in(jax.random.fold_in(stream_key, 6), position), (blocks,), jnp.float32, low / len(cuts), top_value / len(cuts))
        return jnp.repeat(jnp.exp(draws), dims[position] // blocks).reshape((-1,) + (1,) * (len(dims) - position - 1))

    gain = one(*cuts[0])
    for cut in cuts[1:]:
        gain = gain * one(*cut)
    return gain


def bell_draw(key, dims, spread, limit, cuts=(), held_as=jnp.bfloat16):
    values = jax.random.normal(key, dims, jnp.float32) * spread
    if len(cuts) > 0:
        values = block_scale(key, dims, cuts, -0.22, 0.18) * values
    return jnp.clip(values, min=-limit, max=limit).astype(held_as)


def setup_inputs(seed: int = 0) -> dict:
    streams_of = jax.random.split(jax.random.key(seed), 8)
    src_points = bell_draw(streams_of[0], (POINTS, D), 1.0, 6.0, ((0, 32),))
    tgt_points = bell_draw(streams_of[1], (POINTS, D), 4.0, 24.0, ((0, 32),))
    src_factor = jnp.clip(jnp.exp(math.log(4.0) - 2.7725887 * jax.random.uniform(streams_of[2], (POINTS, R), jnp.float32) ** block_scale(streams_of[2], (POINTS, R), ((0, 32),), -0.2, 0.2)), 0.25, 4.0).astype(jnp.bfloat16)
    tgt_factor = jnp.clip(jnp.exp(math.log(4.0) - 2.7725887 * jax.random.uniform(streams_of[3], (POINTS, R), jnp.float32) ** block_scale(streams_of[3], (POINTS, R), ((0, 32),), -0.2, 0.2)), 0.25, 4.0).astype(jnp.bfloat16)
    inner_marginal = jnp.clip(jnp.exp(jax.random.uniform(streams_of[4], (R,), jnp.float32, math.log(0.3), math.log(3.0))), 0.3, 3.0)
    src_cluster = draw_src_cluster(jax.random.fold_in(streams_of[7], 71), 0)
    tgt_cluster = draw_tgt_cluster(jax.random.fold_in(streams_of[7], 71), 0)
    return {"src_points": src_points, "tgt_points": tgt_points, "src_factor": src_factor, "tgt_factor": tgt_factor, "inner_marginal": inner_marginal, "src_cluster": src_cluster, "tgt_cluster": tgt_cluster}


GAMMA = 2.0
TEMPER = 0.03
EPS = 1e-06

def mirror_step(points, total, factor, inner_marginal):
    total_round = total.astype(jnp.bfloat16)
    gradient = -jnp.dot(points, total_round, preferred_element_type=jnp.float32) / inner_marginal[None, :]
    row_scale = lax.optimization_barrier(jnp.max(jnp.abs(gradient), axis=1, keepdims=True)) + EPS
    tilted = factor.astype(jnp.float32) * jnp.exp(-GAMMA * gradient / row_scale)
    return (tilted / lax.optimization_barrier(jnp.mean(tilted, axis=1, keepdims=True))).astype(jnp.bfloat16)

def layout(owners):
    ordering = jnp.argsort(owners, stable=True).astype(jnp.int32)
    counts = jax.ops.segment_sum(jnp.ones_like(owners), owners, num_segments=DEVICES).astype(jnp.int32)
    starts = (jnp.cumsum(counts) - counts).astype(jnp.int32)
    padded = jnp.concatenate([ordering, jnp.full((2 * ROWS,), POINTS, jnp.int32)])
    return (padded, starts, counts)

def reference(src_points, tgt_points, src_factor, tgt_factor, inner_marginal, src_cluster, tgt_cluster):
    tgt_sum = jnp.dot(tgt_points.T, tgt_factor, preferred_element_type=jnp.float32)
    src_sum = jnp.dot(src_points.T, src_factor, preferred_element_type=jnp.float32)
    src_update = mirror_step(src_points, tgt_sum, src_factor, inner_marginal)
    tgt_update = mirror_step(tgt_points, src_sum, tgt_factor, inner_marginal)
    src_pad, src_start, src_count = layout((src_cluster // CL_DEV).astype(jnp.int32))
    tgt_pad, tgt_start, tgt_count = layout((tgt_cluster // CL_DEV).astype(jnp.int32))
    buffer_len = 2 * ROWS
    inv_src = lax.rsqrt(lax.optimization_barrier(jnp.sum(jnp.square(src_points.astype(jnp.float32)), axis=1)) + EPS)
    inv_tgt = lax.rsqrt(lax.optimization_barrier(jnp.sum(jnp.square(tgt_points.astype(jnp.float32)), axis=1)) + EPS)
    positions = jnp.arange(buffer_len, dtype=jnp.int32)

    def one_owner(result, owner_id):
        src_idx = lax.dynamic_slice(src_pad, (src_start[owner_id].astype(jnp.int32),), (buffer_len,))
        src_ok = positions < src_count[owner_id]
        src_safe = jnp.where(src_ok, src_idx, 0)
        tgt_idx = lax.dynamic_slice(tgt_pad, (tgt_start[owner_id].astype(jnp.int32),), (buffer_len,))
        tgt_ok = positions < tgt_count[owner_id]
        tgt_safe = jnp.where(tgt_ok, tgt_idx, 0)
        src_rows = src_points[src_safe]
        tgt_rows = tgt_points[tgt_safe]
        src_labels = jnp.where(src_ok, src_cluster[src_safe], -2)
        tgt_labels = jnp.where(tgt_ok, tgt_cluster[tgt_safe], -1)
        products = jnp.dot(src_rows, tgt_rows.T, preferred_element_type=jnp.float32)
        cosine = products * inv_src[src_safe][:, None] * inv_tgt[tgt_safe][None, :]
        weight = jnp.dot(src_update[src_safe], tgt_update[tgt_safe].T, preferred_element_type=jnp.float32) / R
        kernel = jnp.where(src_labels[:, None] == tgt_labels[None, :], weight * jnp.exp((cosine - 1.0) / TEMPER), 0.0)
        denominator = lax.optimization_barrier(jnp.sum(kernel, axis=1, keepdims=True))
        denominator = jnp.where(denominator > 0, denominator, 1.0)
        transport = (kernel / denominator).astype(jnp.bfloat16)
        images = jnp.dot(transport, tgt_rows, preferred_element_type=jnp.float32).astype(jnp.bfloat16)
        result = result.at[jnp.where(src_ok, src_idx, POINTS)].set(images, mode='drop')
        return (result, None)
    mapped, _ = lax.scan(one_owner, jnp.zeros((POINTS, D), jnp.bfloat16), jnp.arange(DEVICES, dtype=jnp.int32))
    return (src_update, tgt_update, mapped)
```

```python
import math

import jax
import jax.numpy as jnp
from jax import lax
from jax.sharding import PartitionSpec as P

CL_DEV = 2

GAMMA = 2.0
TEMPER = 0.03
EPS = 1e-06

AXES = ("src", "tgt")


def contract_rows(left, right):
    return lax.dot_general(
        left, right, (((0,), (0,)), ((), ())), preferred_element_type=jnp.float32
    )


def mirror_step(points, total_round, factor, inner_marginal):
    gradient = (
        -jnp.dot(points, total_round, preferred_element_type=jnp.float32) / inner_marginal[None, :]
    )
    row_scale = jnp.max(jnp.abs(gradient), axis=1, keepdims=True) + EPS
    tilted = factor.astype(jnp.float32) * jnp.exp(-GAMMA * gradient / row_scale)
    return (tilted / jnp.mean(tilted, axis=1, keepdims=True)).astype(jnp.bfloat16)


def slots_of(cluster, n_dev, capacity):
    rows = cluster.shape[0]
    owners = cluster // CL_DEV
    onehot = (owners[:, None] == jnp.arange(n_dev, dtype=jnp.int32)[None, :]).astype(jnp.bfloat16)
    before = (jnp.arange(rows)[:, None] > jnp.arange(rows)[None, :]).astype(jnp.bfloat16)
    earlier = jnp.dot(before, onehot, preferred_element_type=jnp.float32)
    ranking = jnp.sum(earlier * onehot.astype(jnp.float32), axis=1).astype(jnp.int32)
    return owners * capacity + ranking


def pack_rows(points, factor, slot, buffer_len):
    place = (jnp.arange(buffer_len, dtype=jnp.int32)[:, None] == slot[None, :]).astype(jnp.bfloat16)
    rows = jnp.concatenate([points, factor], axis=1)
    return jnp.dot(place, rows, preferred_element_type=jnp.float32).astype(jnp.bfloat16)


def labels_of(clusters, me, capacity):
    n_dev, rows = clusters.shape
    mine = clusters // CL_DEV == me
    before = (jnp.arange(rows)[:, None] < jnp.arange(rows)[None, :]).astype(jnp.bfloat16)
    earlier = jnp.dot(mine.astype(jnp.bfloat16), before, preferred_element_type=jnp.float32)
    ranking = jnp.where(mine, earlier.astype(jnp.int32), -1)
    value = clusters - me * CL_DEV + 1
    hit = ranking[:, None, :] == jnp.arange(capacity, dtype=jnp.int32)[None, :, None]
    labels = jnp.sum(jnp.where(hit, value[:, None, :], 0), axis=2)
    return labels.reshape(n_dev * capacity)


def exchange(rows):
    return lax.all_to_all(rows, AXES, split_axis=0, concat_axis=0, tiled=True)


def owner_maps(src_rows, src_carried, src_labels, tgt_rows, tgt_carried, tgt_labels):
    factor_width = src_carried.shape[1]
    inv_src = lax.rsqrt(jnp.sum(jnp.square(src_rows.astype(jnp.float32)), axis=1) + EPS)
    inv_tgt = lax.rsqrt(jnp.sum(jnp.square(tgt_rows.astype(jnp.float32)), axis=1) + EPS)
    products = lax.dot_general(
        src_rows, tgt_rows, (((1,), (1,)), ((), ())), preferred_element_type=jnp.float32
    )
    cosine = products * inv_src[:, None] * inv_tgt[None, :]
    weight = (
        lax.dot_general(
            src_carried, tgt_carried, (((1,), (1,)), ((), ())), preferred_element_type=jnp.float32
        )
        / factor_width
    )
    same = jnp.logical_and(src_labels[:, None] == tgt_labels[None, :], src_labels[:, None] > 0)
    kernel = jnp.where(same, weight * jnp.exp((cosine - 1.0) / TEMPER), 0.0)
    denominator = jnp.sum(kernel, axis=1, keepdims=True)
    denominator = jnp.where(denominator > 0, denominator, 1.0)
    transport = (kernel / denominator).astype(jnp.bfloat16)
    return jnp.dot(transport, tgt_rows, preferred_element_type=jnp.float32).astype(jnp.bfloat16)


def per_device(
    src_points, tgt_points, src_factor, tgt_factor, inner_marginal, src_cluster, tgt_cluster
):
    n_dev = lax.axis_size("src") * lax.axis_size("tgt")
    capacity = 2 * src_points.shape[0] // n_dev
    buffer_len = n_dev * capacity
    features = src_points.shape[1]
    me = lax.axis_index(AXES)

    tgt_slot = slots_of(tgt_cluster, n_dev, capacity)
    src_slot = slots_of(src_cluster, n_dev, capacity)
    tgt_arrived = exchange(pack_rows(tgt_points, tgt_factor, tgt_slot, buffer_len))
    src_arrived = exchange(pack_rows(src_points, src_factor, src_slot, buffer_len))
    clusters = lax.all_gather(jnp.stack([src_cluster, tgt_cluster]), AXES, axis=0)
    src_labels = labels_of(clusters[:, 0], me, capacity)
    tgt_labels = labels_of(clusters[:, 1], me, capacity)

    parts = jnp.concatenate(
        [contract_rows(tgt_points, tgt_factor), contract_rows(src_points, src_factor)], axis=1
    )
    totals = lax.psum(parts, AXES).astype(jnp.bfloat16)
    rank = src_factor.shape[1]
    tgt_round = totals[:, :rank]
    src_round = totals[:, rank:]

    tgt_rows, tgt_seen = tgt_arrived[:, :features], tgt_arrived[:, features:]
    src_rows, src_seen = src_arrived[:, :features], src_arrived[:, features:]
    src_seen = jnp.where(src_labels[:, None] > 0, src_seen, jnp.bfloat16(1))
    tgt_seen = jnp.where(tgt_labels[:, None] > 0, tgt_seen, jnp.bfloat16(1))
    src_carried = mirror_step(src_rows, tgt_round, src_seen, inner_marginal)
    tgt_carried = mirror_step(tgt_rows, src_round, tgt_seen, inner_marginal)
    images = owner_maps(src_rows, src_carried, src_labels, tgt_rows, tgt_carried, tgt_labels)
    returned = exchange(images)

    src_update = mirror_step(src_points, tgt_round, src_factor, inner_marginal)
    tgt_update = mirror_step(tgt_points, src_round, tgt_factor, inner_marginal)
    back = (src_slot[:, None] == jnp.arange(buffer_len, dtype=jnp.int32)[None, :]).astype(jnp.bfloat16)
    mapped = jnp.dot(back, returned, preferred_element_type=jnp.float32).astype(jnp.bfloat16)
    return (src_update, tgt_update, mapped)


def solution(mesh):
    rows = P(AXES, None)
    return jax.shard_map(
        per_device,
        mesh=mesh,
        in_specs=(rows, rows, rows, rows, P(), P(AXES), P(AXES)),
        out_specs=(rows, rows, rows),
        check_vma=False,
    )
```

```python
import functools

import jax
import jax.numpy as jnp
from jax import lax
from jax.experimental import pallas as pl
from jax.experimental.pallas import tpu as pltpu
from jax.sharding import Mesh
from jax.sharding import PartitionSpec as P

CL_DEV = 2

GAMMA = 2.0
TEMPER = 0.03
EPS = 1e-06

HALF, REST = "half", "rest"
ALL = ("src", HALF, REST)
GROUP = ("src", REST)
VMEM_BYTES = 48 * 1024 * 1024


def contract_rows(left, right):
    return lax.dot_general(
        left, right, (((0,), (0,)), ((), ())), preferred_element_type=jnp.float32
    )


def contract_columns(left, right):
    return lax.dot_general(
        left, right, (((1,), (1,)), ((), ())), preferred_element_type=jnp.float32
    )


def mirror_step(points, total_round, factor, inner_marginal):
    gradient = -jnp.dot(points, total_round, preferred_element_type=jnp.float32) / inner_marginal
    row_scale = jnp.max(jnp.abs(gradient), axis=1, keepdims=True) + EPS
    tilted = factor.astype(jnp.float32) * jnp.exp(-GAMMA * gradient / row_scale)
    mean = jnp.mean(tilted, axis=1, keepdims=True)
    mean = jnp.where(mean > 0, mean, 1.0)
    return (tilted / mean).astype(jnp.bfloat16)


def inverse_norm(rows):
    return lax.rsqrt(jnp.sum(jnp.square(rows.astype(jnp.float32)), axis=1, keepdims=True) + EPS)


def slot_row(cluster, n_group, capacity, spread, first):
    rows = cluster.shape[1]
    owners = cluster // spread
    onehot = owners == lax.broadcasted_iota(jnp.int32, (n_group, rows), 0)
    before = lax.broadcasted_iota(jnp.int32, (rows, rows), 0) < lax.broadcasted_iota(
        jnp.int32, (rows, rows), 1
    )
    earlier = jnp.dot(
        onehot.astype(jnp.bfloat16), before.astype(jnp.bfloat16), preferred_element_type=jnp.float32
    )
    ranking = jnp.sum(jnp.where(onehot, earlier, 0.0), axis=0, keepdims=True).astype(jnp.int32)
    return owners * capacity + ranking + first


def pack_kernel(n_group, capacity, spread, n_kinds, *refs):
    out_ref = refs[-1]
    features = refs[1].shape[1]
    block = 512
    slots = []
    for kind in range(n_kinds):
        cluster_ref = refs[3 * kind]
        slots.append(
            slot_row(cluster_ref[...], n_group, n_kinds * capacity, spread, kind * capacity)
        )
    for start in range(0, out_ref.shape[0], block):
        moved = carried = None
        for kind in range(n_kinds):
            points_ref, factor_ref = refs[3 * kind + 1 : 3 * kind + 3]
            index = lax.broadcasted_iota(jnp.int32, (block, points_ref.shape[0]), 0) + start
            place = (index == slots[kind]).astype(jnp.bfloat16)
            rows = jnp.dot(place, points_ref[...], preferred_element_type=jnp.float32)
            extra = jnp.dot(place, factor_ref[...], preferred_element_type=jnp.float32)
            moved = rows if moved is None else moved + rows
            carried = extra if carried is None else carried + extra
        out_ref[pl.ds(start, block), :features] = moved.astype(jnp.bfloat16)
        out_ref[pl.ds(start, block), features:] = carried.astype(jnp.bfloat16)


def pack(kinds, n_group, capacity, spread):
    width = kinds[0][1].shape[1] + kinds[0][2].shape[1]
    operands = [array for cluster, points, factor in kinds for array in (cluster[None, :], points, factor)]
    return pl.pallas_call(
        functools.partial(pack_kernel, n_group, capacity, spread, len(kinds)),
        out_shape=jax.ShapeDtypeStruct((len(kinds) * n_group * capacity, width), jnp.bfloat16),
        compiler_params=pltpu.CompilerParams(vmem_limit_bytes=VMEM_BYTES),
        cost_estimate=pl.CostEstimate(
            flops=2 * len(kinds) * n_group * capacity * 256 * width * len(kinds),
            bytes_accessed=4 * n_group * capacity * width * len(kinds),
            transcendentals=0,
        ),
        name="pack_rows",
    )(*operands)


def owner_kernel(
    features,
    src_ref,
    near_ref,
    far_ref,
    src_total_ref,
    tgt_total_ref,
    marginal_ref,
    src_label_ref,
    tgt_label_ref,
    out_ref,
    tgt_rows,
    tgt_update,
    tgt_inv,
):
    slots = src_ref.shape[0] * src_ref.shape[1]
    width = src_ref.shape[2]
    rank = width - features
    block = 256
    marginal = marginal_ref[...]
    piece = block // src_ref.shape[1]

    for which, ref in enumerate((near_ref, far_ref)):
        for part in range(slots // block):
            start = which * slots + part * block
            both = ref[pl.ds(part * piece, piece)].reshape(block, width)
            rows = both[:, :features]
            tgt_rows[pl.ds(start, block), :] = rows
            tgt_update[pl.ds(start, block), :] = mirror_step(
                rows, src_total_ref[...], both[:, features:], marginal
            )
            tgt_inv[:, pl.ds(start, block)] = inverse_norm(rows).reshape(1, block)

    def one_block(part):
        both = src_ref[pl.ds(part * piece, piece)].reshape(block, width)
        rows = both[:, :features]
        update = mirror_step(rows, tgt_total_ref[...], both[:, features:], marginal)
        cosine = contract_columns(rows, tgt_rows[...]) * inverse_norm(rows) * tgt_inv[...]
        weight = contract_columns(update, tgt_update[...]) / rank
        label = src_label_ref[pl.ds(part * block, block), :]
        same = jnp.logical_and(label == tgt_label_ref[...], label > 0)
        kernel = jnp.where(same, weight * jnp.exp((cosine - 1.0) / TEMPER), 0.0)
        denominator = jnp.sum(kernel, axis=1, keepdims=True)
        denominator = jnp.where(denominator > 0, denominator, 1.0)
        transport = (kernel / denominator).astype(jnp.bfloat16)
        out_ref[pl.ds(part * block, block), :] = jnp.dot(
            transport, tgt_rows[...], preferred_element_type=jnp.float32
        ).astype(jnp.bfloat16)

    for part in range(slots // block):
        one_block(part)


def whole(shape):
    return pl.BlockSpec(shape, lambda step: (0,) * len(shape))


def owner_maps(
    near_seen, far_seen, src_total, tgt_total, marginal, src_labels, tgt_labels, features
):
    n_group, capacity, width = far_seen.shape
    slots = n_group * capacity
    rank = width - features
    return pl.pallas_call(
        functools.partial(owner_kernel, features),
        out_shape=jax.ShapeDtypeStruct((slots, features), jnp.bfloat16),
        grid=(1,),
        in_specs=[
            pl.BlockSpec((n_group, None, capacity, width), lambda step: (0, 1, 0, 0)),
            pl.BlockSpec((n_group, None, capacity, width), lambda step: (0, 0, 0, 0)),
            whole((n_group, capacity, width)),
            whole(src_total.shape),
            whole(tgt_total.shape),
            whole((1, rank)),
            whole((slots, 1)),
            whole((1, 2 * slots)),
        ],
        out_specs=whole((slots, features)),
        scratch_shapes=[
            pltpu.VMEM((2 * slots, features), jnp.bfloat16),
            pltpu.VMEM((2 * slots, rank), jnp.bfloat16),
            pltpu.VMEM((1, 2 * slots), jnp.float32),
        ],
        compiler_params=pltpu.CompilerParams(vmem_limit_bytes=VMEM_BYTES),
        cost_estimate=pl.CostEstimate(
            flops=2 * slots * features * (3 * rank + 4 * slots),
            bytes_accessed=8 * slots * width,
            transcendentals=2 * slots * slots,
        ),
        name="owner_maps",
    )(
        near_seen,
        near_seen,
        far_seen,
        src_total,
        tgt_total,
        marginal[None, :],
        src_labels[:, None],
        tgt_labels[None, :],
    )


def labels_of(clusters, owner, capacity, spread):
    rows = clusters.shape[1]
    mine = clusters // spread == owner
    before = (jnp.arange(rows)[:, None] < jnp.arange(rows)[None, :]).astype(jnp.bfloat16)
    earlier = jnp.dot(mine.astype(jnp.bfloat16), before, preferred_element_type=jnp.float32)
    ranking = jnp.where(mine, earlier.astype(jnp.int32), -1)
    value = clusters - owner * spread + 1
    hit = ranking[:, None, :] == jnp.arange(capacity, dtype=jnp.int32)[None, :, None]
    return jnp.sum(jnp.where(hit, value[:, None, :], 0), axis=2).reshape(-1)


def exchange(rows):
    return lax.all_to_all(rows, GROUP, split_axis=0, concat_axis=0, tiled=True)


def per_device(
    src_points, tgt_points, src_factor, tgt_factor, inner_marginal, src_cluster, tgt_cluster
):
    n_src, n_rest = lax.axis_size("src"), lax.axis_size(REST)
    n_group = n_src * n_rest
    n_dev = 2 * n_group
    rows, features = src_points.shape
    capacity = 2 * (2 * rows // n_dev)
    spread = 2 * CL_DEV
    slots = n_group * capacity
    my_half = lax.axis_index(HALF)
    owner = lax.axis_index(GROUP)

    across = [(0, 1), (1, 0)]
    far_cluster, far_points, far_factor = (
        lax.ppermute(array, HALF, across) for array in (tgt_cluster, tgt_points, tgt_factor)
    )
    near = exchange(
        pack(
            [(tgt_cluster, tgt_points, tgt_factor), (src_cluster, src_points, src_factor)],
            n_group,
            capacity,
            spread,
        )
    )

    place = lax.axis_index(ALL)
    mine = (jnp.arange(n_dev) == place)[:, None]
    table = jnp.concatenate([src_cluster, tgt_cluster]).astype(jnp.bfloat16)
    table = jnp.where(mine, table[None, :], jnp.bfloat16(0))
    rank = src_factor.shape[1]
    sums = lax.psum(
        jnp.concatenate(
            [
                contract_rows(tgt_points, tgt_factor).astype(jnp.bfloat16),
                contract_rows(src_points, src_factor).astype(jnp.bfloat16),
                table.reshape(-1, rank),
            ]
        ),
        ALL,
    )
    tgt_total, src_total = sums[:features], sums[features : 2 * features]
    table = sums[2 * features :]
    table = table.astype(jnp.int32).reshape(n_src, 2, n_rest, 2, rows)
    near_table = lax.dynamic_index_in_dim(table, my_half, 1, keepdims=False)
    far_table = lax.dynamic_index_in_dim(table, 1 - my_half, 1, keepdims=False)
    near_table = near_table.reshape(n_group, 2, rows)
    far_table = far_table.reshape(n_group, 2, rows)
    src_labels = labels_of(near_table[:, 0], owner, capacity, spread)
    tgt_labels = jnp.concatenate(
        [
            labels_of(near_table[:, 1], owner, capacity, spread),
            labels_of(far_table[:, 1], owner, capacity, spread),
        ]
    )

    far = exchange(pack([(far_cluster, far_points, far_factor)], n_group, capacity, spread))

    width = near.shape[1]
    near = near.reshape(n_group, 2, capacity, width)
    images = owner_maps(
        near,
        far.reshape(n_group, capacity, width),
        src_total,
        tgt_total,
        inner_marginal,
        src_labels,
        tgt_labels,
        features,
    )
    returned = exchange(images)

    marginal = inner_marginal[None, :]
    src_update = mirror_step(src_points, tgt_total, src_factor, marginal)
    tgt_update = mirror_step(tgt_points, src_total, tgt_factor, marginal)
    slot = slot_row(src_cluster[None, :], n_group, capacity, spread, 0)
    back = (jnp.arange(slots, dtype=jnp.int32)[:, None] == slot).astype(jnp.bfloat16)
    mapped = contract_rows(back, returned).astype(jnp.bfloat16)
    return (src_update, tgt_update, mapped)


def solution(mesh):
    n_src, n_tgt = mesh.shape["src"], mesh.shape["tgt"]
    halves = Mesh(mesh.devices.reshape(n_src, 2, n_tgt // 2), ALL)
    rows = P(ALL, None)
    return jax.shard_map(
        per_device,
        mesh=halves,
        in_specs=(rows, rows, rows, rows, P(), P(ALL), P(ALL)),
        out_specs=(rows, rows, rows),
        check_vma=False,
    )
```

```python
import functools

import jax
import jax.numpy as jnp
from jax import lax
from jax.experimental import pallas as pl
from jax.experimental.pallas import tpu as pltpu
from jax.sharding import PartitionSpec as P

CL_DEV = 2

GAMMA = 2.0
TEMPER = 0.03
EPS = 1e-06

AXES = ("src", "tgt")
VMEM_BYTES = 48 * 1024 * 1024


def contract_rows(left, right):
    return lax.dot_general(
        left, right, (((0,), (0,)), ((), ())), preferred_element_type=jnp.float32
    )


def contract_columns(left, right):
    return lax.dot_general(
        left, right, (((1,), (1,)), ((), ())), preferred_element_type=jnp.float32
    )


def mirror_step(points, total_round, factor, inner_marginal):
    gradient = -jnp.dot(points, total_round, preferred_element_type=jnp.float32) / inner_marginal
    row_scale = jnp.max(jnp.abs(gradient), axis=1, keepdims=True) + EPS
    tilted = factor.astype(jnp.float32) * jnp.exp(-GAMMA * gradient / row_scale)
    mean = jnp.mean(tilted, axis=1, keepdims=True)
    mean = jnp.where(mean > 0, mean, 1.0)
    return (tilted / mean).astype(jnp.bfloat16)


def inverse_norm(rows):
    return lax.rsqrt(jnp.sum(jnp.square(rows.astype(jnp.float32)), axis=1, keepdims=True) + EPS)


def slot_row(cluster, n_group, capacity, spread, first):
    rows = cluster.shape[1]
    owners = cluster // spread
    onehot = owners == lax.broadcasted_iota(jnp.int32, (n_group, rows), 0)
    before = lax.broadcasted_iota(jnp.int32, (rows, rows), 0) < lax.broadcasted_iota(
        jnp.int32, (rows, rows), 1
    )
    earlier = jnp.dot(
        onehot.astype(jnp.bfloat16), before.astype(jnp.bfloat16), preferred_element_type=jnp.float32
    )
    ranking = jnp.sum(jnp.where(onehot, earlier, 0.0), axis=0, keepdims=True).astype(jnp.int32)
    return owners * capacity + ranking + first


def pack_kernel(n_group, capacity, spread, n_kinds, *refs):
    out_ref = refs[-1]
    features = refs[1].shape[1]
    block = 512
    slots = []
    for kind in range(n_kinds):
        cluster_ref = refs[3 * kind]
        slots.append(
            slot_row(cluster_ref[...], n_group, n_kinds * capacity, spread, kind * capacity)
        )
    for start in range(0, out_ref.shape[0], block):
        moved = carried = None
        for kind in range(n_kinds):
            points_ref, factor_ref = refs[3 * kind + 1 : 3 * kind + 3]
            index = lax.broadcasted_iota(jnp.int32, (block, points_ref.shape[0]), 0) + start
            place = (index == slots[kind]).astype(jnp.bfloat16)
            rows = jnp.dot(place, points_ref[...], preferred_element_type=jnp.float32)
            extra = jnp.dot(place, factor_ref[...], preferred_element_type=jnp.float32)
            moved = rows if moved is None else moved + rows
            carried = extra if carried is None else carried + extra
        out_ref[pl.ds(start, block), :features] = moved.astype(jnp.bfloat16)
        out_ref[pl.ds(start, block), features:] = carried.astype(jnp.bfloat16)


def pack(kinds, n_group, capacity, spread):
    width = kinds[0][1].shape[1] + kinds[0][2].shape[1]
    operands = [array for cluster, points, factor in kinds for array in (cluster[None, :], points, factor)]
    return pl.pallas_call(
        functools.partial(pack_kernel, n_group, capacity, spread, len(kinds)),
        out_shape=jax.ShapeDtypeStruct((len(kinds) * n_group * capacity, width), jnp.bfloat16),
        compiler_params=pltpu.CompilerParams(vmem_limit_bytes=VMEM_BYTES),
        cost_estimate=pl.CostEstimate(
            flops=2 * len(kinds) * n_group * capacity * 256 * width * len(kinds),
            bytes_accessed=4 * n_group * capacity * width * len(kinds),
            transcendentals=0,
        ),
        name="pack_rows",
    )(*operands)


def owner_kernel(
    features,
    src_ref,
    tgt_ref,
    src_total_ref,
    tgt_total_ref,
    marginal_ref,
    src_label_ref,
    tgt_label_ref,
    out_ref,
    tgt_rows,
    tgt_update,
    tgt_inv,
):
    n_group, capacity, width = src_ref.shape
    slots = n_group * capacity
    rank = width - features
    block = 256
    marginal = marginal_ref[...]
    piece = block // capacity

    for part in range(slots // block):
        mine = pl.ds(part * block, block)
        both = tgt_ref[pl.ds(part * piece, piece)].reshape(block, width)
        rows = both[:, :features]
        tgt_rows[mine, :] = rows
        tgt_update[mine, :] = mirror_step(rows, src_total_ref[...], both[:, features:], marginal)
        tgt_inv[:, mine] = inverse_norm(rows).reshape(1, block)

    for part in range(slots // block):
        mine = pl.ds(part * block, block)
        both = src_ref[pl.ds(part * piece, piece)].reshape(block, width)
        rows = both[:, :features]
        update = mirror_step(rows, tgt_total_ref[...], both[:, features:], marginal)
        cosine = contract_columns(rows, tgt_rows[...]) * inverse_norm(rows) * tgt_inv[...]
        weight = contract_columns(update, tgt_update[...]) / rank
        label = src_label_ref[mine, :]
        same = jnp.logical_and(label == tgt_label_ref[...], label > 0)
        kernel = jnp.where(same, weight * jnp.exp((cosine - 1.0) / TEMPER), 0.0)
        denominator = jnp.sum(kernel, axis=1, keepdims=True)
        denominator = jnp.where(denominator > 0, denominator, 1.0)
        transport = (kernel / denominator).astype(jnp.bfloat16)
        out_ref[mine, :] = jnp.dot(
            transport, tgt_rows[...], preferred_element_type=jnp.float32
        ).astype(jnp.bfloat16)


def whole(shape):
    return pl.BlockSpec(shape, lambda step: (0,) * len(shape))


def owner_maps(seen, src_total, tgt_total, marginal, src_labels, tgt_labels, features):
    n_group, _, capacity, width = seen.shape
    slots = n_group * capacity
    rank = width - features
    return pl.pallas_call(
        functools.partial(owner_kernel, features),
        out_shape=jax.ShapeDtypeStruct((slots, features), jnp.bfloat16),
        grid=(1,),
        in_specs=[
            pl.BlockSpec((n_group, None, capacity, width), lambda step: (0, 1, 0, 0)),
            pl.BlockSpec((n_group, None, capacity, width), lambda step: (0, 0, 0, 0)),
            whole(src_total.shape),
            whole(tgt_total.shape),
            whole((1, rank)),
            whole((slots, 1)),
            whole((1, slots)),
        ],
        out_specs=whole((slots, features)),
        scratch_shapes=[
            pltpu.VMEM((slots, features), jnp.bfloat16),
            pltpu.VMEM((slots, rank), jnp.bfloat16),
            pltpu.VMEM((1, slots), jnp.float32),
        ],
        compiler_params=pltpu.CompilerParams(vmem_limit_bytes=VMEM_BYTES),
        cost_estimate=pl.CostEstimate(
            flops=2 * slots * features * (2 * rank + 2 * slots),
            bytes_accessed=6 * slots * width,
            transcendentals=slots * slots,
        ),
        name="owner_maps",
    )(
        seen,
        seen,
        src_total,
        tgt_total,
        marginal[None, :],
        src_labels[:, None],
        tgt_labels[None, :],
    )


def labels_of(clusters, owner, capacity, spread):
    rows = clusters.shape[1]
    mine = clusters // spread == owner
    before = (jnp.arange(rows)[:, None] < jnp.arange(rows)[None, :]).astype(jnp.bfloat16)
    earlier = jnp.dot(mine.astype(jnp.bfloat16), before, preferred_element_type=jnp.float32)
    ranking = jnp.where(mine, earlier.astype(jnp.int32), -1)
    value = clusters - owner * spread + 1
    hit = ranking[:, None, :] == jnp.arange(capacity, dtype=jnp.int32)[None, :, None]
    return jnp.sum(jnp.where(hit, value[:, None, :], 0), axis=2).reshape(-1)


def exchange(rows):
    return lax.all_to_all(rows, AXES, split_axis=0, concat_axis=0, tiled=True)


def per_device(
    src_points, tgt_points, src_factor, tgt_factor, inner_marginal, src_cluster, tgt_cluster
):
    n_dev = lax.axis_size("src") * lax.axis_size("tgt")
    rows, features = src_points.shape
    rank = src_factor.shape[1]
    capacity = 2 * rows // n_dev
    slots = n_dev * capacity
    owner = lax.axis_index(AXES)

    seen = exchange(
        pack(
            [(tgt_cluster, tgt_points, tgt_factor), (src_cluster, src_points, src_factor)],
            n_dev,
            capacity,
            CL_DEV,
        )
    ).reshape(n_dev, 2, capacity, features + rank)

    mine = (jnp.arange(n_dev) == owner)[:, None]
    table = jnp.concatenate([src_cluster, tgt_cluster]).astype(jnp.float32)
    table = jnp.where(mine, table[None, :], 0.0)
    sums = lax.psum(
        jnp.concatenate(
            [
                contract_rows(tgt_points, tgt_factor),
                contract_rows(src_points, src_factor),
                table.reshape(-1, rank),
            ]
        ),
        AXES,
    ).astype(jnp.bfloat16)
    tgt_total, src_total = sums[:features], sums[features : 2 * features]
    table = sums[2 * features :].astype(jnp.int32).reshape(n_dev, 2, rows)
    src_labels = labels_of(table[:, 0], owner, capacity, CL_DEV)
    tgt_labels = labels_of(table[:, 1], owner, capacity, CL_DEV)

    images = owner_maps(
        seen, src_total, tgt_total, inner_marginal, src_labels, tgt_labels, features
    )
    returned = exchange(images)

    marginal = inner_marginal[None, :]
    src_update = mirror_step(src_points, tgt_total, src_factor, marginal)
    tgt_update = mirror_step(tgt_points, src_total, tgt_factor, marginal)
    slot = slot_row(src_cluster[None, :], n_dev, capacity, CL_DEV, 0)
    back = (jnp.arange(slots, dtype=jnp.int32)[:, None] == slot).astype(jnp.bfloat16)
    mapped = contract_rows(back, returned).astype(jnp.bfloat16)
    return (src_update, tgt_update, mapped)


def solution(mesh):
    rows = P(AXES, None)
    return jax.shard_map(
        per_device,
        mesh=mesh,
        in_specs=(rows, rows, rows, rows, P(), P(AXES), P(AXES)),
        out_specs=(rows, rows, rows),
        check_vma=False,
    )
```

```python
import functools

import jax
import jax.numpy as jnp
from jax import lax
from jax.experimental import pallas as pl
from jax.experimental.pallas import tpu as pltpu
from jax.sharding import PartitionSpec as P

CL_DEV = 2

GAMMA = 2.0
TEMPER = 0.03
EPS = 1e-06

AXES = ("src", "tgt")
VMEM_BYTES = 48 * 1024 * 1024
TABLE_ROWS = 16


def contract_rows(left, right):
    return lax.dot_general(
        left, right, (((0,), (0,)), ((), ())), preferred_element_type=jnp.float32
    )


def contract_columns(left, right):
    return lax.dot_general(
        left, right, (((1,), (1,)), ((), ())), preferred_element_type=jnp.float32
    )


def mirror_step(points, total_round, factor, inner_marginal):
    gradient = -jnp.dot(points, total_round, preferred_element_type=jnp.float32) / inner_marginal
    row_scale = jnp.max(jnp.abs(gradient), axis=1, keepdims=True) + EPS
    tilted = factor.astype(jnp.float32) * jnp.exp(-GAMMA * gradient / row_scale)
    mean = jnp.mean(tilted, axis=1, keepdims=True)
    mean = jnp.where(mean > 0, mean, 1.0)
    return (tilted / mean).astype(jnp.bfloat16)


def inverse_norm(rows):
    return lax.rsqrt(jnp.sum(jnp.square(rows.astype(jnp.float32)), axis=1, keepdims=True) + EPS)


def totals_of(sums_ref):
    n_dev, chunk, rank = sums_ref.shape
    kept = chunk - TABLE_ROWS
    both = sums_ref[:, :kept, :]
    half = n_dev // 2
    return both[:half].reshape(half * kept, rank), both[half:].reshape(half * kept, rank)


def whole(shape):
    return pl.BlockSpec(shape, lambda *_: (0,) * len(shape))


def in_hbm():
    return pl.BlockSpec(memory_space=pltpu.HBM)


def slot_row(cluster, n_group, capacity, spread, first):
    rows = cluster.shape[1]
    owners = cluster // spread
    onehot = owners == lax.broadcasted_iota(jnp.int32, (n_group, rows), 0)
    before = lax.broadcasted_iota(jnp.int32, (rows, rows), 0) < lax.broadcasted_iota(
        jnp.int32, (rows, rows), 1
    )
    earlier = jnp.dot(
        onehot.astype(jnp.bfloat16), before.astype(jnp.bfloat16), preferred_element_type=jnp.float32
    )
    ranking = jnp.sum(jnp.where(onehot, earlier, 0.0), axis=0, keepdims=True).astype(jnp.int32)
    return owners * capacity + ranking + first


def pack_kernel(
    n_dev,
    capacity,
    me_ref,
    src_cluster_ref,
    tgt_cluster_ref,
    table_ref,
    src_points_hbm,
    tgt_points_hbm,
    src_factor_hbm,
    tgt_factor_hbm,
    packed_hbm,
    parts_ref,
    src_points,
    tgt_points,
    src_factor,
    tgt_factor,
    packed,
    in_sem,
    out_sem,
):
    pairs = [
        (tgt_points_hbm, tgt_points),
        (tgt_factor_hbm, tgt_factor),
        (src_points_hbm, src_points),
        (src_factor_hbm, src_factor),
    ]
    arrivals = [pltpu.make_async_copy(a, b, in_sem.at[i]) for i, (a, b) in enumerate(pairs)]
    for copy in arrivals:
        copy.start()
    features = tgt_points.shape[1]
    tgt_slot = slot_row(tgt_cluster_ref[...], n_dev, 2 * capacity, CL_DEV, 0)
    src_slot = slot_row(src_cluster_ref[...], n_dev, 2 * capacity, CL_DEV, capacity)
    for copy in arrivals:
        copy.wait()

    block = 256
    departures = []
    for part in range(packed.shape[0] // block):
        mine = pl.ds(part * block, block)
        index = lax.broadcasted_iota(jnp.int32, (block, tgt_points.shape[0]), 0) + part * block
        tgt_place = (index == tgt_slot).astype(jnp.bfloat16)
        src_place = (index == src_slot).astype(jnp.bfloat16)
        packed[mine, :features] = (
            jnp.dot(tgt_place, tgt_points[...], preferred_element_type=jnp.float32)
            + jnp.dot(src_place, src_points[...], preferred_element_type=jnp.float32)
        ).astype(jnp.bfloat16)
        packed[mine, features:] = (
            jnp.dot(tgt_place, tgt_factor[...], preferred_element_type=jnp.float32)
            + jnp.dot(src_place, src_factor[...], preferred_element_type=jnp.float32)
        ).astype(jnp.bfloat16)
        departures.append(
            pltpu.make_async_copy(packed.at[mine], packed_hbm.at[mine], out_sem.at[part])
        )
        departures[-1].start()

    _, chunk, rank = parts_ref.shape
    kept = chunk - TABLE_ROWS
    half = n_dev // 2
    parts_ref[:half, :kept, :] = (
        contract_rows(tgt_points[...], tgt_factor[...]).astype(jnp.bfloat16).reshape(half, kept, rank)
    )
    parts_ref[half:, :kept, :] = (
        contract_rows(src_points[...], src_factor[...]).astype(jnp.bfloat16).reshape(half, kept, rank)
    )
    chunk_id = lax.broadcasted_iota(jnp.int32, (n_dev, TABLE_ROWS, rank), 0)
    table = jnp.where(chunk_id == me_ref[0], table_ref[...][None], 0.0)
    parts_ref[:, kept:, :] = table.astype(jnp.bfloat16)
    for copy in departures:
        copy.wait()


def pack(me, src_cluster, tgt_cluster, src_points, tgt_points, src_factor, tgt_factor, n_dev, capacity):
    rows, features = src_points.shape
    rank = src_factor.shape[1]
    slots = 2 * n_dev * capacity
    chunk = 2 * features // n_dev + TABLE_ROWS
    table = jnp.concatenate([src_cluster, tgt_cluster]).astype(jnp.float32).reshape(-1, rank)
    table = jnp.pad(table, ((0, TABLE_ROWS - table.shape[0]), (0, 0)))
    return pl.pallas_call(
        functools.partial(pack_kernel, n_dev, capacity),
        out_shape=(
            jax.ShapeDtypeStruct((slots, features + rank), jnp.bfloat16),
            jax.ShapeDtypeStruct((n_dev, chunk, rank), jnp.bfloat16),
        ),
        in_specs=[
            pl.BlockSpec(memory_space=pltpu.SMEM),
            pl.BlockSpec(memory_space=pltpu.VMEM),
            pl.BlockSpec(memory_space=pltpu.VMEM),
            pl.BlockSpec(memory_space=pltpu.VMEM),
            in_hbm(),
            in_hbm(),
            in_hbm(),
            in_hbm(),
        ],
        out_specs=(in_hbm(), pl.BlockSpec(memory_space=pltpu.VMEM)),
        scratch_shapes=[
            pltpu.VMEM((rows, features), jnp.bfloat16),
            pltpu.VMEM((rows, features), jnp.bfloat16),
            pltpu.VMEM((rows, rank), jnp.bfloat16),
            pltpu.VMEM((rows, rank), jnp.bfloat16),
            pltpu.VMEM((slots, features + rank), jnp.bfloat16),
            pltpu.SemaphoreType.DMA((4,)),
            pltpu.SemaphoreType.DMA((slots // 256,)),
        ],
        compiler_params=pltpu.CompilerParams(vmem_limit_bytes=VMEM_BYTES),
        cost_estimate=pl.CostEstimate(
            flops=4 * slots * rows * (features + rank),
            bytes_accessed=4 * (slots + rows) * (features + rank),
            transcendentals=0,
        ),
        name="pack_rows",
    )(
        me[None],
        src_cluster[None, :],
        tgt_cluster[None, :],
        table,
        src_points,
        tgt_points,
        src_factor,
        tgt_factor,
    )


def digits_of(axis):
    size = lax.axis_size(axis)
    bits = size.bit_length() - 1
    found, stride = [], 1
    while bits:
        take = 1 if bits % 2 else 2
        found.append((axis, stride, 1 << take))
        stride <<= take
        bits -= take
    return found


def sum_over_devices(parts):
    low_first = [digits_of(axis) for axis in AXES]
    dims = [digit for digits in low_first for digit in reversed(digits)]
    order = [digit for digits in low_first for digit in digits]
    x = parts.reshape(tuple(radix for _, _, radix in dims) + parts.shape[1:])

    def sent(array, axis, stride, j):
        pairs = [(i, i ^ (j * stride)) for i in range(lax.axis_size(axis))]
        return lax.ppermute(array, axis, pairs)

    left = list(dims)
    for digit in order:
        axis, stride, radix = digit
        dim = left.index(digit)
        mine = (lax.axis_index(axis) // stride) % radix
        total = lax.dynamic_index_in_dim(x, mine, dim, keepdims=False).astype(jnp.float32)
        for j in range(1, radix):
            piece = lax.dynamic_index_in_dim(x, mine ^ j, dim, keepdims=False)
            total = total + sent(piece, axis, stride, j).astype(jnp.float32)
        x = total.astype(jnp.bfloat16)
        left.remove(digit)
    for digit in reversed(order):
        axis, stride, radix = digit
        mine = (lax.axis_index(axis) // stride) % radix
        got = [x] + [sent(x, axis, stride, j) for j in range(1, radix)]
        kept = [d for d in dims if d in left or d == digit]
        dim = kept.index(digit)
        x = jnp.stack(
            [lax.select_n(mine ^ d, *got) if radix > 2 else jnp.where(mine == d, *got) for d in range(radix)],
            axis=dim,
        )
        left = kept
    return x.reshape(parts.shape)


def update_kernel(
    src_points_ref, tgt_points_ref, src_factor_ref, tgt_factor_ref, marginal_ref, sums_ref, src_ref, tgt_ref
):
    tgt_total, src_total = totals_of(sums_ref)
    src_ref[...] = mirror_step(src_points_ref[...], tgt_total, src_factor_ref[...], marginal_ref[...])
    tgt_ref[...] = mirror_step(tgt_points_ref[...], src_total, tgt_factor_ref[...], marginal_ref[...])


def updates(src_points, tgt_points, src_factor, tgt_factor, marginal, sums):
    rows, features = src_points.shape
    rank = src_factor.shape[1]
    shape = jax.ShapeDtypeStruct(src_factor.shape, jnp.bfloat16)
    return pl.pallas_call(
        update_kernel,
        out_shape=(shape, shape),
        compiler_params=pltpu.CompilerParams(vmem_limit_bytes=VMEM_BYTES),
        cost_estimate=pl.CostEstimate(
            flops=4 * rows * features * rank,
            bytes_accessed=4 * rows * (features + 2 * rank),
            transcendentals=2 * rows * rank,
        ),
        name="mirror_updates",
    )(src_points, tgt_points, src_factor, tgt_factor, marginal[None, :], sums)


def owner_kernel(
    features,
    src_ref,
    tgt_ref,
    sums_ref,
    marginal_ref,
    src_label_ref,
    tgt_label_ref,
    out_hbm,
    tgt_rows,
    tgt_update,
    tgt_inv,
    images,
    out_sem,
):
    n_group, capacity, width = src_ref.shape
    slots = n_group * capacity
    rank = width - features
    block = 256
    marginal = marginal_ref[...]
    piece = block // capacity
    tgt_total, src_total = totals_of(sums_ref)

    for part in range(slots // block):
        mine = pl.ds(part * block, block)
        both = tgt_ref[pl.ds(part * piece, piece)].reshape(block, width)
        rows = both[:, :features]
        tgt_rows[mine, :] = rows
        tgt_update[mine, :] = mirror_step(rows, src_total, both[:, features:], marginal)
        tgt_inv[:, mine] = inverse_norm(rows).reshape(1, block)

    departures = []
    for part in range(slots // block):
        mine = pl.ds(part * block, block)
        both = src_ref[pl.ds(part * piece, piece)].reshape(block, width)
        rows = both[:, :features]
        update = mirror_step(rows, tgt_total, both[:, features:], marginal)
        cosine = contract_columns(rows, tgt_rows[...]) * inverse_norm(rows) * tgt_inv[...]
        weight = contract_columns(update, tgt_update[...]) / rank
        label = src_label_ref[mine, :]
        same = jnp.logical_and(label == tgt_label_ref[...], label > 0)
        kernel = jnp.where(same, weight * jnp.exp((cosine - 1.0) / TEMPER), 0.0)
        denominator = jnp.sum(kernel, axis=1, keepdims=True)
        denominator = jnp.where(denominator > 0, denominator, 1.0)
        transport = (kernel / denominator).astype(jnp.bfloat16)
        images[mine, :] = jnp.dot(
            transport, tgt_rows[...], preferred_element_type=jnp.float32
        ).astype(jnp.bfloat16)
        departures.append(
            pltpu.make_async_copy(images.at[mine], out_hbm.at[mine], out_sem.at[part])
        )
        departures[-1].start()
    for copy in departures:
        copy.wait()


def owner_maps(seen, sums, marginal, src_labels, tgt_labels, features):
    n_group, _, capacity, width = seen.shape
    slots = n_group * capacity
    rank = width - features
    return pl.pallas_call(
        functools.partial(owner_kernel, features),
        out_shape=jax.ShapeDtypeStruct((slots, features), jnp.bfloat16),
        grid=(1,),
        in_specs=[
            pl.BlockSpec((n_group, None, capacity, width), lambda step: (0, 1, 0, 0)),
            pl.BlockSpec((n_group, None, capacity, width), lambda step: (0, 0, 0, 0)),
            whole(sums.shape),
            whole((1, rank)),
            whole((slots, 1)),
            whole((1, slots)),
        ],
        out_specs=in_hbm(),
        scratch_shapes=[
            pltpu.VMEM((slots, features), jnp.bfloat16),
            pltpu.VMEM((slots, rank), jnp.bfloat16),
            pltpu.VMEM((1, slots), jnp.float32),
            pltpu.VMEM((slots, features), jnp.bfloat16),
            pltpu.SemaphoreType.DMA((slots // 256,)),
        ],
        compiler_params=pltpu.CompilerParams(vmem_limit_bytes=VMEM_BYTES),
        cost_estimate=pl.CostEstimate(
            flops=2 * slots * features * (2 * rank + 2 * slots),
            bytes_accessed=6 * slots * width,
            transcendentals=slots * slots,
        ),
        name="owner_maps",
    )(
        seen,
        seen,
        sums,
        marginal[None, :],
        src_labels[:, None],
        tgt_labels[None, :],
    )


def labels_of(clusters, owner, capacity, spread):
    rows = clusters.shape[1]
    mine = clusters // spread == owner
    before = (jnp.arange(rows)[:, None] < jnp.arange(rows)[None, :]).astype(jnp.bfloat16)
    earlier = jnp.dot(mine.astype(jnp.bfloat16), before, preferred_element_type=jnp.float32)
    ranking = jnp.where(mine, earlier.astype(jnp.int32), -1)
    value = clusters - owner * spread + 1
    hit = ranking[:, None, :] == jnp.arange(capacity, dtype=jnp.int32)[None, :, None]
    return jnp.sum(jnp.where(hit, value[:, None, :], 0), axis=2).reshape(-1)


def exchange(rows):
    return lax.all_to_all(rows, AXES, split_axis=0, concat_axis=0, tiled=True)


def per_device(
    src_points, tgt_points, src_factor, tgt_factor, inner_marginal, src_cluster, tgt_cluster
):
    n_dev = lax.axis_size("src") * lax.axis_size("tgt")
    rows, features = src_points.shape
    rank = src_factor.shape[1]
    capacity = 2 * rows // n_dev
    slots = n_dev * capacity
    owner = lax.axis_index(AXES)

    packed, parts = pack(
        owner, src_cluster, tgt_cluster, src_points, tgt_points, src_factor, tgt_factor, n_dev, capacity
    )
    seen = exchange(packed).reshape(n_dev, 2, capacity, features + rank)

    sums = sum_over_devices(parts)
    kept = 2 * features // n_dev
    table = sums[:, kept : kept + 2 * rows // rank].astype(jnp.int32).reshape(n_dev, 2, rows)
    src_labels = labels_of(table[:, 0], owner, capacity, CL_DEV)
    tgt_labels = labels_of(table[:, 1], owner, capacity, CL_DEV)

    images = owner_maps(seen, sums, inner_marginal, src_labels, tgt_labels, features)
    returned = exchange(images)

    src_update, tgt_update = updates(
        src_points, tgt_points, src_factor, tgt_factor, inner_marginal, sums
    )
    slot = slot_row(src_cluster[None, :], n_dev, capacity, CL_DEV, 0)
    back = (jnp.arange(slots, dtype=jnp.int32)[:, None] == slot).astype(jnp.bfloat16)
    mapped = contract_rows(back, returned).astype(jnp.bfloat16)
    return (src_update, tgt_update, mapped)


def solution(mesh):
    rows = P(AXES, None)
    return jax.shard_map(
        per_device,
        mesh=mesh,
        in_specs=(rows, rows, rows, rows, P(), P(AXES), P(AXES)),
        out_specs=(rows, rows, rows),
        check_vma=False,
    )
```

```python
import functools

import jax
import jax.numpy as jnp
from jax import lax
from jax.experimental import pallas as pl
from jax.experimental.pallas import tpu as pltpu
from jax.sharding import PartitionSpec as P

CL_DEV = 2

GAMMA = 2.0
TEMPER = 0.03
EPS = 1e-06

AXES = ("src", "tgt")
VMEM_BYTES = 48 * 1024 * 1024
PACK_VMEM_BYTES = 62 * 1024 * 1024
TABLE_ROWS = 16


def contract_rows(left, right):
    return lax.dot_general(
        left, right, (((0,), (0,)), ((), ())), preferred_element_type=jnp.float32
    )


def contract_columns(left, right):
    return lax.dot_general(
        left, right, (((1,), (1,)), ((), ())), preferred_element_type=jnp.float32
    )


def mirror_step(points, total_round, factor, inner_marginal):
    gradient = -jnp.dot(points, total_round, preferred_element_type=jnp.float32) / inner_marginal
    row_scale = jnp.max(jnp.abs(gradient), axis=1, keepdims=True) + EPS
    tilted = factor.astype(jnp.float32) * jnp.exp(-GAMMA * gradient / row_scale)
    mean = jnp.mean(tilted, axis=1, keepdims=True)
    mean = jnp.where(mean > 0, mean, 1.0)
    return (tilted / mean).astype(jnp.bfloat16)


def inverse_norm(rows):
    return lax.rsqrt(jnp.sum(jnp.square(rows.astype(jnp.float32)), axis=1, keepdims=True) + EPS)


def totals_of(sums_ref):
    n_dev, chunk, rank = sums_ref.shape
    kept = chunk - TABLE_ROWS
    both = sums_ref[:, :kept, :]
    half = n_dev // 2
    return both[:half].reshape(half * kept, rank), both[half:].reshape(half * kept, rank)


def whole(shape):
    return pl.BlockSpec(shape, lambda *_: (0,) * len(shape))


def in_hbm():
    return pl.BlockSpec(memory_space=pltpu.HBM)


def slot_row(cluster, n_group, capacity, spread, first, me):
    rows = cluster.shape[1]
    owners = cluster // spread
    onehot = owners == lax.broadcasted_iota(jnp.int32, (n_group, rows), 0)
    before = lax.broadcasted_iota(jnp.int32, (rows, rows), 0) < lax.broadcasted_iota(
        jnp.int32, (rows, rows), 1
    )
    earlier = jnp.dot(
        onehot.astype(jnp.bfloat16), before.astype(jnp.bfloat16), preferred_element_type=jnp.float32
    )
    ranking = jnp.sum(jnp.where(onehot, earlier, 0.0), axis=0, keepdims=True).astype(jnp.int32)
    return (owners ^ me) * capacity + ranking + first


def pack_kernel(n_dev, capacity, *refs):
    me_ref, src_cluster_ref, tgt_cluster_ref, table_ref = refs[:4]
    hbm = refs[4:8]
    pieces = refs[8 : 8 + n_dev]
    parts_ref = refs[8 + n_dev]
    src_points, tgt_points, src_factor, tgt_factor, in_sem = refs[9 + n_dev :]
    held = (src_points, tgt_points, src_factor, tgt_factor)
    arrivals = [pltpu.make_async_copy(a, b, in_sem.at[i]) for i, (a, b) in enumerate(zip(hbm, held))]
    for copy in arrivals:
        copy.start()
    features = tgt_points.shape[1]
    me = me_ref[0]
    tgt_slot = slot_row(tgt_cluster_ref[...], n_dev, 2 * capacity, CL_DEV, 0, me)
    src_slot = slot_row(src_cluster_ref[...], n_dev, 2 * capacity, CL_DEV, capacity, me)
    for copy in arrivals:
        copy.wait()

    _, chunk, rank = parts_ref.shape
    kept = chunk - TABLE_ROWS
    half = n_dev // 2
    parts_ref[:half, :kept, :] = (
        contract_rows(tgt_points[...], tgt_factor[...]).astype(jnp.bfloat16).reshape(half, kept, rank)
    )
    parts_ref[half:, :kept, :] = (
        contract_rows(src_points[...], src_factor[...]).astype(jnp.bfloat16).reshape(half, kept, rank)
    )
    chunk_id = lax.broadcasted_iota(jnp.int32, (n_dev, TABLE_ROWS, rank), 0)
    table = jnp.where(chunk_id == me, table_ref[...][None], 0.0)
    parts_ref[:, kept:, :] = table.astype(jnp.bfloat16)

    piece = 2 * capacity
    block = 256
    for part in range(n_dev * piece // block):
        index = lax.broadcasted_iota(jnp.int32, (block, tgt_points.shape[0]), 0) + part * block
        tgt_place = (index == tgt_slot).astype(jnp.bfloat16)
        src_place = (index == src_slot).astype(jnp.bfloat16)
        rows = (
            jnp.dot(tgt_place, tgt_points[...], preferred_element_type=jnp.float32)
            + jnp.dot(src_place, src_points[...], preferred_element_type=jnp.float32)
        ).astype(jnp.bfloat16)
        carried = (
            jnp.dot(tgt_place, tgt_factor[...], preferred_element_type=jnp.float32)
            + jnp.dot(src_place, src_factor[...], preferred_element_type=jnp.float32)
        ).astype(jnp.bfloat16)
        for i in range(block // piece):
            out = pieces[part * (block // piece) + i]
            out[:, :features] = rows[i * piece : (i + 1) * piece]
            out[:, features:] = carried[i * piece : (i + 1) * piece]


def pack(me, src_cluster, tgt_cluster, src_points, tgt_points, src_factor, tgt_factor, n_dev, capacity):
    rows, features = src_points.shape
    rank = src_factor.shape[1]
    slots = 2 * n_dev * capacity
    chunk = 2 * features // n_dev + TABLE_ROWS
    table = jnp.concatenate([src_cluster, tgt_cluster]).astype(jnp.float32).reshape(-1, rank)
    table = jnp.pad(table, ((0, TABLE_ROWS - table.shape[0]), (0, 0)))
    vmem = pl.BlockSpec(memory_space=pltpu.VMEM)
    piece = jax.ShapeDtypeStruct((2 * capacity, features + rank), jnp.bfloat16)
    *pieces, parts = pl.pallas_call(
        functools.partial(pack_kernel, n_dev, capacity),
        out_shape=[piece] * n_dev + [jax.ShapeDtypeStruct((n_dev, chunk, rank), jnp.bfloat16)],
        in_specs=[pl.BlockSpec(memory_space=pltpu.SMEM)] + [vmem] * 3 + [in_hbm()] * 4,
        out_specs=[vmem] * (n_dev + 1),
        scratch_shapes=[
            pltpu.VMEM((rows, features), jnp.bfloat16),
            pltpu.VMEM((rows, features), jnp.bfloat16),
            pltpu.VMEM((rows, rank), jnp.bfloat16),
            pltpu.VMEM((rows, rank), jnp.bfloat16),
            pltpu.SemaphoreType.DMA((4,)),
        ],
        compiler_params=pltpu.CompilerParams(vmem_limit_bytes=PACK_VMEM_BYTES),
        cost_estimate=pl.CostEstimate(
            flops=4 * slots * rows * (features + rank),
            bytes_accessed=4 * (slots + rows) * (features + rank),
            transcendentals=0,
        ),
        name="pack_rows",
    )(
        me[None],
        src_cluster[None, :],
        tgt_cluster[None, :],
        table,
        src_points,
        tgt_points,
        src_factor,
        tgt_factor,
    )
    return pieces, parts


def digits_of(axis):
    size = lax.axis_size(axis)
    bits = size.bit_length() - 1
    found, stride = [], 1
    while bits:
        take = 1 if bits % 2 else 2
        found.append((axis, stride, 1 << take))
        stride <<= take
        bits -= take
    return found


def partner_pairs(size, mask):
    return [(i, i ^ mask) for i in range(size)]


def dealt(masks, hands):
    half = lax.axis_size("tgt") // 2
    far = [m for m in masks if m & half]
    near = [m for m in masks if not m & half]
    mixed = [m for pair in zip(far, near) for m in pair]
    mixed += far[len(near) :] + near[len(far) :]
    return [mixed[len(mixed) * h // hands : len(mixed) * (h + 1) // hands] for h in range(hands)]


def sum_and_swap(parts, pieces):
    low_first = [digits_of(axis) for axis in AXES]
    dims = [digit for digits in low_first for digit in reversed(digits)]
    order = [digit for digits in low_first for digit in digits]
    hands = dealt(range(1, len(pieces)), 2 * len(order))
    got_pieces = [pieces[0]] + [None] * (len(pieces) - 1)

    def sent(array, axis, stride, j):
        return lax.ppermute(array, axis, partner_pairs(lax.axis_size(axis), j * stride))

    def let_go(x, step):
        hand = hands[step]
        x, held = lax.optimization_barrier((x, [pieces[m] for m in hand]))
        for m, piece in zip(hand, held):
            got_pieces[m] = lax.ppermute(piece, AXES, partner_pairs(len(pieces), m))
        return x

    x = parts.reshape(tuple(radix for _, _, radix in dims) + parts.shape[1:])
    left = list(dims)
    step = 0
    for digit in order:
        axis, stride, radix = digit
        dim = left.index(digit)
        mine = (lax.axis_index(axis) // stride) % radix
        x = let_go(x, step)
        step += 1
        total = lax.dynamic_index_in_dim(x, mine, dim, keepdims=False).astype(jnp.float32)
        for j in range(1, radix):
            piece = lax.dynamic_index_in_dim(x, mine ^ j, dim, keepdims=False)
            total = total + sent(piece, axis, stride, j).astype(jnp.float32)
        x = total.astype(jnp.bfloat16)
        left.remove(digit)
    for digit in reversed(order):
        axis, stride, radix = digit
        mine = (lax.axis_index(axis) // stride) % radix
        x = let_go(x, step)
        step += 1
        got = [x] + [sent(x, axis, stride, j) for j in range(1, radix)]
        kept = [d for d in dims if d in left or d == digit]
        dim = kept.index(digit)
        x = jnp.stack(
            [lax.select_n(mine ^ d, *got) if radix > 2 else jnp.where(mine == d, *got) for d in range(radix)],
            axis=dim,
        )
        left = kept
    return x.reshape(parts.shape), got_pieces


def update_kernel(
    src_points_ref, tgt_points_ref, src_factor_ref, tgt_factor_ref, marginal_ref, sums_ref, src_ref, tgt_ref
):
    tgt_total, src_total = totals_of(sums_ref)
    src_ref[...] = mirror_step(src_points_ref[...], tgt_total, src_factor_ref[...], marginal_ref[...])
    tgt_ref[...] = mirror_step(tgt_points_ref[...], src_total, tgt_factor_ref[...], marginal_ref[...])


def updates(src_points, tgt_points, src_factor, tgt_factor, marginal, sums):
    rows, features = src_points.shape
    rank = src_factor.shape[1]
    shape = jax.ShapeDtypeStruct(src_factor.shape, jnp.bfloat16)
    return pl.pallas_call(
        update_kernel,
        out_shape=(shape, shape),
        compiler_params=pltpu.CompilerParams(vmem_limit_bytes=VMEM_BYTES),
        cost_estimate=pl.CostEstimate(
            flops=4 * rows * features * rank,
            bytes_accessed=4 * rows * (features + 2 * rank),
            transcendentals=2 * rows * rank,
        ),
        name="mirror_updates",
    )(src_points, tgt_points, src_factor, tgt_factor, marginal[None, :], sums)


def owner_kernel(n_dev, features, *refs):
    pieces = refs[:n_dev]
    me_ref, sums_ref, marginal_ref, src_label_ref, tgt_label_ref, out_hbm = refs[n_dev : n_dev + 6]
    src_seen, tgt_seen, tgt_update, tgt_inv, images, out_sem = refs[n_dev + 6 :]
    capacity = pieces[0].shape[0] // 2
    slots, width = src_seen.shape
    rank = width - features
    block = 256
    marginal = marginal_ref[...]
    tgt_total, src_total = totals_of(sums_ref)
    me = me_ref[0]

    for m, ref in enumerate(pieces):
        tgt_seen[pl.ds(m * capacity, capacity), :] = ref[:capacity, :]
        src_seen[pl.ds(m * capacity, capacity), :] = ref[capacity:, :]

    for part in range(slots // block):
        mine = pl.ds(part * block, block)
        rows = tgt_seen[mine, :features]
        tgt_update[mine, :] = mirror_step(rows, src_total, tgt_seen[mine, features:], marginal)
        tgt_inv[:, mine] = inverse_norm(rows).reshape(1, block)

    departures = []
    for part in range(slots // block):
        mine = pl.ds(part * block, block)
        rows = src_seen[mine, :features]
        update = mirror_step(rows, tgt_total, src_seen[mine, features:], marginal)
        cosine = contract_columns(rows, tgt_seen[:, :features]) * inverse_norm(rows) * tgt_inv[...]
        weight = contract_columns(update, tgt_update[...]) / rank
        label = src_label_ref[mine, :]
        same = jnp.logical_and(label == tgt_label_ref[...], label > 0)
        kernel = jnp.where(same, weight * jnp.exp((cosine - 1.0) / TEMPER), 0.0)
        denominator = jnp.sum(kernel, axis=1, keepdims=True)
        denominator = jnp.where(denominator > 0, denominator, 1.0)
        transport = (kernel / denominator).astype(jnp.bfloat16)
        images[mine, :] = jnp.dot(
            transport, tgt_seen[:, :features], preferred_element_type=jnp.float32
        ).astype(jnp.bfloat16)
        for m in range(part * block // capacity, (part + 1) * block // capacity):
            device = pl.multiple_of((me ^ m) * capacity, capacity)
            departures.append(
                pltpu.make_async_copy(
                    images.at[pl.ds(m * capacity, capacity)],
                    out_hbm.at[pl.ds(device, capacity)],
                    out_sem.at[m],
                )
            )
            departures[-1].start()
    for copy in departures:
        copy.wait()


def owner_maps(me, pieces, sums, marginal, src_labels, tgt_labels, features):
    n_dev = len(pieces)
    capacity = pieces[0].shape[0] // 2
    width = pieces[0].shape[1]
    slots = n_dev * capacity
    rank = width - features
    vmem = pl.BlockSpec(memory_space=pltpu.VMEM)
    return pl.pallas_call(
        functools.partial(owner_kernel, n_dev, features),
        out_shape=jax.ShapeDtypeStruct((slots, features), jnp.bfloat16),
        in_specs=[vmem] * n_dev + [pl.BlockSpec(memory_space=pltpu.SMEM)] + [vmem] * 4,
        out_specs=in_hbm(),
        scratch_shapes=[
            pltpu.VMEM((slots, width), jnp.bfloat16),
            pltpu.VMEM((slots, width), jnp.bfloat16),
            pltpu.VMEM((slots, rank), jnp.bfloat16),
            pltpu.VMEM((1, slots), jnp.float32),
            pltpu.VMEM((slots, features), jnp.bfloat16),
            pltpu.SemaphoreType.DMA((n_dev,)),
        ],
        compiler_params=pltpu.CompilerParams(vmem_limit_bytes=VMEM_BYTES),
        cost_estimate=pl.CostEstimate(
            flops=2 * slots * features * (2 * rank + 2 * slots),
            bytes_accessed=6 * slots * width,
            transcendentals=slots * slots,
        ),
        name="owner_maps",
    )(
        *pieces,
        me[None],
        sums,
        marginal[None, :],
        src_labels[:, None],
        tgt_labels[None, :],
    )


def labels_of(clusters, owner, capacity, spread):
    rows = clusters.shape[1]
    mine = clusters // spread == owner
    before = (jnp.arange(rows)[:, None] < jnp.arange(rows)[None, :]).astype(jnp.bfloat16)
    earlier = jnp.dot(mine.astype(jnp.bfloat16), before, preferred_element_type=jnp.float32)
    ranking = jnp.where(mine, earlier.astype(jnp.int32), -1)
    value = clusters - owner * spread + 1
    hit = ranking[:, None, :] == jnp.arange(capacity, dtype=jnp.int32)[None, :, None]
    return jnp.sum(jnp.where(hit, value[:, None, :], 0), axis=2)


def exchange(rows):
    return lax.all_to_all(rows, AXES, split_axis=0, concat_axis=0, tiled=True)


def per_device(
    src_points, tgt_points, src_factor, tgt_factor, inner_marginal, src_cluster, tgt_cluster
):
    n_dev = lax.axis_size("src") * lax.axis_size("tgt")
    rows, features = src_points.shape
    rank = src_factor.shape[1]
    capacity = 2 * rows // n_dev
    slots = n_dev * capacity
    owner = lax.axis_index(AXES)

    pieces, parts = pack(
        owner, src_cluster, tgt_cluster, src_points, tgt_points, src_factor, tgt_factor, n_dev, capacity
    )
    sums, pieces = sum_and_swap(parts, pieces)

    kept = 2 * features // n_dev
    table = sums[:, kept : kept + 2 * rows // rank].astype(jnp.int32).reshape(n_dev, 2, rows)
    turn = ((jnp.arange(n_dev) ^ owner)[:, None] == jnp.arange(n_dev)[None, :]).astype(jnp.bfloat16)
    table = jnp.dot(
        turn, table.reshape(n_dev, -1).astype(jnp.bfloat16), preferred_element_type=jnp.float32
    )
    table = table.astype(jnp.int32).reshape(n_dev, 2, rows)
    src_labels = labels_of(table[:, 0], owner, capacity, CL_DEV).reshape(-1)
    tgt_labels = labels_of(table[:, 1], owner, capacity, CL_DEV).reshape(-1)
    images = owner_maps(owner, pieces, sums, inner_marginal, src_labels, tgt_labels, features)
    returned = exchange(images)

    src_update, tgt_update = updates(
        src_points, tgt_points, src_factor, tgt_factor, inner_marginal, sums
    )
    slot = slot_row(src_cluster[None, :], n_dev, capacity, CL_DEV, 0, 0)
    back = (jnp.arange(slots, dtype=jnp.int32)[:, None] == slot).astype(jnp.bfloat16)
    mapped = contract_rows(back, returned).astype(jnp.bfloat16)
    return (src_update, tgt_update, mapped)


def solution(mesh):
    rows = P(AXES, None)
    return jax.shard_map(
        per_device,
        mesh=mesh,
        in_specs=(rows, rows, rows, rows, P(), P(AXES), P(AXES)),
        out_specs=(rows, rows, rows),
        check_vma=False,
    )
```

```python
import functools

import jax
import jax.numpy as jnp
from jax import lax
from jax.experimental import pallas as pl
from jax.experimental.pallas import tpu as pltpu
from jax.sharding import PartitionSpec as P

CL_DEV = 2

GAMMA = 2.0
TEMPER = 0.03
EPS = 1e-06

AXES = ("src", "tgt")
VMEM_BYTES = 48 * 1024 * 1024
PACK_VMEM_BYTES = 62 * 1024 * 1024
TABLE_ROWS = 16
LAG = 2


def contract_rows(left, right):
    return lax.dot_general(
        left, right, (((0,), (0,)), ((), ())), preferred_element_type=jnp.float32
    )


def contract_columns(left, right):
    return lax.dot_general(
        left, right, (((1,), (1,)), ((), ())), preferred_element_type=jnp.float32
    )


def mirror_step(points, total_round, factor, inner_marginal):
    gradient = -jnp.dot(points, total_round, preferred_element_type=jnp.float32) / inner_marginal
    row_scale = jnp.max(jnp.abs(gradient), axis=1, keepdims=True) + EPS
    tilted = factor.astype(jnp.float32) * jnp.exp(-GAMMA * gradient / row_scale)
    mean = jnp.mean(tilted, axis=1, keepdims=True)
    mean = jnp.where(mean > 0, mean, 1.0)
    return (tilted / mean).astype(jnp.bfloat16)


def inverse_norm(rows):
    return lax.rsqrt(jnp.sum(jnp.square(rows.astype(jnp.float32)), axis=1, keepdims=True) + EPS)


def totals_of(sums_ref):
    n_dev, chunk, rank = sums_ref.shape
    kept = chunk - TABLE_ROWS
    both = sums_ref[:, :kept, :]
    half = n_dev // 2
    return both[:half].reshape(half * kept, rank), both[half:].reshape(half * kept, rank)


def whole(shape):
    return pl.BlockSpec(shape, lambda *_: (0,) * len(shape))


def in_hbm():
    return pl.BlockSpec(memory_space=pltpu.HBM)


def mates_and_masks(n_dev, n_tgt):
    return n_tgt, [m for m in range(n_dev) if not m & n_tgt]


def ranked(cluster, n_dev):
    rows = cluster.shape[1]
    owners = cluster // CL_DEV
    onehot = owners == lax.broadcasted_iota(jnp.int32, (n_dev, rows), 0)
    before = lax.broadcasted_iota(jnp.int32, (rows, rows), 0) < lax.broadcasted_iota(
        jnp.int32, (rows, rows), 1
    )
    earlier = jnp.dot(
        onehot.astype(jnp.bfloat16), before.astype(jnp.bfloat16), preferred_element_type=jnp.float32
    )
    ranking = jnp.sum(jnp.where(onehot, earlier, 0.0), axis=0, keepdims=True).astype(jnp.int32)
    return owners, ranking


def packed_slot(cluster, n_dev, n_tgt, capacity, kind, me):
    owners, ranking = ranked(cluster, n_dev)
    partner = owners ^ me
    column = (partner // n_tgt) % 2
    block = (partner // (2 * n_tgt)) * n_tgt + partner % n_tgt + column * (n_dev // 2)
    return (block * 2 + kind) * capacity + ranking


def pack_kernel(
    n_dev,
    n_tgt,
    capacity,
    me_ref,
    src_cluster_ref,
    tgt_cluster_ref,
    src_points_hbm,
    tgt_points_hbm,
    src_factor_hbm,
    tgt_factor_hbm,
    keep_ref,
    swap_ref,
    parts_ref,
    src_points,
    tgt_points,
    src_factor,
    tgt_factor,
    in_sem,
):
    hbm = (src_points_hbm, tgt_points_hbm, src_factor_hbm, tgt_factor_hbm)
    held = (src_points, tgt_points, src_factor, tgt_factor)
    arrivals = [pltpu.make_async_copy(a, b, in_sem.at[i]) for i, (a, b) in enumerate(zip(hbm, held))]
    for copy in arrivals:
        copy.start()
    features = tgt_points.shape[1]
    me = me_ref[0]
    tgt_slot = packed_slot(tgt_cluster_ref[...], n_dev, n_tgt, capacity, 0, me)
    src_slot = packed_slot(src_cluster_ref[...], n_dev, n_tgt, capacity, 1, me)
    for copy in arrivals:
        copy.wait()

    _, chunk, rank = parts_ref.shape
    kept = chunk - TABLE_ROWS
    half = n_dev // 2
    parts_ref[:half, :kept, :] = (
        contract_rows(tgt_points[...], tgt_factor[...]).astype(jnp.bfloat16).reshape(half, kept, rank)
    )
    parts_ref[half:, :kept, :] = (
        contract_rows(src_points[...], src_factor[...]).astype(jnp.bfloat16).reshape(half, kept, rank)
    )
    row = lax.broadcasted_iota(jnp.int32, (TABLE_ROWS, rank), 0)
    table = jnp.where(row == 0, src_cluster_ref[...], jnp.where(row == 1, tgt_cluster_ref[...], 0))
    chunk_id = lax.broadcasted_iota(jnp.int32, (n_dev, TABLE_ROWS, rank), 0)
    table = jnp.where(chunk_id == me, table.astype(jnp.float32)[None], 0.0)
    parts_ref[:, kept:, :] = table.astype(jnp.bfloat16)

    slots = keep_ref.shape[0]
    block = 256
    for part in range(2 * slots // block):
        index = lax.broadcasted_iota(jnp.int32, (block, tgt_points.shape[0]), 0) + part * block
        tgt_place = (index == tgt_slot).astype(jnp.bfloat16)
        src_place = (index == src_slot).astype(jnp.bfloat16)
        out = keep_ref if part * block < slots else swap_ref
        mine = pl.ds(part * block % slots, block)
        out[mine, :features] = (
            jnp.dot(tgt_place, tgt_points[...], preferred_element_type=jnp.float32)
            + jnp.dot(src_place, src_points[...], preferred_element_type=jnp.float32)
        ).astype(jnp.bfloat16)
        out[mine, features:] = (
            jnp.dot(tgt_place, tgt_factor[...], preferred_element_type=jnp.float32)
            + jnp.dot(src_place, src_factor[...], preferred_element_type=jnp.float32)
        ).astype(jnp.bfloat16)


def pack(
    me, src_cluster, tgt_cluster, src_points, tgt_points, src_factor, tgt_factor, n_dev, n_tgt, capacity
):
    rows, features = src_points.shape
    rank = src_factor.shape[1]
    slots = n_dev * capacity
    chunk = 2 * features // n_dev + TABLE_ROWS
    vmem = pl.BlockSpec(memory_space=pltpu.VMEM)
    packed = jax.ShapeDtypeStruct((slots, features + rank), jnp.bfloat16)
    return pl.pallas_call(
        functools.partial(pack_kernel, n_dev, n_tgt, capacity),
        out_shape=[packed, packed, jax.ShapeDtypeStruct((n_dev, chunk, rank), jnp.bfloat16)],
        in_specs=[pl.BlockSpec(memory_space=pltpu.SMEM)] + [vmem] * 2 + [in_hbm()] * 4,
        out_specs=[vmem] * 3,
        scratch_shapes=[
            pltpu.VMEM((rows, features), jnp.bfloat16),
            pltpu.VMEM((rows, features), jnp.bfloat16),
            pltpu.VMEM((rows, rank), jnp.bfloat16),
            pltpu.VMEM((rows, rank), jnp.bfloat16),
            pltpu.SemaphoreType.DMA((4,)),
        ],
        compiler_params=pltpu.CompilerParams(vmem_limit_bytes=PACK_VMEM_BYTES),
        cost_estimate=pl.CostEstimate(
            flops=8 * slots * rows * (features + rank),
            bytes_accessed=4 * (2 * slots + rows) * (features + rank),
            transcendentals=0,
        ),
        name="pack_rows",
    )(me[None], src_cluster[None, :], tgt_cluster[None, :], src_points, tgt_points, src_factor, tgt_factor)


def merge_kernel(keep_ref, swap_ref, *out_refs):
    piece = out_refs[0].shape[0] // 2
    for i, out in enumerate(out_refs):
        out[:piece, :] = keep_ref[pl.ds(i * piece, piece), :]
        out[piece:, :] = swap_ref[pl.ds(i * piece, piece), :]


def merge(keep, swapped, n_pieces):
    slots, width = keep.shape
    shape = jax.ShapeDtypeStruct((2 * slots // n_pieces, width), jnp.bfloat16)
    return pl.pallas_call(
        merge_kernel,
        out_shape=[shape] * n_pieces,
        compiler_params=pltpu.CompilerParams(vmem_limit_bytes=VMEM_BYTES),
        cost_estimate=pl.CostEstimate(flops=0, bytes_accessed=8 * slots * width, transcendentals=0),
        name="merge_pieces",
    )(keep, swapped)


def partner_pairs(size, mask):
    return [(i, i ^ mask) for i in range(size)]


def dealt(masks, hands):
    half = lax.axis_size("tgt") // 2
    far = [m for m in masks if m & half]
    near = [m for m in masks if not m & half]
    mixed = [m for pair in zip(far, near) for m in pair]
    mixed += far[len(near) :] + near[len(far) :]
    return [mixed[len(mixed) * h // hands : len(mixed) * (h + 1) // hands] for h in range(hands)]


def sum_and_swap(parts, keep, swap, n_tgt):
    n_dev = parts.shape[0]
    mate, masks = mates_and_masks(n_dev, n_tgt)
    order = []
    for axis in AXES:
        stride = 1
        while stride < lax.axis_size(axis):
            order.append((axis, stride))
            stride *= 2
    dims = [bit for axis in AXES for bit in reversed([o for o in order if o[0] == axis])]
    hands = [[]] + dealt(masks[1:], 2 * len(order) - 1)
    pieces = {}
    got = {}

    def sent(array, axis, stride):
        return lax.ppermute(array, axis, partner_pairs(lax.axis_size(axis), stride))

    def let_go(x, step):
        back = hands[step - LAG] if step >= LAG else []
        x, held, _ = lax.optimization_barrier(
            (x, [pieces[m] for m in hands[step]], [got[m] for m in back])
        )
        for m, piece in zip(hands[step], held):
            got[m] = lax.ppermute(piece, AXES, partner_pairs(n_dev, m))
        return x

    x = parts.reshape((2,) * len(dims) + parts.shape[1:])
    left = list(dims)
    for step, bit in enumerate(order):
        axis, stride = bit
        dim = left.index(bit)
        mine = (lax.axis_index(axis) // stride) % 2
        x = let_go(x, step)
        own = lax.dynamic_index_in_dim(x, mine, dim, keepdims=False).astype(jnp.float32)
        other = sent(lax.dynamic_index_in_dim(x, 1 - mine, dim, keepdims=False), axis, stride)
        if step == 0:
            swapped = lax.ppermute(swap, AXES, partner_pairs(n_dev, mate))
            merged = merge(keep, swapped, len(masks))
            pieces.update(zip(masks, merged))
            got[0] = merged[0]
        x = (own + other.astype(jnp.float32)).astype(jnp.bfloat16)
        left.remove(bit)
    for step, bit in enumerate(reversed(order)):
        axis, stride = bit
        mine = (lax.axis_index(axis) // stride) % 2
        x = let_go(x, step + len(order))
        other = sent(x, axis, stride)
        left = [b for b in dims if b in left or b == bit]
        x = jnp.stack(
            [jnp.where(mine == 0, x, other), jnp.where(mine == 0, other, x)], axis=left.index(bit)
        )
    sources = [m for first in masks for m in (first, first | mate)]
    return x.reshape(parts.shape), [got[m] for m in masks], sources


def update_kernel(
    src_points_ref, tgt_points_ref, src_factor_ref, tgt_factor_ref, marginal_ref, sums_ref, src_ref, tgt_ref
):
    tgt_total, src_total = totals_of(sums_ref)
    src_ref[...] = mirror_step(src_points_ref[...], tgt_total, src_factor_ref[...], marginal_ref[...])
    tgt_ref[...] = mirror_step(tgt_points_ref[...], src_total, tgt_factor_ref[...], marginal_ref[...])


def updates(src_points, tgt_points, src_factor, tgt_factor, marginal, sums):
    rows, features = src_points.shape
    rank = src_factor.shape[1]
    shape = jax.ShapeDtypeStruct(src_factor.shape, jnp.bfloat16)
    return pl.pallas_call(
        update_kernel,
        out_shape=(shape, shape),
        compiler_params=pltpu.CompilerParams(vmem_limit_bytes=VMEM_BYTES),
        cost_estimate=pl.CostEstimate(
            flops=4 * rows * features * rank,
            bytes_accessed=4 * rows * (features + 2 * rank),
            transcendentals=2 * rows * rank,
        ),
        name="mirror_updates",
    )(src_points, tgt_points, src_factor, tgt_factor, marginal[None, :], sums)


def owner_kernel(sources, features, *refs):
    n_pieces = len(sources) // 2
    pieces = refs[:n_pieces]
    me_ref, sums_ref, marginal_ref, src_label_ref, tgt_label_ref, out_hbm = refs[
        n_pieces : n_pieces + 6
    ]
    src_seen, tgt_seen, tgt_update, tgt_inv, images, out_sem = refs[n_pieces + 6 :]
    capacity = pieces[0].shape[0] // 4
    slots, width = src_seen.shape
    rank = width - features
    block = 256
    marginal = marginal_ref[...]
    tgt_total, src_total = totals_of(sums_ref)
    me = me_ref[0]

    for place in range(2 * n_pieces):
        ref, first = pieces[place // 2], place % 2 * 2 * capacity
        mine = pl.ds(place * capacity, capacity)
        tgt_seen[mine, :] = ref[first : first + capacity, :]
        src_seen[mine, :] = ref[first + capacity : first + 2 * capacity, :]

    for part in range(slots // block):
        mine = pl.ds(part * block, block)
        rows = tgt_seen[mine, :features]
        tgt_update[mine, :] = mirror_step(rows, src_total, tgt_seen[mine, features:], marginal)
        tgt_inv[:, mine] = inverse_norm(rows).reshape(1, block)

    departures = []
    for part in range(slots // block):
        mine = pl.ds(part * block, block)
        rows = src_seen[mine, :features]
        update = mirror_step(rows, tgt_total, src_seen[mine, features:], marginal)
        cosine = contract_columns(rows, tgt_seen[:, :features]) * inverse_norm(rows) * tgt_inv[...]
        weight = contract_columns(update, tgt_update[...]) / rank
        label = src_label_ref[mine, :]
        same = jnp.logical_and(label == tgt_label_ref[...], label > 0)
        kernel = jnp.where(same, weight * jnp.exp((cosine - 1.0) / TEMPER), 0.0)
        denominator = jnp.sum(kernel, axis=1, keepdims=True)
        denominator = jnp.where(denominator > 0, denominator, 1.0)
        transport = (kernel / denominator).astype(jnp.bfloat16)
        images[mine, :] = jnp.dot(
            transport, tgt_seen[:, :features], preferred_element_type=jnp.float32
        ).astype(jnp.bfloat16)
        for place in range(part * block // capacity, (part + 1) * block // capacity):
            device = pl.multiple_of((me ^ sources[place]) * capacity, capacity)
            departures.append(
                pltpu.make_async_copy(
                    images.at[pl.ds(place * capacity, capacity)],
                    out_hbm.at[pl.ds(device, capacity)],
                    out_sem.at[place],
                )
            )
            departures[-1].start()
    for copy in departures:
        copy.wait()


def owner_maps(me, pieces, sources, sums, marginal, src_labels, tgt_labels, features):
    n_dev = len(sources)
    capacity = pieces[0].shape[0] // 4
    width = pieces[0].shape[1]
    slots = n_dev * capacity
    rank = width - features
    vmem = pl.BlockSpec(memory_space=pltpu.VMEM)
    return pl.pallas_call(
        functools.partial(owner_kernel, sources, features),
        out_shape=jax.ShapeDtypeStruct((slots, features), jnp.bfloat16),
        in_specs=[vmem] * len(pieces) + [pl.BlockSpec(memory_space=pltpu.SMEM)] + [vmem] * 4,
        out_specs=in_hbm(),
        scratch_shapes=[
            pltpu.VMEM((slots, width), jnp.bfloat16),
            pltpu.VMEM((slots, width), jnp.bfloat16),
            pltpu.VMEM((slots, rank), jnp.bfloat16),
            pltpu.VMEM((1, slots), jnp.float32),
            pltpu.VMEM((slots, features), jnp.bfloat16),
            pltpu.SemaphoreType.DMA((n_dev,)),
        ],
        compiler_params=pltpu.CompilerParams(vmem_limit_bytes=VMEM_BYTES),
        cost_estimate=pl.CostEstimate(
            flops=2 * slots * features * (2 * rank + 2 * slots),
            bytes_accessed=6 * slots * width,
            transcendentals=slots * slots,
        ),
        name="owner_maps",
    )(
        *pieces,
        me[None],
        sums,
        marginal[None, :],
        src_labels[:, None],
        tgt_labels[None, :],
    )


def labels_of(clusters, owner, capacity, spread):
    rows = clusters.shape[1]
    mine = clusters // spread == owner
    before = (jnp.arange(rows)[:, None] < jnp.arange(rows)[None, :]).astype(jnp.bfloat16)
    earlier = jnp.dot(mine.astype(jnp.bfloat16), before, preferred_element_type=jnp.float32)
    ranking = jnp.where(mine, earlier.astype(jnp.int32), -1)
    value = clusters - owner * spread + 1
    hit = ranking[:, None, :] == jnp.arange(capacity, dtype=jnp.int32)[None, :, None]
    return jnp.sum(jnp.where(hit, value[:, None, :], 0), axis=2)


def exchange(rows):
    return lax.all_to_all(rows, AXES, split_axis=0, concat_axis=0, tiled=True)


def per_device(
    src_points, tgt_points, src_factor, tgt_factor, inner_marginal, src_cluster, tgt_cluster
):
    n_tgt = lax.axis_size("tgt")
    n_dev = lax.axis_size("src") * n_tgt
    rows, features = src_points.shape
    rank = src_factor.shape[1]
    capacity = 2 * rows // n_dev
    slots = n_dev * capacity
    owner = lax.axis_index(AXES)

    keep, swap, parts = pack(
        owner,
        src_cluster,
        tgt_cluster,
        src_points,
        tgt_points,
        src_factor,
        tgt_factor,
        n_dev,
        n_tgt,
        capacity,
    )
    sums, pieces, sources = sum_and_swap(parts, keep, swap, n_tgt)

    kept = 2 * features // n_dev
    table = sums[:, kept : kept + 2 * rows // rank].astype(jnp.int32).reshape(n_dev, 2, rows)
    turn = (jnp.array(sources) ^ owner)[:, None] == jnp.arange(n_dev)[None, :]
    turn = turn.astype(jnp.bfloat16)
    table = jnp.dot(
        turn, table.reshape(n_dev, -1).astype(jnp.bfloat16), preferred_element_type=jnp.float32
    )
    table = table.astype(jnp.int32).reshape(n_dev, 2, rows)
    src_labels = labels_of(table[:, 0], owner, capacity, CL_DEV).reshape(-1)
    tgt_labels = labels_of(table[:, 1], owner, capacity, CL_DEV).reshape(-1)
    images = owner_maps(
        owner, pieces, sources, sums, inner_marginal, src_labels, tgt_labels, features
    )
    returned = exchange(images)

    src_update, tgt_update = updates(
        src_points, tgt_points, src_factor, tgt_factor, inner_marginal, sums
    )
    owners, ranking = ranked(src_cluster[None, :], n_dev)
    slot = owners * capacity + ranking
    back = (jnp.arange(slots, dtype=jnp.int32)[:, None] == slot).astype(jnp.bfloat16)
    mapped = contract_rows(back, returned).astype(jnp.bfloat16)
    return (src_update, tgt_update, mapped)


def solution(mesh):
    rows = P(AXES, None)
    return jax.shard_map(
        per_device,
        mesh=mesh,
        in_specs=(rows, rows, rows, rows, P(), P(AXES), P(AXES)),
        out_specs=(rows, rows, rows),
        check_vma=False,
    )
```

```python
import functools

import jax
import jax.numpy as jnp
from jax import lax
from jax.experimental import pallas as pl
from jax.experimental.pallas import tpu as pltpu
from jax.sharding import Mesh
from jax.sharding import PartitionSpec as P

CL_DEV = 2

GAMMA = 2.0
TEMPER = 0.03
EPS = 1e-06

HALF, REST = "half", "rest"
ALL = ("src", HALF, REST)
GROUP = ("src", REST)
VMEM_BYTES = 48 * 1024 * 1024
PACK_VMEM_BYTES = 62 * 1024 * 1024
TABLE_ROWS = 8


def contract_rows(left, right):
    return lax.dot_general(
        left, right, (((0,), (0,)), ((), ())), preferred_element_type=jnp.float32
    )


def contract_columns(left, right):
    return lax.dot_general(
        left, right, (((1,), (1,)), ((), ())), preferred_element_type=jnp.float32
    )


def mirror_step(points, total_round, factor, inner_marginal):
    gradient = -jnp.dot(points, total_round, preferred_element_type=jnp.float32) / inner_marginal
    row_scale = jnp.max(jnp.abs(gradient), axis=1, keepdims=True) + EPS
    tilted = factor.astype(jnp.float32) * jnp.exp(-GAMMA * gradient / row_scale)
    mean = jnp.mean(tilted, axis=1, keepdims=True)
    mean = jnp.where(mean > 0, mean, 1.0)
    return (tilted / mean).astype(jnp.bfloat16)


def inverse_norm(rows):
    return lax.rsqrt(jnp.sum(jnp.square(rows.astype(jnp.float32)), axis=1, keepdims=True) + EPS)


def totals_of(sums_ref):
    n_dev, chunk, rank = sums_ref.shape
    kept = chunk - TABLE_ROWS
    both = sums_ref[:, :kept, :]
    half = n_dev // 2
    return both[:half].reshape(half * kept, rank), both[half:].reshape(half * kept, rank)


def whole(shape):
    return pl.BlockSpec(shape, lambda *_: (0,) * len(shape))


def in_hbm():
    return pl.BlockSpec(memory_space=pltpu.HBM)


def slot_row(cluster, n_group, capacity, spread, first):
    rows = cluster.shape[1]
    owners = cluster // spread
    onehot = owners == lax.broadcasted_iota(jnp.int32, (n_group, rows), 0)
    before = lax.broadcasted_iota(jnp.int32, (rows, rows), 0) < lax.broadcasted_iota(
        jnp.int32, (rows, rows), 1
    )
    earlier = jnp.dot(
        onehot.astype(jnp.bfloat16), before.astype(jnp.bfloat16), preferred_element_type=jnp.float32
    )
    ranking = jnp.sum(jnp.where(onehot, earlier, 0.0), axis=0, keepdims=True).astype(jnp.int32)
    return owners * capacity + ranking + first


def contract_kernel(n_dev, me_ref, src_cluster_ref, tgt_cluster_ref, *refs):
    hbm, parts_ref, held, in_sem = refs[:4], refs[4], refs[5:9], refs[9]
    arrivals = [pltpu.make_async_copy(a, b, in_sem.at[i]) for i, (a, b) in enumerate(zip(hbm, held))]
    for copy in arrivals:
        copy.start()
    tgt_points, tgt_factor, src_points, src_factor = held
    _, chunk, rank = parts_ref.shape
    kept = chunk - TABLE_ROWS
    half = n_dev // 2
    row = lax.broadcasted_iota(jnp.int32, (TABLE_ROWS, rank), 0)
    table = jnp.where(row == 0, src_cluster_ref[...], jnp.where(row == 1, tgt_cluster_ref[...], 0))
    chunk_id = lax.broadcasted_iota(jnp.int32, (n_dev, TABLE_ROWS, rank), 0)
    parts_ref[:, kept:, :] = jnp.where(chunk_id == me_ref[0], table.astype(jnp.float32)[None], 0.0)
    arrivals[0].wait()
    arrivals[1].wait()
    parts_ref[:half, :kept, :] = contract_rows(tgt_points[...], tgt_factor[...]).reshape(
        half, kept, rank
    )
    arrivals[2].wait()
    arrivals[3].wait()
    parts_ref[half:, :kept, :] = contract_rows(src_points[...], src_factor[...]).reshape(
        half, kept, rank
    )


def partial_sums(me, src_cluster, tgt_cluster, src_points, tgt_points, src_factor, tgt_factor, n_dev):
    rows, features = src_points.shape
    rank = src_factor.shape[1]
    chunk = 2 * features // n_dev + TABLE_ROWS
    vmem = pl.BlockSpec(memory_space=pltpu.VMEM)
    return pl.pallas_call(
        functools.partial(contract_kernel, n_dev),
        out_shape=jax.ShapeDtypeStruct((n_dev, chunk, rank), jnp.float32),
        in_specs=[pl.BlockSpec(memory_space=pltpu.SMEM)] + [vmem] * 2 + [in_hbm()] * 4,
        out_specs=vmem,
        scratch_shapes=[
            pltpu.VMEM((rows, features), jnp.bfloat16),
            pltpu.VMEM((rows, rank), jnp.bfloat16),
            pltpu.VMEM((rows, features), jnp.bfloat16),
            pltpu.VMEM((rows, rank), jnp.bfloat16),
            pltpu.SemaphoreType.DMA((4,)),
        ],
        compiler_params=pltpu.CompilerParams(vmem_limit_bytes=PACK_VMEM_BYTES),
        cost_estimate=pl.CostEstimate(
            flops=4 * rows * features * rank,
            bytes_accessed=4 * rows * (features + rank) + 4 * n_dev * chunk * rank,
            transcendentals=0,
        ),
        name="partial_sums",
    )(me[None], src_cluster[None, :], tgt_cluster[None, :], tgt_points, tgt_factor, src_points, src_factor)


def pack_kernel(n_group, capacity, spread, n_kinds, *refs):
    clusters = refs[:n_kinds]
    hbm = refs[n_kinds : 3 * n_kinds]
    packed_hbm = refs[3 * n_kinds]
    held = refs[3 * n_kinds + 1 : 5 * n_kinds + 1]
    packed, in_sem, out_sem = refs[5 * n_kinds + 1 :]
    arrivals = [pltpu.make_async_copy(a, b, in_sem.at[i]) for i, (a, b) in enumerate(zip(hbm, held))]
    for copy in arrivals:
        copy.start()
    slots = [
        slot_row(cluster[...], n_group, n_kinds * capacity, spread, kind * capacity)
        for kind, cluster in enumerate(clusters)
    ]
    for copy in arrivals:
        copy.wait()
    rows, features = held[0].shape
    block = 256
    departures = []
    for part in range(packed.shape[0] // block):
        mine = pl.ds(part * block, block)
        index = lax.broadcasted_iota(jnp.int32, (block, rows), 0) + part * block
        moved = carried = None
        for kind in range(n_kinds):
            place = (index == slots[kind]).astype(jnp.bfloat16)
            a = jnp.dot(place, held[2 * kind][...], preferred_element_type=jnp.float32)
            b = jnp.dot(place, held[2 * kind + 1][...], preferred_element_type=jnp.float32)
            moved = a if moved is None else moved + a
            carried = b if carried is None else carried + b
        packed[mine, :features] = moved.astype(jnp.bfloat16)
        packed[mine, features:] = carried.astype(jnp.bfloat16)
        departures.append(
            pltpu.make_async_copy(packed.at[mine], packed_hbm.at[mine], out_sem.at[part])
        )
        departures[-1].start()
    for copy in departures:
        copy.wait()


def pack(kinds, n_group, capacity, spread):
    n_kinds = len(kinds)
    rows, features = kinds[0][1].shape
    rank = kinds[0][2].shape[1]
    slots = n_kinds * n_group * capacity
    held = [pltpu.VMEM((rows, features), jnp.bfloat16), pltpu.VMEM((rows, rank), jnp.bfloat16)]
    return pl.pallas_call(
        functools.partial(pack_kernel, n_group, capacity, spread, n_kinds),
        out_shape=jax.ShapeDtypeStruct((slots, features + rank), jnp.bfloat16),
        in_specs=[pl.BlockSpec(memory_space=pltpu.VMEM)] * n_kinds + [in_hbm()] * (2 * n_kinds),
        out_specs=in_hbm(),
        scratch_shapes=held * n_kinds
        + [
            pltpu.VMEM((slots, features + rank), jnp.bfloat16),
            pltpu.SemaphoreType.DMA((2 * n_kinds,)),
            pltpu.SemaphoreType.DMA((slots // 256,)),
        ],
        compiler_params=pltpu.CompilerParams(vmem_limit_bytes=PACK_VMEM_BYTES),
        cost_estimate=pl.CostEstimate(
            flops=2 * n_kinds * slots * rows * (features + rank),
            bytes_accessed=2 * (slots + n_kinds * rows) * (features + rank),
            transcendentals=0,
        ),
        name="pack_rows",
    )(
        *[cluster[None, :] for cluster, _, _ in kinds],
        *[array for _, points, factor in kinds for array in (points, factor)],
    )


def digits_of(size, stride):
    bits = size.bit_length() - 1
    found = []
    while bits:
        take = 1 if bits % 2 else 2
        found.append((stride, 1 << take))
        stride <<= take
        bits -= take
    return found


class Chain:
    def __init__(self, parts, n_src, n_tgt):
        self.n_dev = n_src * n_tgt
        src, tgt = digits_of(n_src, n_tgt), digits_of(n_tgt, 1)
        self.order = src + tgt
        self.dims = src[::-1] + tgt[::-1]
        self.left = list(self.dims)
        self.x = parts.reshape(tuple(radix for _, radix in self.dims) + parts.shape[1:])

    def sent(self, array, mask):
        return lax.ppermute(array, ALL, [(i, i ^ mask) for i in range(self.n_dev)])

    def scatter(self, digit):
        stride, radix = digit
        dim = self.left.index(digit)
        mine = (lax.axis_index(ALL) // stride) % radix
        total = lax.dynamic_index_in_dim(self.x, mine, dim, keepdims=False)
        for j in range(1, radix):
            piece = lax.dynamic_index_in_dim(self.x, mine ^ j, dim, keepdims=False)
            total = total + self.sent(piece.astype(jnp.bfloat16), j * stride).astype(jnp.float32)
        self.x = total
        self.left.remove(digit)

    def gather(self, digit):
        stride, radix = digit
        mine = (lax.axis_index(ALL) // stride) % radix
        x = self.x.astype(jnp.bfloat16)
        got = [x] + [self.sent(x, j * stride) for j in range(1, radix)]
        self.left = [d for d in self.dims if d in self.left or d == digit]
        self.x = jnp.stack(
            [lax.select_n(mine ^ d, *got) if radix > 2 else jnp.where(mine == d, *got) for d in range(radix)],
            axis=self.left.index(digit),
        )


def update_kernel(
    src_points_ref, tgt_points_ref, src_factor_ref, tgt_factor_ref, marginal_ref, sums_ref, src_ref, tgt_ref
):
    tgt_total, src_total = totals_of(sums_ref)
    src_ref[...] = mirror_step(src_points_ref[...], tgt_total, src_factor_ref[...], marginal_ref[...])
    tgt_ref[...] = mirror_step(tgt_points_ref[...], src_total, tgt_factor_ref[...], marginal_ref[...])


def updates(src_points, tgt_points, src_factor, tgt_factor, marginal, sums):
    rows, features = src_points.shape
    rank = src_factor.shape[1]
    shape = jax.ShapeDtypeStruct(src_factor.shape, jnp.bfloat16)
    return pl.pallas_call(
        update_kernel,
        out_shape=(shape, shape),
        compiler_params=pltpu.CompilerParams(vmem_limit_bytes=VMEM_BYTES),
        cost_estimate=pl.CostEstimate(
            flops=4 * rows * features * rank,
            bytes_accessed=4 * rows * (features + 2 * rank),
            transcendentals=2 * rows * rank,
        ),
        name="mirror_updates",
    )(src_points, tgt_points, src_factor, tgt_factor, marginal[None, :], sums)


def owner_kernel(
    features,
    src_ref,
    near_ref,
    far_ref,
    sums_ref,
    marginal_ref,
    src_label_ref,
    tgt_label_ref,
    out_hbm,
    tgt_rows,
    tgt_update,
    tgt_inv,
    images,
    out_sem,
):
    n_group, capacity, width = src_ref.shape
    slots = n_group * capacity
    rank = width - features
    block = 256
    marginal = marginal_ref[...]
    piece = block // capacity
    tgt_total, src_total = totals_of(sums_ref)

    for which, ref in enumerate((near_ref, far_ref)):
        for part in range(slots // block):
            mine = pl.ds(which * slots + part * block, block)
            both = ref[pl.ds(part * piece, piece)].reshape(block, width)
            rows = both[:, :features]
            tgt_rows[mine, :] = rows
            tgt_update[mine, :] = mirror_step(rows, src_total, both[:, features:], marginal)
            tgt_inv[:, mine] = inverse_norm(rows).reshape(1, block)

    departures = []
    for part in range(slots // block):
        mine = pl.ds(part * block, block)
        both = src_ref[pl.ds(part * piece, piece)].reshape(block, width)
        rows = both[:, :features]
        update = mirror_step(rows, tgt_total, both[:, features:], marginal)
        cosine = contract_columns(rows, tgt_rows[...]) * inverse_norm(rows) * tgt_inv[...]
        weight = contract_columns(update, tgt_update[...]) / rank
        label = src_label_ref[mine, :]
        same = jnp.logical_and(label == tgt_label_ref[...], label > 0)
        kernel = jnp.where(same, weight * jnp.exp((cosine - 1.0) / TEMPER), 0.0)
        denominator = jnp.sum(kernel, axis=1, keepdims=True)
        denominator = jnp.where(denominator > 0, denominator, 1.0)
        transport = (kernel / denominator).astype(jnp.bfloat16)
        images[mine, :] = jnp.dot(
            transport, tgt_rows[...], preferred_element_type=jnp.float32
        ).astype(jnp.bfloat16)
        departures.append(
            pltpu.make_async_copy(images.at[mine], out_hbm.at[mine], out_sem.at[part])
        )
        departures[-1].start()
    for copy in departures:
        copy.wait()


def owner_maps(near, far, sums, marginal, src_labels, tgt_labels, features):
    n_group, capacity, width = far.shape
    slots = n_group * capacity
    rank = width - features
    return pl.pallas_call(
        functools.partial(owner_kernel, features),
        out_shape=jax.ShapeDtypeStruct((slots, features), jnp.bfloat16),
        grid=(1,),
        in_specs=[
            pl.BlockSpec((n_group, None, capacity, width), lambda step: (0, 1, 0, 0)),
            pl.BlockSpec((n_group, None, capacity, width), lambda step: (0, 0, 0, 0)),
            whole(far.shape),
            whole(sums.shape),
            whole((1, rank)),
            whole((slots, 1)),
            whole((1, 2 * slots)),
        ],
        out_specs=in_hbm(),
        scratch_shapes=[
            pltpu.VMEM((2 * slots, features), jnp.bfloat16),
            pltpu.VMEM((2 * slots, rank), jnp.bfloat16),
            pltpu.VMEM((1, 2 * slots), jnp.float32),
            pltpu.VMEM((slots, features), jnp.bfloat16),
            pltpu.SemaphoreType.DMA((slots // 256,)),
        ],
        compiler_params=pltpu.CompilerParams(vmem_limit_bytes=VMEM_BYTES),
        cost_estimate=pl.CostEstimate(
            flops=2 * slots * features * (3 * rank + 4 * slots),
            bytes_accessed=8 * slots * width,
            transcendentals=2 * slots * slots,
        ),
        name="owner_maps",
    )(
        near,
        near,
        far,
        sums,
        marginal[None, :],
        src_labels[:, None],
        tgt_labels[None, :],
    )


def labels_of(clusters, owner, capacity, spread):
    rows = clusters.shape[1]
    mine = clusters // spread == owner
    before = (jnp.arange(rows)[:, None] < jnp.arange(rows)[None, :]).astype(jnp.bfloat16)
    earlier = jnp.dot(mine.astype(jnp.bfloat16), before, preferred_element_type=jnp.float32)
    ranking = jnp.where(mine, earlier.astype(jnp.int32), -1)
    value = clusters - owner * spread + 1
    hit = ranking[:, None, :] == jnp.arange(capacity, dtype=jnp.int32)[None, :, None]
    return jnp.sum(jnp.where(hit, value[:, None, :], 0), axis=2).reshape(-1)


def exchange(rows):
    return lax.all_to_all(rows, GROUP, split_axis=0, concat_axis=0, tiled=True)


def per_device(
    src_points, tgt_points, src_factor, tgt_factor, inner_marginal, src_cluster, tgt_cluster
):
    n_src, n_rest = lax.axis_size("src"), lax.axis_size(REST)
    n_group = n_src * n_rest
    n_dev = 2 * n_group
    rows, features = src_points.shape
    rank = src_factor.shape[1]
    capacity = 2 * (2 * rows // n_dev)
    spread = 2 * CL_DEV
    slots = n_group * capacity
    me = lax.axis_index(ALL)
    my_half = lax.axis_index(HALF)
    owner = lax.axis_index(GROUP)

    across = [(0, 1), (1, 0)]
    far_points, far_factor, far_cluster = (
        lax.ppermute(array, HALF, across) for array in (tgt_points, tgt_factor, tgt_cluster)
    )
    chain = Chain(
        partial_sums(
            me, src_cluster, tgt_cluster, src_points, tgt_points, src_factor, tgt_factor, n_dev
        ),
        n_src,
        2 * n_rest,
    )
    n_tgt_digits = len(digits_of(2 * n_rest, 1))
    near = pack(
        [(tgt_cluster, tgt_points, tgt_factor), (src_cluster, src_points, src_factor)],
        n_group,
        capacity,
        spread,
    )
    for digit in chain.order[:-n_tgt_digits]:
        chain.scatter(digit)
    near, chain.x = lax.optimization_barrier((near, chain.x))
    near = exchange(near)
    for digit in chain.order[-n_tgt_digits:]:
        chain.scatter(digit)
    for digit in chain.order[:-n_tgt_digits-1:-1]:
        chain.gather(digit)
    far = pack([(far_cluster, far_points, far_factor)], n_group, capacity, spread)
    far, near, chain.x = lax.optimization_barrier((far, near, chain.x))
    far = exchange(far)
    for digit in chain.order[-n_tgt_digits-1::-1]:
        chain.gather(digit)
    sums = chain.x.reshape(n_dev, -1, rank)

    kept = 2 * features // n_dev
    table = sums[:, kept : kept + 2].astype(jnp.int32).reshape(n_src, 2, n_rest, 2, rows)
    near_table = lax.dynamic_index_in_dim(table, my_half, 1, keepdims=False)
    far_table = lax.dynamic_index_in_dim(table, 1 - my_half, 1, keepdims=False)
    near_table = near_table.reshape(n_group, 2, rows)
    far_table = far_table.reshape(n_group, 2, rows)
    src_labels = labels_of(near_table[:, 0], owner, capacity, spread)
    tgt_labels = jnp.concatenate(
        [
            labels_of(near_table[:, 1], owner, capacity, spread),
            labels_of(far_table[:, 1], owner, capacity, spread),
        ]
    )

    width = features + rank
    images = owner_maps(
        near.reshape(n_group, 2, capacity, width),
        far.reshape(n_group, capacity, width),
        sums,
        inner_marginal,
        src_labels,
        tgt_labels,
        features,
    )
    returned = exchange(images)

    src_update, tgt_update = updates(
        src_points, tgt_points, src_factor, tgt_factor, inner_marginal, sums
    )
    slot = slot_row(src_cluster[None, :], n_group, capacity, spread, 0)
    back = (jnp.arange(slots, dtype=jnp.int32)[:, None] == slot).astype(jnp.bfloat16)
    mapped = contract_rows(back, returned).astype(jnp.bfloat16)
    return (src_update, tgt_update, mapped)


def solution(mesh):
    n_src, n_tgt = mesh.shape["src"], mesh.shape["tgt"]
    halves = Mesh(mesh.devices.reshape(n_src, 2, n_tgt // 2), ALL)
    rows = P(ALL, None)
    return jax.shard_map(
        per_device,
        mesh=halves,
        in_specs=(rows, rows, rows, rows, P(), P(ALL), P(ALL)),
        out_specs=(rows, rows, rows),
        check_vma=False,
    )
```

```python
import functools

import jax
import jax.numpy as jnp
from jax import lax
from jax.experimental import pallas as pl
from jax.experimental.pallas import tpu as pltpu
from jax.sharding import Mesh
from jax.sharding import PartitionSpec as P

CL_DEV = 2

GAMMA = 2.0
TEMPER = 0.03
EPS = 1e-06

HALF, REST = "half", "rest"
ALL = ("src", HALF, REST)
GROUP = ("src", REST)
VMEM_BYTES = 48 * 1024 * 1024
PACK_VMEM_BYTES = 62 * 1024 * 1024
TABLE_ROWS = 8


def contract_rows(left, right):
    return lax.dot_general(
        left, right, (((0,), (0,)), ((), ())), preferred_element_type=jnp.float32
    )


def contract_columns(left, right):
    return lax.dot_general(
        left, right, (((1,), (1,)), ((), ())), preferred_element_type=jnp.float32
    )


def mirror_step(points, total_round, factor, inner_marginal):
    gradient = -jnp.dot(points, total_round, preferred_element_type=jnp.float32) / inner_marginal
    row_scale = jnp.max(jnp.abs(gradient), axis=1, keepdims=True) + EPS
    tilted = factor.astype(jnp.float32) * jnp.exp(-GAMMA * gradient / row_scale)
    mean = jnp.mean(tilted, axis=1, keepdims=True)
    mean = jnp.where(mean > 0, mean, 1.0)
    return (tilted / mean).astype(jnp.bfloat16)


def inverse_norm(rows):
    return lax.rsqrt(jnp.sum(jnp.square(rows.astype(jnp.float32)), axis=1, keepdims=True) + EPS)


def totals_of(sums_ref):
    n_dev, chunk, rank = sums_ref.shape
    kept = chunk - TABLE_ROWS
    both = sums_ref[:, :kept, :]
    half = n_dev // 2
    return both[:half].reshape(half * kept, rank), both[half:].reshape(half * kept, rank)


def whole(shape):
    return pl.BlockSpec(shape, lambda *_: (0,) * len(shape))


def in_hbm():
    return pl.BlockSpec(memory_space=pltpu.HBM)


def slot_row(cluster, n_group, capacity, spread, first):
    rows = cluster.shape[1]
    owners = cluster // spread
    onehot = owners == lax.broadcasted_iota(jnp.int32, (n_group, rows), 0)
    before = lax.broadcasted_iota(jnp.int32, (rows, rows), 0) < lax.broadcasted_iota(
        jnp.int32, (rows, rows), 1
    )
    earlier = jnp.dot(
        onehot.astype(jnp.bfloat16), before.astype(jnp.bfloat16), preferred_element_type=jnp.float32
    )
    ranking = jnp.sum(jnp.where(onehot, earlier, 0.0), axis=0, keepdims=True).astype(jnp.int32)
    return owners * capacity + ranking + first


def contract_kernel(n_dev, n_tgt, me_ref, src_cluster_ref, tgt_cluster_ref, *refs):
    hbm, (own_ref, other_ref), held, parts, in_sem = refs[:4], refs[4:6], refs[6:10], refs[10], refs[11]
    arrivals = [pltpu.make_async_copy(a, b, in_sem.at[i]) for i, (a, b) in enumerate(zip(hbm, held))]
    for copy in arrivals:
        copy.start()
    tgt_points, tgt_factor, src_points, src_factor = held
    _, _, _, chunk, rank = parts.shape
    kept = chunk - TABLE_ROWS
    half = n_dev // 2
    me = me_ref[0]
    mine = (me // n_tgt) % 2
    row = lax.broadcasted_iota(jnp.int32, (TABLE_ROWS, rank), 0)
    table = jnp.where(row == 0, src_cluster_ref[...], jnp.where(row == 1, tgt_cluster_ref[...], 0))
    parts[:, :, :, kept:, :] = jnp.zeros(parts.shape[:3] + (TABLE_ROWS, rank), jnp.float32)
    parts[me // (2 * n_tgt), mine, me % n_tgt, kept:, :] = table.astype(jnp.float32)
    split = (half // (2 * n_tgt), 2, n_tgt, kept, rank)
    arrivals[0].wait()
    arrivals[1].wait()
    total = contract_rows(tgt_points[...], tgt_factor[...])
    parts[: split[0], :, :, :kept, :] = total.reshape(split)
    arrivals[2].wait()
    arrivals[3].wait()
    total = contract_rows(src_points[...], src_factor[...])
    parts[split[0] :, :, :, :kept, :] = total.reshape(split)
    for i in range(parts.shape[0]):
        own_ref[i] = parts[i, mine]
        other_ref[i] = parts[i, 1 - mine].astype(jnp.bfloat16)


def partial_sums(
    me, src_cluster, tgt_cluster, src_points, tgt_points, src_factor, tgt_factor, n_dev, n_tgt
):
    rows, features = src_points.shape
    rank = src_factor.shape[1]
    chunk = 2 * features // n_dev + TABLE_ROWS
    shape = (n_dev // (2 * n_tgt), n_tgt, chunk, rank)
    vmem = pl.BlockSpec(memory_space=pltpu.VMEM)
    return pl.pallas_call(
        functools.partial(contract_kernel, n_dev, n_tgt),
        out_shape=(
            jax.ShapeDtypeStruct(shape, jnp.float32),
            jax.ShapeDtypeStruct(shape, jnp.bfloat16),
        ),
        in_specs=[pl.BlockSpec(memory_space=pltpu.SMEM)] + [vmem] * 2 + [in_hbm()] * 4,
        out_specs=(vmem, vmem),
        scratch_shapes=[
            pltpu.VMEM((rows, features), jnp.bfloat16),
            pltpu.VMEM((rows, rank), jnp.bfloat16),
            pltpu.VMEM((rows, features), jnp.bfloat16),
            pltpu.VMEM((rows, rank), jnp.bfloat16),
            pltpu.VMEM((n_dev // (2 * n_tgt), 2, n_tgt, chunk, rank), jnp.float32),
            pltpu.SemaphoreType.DMA((4,)),
        ],
        compiler_params=pltpu.CompilerParams(vmem_limit_bytes=PACK_VMEM_BYTES),
        cost_estimate=pl.CostEstimate(
            flops=4 * rows * features * rank,
            bytes_accessed=4 * rows * (features + rank) + 4 * n_dev * chunk * rank,
            transcendentals=0,
        ),
        name="partial_sums",
    )(me[None], src_cluster[None, :], tgt_cluster[None, :], tgt_points, tgt_factor, src_points, src_factor)


def pack_kernel(n_group, capacity, spread, n_kinds, *refs):
    clusters = refs[:n_kinds]
    hbm = refs[n_kinds : 3 * n_kinds]
    packed_hbm = refs[3 * n_kinds]
    held = refs[3 * n_kinds + 1 : 5 * n_kinds + 1]
    packed, in_sem, out_sem = refs[5 * n_kinds + 1 :]
    arrivals = [pltpu.make_async_copy(a, b, in_sem.at[i]) for i, (a, b) in enumerate(zip(hbm, held))]
    for copy in arrivals:
        copy.start()
    slots = [
        slot_row(cluster[...], n_group, n_kinds * capacity, spread, kind * capacity)
        for kind, cluster in enumerate(clusters)
    ]
    for copy in arrivals:
        copy.wait()
    rows, features = held[0].shape
    block = 256
    departures = []
    for part in range(packed.shape[0] // block):
        mine = pl.ds(part * block, block)
        index = lax.broadcasted_iota(jnp.int32, (block, rows), 0) + part * block
        moved = carried = None
        for kind in range(n_kinds):
            place = (index == slots[kind]).astype(jnp.bfloat16)
            a = jnp.dot(place, held[2 * kind][...], preferred_element_type=jnp.float32)
            b = jnp.dot(place, held[2 * kind + 1][...], preferred_element_type=jnp.float32)
            moved = a if moved is None else moved + a
            carried = b if carried is None else carried + b
        packed[mine, :features] = moved.astype(jnp.bfloat16)
        packed[mine, features:] = carried.astype(jnp.bfloat16)
        departures.append(
            pltpu.make_async_copy(packed.at[mine], packed_hbm.at[mine], out_sem.at[part])
        )
        departures[-1].start()
    for copy in departures:
        copy.wait()


def pack(kinds, n_group, capacity, spread):
    n_kinds = len(kinds)
    rows, features = kinds[0][1].shape
    rank = kinds[0][2].shape[1]
    slots = n_kinds * n_group * capacity
    held = [pltpu.VMEM((rows, features), jnp.bfloat16), pltpu.VMEM((rows, rank), jnp.bfloat16)]
    return pl.pallas_call(
        functools.partial(pack_kernel, n_group, capacity, spread, n_kinds),
        out_shape=jax.ShapeDtypeStruct((slots, features + rank), jnp.bfloat16),
        in_specs=[pl.BlockSpec(memory_space=pltpu.VMEM)] * n_kinds + [in_hbm()] * (2 * n_kinds),
        out_specs=in_hbm(),
        scratch_shapes=held * n_kinds
        + [
            pltpu.VMEM((slots, features + rank), jnp.bfloat16),
            pltpu.SemaphoreType.DMA((2 * n_kinds,)),
            pltpu.SemaphoreType.DMA((slots // 256,)),
        ],
        compiler_params=pltpu.CompilerParams(vmem_limit_bytes=PACK_VMEM_BYTES),
        cost_estimate=pl.CostEstimate(
            flops=2 * n_kinds * slots * rows * (features + rank),
            bytes_accessed=2 * (slots + n_kinds * rows) * (features + rank),
            transcendentals=0,
        ),
        name="pack_rows",
    )(
        *[cluster[None, :] for cluster, _, _ in kinds],
        *[array for _, points, factor in kinds for array in (points, factor)],
    )


def digits_of(size, stride):
    bits = size.bit_length() - 1
    found = []
    while bits:
        take = 1 if bits % 2 else 2
        found.append((stride, 1 << take))
        stride <<= take
        bits -= take
    return found


class Chain:
    def __init__(self, own, other, n_src, n_tgt):
        self.n_dev = n_src * n_tgt
        first = (n_tgt, 2)
        src, tgt = digits_of(n_src // 2, 2 * n_tgt), digits_of(n_tgt, 1)
        self.plane, self.along = [first] + src, tgt
        self.dims = src[::-1] + [first] + tgt[::-1]
        self.left = [d for d in self.dims if d != first]
        x = own + self.sent(other, n_tgt).astype(jnp.float32)
        self.x = x.reshape(tuple(radix for _, radix in self.left) + own.shape[2:])

    def sent(self, array, mask):
        return lax.ppermute(array, ALL, [(i, i ^ mask) for i in range(self.n_dev)])

    def scatter(self, digit):
        stride, radix = digit
        dim = self.left.index(digit)
        mine = (lax.axis_index(ALL) // stride) % radix
        total = lax.dynamic_index_in_dim(self.x, mine, dim, keepdims=False)
        for j in range(1, radix):
            piece = lax.dynamic_index_in_dim(self.x, mine ^ j, dim, keepdims=False)
            total = total + self.sent(piece.astype(jnp.bfloat16), j * stride).astype(jnp.float32)
        self.x = total
        self.left.remove(digit)

    def gather(self, digit):
        stride, radix = digit
        mine = (lax.axis_index(ALL) // stride) % radix
        x = self.x.astype(jnp.bfloat16)
        got = [x] + [self.sent(x, j * stride) for j in range(1, radix)]
        self.left = [d for d in self.dims if d in self.left or d == digit]
        self.x = jnp.stack(
            [lax.select_n(mine ^ d, *got) if radix > 2 else jnp.where(mine == d, *got) for d in range(radix)],
            axis=self.left.index(digit),
        )


def update_kernel(
    src_points_ref, tgt_points_ref, src_factor_ref, tgt_factor_ref, marginal_ref, sums_ref, src_ref, tgt_ref
):
    tgt_total, src_total = totals_of(sums_ref)
    src_ref[...] = mirror_step(src_points_ref[...], tgt_total, src_factor_ref[...], marginal_ref[...])
    tgt_ref[...] = mirror_step(tgt_points_ref[...], src_total, tgt_factor_ref[...], marginal_ref[...])


def updates(src_points, tgt_points, src_factor, tgt_factor, marginal, sums):
    rows, features = src_points.shape
    rank = src_factor.shape[1]
    shape = jax.ShapeDtypeStruct(src_factor.shape, jnp.bfloat16)
    return pl.pallas_call(
        update_kernel,
        out_shape=(shape, shape),
        compiler_params=pltpu.CompilerParams(vmem_limit_bytes=VMEM_BYTES),
        cost_estimate=pl.CostEstimate(
            flops=4 * rows * features * rank,
            bytes_accessed=4 * rows * (features + 2 * rank),
            transcendentals=2 * rows * rank,
        ),
        name="mirror_updates",
    )(src_points, tgt_points, src_factor, tgt_factor, marginal[None, :], sums)


def owner_kernel(
    features,
    src_ref,
    near_ref,
    far_ref,
    sums_ref,
    marginal_ref,
    src_label_ref,
    tgt_label_ref,
    out_hbm,
    tgt_rows,
    tgt_update,
    tgt_inv,
    images,
    out_sem,
):
    n_group, capacity, width = src_ref.shape
    slots = n_group * capacity
    rank = width - features
    block = 256
    marginal = marginal_ref[...]
    piece = block // capacity
    tgt_total, src_total = totals_of(sums_ref)

    for which, ref in enumerate((near_ref, far_ref)):
        for part in range(slots // block):
            mine = pl.ds(which * slots + part * block, block)
            both = ref[pl.ds(part * piece, piece)].reshape(block, width)
            rows = both[:, :features]
            tgt_rows[mine, :] = rows
            tgt_update[mine, :] = mirror_step(rows, src_total, both[:, features:], marginal)
            tgt_inv[:, mine] = inverse_norm(rows).reshape(1, block)

    departures = []
    for part in range(slots // block):
        mine = pl.ds(part * block, block)
        both = src_ref[pl.ds(part * piece, piece)].reshape(block, width)
        rows = both[:, :features]
        update = mirror_step(rows, tgt_total, both[:, features:], marginal)
        cosine = contract_columns(rows, tgt_rows[...]) * inverse_norm(rows) * tgt_inv[...]
        weight = contract_columns(update, tgt_update[...]) / rank
        label = src_label_ref[mine, :]
        same = jnp.logical_and(label == tgt_label_ref[...], label > 0)
        kernel = jnp.where(same, weight * jnp.exp((cosine - 1.0) / TEMPER), 0.0)
        denominator = jnp.sum(kernel, axis=1, keepdims=True)
        denominator = jnp.where(denominator > 0, denominator, 1.0)
        transport = (kernel / denominator).astype(jnp.bfloat16)
        images[mine, :] = jnp.dot(
            transport, tgt_rows[...], preferred_element_type=jnp.float32
        ).astype(jnp.bfloat16)
        departures.append(
            pltpu.make_async_copy(images.at[mine], out_hbm.at[mine], out_sem.at[part])
        )
        departures[-1].start()
    for copy in departures:
        copy.wait()


def owner_maps(near, far, sums, marginal, src_labels, tgt_labels, features):
    n_group, capacity, width = far.shape
    slots = n_group * capacity
    rank = width - features
    return pl.pallas_call(
        functools.partial(owner_kernel, features),
        out_shape=jax.ShapeDtypeStruct((slots, features), jnp.bfloat16),
        grid=(1,),
        in_specs=[
            pl.BlockSpec((n_group, None, capacity, width), lambda step: (0, 1, 0, 0)),
            pl.BlockSpec((n_group, None, capacity, width), lambda step: (0, 0, 0, 0)),
            whole(far.shape),
            whole(sums.shape),
            whole((1, rank)),
            whole((slots, 1)),
            whole((1, 2 * slots)),
        ],
        out_specs=in_hbm(),
        scratch_shapes=[
            pltpu.VMEM((2 * slots, features), jnp.bfloat16),
            pltpu.VMEM((2 * slots, rank), jnp.bfloat16),
            pltpu.VMEM((1, 2 * slots), jnp.float32),
            pltpu.VMEM((slots, features), jnp.bfloat16),
            pltpu.SemaphoreType.DMA((slots // 256,)),
        ],
        compiler_params=pltpu.CompilerParams(vmem_limit_bytes=VMEM_BYTES),
        cost_estimate=pl.CostEstimate(
            flops=2 * slots * features * (3 * rank + 4 * slots),
            bytes_accessed=8 * slots * width,
            transcendentals=2 * slots * slots,
        ),
        name="owner_maps",
    )(
        near,
        near,
        far,
        sums,
        marginal[None, :],
        src_labels[:, None],
        tgt_labels[None, :],
    )


def labels_of(clusters, owner, capacity, spread):
    rows = clusters.shape[1]
    mine = clusters // spread == owner
    before = (jnp.arange(rows)[:, None] < jnp.arange(rows)[None, :]).astype(jnp.bfloat16)
    earlier = jnp.dot(mine.astype(jnp.bfloat16), before, preferred_element_type=jnp.float32)
    ranking = jnp.where(mine, earlier.astype(jnp.int32), -1)
    value = clusters - owner * spread + 1
    hit = ranking[:, None, :] == jnp.arange(capacity, dtype=jnp.int32)[None, :, None]
    return jnp.sum(jnp.where(hit, value[:, None, :], 0), axis=2).reshape(-1)


def exchange(rows):
    return lax.all_to_all(rows, GROUP, split_axis=0, concat_axis=0, tiled=True)


def per_device(
    src_points, tgt_points, src_factor, tgt_factor, inner_marginal, src_cluster, tgt_cluster
):
    n_src, n_rest = lax.axis_size("src"), lax.axis_size(REST)
    n_group = n_src * n_rest
    n_dev = 2 * n_group
    rows, features = src_points.shape
    rank = src_factor.shape[1]
    capacity = 2 * (2 * rows // n_dev)
    spread = 2 * CL_DEV
    slots = n_group * capacity
    me = lax.axis_index(ALL)
    my_half = lax.axis_index(HALF)
    owner = lax.axis_index(GROUP)

    across = [(0, 1), (1, 0)]
    far_points, far_factor, far_cluster = (
        lax.ppermute(array, HALF, across) for array in (tgt_points, tgt_factor, tgt_cluster)
    )
    own, other = partial_sums(
        me,
        src_cluster,
        tgt_cluster,
        src_points,
        tgt_points,
        src_factor,
        tgt_factor,
        n_dev,
        2 * n_rest,
    )
    chain = Chain(own, other, n_src, 2 * n_rest)
    for digit in chain.plane[1:]:
        chain.scatter(digit)
    near_tgt_cluster, near_src_cluster, chain.x = lax.optimization_barrier(
        (tgt_cluster, src_cluster, chain.x)
    )
    near = exchange(
        pack(
            [
                (near_tgt_cluster, tgt_points, tgt_factor),
                (near_src_cluster, src_points, src_factor),
            ],
            n_group,
            capacity,
            spread,
        )
    )
    for digit in chain.along:
        chain.scatter(digit)
    chain.x, far_points, far_factor, far_cluster = lax.optimization_barrier(
        (chain.x, far_points, far_factor, far_cluster)
    )
    for digit in reversed(chain.along):
        chain.gather(digit)
    far_cluster, near, chain.x = lax.optimization_barrier((far_cluster, near, chain.x))
    far = exchange(pack([(far_cluster, far_points, far_factor)], n_group, capacity, spread))
    for digit in reversed(chain.plane):
        chain.gather(digit)
    sums = chain.x.reshape(n_dev, -1, rank)

    kept = 2 * features // n_dev
    table = sums[:, kept : kept + 2].astype(jnp.int32).reshape(n_src, 2, n_rest, 2, rows)
    near_table = lax.dynamic_index_in_dim(table, my_half, 1, keepdims=False)
    far_table = lax.dynamic_index_in_dim(table, 1 - my_half, 1, keepdims=False)
    near_table = near_table.reshape(n_group, 2, rows)
    far_table = far_table.reshape(n_group, 2, rows)
    src_labels = labels_of(near_table[:, 0], owner, capacity, spread)
    tgt_labels = jnp.concatenate(
        [
            labels_of(near_table[:, 1], owner, capacity, spread),
            labels_of(far_table[:, 1], owner, capacity, spread),
        ]
    )

    width = features + rank
    images = owner_maps(
        near.reshape(n_group, 2, capacity, width),
        far.reshape(n_group, capacity, width),
        sums,
        inner_marginal,
        src_labels,
        tgt_labels,
        features,
    )
    returned = exchange(images)

    src_update, tgt_update = updates(
        src_points, tgt_points, src_factor, tgt_factor, inner_marginal, sums
    )
    slot = slot_row(src_cluster[None, :], n_group, capacity, spread, 0)
    back = (jnp.arange(slots, dtype=jnp.int32)[:, None] == slot).astype(jnp.bfloat16)
    back = lax.optimization_barrier(back)
    mapped = contract_rows(back, returned).astype(jnp.bfloat16)
    return (src_update, tgt_update, mapped)


def solution(mesh):
    n_src, n_tgt = mesh.shape["src"], mesh.shape["tgt"]
    halves = Mesh(mesh.devices.reshape(n_src, 2, n_tgt // 2), ALL)
    rows = P(ALL, None)
    return jax.shard_map(
        per_device,
        mesh=halves,
        in_specs=(rows, rows, rows, rows, P(), P(ALL), P(ALL)),
        out_specs=(rows, rows, rows),
        check_vma=False,
    )
```

```python
import functools

import jax
import jax.numpy as jnp
from jax import lax
from jax.experimental import pallas as pl
from jax.experimental.pallas import tpu as pltpu
from jax.sharding import Mesh
from jax.sharding import PartitionSpec as P

CL_DEV = 2

GAMMA = 2.0
TEMPER = 0.03
EPS = 1e-06

HALF, REST = "half", "rest"
ALL = ("src", HALF, REST)
GROUP = ("src", REST)
VMEM_BYTES = 48 * 1024 * 1024
PACK_VMEM_BYTES = 62 * 1024 * 1024
TABLE_ROWS = 8
BLOCK_ROWS = 16
OWNER_BLOCK = 256


def contract_rows(left, right):
    return lax.dot_general(
        left, right, (((0,), (0,)), ((), ())), preferred_element_type=jnp.float32
    )


def contract_columns(left, right):
    return lax.dot_general(
        left, right, (((1,), (1,)), ((), ())), preferred_element_type=jnp.float32
    )


def mirror_step(points, total_round, factor, inner_marginal):
    gradient = -contract_columns(points, total_round) / inner_marginal
    row_scale = jnp.max(jnp.abs(gradient), axis=1, keepdims=True) + EPS
    tilted = factor.astype(jnp.float32) * jnp.exp(-GAMMA * gradient / row_scale)
    mean = jnp.mean(tilted, axis=1, keepdims=True)
    mean = jnp.where(mean > 0, mean, 1.0)
    return (tilted / mean).astype(jnp.bfloat16)


def inverse_norm(rows):
    return lax.rsqrt(jnp.sum(jnp.square(rows.astype(jnp.float32)), axis=1, keepdims=True) + EPS)


def blocks_of(n_dev, chunk, rank, features):
    kept = (chunk - TABLE_ROWS) // BLOCK_ROWS
    wide = features // rank
    return [
        (b // kept, b % kept * BLOCK_ROWS, b // wide * BLOCK_ROWS, b % wide * rank)
        for b in range(n_dev * kept)
    ]


def totals_of(sums_ref, total, features):
    n_dev, chunk, rank = sums_ref.shape
    for c, row, first, column in blocks_of(n_dev, chunk, rank, features):
        total[pl.ds(first, BLOCK_ROWS), pl.ds(column, rank)] = sums_ref[c, pl.ds(row, BLOCK_ROWS), :]


def whole(shape):
    return pl.BlockSpec(shape, lambda *_: (0,) * len(shape))


def in_hbm():
    return pl.BlockSpec(memory_space=pltpu.HBM)


def slot_row(cluster, n_group, capacity, spread, first):
    rows = cluster.shape[1]
    owners = cluster // spread
    onehot = owners == lax.broadcasted_iota(jnp.int32, (n_group, rows), 0)
    before = lax.broadcasted_iota(jnp.int32, (rows, rows), 0) < lax.broadcasted_iota(
        jnp.int32, (rows, rows), 1
    )
    earlier = jnp.dot(
        onehot.astype(jnp.bfloat16), before.astype(jnp.bfloat16), preferred_element_type=jnp.float32
    )
    ranking = jnp.sum(jnp.where(onehot, earlier, 0.0), axis=0, keepdims=True).astype(jnp.int32)
    return owners * capacity + ranking + first


def contract_kernel(n_dev, n_tgt, me_ref, src_cluster_ref, tgt_cluster_ref, *refs):
    hbm, (own_ref, other_ref), held, parts, in_sem = refs[:4], refs[4:6], refs[6:10], refs[10], refs[11]
    arrivals = [pltpu.make_async_copy(a, b, in_sem.at[i]) for i, (a, b) in enumerate(zip(hbm, held))]
    for copy in arrivals:
        copy.start()
    tgt_points, tgt_factor, src_points, src_factor = held
    _, _, _, chunk, rank = parts.shape
    kept = chunk - TABLE_ROWS
    me = me_ref[0]
    mine = (me // n_tgt) % 2
    row = lax.broadcasted_iota(jnp.int32, (TABLE_ROWS, rank), 0)
    table = jnp.where(row == 0, src_cluster_ref[...], jnp.where(row == 1, tgt_cluster_ref[...], 0))
    parts[:, :, :, kept:, :] = jnp.zeros(parts.shape[:3] + (TABLE_ROWS, rank), jnp.float32)
    parts[me // (2 * n_tgt), mine, me % n_tgt, kept:, :] = table.astype(jnp.float32)
    features = tgt_points.shape[1]
    blocks = blocks_of(n_dev, chunk, rank, features)
    for which, (points, factor) in enumerate(((tgt_points, tgt_factor), (src_points, src_factor))):
        arrivals[2 * which].wait()
        arrivals[2 * which + 1].wait()
        total = contract_rows(factor[...], points[...])
        for c, row, first, column in blocks:
            first -= which * rank
            if 0 <= first < rank:
                place = (c // (2 * n_tgt), c // n_tgt % 2, c % n_tgt)
                parts[(*place, pl.ds(row, BLOCK_ROWS))] = total[
                    first : first + BLOCK_ROWS, column : column + rank
                ]
    for i in range(parts.shape[0]):
        own_ref[i] = parts[i, mine]
        other_ref[i] = parts[i, 1 - mine].astype(jnp.bfloat16)


def partial_sums(
    me, src_cluster, tgt_cluster, src_points, tgt_points, src_factor, tgt_factor, n_dev, n_tgt
):
    rows, features = src_points.shape
    rank = src_factor.shape[1]
    chunk = 2 * features // n_dev + TABLE_ROWS
    shape = (n_dev // (2 * n_tgt), n_tgt, chunk, rank)
    vmem = pl.BlockSpec(memory_space=pltpu.VMEM)
    return pl.pallas_call(
        functools.partial(contract_kernel, n_dev, n_tgt),
        out_shape=(
            jax.ShapeDtypeStruct(shape, jnp.float32),
            jax.ShapeDtypeStruct(shape, jnp.bfloat16),
        ),
        in_specs=[pl.BlockSpec(memory_space=pltpu.SMEM)] + [vmem] * 2 + [in_hbm()] * 4,
        out_specs=(vmem, vmem),
        scratch_shapes=[
            pltpu.VMEM((rows, features), jnp.bfloat16),
            pltpu.VMEM((rows, rank), jnp.bfloat16),
            pltpu.VMEM((rows, features), jnp.bfloat16),
            pltpu.VMEM((rows, rank), jnp.bfloat16),
            pltpu.VMEM((n_dev // (2 * n_tgt), 2, n_tgt, chunk, rank), jnp.float32),
            pltpu.SemaphoreType.DMA((4,)),
        ],
        compiler_params=pltpu.CompilerParams(vmem_limit_bytes=PACK_VMEM_BYTES),
        cost_estimate=pl.CostEstimate(
            flops=4 * rows * features * rank,
            bytes_accessed=4 * rows * (features + rank) + 4 * n_dev * chunk * rank,
            transcendentals=0,
        ),
        name="partial_sums",
    )(me[None], src_cluster[None, :], tgt_cluster[None, :], tgt_points, tgt_factor, src_points, src_factor)


def pack_kernel(n_group, capacity, spread, n_kinds, *refs):
    clusters = refs[:n_kinds]
    hbm = refs[n_kinds : 3 * n_kinds]
    packed_hbm = refs[3 * n_kinds]
    held = refs[3 * n_kinds + 1 : 5 * n_kinds + 1]
    packed, in_sem, out_sem = refs[5 * n_kinds + 1 :]
    arrivals = [pltpu.make_async_copy(a, b, in_sem.at[i]) for i, (a, b) in enumerate(zip(hbm, held))]
    for copy in arrivals:
        copy.start()
    slots = [
        slot_row(cluster[...], n_group, n_kinds * capacity, spread, kind * capacity)
        for kind, cluster in enumerate(clusters)
    ]
    for copy in arrivals:
        copy.wait()
    rows, features = held[0].shape
    block = 256
    departures = []
    for part in range(packed.shape[0] // block):
        mine = pl.ds(part * block, block)
        index = lax.broadcasted_iota(jnp.int32, (block, rows), 0) + part * block
        moved = carried = None
        for kind in range(n_kinds):
            place = (index == slots[kind]).astype(jnp.bfloat16)
            a = jnp.dot(place, held[2 * kind][...], preferred_element_type=jnp.float32)
            b = jnp.dot(place, held[2 * kind + 1][...], preferred_element_type=jnp.float32)
            moved = a if moved is None else moved + a
            carried = b if carried is None else carried + b
        packed[mine, :features] = moved.astype(jnp.bfloat16)
        packed[mine, features:] = carried.astype(jnp.bfloat16)
        departures.append(
            pltpu.make_async_copy(packed.at[mine], packed_hbm.at[mine], out_sem.at[part])
        )
        departures[-1].start()
    for copy in departures:
        copy.wait()


def pack(kinds, n_group, capacity, spread):
    n_kinds = len(kinds)
    rows, features = kinds[0][1].shape
    rank = kinds[0][2].shape[1]
    slots = n_kinds * n_group * capacity
    held = [pltpu.VMEM((rows, features), jnp.bfloat16), pltpu.VMEM((rows, rank), jnp.bfloat16)]
    return pl.pallas_call(
        functools.partial(pack_kernel, n_group, capacity, spread, n_kinds),
        out_shape=jax.ShapeDtypeStruct((slots, features + rank), jnp.bfloat16),
        in_specs=[pl.BlockSpec(memory_space=pltpu.VMEM)] * n_kinds + [in_hbm()] * (2 * n_kinds),
        out_specs=in_hbm(),
        scratch_shapes=held * n_kinds
        + [
            pltpu.VMEM((slots, features + rank), jnp.bfloat16),
            pltpu.SemaphoreType.DMA((2 * n_kinds,)),
            pltpu.SemaphoreType.DMA((slots // 256,)),
        ],
        compiler_params=pltpu.CompilerParams(vmem_limit_bytes=PACK_VMEM_BYTES),
        cost_estimate=pl.CostEstimate(
            flops=2 * n_kinds * slots * rows * (features + rank),
            bytes_accessed=2 * (slots + n_kinds * rows) * (features + rank),
            transcendentals=0,
        ),
        name="pack_rows",
    )(
        *[cluster[None, :] for cluster, _, _ in kinds],
        *[array for _, points, factor in kinds for array in (points, factor)],
    )


def digits_of(size, stride):
    bits = size.bit_length() - 1
    found = []
    while bits:
        take = 1 if bits % 2 else 2
        found.append((stride, 1 << take))
        stride <<= take
        bits -= take
    return found


class Chain:
    def __init__(self, own, other, n_src, n_tgt):
        self.n_dev = n_src * n_tgt
        first = (n_tgt, 2)
        src, tgt = digits_of(n_src // 2, 2 * n_tgt), digits_of(n_tgt, 1)
        self.plane, self.along = [first] + src, tgt
        self.dims = src[::-1] + [first] + tgt[::-1]
        self.left = [d for d in self.dims if d != first]
        x = own + self.sent(other, n_tgt).astype(jnp.float32)
        self.x = x.reshape(tuple(radix for _, radix in self.left) + own.shape[2:])

    def sent(self, array, mask):
        return lax.ppermute(array, ALL, [(i, i ^ mask) for i in range(self.n_dev)])

    def scatter(self, digit):
        stride, radix = digit
        dim = self.left.index(digit)
        mine = (lax.axis_index(ALL) // stride) % radix
        total = lax.dynamic_index_in_dim(self.x, mine, dim, keepdims=False)
        for j in range(1, radix):
            piece = lax.dynamic_index_in_dim(self.x, mine ^ j, dim, keepdims=False)
            total = total + self.sent(piece.astype(jnp.bfloat16), j * stride).astype(jnp.float32)
        self.x = total
        self.left.remove(digit)

    def gather(self, digit):
        stride, radix = digit
        mine = (lax.axis_index(ALL) // stride) % radix
        x = self.x.astype(jnp.bfloat16)
        got = [x] + [self.sent(x, j * stride) for j in range(1, radix)]
        self.left = [d for d in self.dims if d in self.left or d == digit]
        self.x = jnp.stack(
            [lax.select_n(mine ^ d, *got) if radix > 2 else jnp.where(mine == d, *got) for d in range(radix)],
            axis=self.left.index(digit),
        )


def update_kernel(
    src_points_ref,
    tgt_points_ref,
    src_factor_ref,
    tgt_factor_ref,
    marginal_ref,
    sums_ref,
    src_ref,
    tgt_ref,
    total,
):
    totals_of(sums_ref, total, src_points_ref.shape[1])
    rank = src_ref.shape[1]
    marginal = marginal_ref[...]
    src_ref[...] = mirror_step(src_points_ref[...], total[:rank], src_factor_ref[...], marginal)
    tgt_ref[...] = mirror_step(tgt_points_ref[...], total[rank:], tgt_factor_ref[...], marginal)


def updates(src_points, tgt_points, src_factor, tgt_factor, marginal, sums):
    rows, features = src_points.shape
    rank = src_factor.shape[1]
    shape = jax.ShapeDtypeStruct(src_factor.shape, jnp.bfloat16)
    return pl.pallas_call(
        update_kernel,
        out_shape=(shape, shape),
        scratch_shapes=[pltpu.VMEM((2 * rank, features), jnp.bfloat16)],
        compiler_params=pltpu.CompilerParams(vmem_limit_bytes=VMEM_BYTES),
        cost_estimate=pl.CostEstimate(
            flops=4 * rows * features * rank,
            bytes_accessed=4 * rows * (features + 2 * rank),
            transcendentals=2 * rows * rank,
        ),
        name="mirror_updates",
    )(src_points, tgt_points, src_factor, tgt_factor, marginal[None, :], sums)


def seen_block(ref, part, block):
    piece = block // ref.shape[1]
    return ref[pl.ds(part * piece, piece)].reshape(block, ref.shape[2])


def prepare_targets(ref, src_total, marginal, features, tgt_rows, tgt_update, tgt_inv):
    block = OWNER_BLOCK
    for part in range(tgt_rows.shape[0] // block):
        mine = pl.ds(part * block, block)
        both = seen_block(ref, part, block)
        rows = both[:, :features]
        tgt_rows[mine, :] = rows
        tgt_update[mine, :] = mirror_step(rows, src_total, both[:, features:], marginal)
        tgt_inv[:, mine] = inverse_norm(rows).reshape(1, block)


def block_terms(rows, update, src_label, tgt_label, tgt_rows, tgt_update, tgt_inv):
    cosine = contract_columns(rows, tgt_rows[...]) * inverse_norm(rows) * tgt_inv[...]
    weight = contract_columns(update, tgt_update[...]) / update.shape[1]
    same = jnp.logical_and(src_label == tgt_label, src_label > 0)
    kernel = jnp.where(same, weight * jnp.exp((cosine - 1.0) / TEMPER), 0.0)
    image = jnp.dot(
        kernel.astype(jnp.bfloat16), tgt_rows[...], preferred_element_type=jnp.float32
    )
    return image, jnp.sum(kernel, axis=1, keepdims=True)


def near_kernel(
    features,
    src_ref,
    tgt_ref,
    sums_ref,
    marginal_ref,
    src_label_ref,
    tgt_label_ref,
    image_ref,
    denominator_ref,
    update_ref,
    total,
    tgt_rows,
    tgt_update,
    tgt_inv,
):
    totals_of(sums_ref, total, features)
    rank = update_ref.shape[1]
    marginal = marginal_ref[...]
    prepare_targets(tgt_ref, total[rank:], marginal, features, tgt_rows, tgt_update, tgt_inv)
    block = OWNER_BLOCK
    for part in range(update_ref.shape[0] // block):
        mine = pl.ds(part * block, block)
        both = seen_block(src_ref, part, block)
        rows = both[:, :features]
        update = mirror_step(rows, total[:rank], both[:, features:], marginal)
        update_ref[mine, :] = update
        image, denominator = block_terms(
            rows, update, src_label_ref[mine, :], tgt_label_ref[...], tgt_rows, tgt_update, tgt_inv
        )
        image_ref[mine, :] = image
        denominator_ref[mine, :] = denominator


def far_kernel(
    features,
    src_ref,
    tgt_ref,
    sums_ref,
    marginal_ref,
    src_label_ref,
    tgt_label_ref,
    image_ref,
    denominator_ref,
    update_ref,
    out_hbm,
    total,
    tgt_rows,
    tgt_update,
    tgt_inv,
    images,
    out_sem,
):
    totals_of(sums_ref, total, features)
    rank = update_ref.shape[1]
    prepare_targets(tgt_ref, total[rank:], marginal_ref[...], features, tgt_rows, tgt_update, tgt_inv)
    block = OWNER_BLOCK
    departures = []
    for part in range(update_ref.shape[0] // block):
        mine = pl.ds(part * block, block)
        rows = seen_block(src_ref, part, block)[:, :features]
        image, denominator = block_terms(
            rows,
            update_ref[mine, :],
            src_label_ref[mine, :],
            tgt_label_ref[...],
            tgt_rows,
            tgt_update,
            tgt_inv,
        )
        denominator = denominator + denominator_ref[mine, :]
        denominator = jnp.where(denominator > 0, denominator, 1.0)
        images[mine, :] = ((image_ref[mine, :] + image) / denominator).astype(jnp.bfloat16)
        departures.append(
            pltpu.make_async_copy(images.at[mine], out_hbm.at[mine], out_sem.at[part])
        )
        departures[-1].start()
    for copy in departures:
        copy.wait()


def owner_cost(slots, width):
    return pl.CostEstimate(
        flops=2 * slots * width * (512 + 2 * slots),
        bytes_accessed=8 * slots * width,
        transcendentals=slots * slots,
    )


def near_maps(near, sums, marginal, src_labels, tgt_labels, features):
    n_group, _, capacity, width = near.shape
    slots = n_group * capacity
    rank = width - features
    shapes = [((slots, features), jnp.float32), ((slots, 1), jnp.float32), ((slots, rank), jnp.bfloat16)]
    return pl.pallas_call(
        functools.partial(near_kernel, features),
        out_shape=[jax.ShapeDtypeStruct(*shape) for shape in shapes],
        grid=(1,),
        in_specs=[
            pl.BlockSpec((n_group, None, capacity, width), lambda step: (0, 1, 0, 0)),
            pl.BlockSpec((n_group, None, capacity, width), lambda step: (0, 0, 0, 0)),
            whole(sums.shape),
            whole((1, rank)),
            whole((slots, 1)),
            whole((1, slots)),
        ],
        out_specs=[whole(shape) for shape, _ in shapes],
        scratch_shapes=[
            pltpu.VMEM((2 * rank, features), jnp.bfloat16),
            pltpu.VMEM((slots, features), jnp.bfloat16),
            pltpu.VMEM((slots, rank), jnp.bfloat16),
            pltpu.VMEM((1, slots), jnp.float32),
        ],
        compiler_params=pltpu.CompilerParams(vmem_limit_bytes=VMEM_BYTES),
        cost_estimate=owner_cost(slots, width),
        name="near_maps",
    )(near, near, sums, marginal[None, :], src_labels[:, None], tgt_labels[None, :])


def far_maps(near, far, sums, marginal, src_labels, tgt_labels, image, denominator, update):
    n_group, capacity, width = far.shape
    slots = n_group * capacity
    rank = update.shape[1]
    features = width - rank
    return pl.pallas_call(
        functools.partial(far_kernel, features),
        out_shape=jax.ShapeDtypeStruct((slots, features), jnp.bfloat16),
        grid=(1,),
        in_specs=[
            pl.BlockSpec((n_group, None, capacity, width), lambda step: (0, 1, 0, 0)),
            whole(far.shape),
            whole(sums.shape),
            whole((1, rank)),
            whole((slots, 1)),
            whole((1, slots)),
            whole(image.shape),
            whole(denominator.shape),
            whole(update.shape),
        ],
        out_specs=in_hbm(),
        scratch_shapes=[
            pltpu.VMEM((2 * rank, features), jnp.bfloat16),
            pltpu.VMEM((slots, features), jnp.bfloat16),
            pltpu.VMEM((slots, rank), jnp.bfloat16),
            pltpu.VMEM((1, slots), jnp.float32),
            pltpu.VMEM((slots, features), jnp.bfloat16),
            pltpu.SemaphoreType.DMA((slots // OWNER_BLOCK,)),
        ],
        compiler_params=pltpu.CompilerParams(vmem_limit_bytes=VMEM_BYTES),
        cost_estimate=owner_cost(slots, width),
        name="far_maps",
    )(
        near,
        far,
        sums,
        marginal[None, :],
        src_labels[:, None],
        tgt_labels[None, :],
        image,
        denominator,
        update,
    )


def labels_of(clusters, owner, capacity, spread):
    rows = clusters.shape[1]
    mine = clusters // spread == owner
    before = (jnp.arange(rows)[:, None] < jnp.arange(rows)[None, :]).astype(jnp.bfloat16)
    earlier = jnp.dot(mine.astype(jnp.bfloat16), before, preferred_element_type=jnp.float32)
    ranking = jnp.where(mine, earlier.astype(jnp.int32), -1)
    value = clusters - owner * spread + 1
    hit = ranking[:, None, :] == jnp.arange(capacity, dtype=jnp.int32)[None, :, None]
    return jnp.sum(jnp.where(hit, value[:, None, :], 0), axis=2).reshape(-1)


def exchange(rows):
    return lax.all_to_all(rows, GROUP, split_axis=0, concat_axis=0, tiled=True)


def per_device(
    src_points, tgt_points, src_factor, tgt_factor, inner_marginal, src_cluster, tgt_cluster
):
    n_src, n_rest = lax.axis_size("src"), lax.axis_size(REST)
    n_group = n_src * n_rest
    n_dev = 2 * n_group
    rows, features = src_points.shape
    rank = src_factor.shape[1]
    capacity = 2 * (2 * rows // n_dev)
    spread = 2 * CL_DEV
    slots = n_group * capacity
    me = lax.axis_index(ALL)
    my_half = lax.axis_index(HALF)
    owner = lax.axis_index(GROUP)

    across = [(0, 1), (1, 0)]
    far_points, far_factor, far_cluster = (
        lax.ppermute(array, HALF, across) for array in (tgt_points, tgt_factor, tgt_cluster)
    )
    own, other = partial_sums(
        me,
        src_cluster,
        tgt_cluster,
        src_points,
        tgt_points,
        src_factor,
        tgt_factor,
        n_dev,
        2 * n_rest,
    )
    chain = Chain(own, other, n_src, 2 * n_rest)
    for digit in chain.plane[1:]:
        chain.scatter(digit)
    for digit in chain.along:
        chain.scatter(digit)
    for digit in reversed(chain.along):
        chain.gather(digit)
    near = pack(
        [(tgt_cluster, tgt_points, tgt_factor), (src_cluster, src_points, src_factor)],
        n_group,
        capacity,
        spread,
    )
    near, chain.x, far_points, far_factor, far_cluster = lax.optimization_barrier(
        (near, chain.x, far_points, far_factor, far_cluster)
    )
    near = exchange(near)
    far = pack([(far_cluster, far_points, far_factor)], n_group, capacity, spread)
    far, near = lax.optimization_barrier((far, near))
    far = exchange(far)
    for digit in reversed(chain.plane):
        chain.gather(digit)
    sums = chain.x.reshape(n_dev, -1, rank)

    kept = 2 * features // n_dev
    table = sums[:, kept : kept + 2].astype(jnp.int32).reshape(n_src, 2, n_rest, 2, rows)
    near_table = lax.dynamic_index_in_dim(table, my_half, 1, keepdims=False)
    far_table = lax.dynamic_index_in_dim(table, 1 - my_half, 1, keepdims=False)
    near_table = near_table.reshape(n_group, 2, rows)
    far_table = far_table.reshape(n_group, 2, rows)
    src_labels = labels_of(near_table[:, 0], owner, capacity, spread)
    near_labels = labels_of(near_table[:, 1], owner, capacity, spread)
    far_labels = labels_of(far_table[:, 1], owner, capacity, spread)

    near = near.reshape(n_group, 2, capacity, features + rank)
    far = far.reshape(n_group, capacity, features + rank)
    found = near_maps(near, sums, inner_marginal, src_labels, near_labels, features)
    images = far_maps(near, far, sums, inner_marginal, src_labels, far_labels, *found)
    returned = exchange(images)

    src_update, tgt_update = updates(
        src_points, tgt_points, src_factor, tgt_factor, inner_marginal, sums
    )
    slot = slot_row(src_cluster[None, :], n_group, capacity, spread, 0)
    back = slot.reshape(rows, 1) == jnp.arange(slots, dtype=jnp.int32)[None, :]
    back = lax.optimization_barrier(back.astype(jnp.bfloat16))
    mapped = jnp.dot(back, returned, preferred_element_type=jnp.float32).astype(jnp.bfloat16)
    return (src_update, tgt_update, mapped)


def solution(mesh):
    n_src, n_tgt = mesh.shape["src"], mesh.shape["tgt"]
    halves = Mesh(mesh.devices.reshape(n_src, 2, n_tgt // 2), ALL)
    rows = P(ALL, None)
    return jax.shard_map(
        per_device,
        mesh=halves,
        in_specs=(rows, rows, rows, rows, P(), P(ALL), P(ALL)),
        out_specs=(rows, rows, rows),
        check_vma=False,
    )
```

```python
import functools

import jax
import jax.numpy as jnp
from jax import lax
from jax.experimental import pallas as pl
from jax.experimental.pallas import tpu as pltpu
from jax.sharding import Mesh
from jax.sharding import PartitionSpec as P

CL_DEV = 2

GAMMA = 2.0
TEMPER = 0.03
EPS = 1e-06

HALF, REST = "half", "rest"
ALL = ("src", HALF, REST)
GROUP = ("src", REST)
VMEM_BYTES = 48 * 1024 * 1024
PACK_VMEM_BYTES = 62 * 1024 * 1024
TABLE_ROWS = 8
BLOCK_ROWS = 16
OWNER_BLOCK = 256


def contract_rows(left, right):
    return lax.dot_general(
        left, right, (((0,), (0,)), ((), ())), preferred_element_type=jnp.float32
    )


def contract_columns(left, right):
    return lax.dot_general(
        left, right, (((1,), (1,)), ((), ())), preferred_element_type=jnp.float32
    )


def mirror_step(points, total_round, factor, inner_marginal):
    gradient = -contract_columns(points, total_round) / inner_marginal
    row_scale = jnp.max(jnp.abs(gradient), axis=1, keepdims=True) + EPS
    tilted = factor.astype(jnp.float32) * jnp.exp(-GAMMA * gradient / row_scale)
    mean = jnp.mean(tilted, axis=1, keepdims=True)
    mean = jnp.where(mean > 0, mean, 1.0)
    return (tilted / mean).astype(jnp.bfloat16)


def inverse_norm(rows):
    return lax.rsqrt(jnp.sum(jnp.square(rows.astype(jnp.float32)), axis=1, keepdims=True) + EPS)


def blocks_of(n_dev, chunk, rank, features):
    kept = (chunk - TABLE_ROWS) // BLOCK_ROWS
    wide = features // rank
    return [
        (b // kept, b % kept * BLOCK_ROWS, b // wide * BLOCK_ROWS, b % wide * rank)
        for b in range(n_dev * kept)
    ]


def totals_of(sums_ref, total, features):
    n_dev, chunk, rank = sums_ref.shape
    for c, row, first, column in blocks_of(n_dev, chunk, rank, features):
        total[pl.ds(first, BLOCK_ROWS), pl.ds(column, rank)] = sums_ref[c, pl.ds(row, BLOCK_ROWS), :]


def whole(shape):
    return pl.BlockSpec(shape, lambda *_: (0,) * len(shape))


def in_hbm():
    return pl.BlockSpec(memory_space=pltpu.HBM)


def slot_row(cluster, n_group, capacity, spread, first):
    rows = cluster.shape[1]
    owners = cluster // spread
    onehot = owners == lax.broadcasted_iota(jnp.int32, (n_group, rows), 0)
    before = lax.broadcasted_iota(jnp.int32, (rows, rows), 0) < lax.broadcasted_iota(
        jnp.int32, (rows, rows), 1
    )
    earlier = jnp.dot(
        onehot.astype(jnp.bfloat16), before.astype(jnp.bfloat16), preferred_element_type=jnp.float32
    )
    ranking = jnp.sum(jnp.where(onehot, earlier, 0.0), axis=0, keepdims=True).astype(jnp.int32)
    return owners * capacity + ranking + first


def contract_kernel(n_dev, n_tgt, me_ref, src_cluster_ref, tgt_cluster_ref, *refs):
    hbm, (own_ref, other_ref), held, parts, in_sem = refs[:4], refs[4:6], refs[6:10], refs[10], refs[11]
    arrivals = [pltpu.make_async_copy(a, b, in_sem.at[i]) for i, (a, b) in enumerate(zip(hbm, held))]
    for copy in arrivals:
        copy.start()
    tgt_points, tgt_factor, src_points, src_factor = held
    _, _, _, chunk, rank = parts.shape
    kept = chunk - TABLE_ROWS
    me = me_ref[0]
    mine = (me // n_tgt) % 2
    row = lax.broadcasted_iota(jnp.int32, (TABLE_ROWS, rank), 0)
    table = jnp.where(row == 0, src_cluster_ref[...], jnp.where(row == 1, tgt_cluster_ref[...], 0))
    parts[:, :, :, kept:, :] = jnp.zeros(parts.shape[:3] + (TABLE_ROWS, rank), jnp.float32)
    parts[me // (2 * n_tgt), mine, me % n_tgt, kept:, :] = table.astype(jnp.float32)
    features = tgt_points.shape[1]
    blocks = blocks_of(n_dev, chunk, rank, features)
    for which, (points, factor) in enumerate(((tgt_points, tgt_factor), (src_points, src_factor))):
        arrivals[2 * which].wait()
        arrivals[2 * which + 1].wait()
        total = contract_rows(factor[...], points[...])
        for c, row, first, column in blocks:
            first -= which * rank
            if 0 <= first < rank:
                place = (c // (2 * n_tgt), c // n_tgt % 2, c % n_tgt)
                parts[(*place, pl.ds(row, BLOCK_ROWS))] = total[
                    first : first + BLOCK_ROWS, column : column + rank
                ]
    for i in range(parts.shape[0]):
        own_ref[i] = parts[i, mine]
        other_ref[i] = parts[i, 1 - mine].astype(jnp.bfloat16)


def partial_sums(
    me, src_cluster, tgt_cluster, src_points, tgt_points, src_factor, tgt_factor, n_dev, n_tgt
):
    rows, features = src_points.shape
    rank = src_factor.shape[1]
    chunk = 2 * features // n_dev + TABLE_ROWS
    shape = (n_dev // (2 * n_tgt), n_tgt, chunk, rank)
    vmem = pl.BlockSpec(memory_space=pltpu.VMEM)
    return pl.pallas_call(
        functools.partial(contract_kernel, n_dev, n_tgt),
        out_shape=(
            jax.ShapeDtypeStruct(shape, jnp.float32),
            jax.ShapeDtypeStruct(shape, jnp.bfloat16),
        ),
        in_specs=[pl.BlockSpec(memory_space=pltpu.SMEM)] + [vmem] * 2 + [in_hbm()] * 4,
        out_specs=(vmem, vmem),
        scratch_shapes=[
            pltpu.VMEM((rows, features), jnp.bfloat16),
            pltpu.VMEM((rows, rank), jnp.bfloat16),
            pltpu.VMEM((rows, features), jnp.bfloat16),
            pltpu.VMEM((rows, rank), jnp.bfloat16),
            pltpu.VMEM((n_dev // (2 * n_tgt), 2, n_tgt, chunk, rank), jnp.float32),
            pltpu.SemaphoreType.DMA((4,)),
        ],
        compiler_params=pltpu.CompilerParams(vmem_limit_bytes=PACK_VMEM_BYTES),
        cost_estimate=pl.CostEstimate(
            flops=4 * rows * features * rank,
            bytes_accessed=4 * rows * (features + rank) + 4 * n_dev * chunk * rank,
            transcendentals=0,
        ),
        name="partial_sums",
    )(me[None], src_cluster[None, :], tgt_cluster[None, :], tgt_points, tgt_factor, src_points, src_factor)


def pack_kernel(n_group, capacity, spread, n_kinds, *refs):
    clusters = refs[:n_kinds]
    hbm = refs[n_kinds : 3 * n_kinds]
    packed_hbm = refs[3 * n_kinds]
    held = refs[3 * n_kinds + 1 : 5 * n_kinds + 1]
    packed, in_sem, out_sem = refs[5 * n_kinds + 1 :]
    arrivals = [pltpu.make_async_copy(a, b, in_sem.at[i]) for i, (a, b) in enumerate(zip(hbm, held))]
    for copy in arrivals:
        copy.start()
    slots = [
        slot_row(cluster[...], n_group, n_kinds * capacity, spread, kind * capacity)
        for kind, cluster in enumerate(clusters)
    ]
    for copy in arrivals:
        copy.wait()
    rows, features = held[0].shape
    block = 256
    departures = []
    for part in range(packed.shape[0] // block):
        mine = pl.ds(part * block, block)
        index = lax.broadcasted_iota(jnp.int32, (block, rows), 0) + part * block
        moved = carried = None
        for kind in range(n_kinds):
            place = (index == slots[kind]).astype(jnp.bfloat16)
            a = jnp.dot(place, held[2 * kind][...], preferred_element_type=jnp.float32)
            b = jnp.dot(place, held[2 * kind + 1][...], preferred_element_type=jnp.float32)
            moved = a if moved is None else moved + a
            carried = b if carried is None else carried + b
        packed[mine, :features] = moved.astype(jnp.bfloat16)
        packed[mine, features:] = carried.astype(jnp.bfloat16)
        departures.append(
            pltpu.make_async_copy(packed.at[mine], packed_hbm.at[mine], out_sem.at[part])
        )
        departures[-1].start()
    for copy in departures:
        copy.wait()


def pack(kinds, n_group, capacity, spread):
    n_kinds = len(kinds)
    rows, features = kinds[0][1].shape
    rank = kinds[0][2].shape[1]
    slots = n_kinds * n_group * capacity
    held = [pltpu.VMEM((rows, features), jnp.bfloat16), pltpu.VMEM((rows, rank), jnp.bfloat16)]
    return pl.pallas_call(
        functools.partial(pack_kernel, n_group, capacity, spread, n_kinds),
        out_shape=jax.ShapeDtypeStruct((slots, features + rank), jnp.bfloat16),
        in_specs=[pl.BlockSpec(memory_space=pltpu.VMEM)] * n_kinds + [in_hbm()] * (2 * n_kinds),
        out_specs=in_hbm(),
        scratch_shapes=held * n_kinds
        + [
            pltpu.VMEM((slots, features + rank), jnp.bfloat16),
            pltpu.SemaphoreType.DMA((2 * n_kinds,)),
            pltpu.SemaphoreType.DMA((slots // 256,)),
        ],
        compiler_params=pltpu.CompilerParams(vmem_limit_bytes=PACK_VMEM_BYTES),
        cost_estimate=pl.CostEstimate(
            flops=2 * n_kinds * slots * rows * (features + rank),
            bytes_accessed=2 * (slots + n_kinds * rows) * (features + rank),
            transcendentals=0,
        ),
        name="pack_rows",
    )(
        *[cluster[None, :] for cluster, _, _ in kinds],
        *[array for _, points, factor in kinds for array in (points, factor)],
    )


def digits_of(size, stride):
    bits = size.bit_length() - 1
    found = []
    while bits:
        take = 1 if bits % 2 else 2
        found.append((stride, 1 << take))
        stride <<= take
        bits -= take
    return found


class Chain:
    def __init__(self, own, other, n_src, n_tgt):
        self.n_dev = n_src * n_tgt
        first = (n_tgt, 2)
        src, tgt = digits_of(n_src // 2, 2 * n_tgt), digits_of(n_tgt, 1)
        self.plane, self.along = [first] + src, tgt
        self.dims = src[::-1] + [first] + tgt[::-1]
        self.left = [d for d in self.dims if d != first]
        x = own + self.sent(other, n_tgt).astype(jnp.float32)
        self.x = x.reshape(tuple(radix for _, radix in self.left) + own.shape[2:])

    def sent(self, array, mask):
        return lax.ppermute(array, ALL, [(i, i ^ mask) for i in range(self.n_dev)])

    def scatter(self, digit):
        stride, radix = digit
        dim = self.left.index(digit)
        mine = (lax.axis_index(ALL) // stride) % radix
        total = lax.dynamic_index_in_dim(self.x, mine, dim, keepdims=False)
        for j in range(1, radix):
            piece = lax.dynamic_index_in_dim(self.x, mine ^ j, dim, keepdims=False)
            total = total + self.sent(piece.astype(jnp.bfloat16), j * stride).astype(jnp.float32)
        self.x = total
        self.left.remove(digit)

    def swap(self, digit):
        stride, radix = digit
        piece = self.x.astype(jnp.bfloat16)
        for j in range(1, radix):
            self.x = self.x + self.sent(piece, j * stride).astype(jnp.float32)

    def gather(self, digit):
        stride, radix = digit
        mine = (lax.axis_index(ALL) // stride) % radix
        x = self.x.astype(jnp.bfloat16)
        got = [x] + [self.sent(x, j * stride) for j in range(1, radix)]
        self.left = [d for d in self.dims if d in self.left or d == digit]
        self.x = jnp.stack(
            [lax.select_n(mine ^ d, *got) if radix > 2 else jnp.where(mine == d, *got) for d in range(radix)],
            axis=self.left.index(digit),
        )


def update_kernel(
    src_points_ref,
    tgt_points_ref,
    src_factor_ref,
    tgt_factor_ref,
    marginal_ref,
    sums_ref,
    src_ref,
    tgt_ref,
    total,
):
    totals_of(sums_ref, total, src_points_ref.shape[1])
    rank = src_ref.shape[1]
    marginal = marginal_ref[...]
    src_ref[...] = mirror_step(src_points_ref[...], total[:rank], src_factor_ref[...], marginal)
    tgt_ref[...] = mirror_step(tgt_points_ref[...], total[rank:], tgt_factor_ref[...], marginal)


def updates(src_points, tgt_points, src_factor, tgt_factor, marginal, sums):
    rows, features = src_points.shape
    rank = src_factor.shape[1]
    shape = jax.ShapeDtypeStruct(src_factor.shape, jnp.bfloat16)
    return pl.pallas_call(
        update_kernel,
        out_shape=(shape, shape),
        scratch_shapes=[pltpu.VMEM((2 * rank, features), jnp.bfloat16)],
        compiler_params=pltpu.CompilerParams(vmem_limit_bytes=VMEM_BYTES),
        cost_estimate=pl.CostEstimate(
            flops=4 * rows * features * rank,
            bytes_accessed=4 * rows * (features + 2 * rank),
            transcendentals=2 * rows * rank,
        ),
        name="mirror_updates",
    )(src_points, tgt_points, src_factor, tgt_factor, marginal[None, :], sums)


def seen_block(ref, part, block):
    piece = block // ref.shape[1]
    return ref[pl.ds(part * piece, piece)].reshape(block, ref.shape[2])


def prepare_targets(ref, src_total, marginal, features, tgt_rows, tgt_update, tgt_inv):
    block = OWNER_BLOCK
    for part in range(tgt_rows.shape[0] // block):
        mine = pl.ds(part * block, block)
        both = seen_block(ref, part, block)
        rows = both[:, :features]
        tgt_rows[mine, :] = rows
        tgt_update[mine, :] = mirror_step(rows, src_total, both[:, features:], marginal)
        tgt_inv[:, mine] = inverse_norm(rows).reshape(1, block)


def block_terms(rows, update, src_label, tgt_label, tgt_rows, tgt_update, tgt_inv):
    cosine = contract_columns(rows, tgt_rows[...]) * inverse_norm(rows) * tgt_inv[...]
    weight = contract_columns(update, tgt_update[...]) / update.shape[1]
    same = jnp.logical_and(src_label == tgt_label, src_label > 0)
    kernel = jnp.where(same, weight * jnp.exp((cosine - 1.0) / TEMPER), 0.0)
    image = jnp.dot(
        kernel.astype(jnp.bfloat16), tgt_rows[...], preferred_element_type=jnp.float32
    )
    return image, jnp.sum(kernel, axis=1, keepdims=True)


def near_kernel(
    features,
    src_ref,
    tgt_ref,
    sums_ref,
    marginal_ref,
    src_label_ref,
    tgt_label_ref,
    image_ref,
    denominator_ref,
    update_ref,
    total,
    tgt_rows,
    tgt_update,
    tgt_inv,
):
    totals_of(sums_ref, total, features)
    rank = update_ref.shape[1]
    marginal = marginal_ref[...]
    prepare_targets(tgt_ref, total[rank:], marginal, features, tgt_rows, tgt_update, tgt_inv)
    block = OWNER_BLOCK
    for part in range(update_ref.shape[0] // block):
        mine = pl.ds(part * block, block)
        both = seen_block(src_ref, part, block)
        rows = both[:, :features]
        update = mirror_step(rows, total[:rank], both[:, features:], marginal)
        update_ref[mine, :] = update
        image, denominator = block_terms(
            rows, update, src_label_ref[mine, :], tgt_label_ref[...], tgt_rows, tgt_update, tgt_inv
        )
        image_ref[mine, :] = image
        denominator_ref[mine, :] = denominator


def far_kernel(
    features,
    src_ref,
    tgt_ref,
    sums_ref,
    marginal_ref,
    src_label_ref,
    tgt_label_ref,
    image_ref,
    denominator_ref,
    update_ref,
    out_hbm,
    total,
    tgt_rows,
    tgt_update,
    tgt_inv,
    images,
    out_sem,
):
    totals_of(sums_ref, total, features)
    rank = update_ref.shape[1]
    prepare_targets(tgt_ref, total[rank:], marginal_ref[...], features, tgt_rows, tgt_update, tgt_inv)
    block = OWNER_BLOCK
    departures = []
    for part in range(update_ref.shape[0] // block):
        mine = pl.ds(part * block, block)
        rows = seen_block(src_ref, part, block)[:, :features]
        image, denominator = block_terms(
            rows,
            update_ref[mine, :],
            src_label_ref[mine, :],
            tgt_label_ref[...],
            tgt_rows,
            tgt_update,
            tgt_inv,
        )
        denominator = denominator + denominator_ref[mine, :]
        denominator = jnp.where(denominator > 0, denominator, 1.0)
        images[mine, :] = ((image_ref[mine, :] + image) / denominator).astype(jnp.bfloat16)
        departures.append(
            pltpu.make_async_copy(images.at[mine], out_hbm.at[mine], out_sem.at[part])
        )
        departures[-1].start()
    for copy in departures:
        copy.wait()


def owner_cost(slots, width):
    return pl.CostEstimate(
        flops=2 * slots * width * (512 + 2 * slots),
        bytes_accessed=8 * slots * width,
        transcendentals=slots * slots,
    )


def near_maps(near, sums, marginal, src_labels, tgt_labels, features):
    n_group, _, capacity, width = near.shape
    slots = n_group * capacity
    rank = width - features
    shapes = [((slots, features), jnp.float32), ((slots, 1), jnp.float32), ((slots, rank), jnp.bfloat16)]
    return pl.pallas_call(
        functools.partial(near_kernel, features),
        out_shape=[jax.ShapeDtypeStruct(*shape) for shape in shapes],
        grid=(1,),
        in_specs=[
            pl.BlockSpec((n_group, None, capacity, width), lambda step: (0, 1, 0, 0)),
            pl.BlockSpec((n_group, None, capacity, width), lambda step: (0, 0, 0, 0)),
            whole(sums.shape),
            whole((1, rank)),
            whole((slots, 1)),
            whole((1, slots)),
        ],
        out_specs=[whole(shape) for shape, _ in shapes],
        scratch_shapes=[
            pltpu.VMEM((2 * rank, features), jnp.bfloat16),
            pltpu.VMEM((slots, features), jnp.bfloat16),
            pltpu.VMEM((slots, rank), jnp.bfloat16),
            pltpu.VMEM((1, slots), jnp.float32),
        ],
        compiler_params=pltpu.CompilerParams(vmem_limit_bytes=VMEM_BYTES),
        cost_estimate=owner_cost(slots, width),
        name="near_maps",
    )(near, near, sums, marginal[None, :], src_labels[:, None], tgt_labels[None, :])


def far_maps(near, far, sums, marginal, src_labels, tgt_labels, image, denominator, update):
    n_group, capacity, width = far.shape
    slots = n_group * capacity
    rank = update.shape[1]
    features = width - rank
    return pl.pallas_call(
        functools.partial(far_kernel, features),
        out_shape=jax.ShapeDtypeStruct((slots, features), jnp.bfloat16),
        grid=(1,),
        in_specs=[
            pl.BlockSpec((n_group, None, capacity, width), lambda step: (0, 1, 0, 0)),
            whole(far.shape),
            whole(sums.shape),
            whole((1, rank)),
            whole((slots, 1)),
            whole((1, slots)),
            whole(image.shape),
            whole(denominator.shape),
            whole(update.shape),
        ],
        out_specs=in_hbm(),
        scratch_shapes=[
            pltpu.VMEM((2 * rank, features), jnp.bfloat16),
            pltpu.VMEM((slots, features), jnp.bfloat16),
            pltpu.VMEM((slots, rank), jnp.bfloat16),
            pltpu.VMEM((1, slots), jnp.float32),
            pltpu.VMEM((slots, features), jnp.bfloat16),
            pltpu.SemaphoreType.DMA((slots // OWNER_BLOCK,)),
        ],
        compiler_params=pltpu.CompilerParams(vmem_limit_bytes=VMEM_BYTES),
        cost_estimate=owner_cost(slots, width),
        name="far_maps",
    )(
        near,
        far,
        sums,
        marginal[None, :],
        src_labels[:, None],
        tgt_labels[None, :],
        image,
        denominator,
        update,
    )


def labels_of(clusters, owner, capacity, spread):
    rows = clusters.shape[1]
    mine = clusters // spread == owner
    before = (jnp.arange(rows)[:, None] < jnp.arange(rows)[None, :]).astype(jnp.bfloat16)
    earlier = jnp.dot(mine.astype(jnp.bfloat16), before, preferred_element_type=jnp.float32)
    ranking = jnp.where(mine, earlier.astype(jnp.int32), -1)
    value = clusters - owner * spread + 1
    hit = ranking[:, None, :] == jnp.arange(capacity, dtype=jnp.int32)[None, :, None]
    return jnp.sum(jnp.where(hit, value[:, None, :], 0), axis=2).reshape(-1)


def exchange(rows):
    return lax.all_to_all(rows, GROUP, split_axis=0, concat_axis=0, tiled=True)


def per_device(
    src_points, tgt_points, src_factor, tgt_factor, inner_marginal, src_cluster, tgt_cluster
):
    n_src, n_rest = lax.axis_size("src"), lax.axis_size(REST)
    n_group = n_src * n_rest
    n_dev = 2 * n_group
    rows, features = src_points.shape
    rank = src_factor.shape[1]
    capacity = 2 * (2 * rows // n_dev)
    spread = 2 * CL_DEV
    slots = n_group * capacity
    me = lax.axis_index(ALL)
    my_half = lax.axis_index(HALF)
    owner = lax.axis_index(GROUP)

    across = [(0, 1), (1, 0)]
    far_points, far_factor, far_cluster = (
        lax.ppermute(array, HALF, across) for array in (tgt_points, tgt_factor, tgt_cluster)
    )
    near = pack(
        [(tgt_cluster, tgt_points, tgt_factor), (src_cluster, src_points, src_factor)],
        n_group,
        capacity,
        spread,
    )
    near, me = lax.optimization_barrier((near, me))
    near = exchange(near)
    own, other = partial_sums(
        me,
        src_cluster,
        tgt_cluster,
        src_points,
        tgt_points,
        src_factor,
        tgt_factor,
        n_dev,
        2 * n_rest,
    )
    chain = Chain(own, other, n_src, 2 * n_rest)
    for digit in chain.plane[1:]:
        chain.scatter(digit)
    for digit in chain.along:
        chain.swap(digit)
    far = pack([(far_cluster, far_points, far_factor)], n_group, capacity, spread)
    far, near = lax.optimization_barrier((far, near))
    far = exchange(far)
    for digit in reversed(chain.plane):
        chain.gather(digit)
    sums = chain.x.reshape(n_dev, -1, rank)

    kept = 2 * features // n_dev
    table = sums[:, kept : kept + 2].astype(jnp.int32).reshape(n_src, 2, n_rest, 2, rows)
    near_table = lax.dynamic_index_in_dim(table, my_half, 1, keepdims=False)
    far_table = lax.dynamic_index_in_dim(table, 1 - my_half, 1, keepdims=False)
    near_table = near_table.reshape(n_group, 2, rows)
    far_table = far_table.reshape(n_group, 2, rows)
    src_labels = labels_of(near_table[:, 0], owner, capacity, spread)
    near_labels = labels_of(near_table[:, 1], owner, capacity, spread)
    far_labels = labels_of(far_table[:, 1], owner, capacity, spread)

    near = near.reshape(n_group, 2, capacity, features + rank)
    far = far.reshape(n_group, capacity, features + rank)
    found = near_maps(near, sums, inner_marginal, src_labels, near_labels, features)
    images = far_maps(near, far, sums, inner_marginal, src_labels, far_labels, *found)
    returned = exchange(images)

    src_update, tgt_update = updates(
        src_points, tgt_points, src_factor, tgt_factor, inner_marginal, sums
    )
    slot = slot_row(src_cluster[None, :], n_group, capacity, spread, 0)
    back = slot.reshape(rows, 1) == jnp.arange(slots, dtype=jnp.int32)[None, :]
    back = lax.optimization_barrier(back.astype(jnp.bfloat16))
    mapped = jnp.dot(back, returned, preferred_element_type=jnp.float32).astype(jnp.bfloat16)
    return (src_update, tgt_update, mapped)


def solution(mesh):
    n_src, n_tgt = mesh.shape["src"], mesh.shape["tgt"]
    halves = Mesh(mesh.devices.reshape(n_src, 2, n_tgt // 2), ALL)
    rows = P(ALL, None)
    return jax.shard_map(
        per_device,
        mesh=halves,
        in_specs=(rows, rows, rows, rows, P(), P(ALL), P(ALL)),
        out_specs=(rows, rows, rows),
        check_vma=False,
    )
```

```python
import functools

import jax
import jax.numpy as jnp
from jax import lax
from jax.experimental import pallas as pl
from jax.experimental.pallas import tpu as pltpu
from jax.sharding import Mesh
from jax.sharding import PartitionSpec as P

CL_DEV = 2

GAMMA = 2.0
TEMPER = 0.03
EPS = 1e-06

HALF, REST = "half", "rest"
ALL = ("src", HALF, REST)
GROUP = ("src", REST)
VMEM_BYTES = 48 * 1024 * 1024
PACK_VMEM_BYTES = 62 * 1024 * 1024
TABLE_ROWS = 8
BLOCK_ROWS = 16
OWNER_BLOCK = 256


def contract_rows(left, right):
    return lax.dot_general(
        left, right, (((0,), (0,)), ((), ())), preferred_element_type=jnp.float32
    )


def contract_columns(left, right):
    return lax.dot_general(
        left, right, (((1,), (1,)), ((), ())), preferred_element_type=jnp.float32
    )


def mirror_step(points, total_round, factor, inner_marginal):
    gradient = -contract_columns(points, total_round) / inner_marginal
    row_scale = jnp.max(jnp.abs(gradient), axis=1, keepdims=True) + EPS
    tilted = factor.astype(jnp.float32) * jnp.exp(-GAMMA * gradient / row_scale)
    mean = jnp.mean(tilted, axis=1, keepdims=True)
    mean = jnp.where(mean > 0, mean, 1.0)
    return (tilted / mean).astype(jnp.bfloat16)


def inverse_norm(rows):
    return lax.rsqrt(jnp.sum(jnp.square(rows.astype(jnp.float32)), axis=1, keepdims=True) + EPS)


def blocks_of(n_dev, chunk, rank, features):
    kept = (chunk - TABLE_ROWS) // BLOCK_ROWS
    wide = features // rank
    return [
        (b // kept, b % kept * BLOCK_ROWS, b // wide * BLOCK_ROWS, b % wide * rank)
        for b in range(n_dev * kept)
    ]


def totals_of(sums_ref, total, features):
    n_dev, chunk, rank = sums_ref.shape
    for c, row, first, column in blocks_of(n_dev, chunk, rank, features):
        total[pl.ds(first, BLOCK_ROWS), pl.ds(column, rank)] = sums_ref[c, pl.ds(row, BLOCK_ROWS), :]


def whole(shape):
    return pl.BlockSpec(shape, lambda *_: (0,) * len(shape))


def in_hbm():
    return pl.BlockSpec(memory_space=pltpu.HBM)


def slot_row(cluster, n_group, capacity, spread, first):
    rows = cluster.shape[1]
    owners = cluster // spread
    onehot = owners == lax.broadcasted_iota(jnp.int32, (n_group, rows), 0)
    before = lax.broadcasted_iota(jnp.int32, (rows, rows), 0) < lax.broadcasted_iota(
        jnp.int32, (rows, rows), 1
    )
    earlier = jnp.dot(
        onehot.astype(jnp.bfloat16), before.astype(jnp.bfloat16), preferred_element_type=jnp.float32
    )
    ranking = jnp.sum(jnp.where(onehot, earlier, 0.0), axis=0, keepdims=True).astype(jnp.int32)
    return owners * capacity + ranking + first


def contract_kernel(n_dev, n_tgt, me_ref, src_cluster_ref, tgt_cluster_ref, *refs):
    hbm, (own_ref, other_ref), held, parts, in_sem = refs[:4], refs[4:6], refs[6:10], refs[10], refs[11]
    arrivals = [pltpu.make_async_copy(a, b, in_sem.at[i]) for i, (a, b) in enumerate(zip(hbm, held))]
    for copy in arrivals:
        copy.start()
    tgt_points, tgt_factor, src_points, src_factor = held
    _, _, _, chunk, rank = parts.shape
    kept = chunk - TABLE_ROWS
    me = me_ref[0]
    mine = (me // n_tgt) % 2
    row = lax.broadcasted_iota(jnp.int32, (TABLE_ROWS, rank), 0)
    table = jnp.where(row == 0, src_cluster_ref[...], jnp.where(row == 1, tgt_cluster_ref[...], 0))
    parts[:, :, :, kept:, :] = jnp.zeros(parts.shape[:3] + (TABLE_ROWS, rank), jnp.float32)
    parts[me // (2 * n_tgt), mine, me % n_tgt, kept:, :] = table.astype(jnp.float32)
    features = tgt_points.shape[1]
    blocks = blocks_of(n_dev, chunk, rank, features)
    for which, (points, factor) in enumerate(((tgt_points, tgt_factor), (src_points, src_factor))):
        arrivals[2 * which].wait()
        arrivals[2 * which + 1].wait()
        total = contract_rows(factor[...], points[...])
        for c, row, first, column in blocks:
            first -= which * rank
            if 0 <= first < rank:
                place = (c // (2 * n_tgt), c // n_tgt % 2, c % n_tgt)
                parts[(*place, pl.ds(row, BLOCK_ROWS))] = total[
                    first : first + BLOCK_ROWS, column : column + rank
                ]
    for i in range(parts.shape[0]):
        own_ref[i] = parts[i, mine]
        other_ref[i] = parts[i, 1 - mine].astype(jnp.bfloat16)


def partial_sums(
    me, src_cluster, tgt_cluster, src_points, tgt_points, src_factor, tgt_factor, n_dev, n_tgt
):
    rows, features = src_points.shape
    rank = src_factor.shape[1]
    chunk = 2 * features // n_dev + TABLE_ROWS
    shape = (n_dev // (2 * n_tgt), n_tgt, chunk, rank)
    vmem = pl.BlockSpec(memory_space=pltpu.VMEM)
    return pl.pallas_call(
        functools.partial(contract_kernel, n_dev, n_tgt),
        out_shape=(
            jax.ShapeDtypeStruct(shape, jnp.float32),
            jax.ShapeDtypeStruct(shape, jnp.bfloat16),
        ),
        in_specs=[pl.BlockSpec(memory_space=pltpu.SMEM)] + [vmem] * 2 + [in_hbm()] * 4,
        out_specs=(vmem, vmem),
        scratch_shapes=[
            pltpu.VMEM((rows, features), jnp.bfloat16),
            pltpu.VMEM((rows, rank), jnp.bfloat16),
            pltpu.VMEM((rows, features), jnp.bfloat16),
            pltpu.VMEM((rows, rank), jnp.bfloat16),
            pltpu.VMEM((n_dev // (2 * n_tgt), 2, n_tgt, chunk, rank), jnp.float32),
            pltpu.SemaphoreType.DMA((4,)),
        ],
        compiler_params=pltpu.CompilerParams(vmem_limit_bytes=PACK_VMEM_BYTES),
        cost_estimate=pl.CostEstimate(
            flops=4 * rows * features * rank,
            bytes_accessed=4 * rows * (features + rank) + 4 * n_dev * chunk * rank,
            transcendentals=0,
        ),
        name="partial_sums",
    )(me[None], src_cluster[None, :], tgt_cluster[None, :], tgt_points, tgt_factor, src_points, src_factor)


def pack_kernel(n_group, capacity, spread, n_kinds, *refs):
    clusters = refs[:n_kinds]
    hbm = refs[n_kinds : 3 * n_kinds]
    packed_hbm = refs[3 * n_kinds]
    held = refs[3 * n_kinds + 1 : 5 * n_kinds + 1]
    packed, in_sem, out_sem = refs[5 * n_kinds + 1 :]
    arrivals = [pltpu.make_async_copy(a, b, in_sem.at[i]) for i, (a, b) in enumerate(zip(hbm, held))]
    for copy in arrivals:
        copy.start()
    slots = [
        slot_row(cluster[...], n_group, n_kinds * capacity, spread, kind * capacity)
        for kind, cluster in enumerate(clusters)
    ]
    for copy in arrivals:
        copy.wait()
    rows, features = held[0].shape
    block = 256
    departures = []
    for part in range(packed.shape[0] // block):
        mine = pl.ds(part * block, block)
        index = lax.broadcasted_iota(jnp.int32, (block, rows), 0) + part * block
        moved = carried = None
        for kind in range(n_kinds):
            place = (index == slots[kind]).astype(jnp.bfloat16)
            a = jnp.dot(place, held[2 * kind][...], preferred_element_type=jnp.float32)
            b = jnp.dot(place, held[2 * kind + 1][...], preferred_element_type=jnp.float32)
            moved = a if moved is None else moved + a
            carried = b if carried is None else carried + b
        packed[mine, :features] = moved.astype(jnp.bfloat16)
        packed[mine, features:] = carried.astype(jnp.bfloat16)
        departures.append(
            pltpu.make_async_copy(packed.at[mine], packed_hbm.at[mine], out_sem.at[part])
        )
        departures[-1].start()
    for copy in departures:
        copy.wait()


def pack(kinds, n_group, capacity, spread):
    n_kinds = len(kinds)
    rows, features = kinds[0][1].shape
    rank = kinds[0][2].shape[1]
    slots = n_kinds * n_group * capacity
    held = [pltpu.VMEM((rows, features), jnp.bfloat16), pltpu.VMEM((rows, rank), jnp.bfloat16)]
    return pl.pallas_call(
        functools.partial(pack_kernel, n_group, capacity, spread, n_kinds),
        out_shape=jax.ShapeDtypeStruct((slots, features + rank), jnp.bfloat16),
        in_specs=[pl.BlockSpec(memory_space=pltpu.VMEM)] * n_kinds + [in_hbm()] * (2 * n_kinds),
        out_specs=in_hbm(),
        scratch_shapes=held * n_kinds
        + [
            pltpu.VMEM((slots, features + rank), jnp.bfloat16),
            pltpu.SemaphoreType.DMA((2 * n_kinds,)),
            pltpu.SemaphoreType.DMA((slots // 256,)),
        ],
        compiler_params=pltpu.CompilerParams(vmem_limit_bytes=PACK_VMEM_BYTES),
        cost_estimate=pl.CostEstimate(
            flops=2 * n_kinds * slots * rows * (features + rank),
            bytes_accessed=2 * (slots + n_kinds * rows) * (features + rank),
            transcendentals=0,
        ),
        name="pack_rows",
    )(
        *[cluster[None, :] for cluster, _, _ in kinds],
        *[array for _, points, factor in kinds for array in (points, factor)],
    )


def digits_of(size, stride):
    bits = size.bit_length() - 1
    found = []
    while bits:
        take = 1 if bits % 2 else 2
        found.append((stride, 1 << take))
        stride <<= take
        bits -= take
    return found


class Chain:
    def __init__(self, own, other, n_src, n_tgt):
        self.n_dev = n_src * n_tgt
        first = (n_tgt, 2)
        src, tgt = digits_of(n_src // 2, 2 * n_tgt), digits_of(n_tgt, 1)
        self.plane, self.along = [first] + src, tgt
        self.dims = src[::-1] + [first] + tgt[::-1]
        self.left = [d for d in self.dims if d != first]
        x = own + self.sent(other, n_tgt).astype(jnp.float32)
        self.x = x.reshape(tuple(radix for _, radix in self.left) + own.shape[2:])

    def sent(self, array, mask):
        return lax.ppermute(array, ALL, [(i, i ^ mask) for i in range(self.n_dev)])

    def scatter(self, digit):
        stride, radix = digit
        dim = self.left.index(digit)
        mine = (lax.axis_index(ALL) // stride) % radix
        total = lax.dynamic_index_in_dim(self.x, mine, dim, keepdims=False)
        for j in range(1, radix):
            piece = lax.dynamic_index_in_dim(self.x, mine ^ j, dim, keepdims=False)
            total = total + self.sent(piece.astype(jnp.bfloat16), j * stride).astype(jnp.float32)
        self.x = total
        self.left.remove(digit)

    def swap(self, digit):
        stride, radix = digit
        piece = self.x.astype(jnp.bfloat16)
        for j in range(1, radix):
            self.x = self.x + self.sent(piece, j * stride).astype(jnp.float32)

    def gather(self, digit):
        stride, radix = digit
        mine = (lax.axis_index(ALL) // stride) % radix
        x = self.x.astype(jnp.bfloat16)
        got = [x] + [self.sent(x, j * stride) for j in range(1, radix)]
        self.left = [d for d in self.dims if d in self.left or d == digit]
        self.x = jnp.stack(
            [lax.select_n(mine ^ d, *got) if radix > 2 else jnp.where(mine == d, *got) for d in range(radix)],
            axis=self.left.index(digit),
        )


def update_kernel(
    src_points_ref,
    tgt_points_ref,
    src_factor_ref,
    tgt_factor_ref,
    marginal_ref,
    sums_ref,
    src_ref,
    tgt_ref,
    total,
):
    totals_of(sums_ref, total, src_points_ref.shape[1])
    rank = src_ref.shape[1]
    marginal = marginal_ref[...]
    src_ref[...] = mirror_step(src_points_ref[...], total[:rank], src_factor_ref[...], marginal)
    tgt_ref[...] = mirror_step(tgt_points_ref[...], total[rank:], tgt_factor_ref[...], marginal)


def updates(src_points, tgt_points, src_factor, tgt_factor, marginal, sums):
    rows, features = src_points.shape
    rank = src_factor.shape[1]
    shape = jax.ShapeDtypeStruct(src_factor.shape, jnp.bfloat16)
    return pl.pallas_call(
        update_kernel,
        out_shape=(shape, shape),
        scratch_shapes=[pltpu.VMEM((2 * rank, features), jnp.bfloat16)],
        compiler_params=pltpu.CompilerParams(vmem_limit_bytes=VMEM_BYTES),
        cost_estimate=pl.CostEstimate(
            flops=4 * rows * features * rank,
            bytes_accessed=4 * rows * (features + 2 * rank),
            transcendentals=2 * rows * rank,
        ),
        name="mirror_updates",
    )(src_points, tgt_points, src_factor, tgt_factor, marginal[None, :], sums)


def seen_block(ref, part, block):
    piece = block // ref.shape[1]
    return ref[pl.ds(part * piece, piece)].reshape(block, ref.shape[2])


def prepare_targets(ref, src_total, marginal, features, tgt_rows, tgt_update, tgt_inv):
    block = OWNER_BLOCK
    for part in range(tgt_rows.shape[0] // block):
        mine = pl.ds(part * block, block)
        both = seen_block(ref, part, block)
        rows = both[:, :features]
        tgt_rows[mine, :] = rows
        tgt_update[mine, :] = mirror_step(rows, src_total, both[:, features:], marginal)
        tgt_inv[:, mine] = inverse_norm(rows).reshape(1, block)


def block_terms(rows, update, src_label, tgt_label, tgt_rows, tgt_update, tgt_inv):
    cosine = contract_columns(rows, tgt_rows[...]) * inverse_norm(rows) * tgt_inv[...]
    weight = contract_columns(update, tgt_update[...]) / update.shape[1]
    same = jnp.logical_and(src_label == tgt_label, src_label > 0)
    kernel = jnp.where(same, weight * jnp.exp((cosine - 1.0) / TEMPER), 0.0)
    image = jnp.dot(
        kernel.astype(jnp.bfloat16), tgt_rows[...], preferred_element_type=jnp.float32
    )
    return image, jnp.sum(kernel, axis=1, keepdims=True)


def near_kernel(
    features,
    src_ref,
    tgt_ref,
    sums_ref,
    marginal_ref,
    src_label_ref,
    tgt_label_ref,
    image_ref,
    denominator_ref,
    update_ref,
    total,
    tgt_rows,
    tgt_update,
    tgt_inv,
):
    totals_of(sums_ref, total, features)
    rank = update_ref.shape[1]
    marginal = marginal_ref[...]
    prepare_targets(tgt_ref, total[rank:], marginal, features, tgt_rows, tgt_update, tgt_inv)
    block = OWNER_BLOCK
    for part in range(update_ref.shape[0] // block):
        mine = pl.ds(part * block, block)
        both = seen_block(src_ref, part, block)
        rows = both[:, :features]
        update = mirror_step(rows, total[:rank], both[:, features:], marginal)
        update_ref[mine, :] = update
        image, denominator = block_terms(
            rows, update, src_label_ref[mine, :], tgt_label_ref[...], tgt_rows, tgt_update, tgt_inv
        )
        image_ref[mine, :] = image
        denominator_ref[mine, :] = denominator


def far_kernel(
    features,
    src_ref,
    tgt_ref,
    sums_ref,
    marginal_ref,
    src_label_ref,
    tgt_label_ref,
    image_ref,
    denominator_ref,
    update_ref,
    out_hbm,
    total,
    tgt_rows,
    tgt_update,
    tgt_inv,
    images,
    out_sem,
):
    totals_of(sums_ref, total, features)
    rank = update_ref.shape[1]
    prepare_targets(tgt_ref, total[rank:], marginal_ref[...], features, tgt_rows, tgt_update, tgt_inv)
    block = OWNER_BLOCK
    departures = []
    for part in range(update_ref.shape[0] // block):
        mine = pl.ds(part * block, block)
        rows = seen_block(src_ref, part, block)[:, :features]
        image, denominator = block_terms(
            rows,
            update_ref[mine, :],
            src_label_ref[mine, :],
            tgt_label_ref[...],
            tgt_rows,
            tgt_update,
            tgt_inv,
        )
        denominator = denominator + denominator_ref[mine, :]
        denominator = jnp.where(denominator > 0, denominator, 1.0)
        images[mine, :] = ((image_ref[mine, :] + image) / denominator).astype(jnp.bfloat16)
        departures.append(
            pltpu.make_async_copy(images.at[mine], out_hbm.at[mine], out_sem.at[part])
        )
        departures[-1].start()
    for copy in departures:
        copy.wait()


def owner_cost(slots, width):
    return pl.CostEstimate(
        flops=2 * slots * width * (512 + 2 * slots),
        bytes_accessed=8 * slots * width,
        transcendentals=slots * slots,
    )


def near_maps(near, sums, marginal, src_labels, tgt_labels, features):
    n_group, _, capacity, width = near.shape
    slots = n_group * capacity
    rank = width - features
    shapes = [((slots, features), jnp.float32), ((slots, 1), jnp.float32), ((slots, rank), jnp.bfloat16)]
    return pl.pallas_call(
        functools.partial(near_kernel, features),
        out_shape=[jax.ShapeDtypeStruct(*shape) for shape in shapes],
        grid=(1,),
        in_specs=[
            pl.BlockSpec((n_group, None, capacity, width), lambda step: (0, 1, 0, 0)),
            pl.BlockSpec((n_group, None, capacity, width), lambda step: (0, 0, 0, 0)),
            whole(sums.shape),
            whole((1, rank)),
            whole((slots, 1)),
            whole((1, slots)),
        ],
        out_specs=[whole(shape) for shape, _ in shapes],
        scratch_shapes=[
            pltpu.VMEM((2 * rank, features), jnp.bfloat16),
            pltpu.VMEM((slots, features), jnp.bfloat16),
            pltpu.VMEM((slots, rank), jnp.bfloat16),
            pltpu.VMEM((1, slots), jnp.float32),
        ],
        compiler_params=pltpu.CompilerParams(vmem_limit_bytes=VMEM_BYTES),
        cost_estimate=owner_cost(slots, width),
        name="near_maps",
    )(near, near, sums, marginal[None, :], src_labels[:, None], tgt_labels[None, :])


def far_maps(near, far, sums, marginal, src_labels, tgt_labels, image, denominator, update):
    n_group, capacity, width = far.shape
    slots = n_group * capacity
    rank = update.shape[1]
    features = width - rank
    return pl.pallas_call(
        functools.partial(far_kernel, features),
        out_shape=jax.ShapeDtypeStruct((slots, features), jnp.bfloat16),
        grid=(1,),
        in_specs=[
            pl.BlockSpec((n_group, None, capacity, width), lambda step: (0, 1, 0, 0)),
            whole(far.shape),
            whole(sums.shape),
            whole((1, rank)),
            whole((slots, 1)),
            whole((1, slots)),
            whole(image.shape),
            whole(denominator.shape),
            whole(update.shape),
        ],
        out_specs=in_hbm(),
        scratch_shapes=[
            pltpu.VMEM((2 * rank, features), jnp.bfloat16),
            pltpu.VMEM((slots, features), jnp.bfloat16),
            pltpu.VMEM((slots, rank), jnp.bfloat16),
            pltpu.VMEM((1, slots), jnp.float32),
            pltpu.VMEM((slots, features), jnp.bfloat16),
            pltpu.SemaphoreType.DMA((slots // OWNER_BLOCK,)),
        ],
        compiler_params=pltpu.CompilerParams(vmem_limit_bytes=PACK_VMEM_BYTES),
        cost_estimate=owner_cost(slots, width),
        name="far_maps",
    )(
        near,
        far,
        sums,
        marginal[None, :],
        src_labels[:, None],
        tgt_labels[None, :],
        image,
        denominator,
        update,
    )


def unpack_kernel(n_group, capacity, spread, cluster_ref, images_hbm, out_ref, images, in_sem):
    arrival = pltpu.make_async_copy(images_hbm, images, in_sem)
    arrival.start()
    slot = slot_row(cluster_ref[...], n_group, capacity, spread, 0)
    index = lax.broadcasted_iota(jnp.int32, (images.shape[0], out_ref.shape[0]), 0)
    place = (index == slot).astype(jnp.bfloat16)
    arrival.wait()
    out_ref[...] = contract_rows(place, images[...]).astype(jnp.bfloat16)


def unpack(images, cluster, n_group, capacity, spread):
    rows = cluster.shape[0]
    slots, features = images.shape
    return pl.pallas_call(
        functools.partial(unpack_kernel, n_group, capacity, spread),
        out_shape=jax.ShapeDtypeStruct((rows, features), jnp.bfloat16),
        in_specs=[pl.BlockSpec(memory_space=pltpu.VMEM), in_hbm()],
        out_specs=pl.BlockSpec(memory_space=pltpu.VMEM),
        scratch_shapes=[pltpu.VMEM((slots, features), jnp.bfloat16), pltpu.SemaphoreType.DMA],
        compiler_params=pltpu.CompilerParams(vmem_limit_bytes=PACK_VMEM_BYTES),
        cost_estimate=pl.CostEstimate(
            flops=2 * rows * slots * features,
            bytes_accessed=2 * (rows + slots) * features,
            transcendentals=0,
        ),
        name="unpack_rows",
    )(cluster[None, :], images)


def labels_of(clusters, owner, capacity, spread):
    rows = clusters.shape[1]
    mine = clusters // spread == owner
    before = (jnp.arange(rows)[:, None] < jnp.arange(rows)[None, :]).astype(jnp.bfloat16)
    earlier = jnp.dot(mine.astype(jnp.bfloat16), before, preferred_element_type=jnp.float32)
    ranking = jnp.where(mine, earlier.astype(jnp.int32), -1)
    value = clusters - owner * spread + 1
    hit = ranking[:, None, :] == jnp.arange(capacity, dtype=jnp.int32)[None, :, None]
    return jnp.sum(jnp.where(hit, value[:, None, :], 0), axis=2).reshape(-1)


def exchange(rows):
    return lax.all_to_all(rows, GROUP, split_axis=0, concat_axis=0, tiled=True)


def per_device(
    src_points, tgt_points, src_factor, tgt_factor, inner_marginal, src_cluster, tgt_cluster
):
    n_src, n_rest = lax.axis_size("src"), lax.axis_size(REST)
    n_group = n_src * n_rest
    n_dev = 2 * n_group
    rows, features = src_points.shape
    rank = src_factor.shape[1]
    capacity = 2 * (2 * rows // n_dev)
    spread = 2 * CL_DEV
    me = lax.axis_index(ALL)
    my_half = lax.axis_index(HALF)
    owner = lax.axis_index(GROUP)

    across = [(0, 1), (1, 0)]
    far_points, far_factor, far_cluster = (
        lax.ppermute(array, HALF, across) for array in (tgt_points, tgt_factor, tgt_cluster)
    )
    near = pack(
        [(tgt_cluster, tgt_points, tgt_factor), (src_cluster, src_points, src_factor)],
        n_group,
        capacity,
        spread,
    )
    near, me = lax.optimization_barrier((near, me))
    near = exchange(near)
    own, other = partial_sums(
        me,
        src_cluster,
        tgt_cluster,
        src_points,
        tgt_points,
        src_factor,
        tgt_factor,
        n_dev,
        2 * n_rest,
    )
    chain = Chain(own, other, n_src, 2 * n_rest)
    for digit in chain.plane[1:]:
        chain.scatter(digit)
    chain.x, far_points, far_factor, far_cluster = lax.optimization_barrier(
        (chain.x, far_points, far_factor, far_cluster)
    )
    for digit in chain.along:
        chain.swap(digit)
    far = pack([(far_cluster, far_points, far_factor)], n_group, capacity, spread)
    far, near = lax.optimization_barrier((far, near))
    far = exchange(far)
    for digit in reversed(chain.plane):
        chain.gather(digit)
    sums = chain.x.reshape(n_dev, -1, rank)

    kept = 2 * features // n_dev
    table = sums[:, kept : kept + 2].astype(jnp.int32).reshape(n_src, 2, n_rest, 2, rows)
    near_table = lax.dynamic_index_in_dim(table, my_half, 1, keepdims=False)
    far_table = lax.dynamic_index_in_dim(table, 1 - my_half, 1, keepdims=False)
    near_table = near_table.reshape(n_group, 2, rows)
    far_table = far_table.reshape(n_group, 2, rows)
    src_labels = labels_of(near_table[:, 0], owner, capacity, spread)
    near_labels = labels_of(near_table[:, 1], owner, capacity, spread)
    far_labels = labels_of(far_table[:, 1], owner, capacity, spread)

    near = near.reshape(n_group, 2, capacity, features + rank)
    far = far.reshape(n_group, capacity, features + rank)
    found = near_maps(near, sums, inner_marginal, src_labels, near_labels, features)
    images = far_maps(near, far, sums, inner_marginal, src_labels, far_labels, *found)
    returned = exchange(images)

    src_update, tgt_update = updates(
        src_points, tgt_points, src_factor, tgt_factor, inner_marginal, sums
    )
    mapped = unpack(returned, src_cluster, n_group, capacity, spread)
    return (src_update, tgt_update, mapped)


def solution(mesh):
    n_src, n_tgt = mesh.shape["src"], mesh.shape["tgt"]
    halves = Mesh(mesh.devices.reshape(n_src, 2, n_tgt // 2), ALL)
    rows = P(ALL, None)
    return jax.shard_map(
        per_device,
        mesh=halves,
        in_specs=(rows, rows, rows, rows, P(), P(ALL), P(ALL)),
        out_specs=(rows, rows, rows),
        check_vma=False,
    )
```

```python
import functools

import jax
import jax.numpy as jnp
from jax import lax
from jax.experimental import pallas as pl
from jax.experimental.pallas import tpu as pltpu
from jax.sharding import Mesh
from jax.sharding import PartitionSpec as P

CL_DEV = 2

GAMMA = 2.0
TEMPER = 0.03
EPS = 1e-06

HALF, REST = "half", "rest"
ALL = ("src", HALF, REST)
GROUP = ("src", REST)
VMEM_BYTES = 48 * 1024 * 1024
PACK_VMEM_BYTES = 62 * 1024 * 1024
TABLE_ROWS = 8
BLOCK_ROWS = 16
OWNER_BLOCK = 256
LABEL_ROWS = 16
LANES = 128


def contract_rows(left, right):
    return lax.dot_general(
        left, right, (((0,), (0,)), ((), ())), preferred_element_type=jnp.float32
    )


def contract_columns(left, right):
    return lax.dot_general(
        left, right, (((1,), (1,)), ((), ())), preferred_element_type=jnp.float32
    )


def mirror_step(points, total_round, factor, inner_marginal):
    gradient = -contract_columns(points, total_round) / inner_marginal
    row_scale = jnp.max(jnp.abs(gradient), axis=1, keepdims=True) + EPS
    tilted = factor.astype(jnp.float32) * jnp.exp(-GAMMA * gradient / row_scale)
    mean = jnp.mean(tilted, axis=1, keepdims=True)
    mean = jnp.where(mean > 0, mean, 1.0)
    return (tilted / mean).astype(jnp.bfloat16)


def inverse_norm(rows):
    return lax.rsqrt(jnp.sum(jnp.square(rows.astype(jnp.float32)), axis=1, keepdims=True) + EPS)


def blocks_of(n_dev, chunk, rank, features):
    kept = (chunk - TABLE_ROWS) // BLOCK_ROWS
    wide = features // rank
    return [
        (b // kept, b % kept * BLOCK_ROWS, b // wide * BLOCK_ROWS, b % wide * rank)
        for b in range(n_dev * kept)
    ]


def totals_of(sums_ref, total, features):
    n_dev, chunk, rank = sums_ref.shape
    for c, row, first, column in blocks_of(n_dev, chunk, rank, features):
        total[pl.ds(first, BLOCK_ROWS), pl.ds(column, rank)] = sums_ref[c, pl.ds(row, BLOCK_ROWS), :]


def whole(shape):
    return pl.BlockSpec(shape, lambda *_: (0,) * len(shape))


def in_hbm():
    return pl.BlockSpec(memory_space=pltpu.HBM)


def slot_row(cluster, n_group, capacity, spread, first):
    rows = cluster.shape[1]
    owners = cluster // spread
    onehot = owners == lax.broadcasted_iota(jnp.int32, (n_group, rows), 0)
    before = lax.broadcasted_iota(jnp.int32, (rows, rows), 0) < lax.broadcasted_iota(
        jnp.int32, (rows, rows), 1
    )
    earlier = jnp.dot(
        onehot.astype(jnp.bfloat16), before.astype(jnp.bfloat16), preferred_element_type=jnp.float32
    )
    ranking = jnp.sum(jnp.where(onehot, earlier, 0.0), axis=0, keepdims=True).astype(jnp.int32)
    return owners * capacity + ranking + first


def contract_kernel(n_dev, n_tgt, me_ref, src_cluster_ref, tgt_cluster_ref, *refs):
    hbm, (own_ref, other_ref), held, parts, in_sem = refs[:4], refs[4:6], refs[6:10], refs[10], refs[11]
    arrivals = [pltpu.make_async_copy(a, b, in_sem.at[i]) for i, (a, b) in enumerate(zip(hbm, held))]
    for copy in arrivals:
        copy.start()
    tgt_points, tgt_factor, src_points, src_factor = held
    _, _, _, chunk, rank = parts.shape
    kept = chunk - TABLE_ROWS
    me = me_ref[0]
    mine = (me // n_tgt) % 2
    row = lax.broadcasted_iota(jnp.int32, (TABLE_ROWS, rank), 0)
    table = jnp.where(row == 0, src_cluster_ref[...], jnp.where(row == 1, tgt_cluster_ref[...], 0))
    parts[:, :, :, kept:, :] = jnp.zeros(parts.shape[:3] + (TABLE_ROWS, rank), jnp.float32)
    parts[me // (2 * n_tgt), mine, me % n_tgt, kept:, :] = table.astype(jnp.float32)
    features = tgt_points.shape[1]
    blocks = blocks_of(n_dev, chunk, rank, features)
    for which, (points, factor) in enumerate(((tgt_points, tgt_factor), (src_points, src_factor))):
        arrivals[2 * which].wait()
        arrivals[2 * which + 1].wait()
        total = contract_rows(factor[...], points[...])
        for c, row, first, column in blocks:
            first -= which * rank
            if 0 <= first < rank:
                place = (c // (2 * n_tgt), c // n_tgt % 2, c % n_tgt)
                parts[(*place, pl.ds(row, BLOCK_ROWS))] = total[
                    first : first + BLOCK_ROWS, column : column + rank
                ]
    for i in range(parts.shape[0]):
        own_ref[i] = parts[i, mine]
        other_ref[i] = parts[i, 1 - mine].astype(jnp.bfloat16)


def partial_sums(
    me, src_cluster, tgt_cluster, src_points, tgt_points, src_factor, tgt_factor, n_dev, n_tgt
):
    rows, features = src_points.shape
    rank = src_factor.shape[1]
    chunk = 2 * features // n_dev + TABLE_ROWS
    shape = (n_dev // (2 * n_tgt), n_tgt, chunk, rank)
    vmem = pl.BlockSpec(memory_space=pltpu.VMEM)
    return pl.pallas_call(
        functools.partial(contract_kernel, n_dev, n_tgt),
        out_shape=(
            jax.ShapeDtypeStruct(shape, jnp.float32),
            jax.ShapeDtypeStruct(shape, jnp.bfloat16),
        ),
        in_specs=[pl.BlockSpec(memory_space=pltpu.SMEM)] + [vmem] * 2 + [in_hbm()] * 4,
        out_specs=(vmem, vmem),
        scratch_shapes=[
            pltpu.VMEM((rows, features), jnp.bfloat16),
            pltpu.VMEM((rows, rank), jnp.bfloat16),
            pltpu.VMEM((rows, features), jnp.bfloat16),
            pltpu.VMEM((rows, rank), jnp.bfloat16),
            pltpu.VMEM((n_dev // (2 * n_tgt), 2, n_tgt, chunk, rank), jnp.float32),
            pltpu.SemaphoreType.DMA((4,)),
        ],
        compiler_params=pltpu.CompilerParams(vmem_limit_bytes=PACK_VMEM_BYTES),
        cost_estimate=pl.CostEstimate(
            flops=4 * rows * features * rank,
            bytes_accessed=4 * rows * (features + rank) + 4 * n_dev * chunk * rank,
            transcendentals=0,
        ),
        name="partial_sums",
    )(me[None], src_cluster[None, :], tgt_cluster[None, :], tgt_points, tgt_factor, src_points, src_factor)


def near_pack_kernel(
    n_group,
    capacity,
    spread,
    tgt_cluster_ref,
    src_cluster_ref,
    tgt_points_hbm,
    tgt_factor_hbm,
    src_points_hbm,
    src_factor_hbm,
    packed_hbm,
    raw_hbm,
    tgt_points,
    tgt_factor,
    src_points,
    src_factor,
    packed,
    labels,
    in_sem,
    out_sem,
    raw_sem,
):
    hbm = (tgt_points_hbm, tgt_factor_hbm, src_points_hbm, src_factor_hbm)
    held = (tgt_points, tgt_factor, src_points, src_factor)
    arrivals = [pltpu.make_async_copy(a, b, in_sem.at[i]) for i, (a, b) in enumerate(zip(hbm, held))]
    for copy in arrivals:
        copy.start()
    rows, features = tgt_points.shape
    width = packed.shape[1]
    first = lax.broadcasted_iota(jnp.int32, (LABEL_ROWS, rows), 0) == 0
    labels[...] = jnp.zeros(labels.shape, jnp.bfloat16)
    labels[:, :rows] = jnp.where(first, tgt_cluster_ref[...], 0).astype(jnp.float32).astype(jnp.bfloat16)
    tgt_slot = slot_row(tgt_cluster_ref[...], n_group, 2 * capacity, spread, 0)
    src_slot = slot_row(src_cluster_ref[...], n_group, 2 * capacity, spread, capacity)
    for copy in arrivals:
        copy.wait()
    departures = [
        pltpu.make_async_copy(
            tgt_points, raw_hbm.at[pl.ds(0, rows), pl.ds(0, features)], raw_sem.at[0]
        ),
        pltpu.make_async_copy(
            tgt_factor, raw_hbm.at[pl.ds(0, rows), pl.ds(features, width - features)], raw_sem.at[1]
        ),
        pltpu.make_async_copy(labels, raw_hbm.at[pl.ds(rows, LABEL_ROWS)], raw_sem.at[2]),
    ]
    for copy in departures:
        copy.start()
    block = 256
    for part in range(packed.shape[0] // block):
        mine = pl.ds(part * block, block)
        index = lax.broadcasted_iota(jnp.int32, (block, rows), 0) + part * block
        tgt_place = (index == tgt_slot).astype(jnp.bfloat16)
        src_place = (index == src_slot).astype(jnp.bfloat16)
        packed[mine, :features] = (
            jnp.dot(tgt_place, tgt_points[...], preferred_element_type=jnp.float32)
            + jnp.dot(src_place, src_points[...], preferred_element_type=jnp.float32)
        ).astype(jnp.bfloat16)
        packed[mine, features:] = (
            jnp.dot(tgt_place, tgt_factor[...], preferred_element_type=jnp.float32)
            + jnp.dot(src_place, src_factor[...], preferred_element_type=jnp.float32)
        ).astype(jnp.bfloat16)
        departures.append(
            pltpu.make_async_copy(packed.at[mine], packed_hbm.at[mine], out_sem.at[part])
        )
        departures[-1].start()
    for copy in departures:
        copy.wait()


def near_pack(
    tgt_cluster, src_cluster, tgt_points, tgt_factor, src_points, src_factor, n_group, capacity, spread
):
    rows, features = tgt_points.shape
    rank = tgt_factor.shape[1]
    slots = 2 * n_group * capacity
    vmem = pl.BlockSpec(memory_space=pltpu.VMEM)
    held = [pltpu.VMEM((rows, features), jnp.bfloat16), pltpu.VMEM((rows, rank), jnp.bfloat16)]
    return pl.pallas_call(
        functools.partial(near_pack_kernel, n_group, capacity, spread),
        out_shape=(
            jax.ShapeDtypeStruct((slots, features + rank), jnp.bfloat16),
            jax.ShapeDtypeStruct((rows + LABEL_ROWS, features + rank), jnp.bfloat16),
        ),
        in_specs=[vmem] * 2 + [in_hbm()] * 4,
        out_specs=(in_hbm(), in_hbm()),
        scratch_shapes=held * 2
        + [
            pltpu.VMEM((slots, features + rank), jnp.bfloat16),
            pltpu.VMEM((LABEL_ROWS, features + rank), jnp.bfloat16),
            pltpu.SemaphoreType.DMA((4,)),
            pltpu.SemaphoreType.DMA((slots // 256,)),
            pltpu.SemaphoreType.DMA((3,)),
        ],
        compiler_params=pltpu.CompilerParams(vmem_limit_bytes=PACK_VMEM_BYTES),
        cost_estimate=pl.CostEstimate(
            flops=4 * slots * rows * (features + rank),
            bytes_accessed=2 * (slots + 3 * rows) * (features + rank),
            transcendentals=0,
        ),
        name="near_pack",
    )(tgt_cluster[None, :], src_cluster[None, :], tgt_points, tgt_factor, src_points, src_factor)


def far_pack_kernel(n_group, capacity, spread, raw_hbm, packed_hbm, raw, packed, in_sem, out_sem):
    rows = raw.shape[0] - LABEL_ROWS
    labels_in = pltpu.make_async_copy(
        raw_hbm.at[pl.ds(rows, LABEL_ROWS)], raw.at[pl.ds(rows, LABEL_ROWS)], in_sem.at[0]
    )
    rows_in = pltpu.make_async_copy(
        raw_hbm.at[pl.ds(0, rows)], raw.at[pl.ds(0, rows)], in_sem.at[1]
    )
    labels_in.start()
    rows_in.start()
    labels_in.wait()
    labels = raw[rows:, :rows].astype(jnp.float32)[:1].astype(jnp.int32)
    slot = slot_row(labels, n_group, capacity, spread, 0)
    rows_in.wait()
    block = 256
    departures = []
    for part in range(packed.shape[0] // block):
        mine = pl.ds(part * block, block)
        index = lax.broadcasted_iota(jnp.int32, (block, rows), 0) + part * block
        place = (index == slot).astype(jnp.bfloat16)
        packed[mine, :] = jnp.dot(
            place, raw[:rows, :], preferred_element_type=jnp.float32
        ).astype(jnp.bfloat16)
        departures.append(
            pltpu.make_async_copy(packed.at[mine], packed_hbm.at[mine], out_sem.at[part])
        )
        departures[-1].start()
    for copy in departures:
        copy.wait()


def far_pack(raw, n_group, capacity, spread):
    rows, width = raw.shape
    slots = n_group * capacity
    return pl.pallas_call(
        functools.partial(far_pack_kernel, n_group, capacity, spread),
        out_shape=jax.ShapeDtypeStruct((slots, width), jnp.bfloat16),
        in_specs=[in_hbm()],
        out_specs=in_hbm(),
        scratch_shapes=[
            pltpu.VMEM((rows, width), jnp.bfloat16),
            pltpu.VMEM((slots, width), jnp.bfloat16),
            pltpu.SemaphoreType.DMA((2,)),
            pltpu.SemaphoreType.DMA((slots // 256,)),
        ],
        compiler_params=pltpu.CompilerParams(vmem_limit_bytes=PACK_VMEM_BYTES),
        cost_estimate=pl.CostEstimate(
            flops=2 * slots * rows * width,
            bytes_accessed=2 * (slots + rows) * width,
            transcendentals=0,
        ),
        name="far_pack",
    )(raw)


def digits_of(size, stride):
    bits = size.bit_length() - 1
    found = []
    while bits:
        take = 1 if bits % 2 else 2
        found.append((stride, 1 << take))
        stride <<= take
        bits -= take
    return found


class Chain:
    def __init__(self, own, other, n_src, n_tgt):
        self.n_dev = n_src * n_tgt
        first = (n_tgt, 2)
        src, tgt = digits_of(n_src // 2, 2 * n_tgt), digits_of(n_tgt, 1)
        self.plane, self.along = [first] + src, tgt
        self.dims = src[::-1] + [first] + tgt[::-1]
        self.left = [d for d in self.dims if d != first]
        x = own + self.sent(other, n_tgt).astype(jnp.float32)
        self.x = x.reshape(tuple(radix for _, radix in self.left) + own.shape[2:])

    def sent(self, array, mask):
        return lax.ppermute(array, ALL, [(i, i ^ mask) for i in range(self.n_dev)])

    def scatter(self, digit):
        stride, radix = digit
        dim = self.left.index(digit)
        mine = (lax.axis_index(ALL) // stride) % radix
        total = lax.dynamic_index_in_dim(self.x, mine, dim, keepdims=False)
        for j in range(1, radix):
            piece = lax.dynamic_index_in_dim(self.x, mine ^ j, dim, keepdims=False)
            total = total + self.sent(piece.astype(jnp.bfloat16), j * stride).astype(jnp.float32)
        self.x = total
        self.left.remove(digit)

    def swap(self, digit):
        stride, radix = digit
        piece = self.x.astype(jnp.bfloat16)
        for j in range(1, radix):
            self.x = self.x + self.sent(piece, j * stride).astype(jnp.float32)

    def gather(self, digit):
        stride, radix = digit
        mine = (lax.axis_index(ALL) // stride) % radix
        x = self.x.astype(jnp.bfloat16)
        got = [x] + [self.sent(x, j * stride) for j in range(1, radix)]
        self.left = [d for d in self.dims if d in self.left or d == digit]
        self.x = jnp.stack(
            [lax.select_n(mine ^ d, *got) if radix > 2 else jnp.where(mine == d, *got) for d in range(radix)],
            axis=self.left.index(digit),
        )


def update_kernel(
    src_points_ref,
    tgt_points_ref,
    src_factor_ref,
    tgt_factor_ref,
    marginal_ref,
    sums_ref,
    src_ref,
    tgt_ref,
    total,
):
    totals_of(sums_ref, total, src_points_ref.shape[1])
    rank = src_ref.shape[1]
    marginal = marginal_ref[...]
    src_ref[...] = mirror_step(src_points_ref[...], total[:rank], src_factor_ref[...], marginal)
    tgt_ref[...] = mirror_step(tgt_points_ref[...], total[rank:], tgt_factor_ref[...], marginal)


def updates(src_points, tgt_points, src_factor, tgt_factor, marginal, sums):
    rows, features = src_points.shape
    rank = src_factor.shape[1]
    shape = jax.ShapeDtypeStruct(src_factor.shape, jnp.bfloat16)
    return pl.pallas_call(
        update_kernel,
        out_shape=(shape, shape),
        scratch_shapes=[pltpu.VMEM((2 * rank, features), jnp.bfloat16)],
        compiler_params=pltpu.CompilerParams(vmem_limit_bytes=VMEM_BYTES),
        cost_estimate=pl.CostEstimate(
            flops=4 * rows * features * rank,
            bytes_accessed=4 * rows * (features + 2 * rank),
            transcendentals=2 * rows * rank,
        ),
        name="mirror_updates",
    )(src_points, tgt_points, src_factor, tgt_factor, marginal[None, :], sums)


def seen_block(ref, part, block):
    piece = block // ref.shape[1]
    return ref[pl.ds(part * piece, piece)].reshape(block, ref.shape[2])


def prepare_targets(ref, src_total, marginal, features, tgt_rows, tgt_update, tgt_inv):
    block = OWNER_BLOCK
    for part in range(tgt_rows.shape[0] // block):
        mine = pl.ds(part * block, block)
        both = seen_block(ref, part, block)
        rows = both[:, :features]
        tgt_rows[mine, :] = rows
        tgt_update[mine, :] = mirror_step(rows, src_total, both[:, features:], marginal)
        tgt_inv[:, mine] = inverse_norm(rows).reshape(1, block)


def block_terms(rows, update, src_label, tgt_label, tgt_rows, tgt_update, tgt_inv):
    cosine = contract_columns(rows, tgt_rows[...]) * inverse_norm(rows) * tgt_inv[...]
    weight = contract_columns(update, tgt_update[...]) / update.shape[1]
    same = jnp.logical_and(src_label == tgt_label, src_label > 0)
    kernel = jnp.where(same, weight * jnp.exp((cosine - 1.0) / TEMPER), 0.0)
    image = jnp.dot(
        kernel.astype(jnp.bfloat16), tgt_rows[...], preferred_element_type=jnp.float32
    )
    return image, jnp.sum(kernel, axis=1, keepdims=True)


def source_block(src_ref, part, total, marginal, features):
    both = seen_block(src_ref, part, OWNER_BLOCK)
    rows = both[:, :features]
    return rows, mirror_step(rows, total[: both.shape[1] - features], both[:, features:], marginal)


def near_kernel(
    features,
    src_ref,
    tgt_ref,
    sums_ref,
    marginal_ref,
    src_label_ref,
    tgt_label_ref,
    image_ref,
    total,
    tgt_rows,
    tgt_update,
    tgt_inv,
):
    totals_of(sums_ref, total, features)
    rank = tgt_update.shape[1]
    marginal = marginal_ref[...]
    prepare_targets(tgt_ref, total[rank:], marginal, features, tgt_rows, tgt_update, tgt_inv)
    block = OWNER_BLOCK
    for part in range(image_ref.shape[0] // block):
        mine = pl.ds(part * block, block)
        rows, update = source_block(src_ref, part, total, marginal, features)
        image, denominator = block_terms(
            rows, update, src_label_ref[mine, :], tgt_label_ref[...], tgt_rows, tgt_update, tgt_inv
        )
        image_ref[mine, :features] = image
        image_ref[mine, features:] = jnp.broadcast_to(denominator, (block, LANES))


def far_kernel(
    features,
    src_ref,
    tgt_ref,
    sums_ref,
    marginal_ref,
    src_label_ref,
    tgt_label_ref,
    image_ref,
    out_hbm,
    total,
    tgt_rows,
    tgt_update,
    tgt_inv,
    images,
    out_sem,
):
    totals_of(sums_ref, total, features)
    rank = tgt_update.shape[1]
    marginal = marginal_ref[...]
    prepare_targets(tgt_ref, total[rank:], marginal, features, tgt_rows, tgt_update, tgt_inv)
    block = OWNER_BLOCK
    departures = []
    for part in range(image_ref.shape[0] // block):
        mine = pl.ds(part * block, block)
        rows, update = source_block(src_ref, part, total, marginal, features)
        image, denominator = block_terms(
            rows, update, src_label_ref[mine, :], tgt_label_ref[...], tgt_rows, tgt_update, tgt_inv
        )
        denominator = denominator + image_ref[mine, features : features + 1]
        denominator = jnp.where(denominator > 0, denominator, 1.0)
        images[mine, :] = ((image_ref[mine, :features] + image) / denominator).astype(jnp.bfloat16)
        departures.append(
            pltpu.make_async_copy(images.at[mine], out_hbm.at[mine], out_sem.at[part])
        )
        departures[-1].start()
    for copy in departures:
        copy.wait()


def owner_cost(slots, width):
    return pl.CostEstimate(
        flops=2 * slots * width * (512 + 2 * slots),
        bytes_accessed=8 * slots * width,
        transcendentals=slots * slots,
    )


def near_maps(near, sums, marginal, src_labels, tgt_labels, features):
    n_group, _, capacity, width = near.shape
    slots = n_group * capacity
    rank = width - features
    return pl.pallas_call(
        functools.partial(near_kernel, features),
        out_shape=jax.ShapeDtypeStruct((slots, features + LANES), jnp.float32),
        grid=(1,),
        in_specs=[
            pl.BlockSpec((n_group, None, capacity, width), lambda step: (0, 1, 0, 0)),
            pl.BlockSpec((n_group, None, capacity, width), lambda step: (0, 0, 0, 0)),
            whole(sums.shape),
            whole((1, rank)),
            whole((slots, 1)),
            whole((1, slots)),
        ],
        out_specs=whole((slots, features + LANES)),
        scratch_shapes=[
            pltpu.VMEM((2 * rank, features), jnp.bfloat16),
            pltpu.VMEM((slots, features), jnp.bfloat16),
            pltpu.VMEM((slots, rank), jnp.bfloat16),
            pltpu.VMEM((1, slots), jnp.float32),
        ],
        compiler_params=pltpu.CompilerParams(vmem_limit_bytes=VMEM_BYTES),
        cost_estimate=owner_cost(slots, width),
        name="near_maps",
    )(near, near, sums, marginal[None, :], src_labels[:, None], tgt_labels[None, :])


def far_maps(near, far, sums, marginal, src_labels, tgt_labels, image, features):
    n_group, capacity, width = far.shape
    slots = n_group * capacity
    rank = width - features
    return pl.pallas_call(
        functools.partial(far_kernel, features),
        out_shape=jax.ShapeDtypeStruct((slots, features), jnp.bfloat16),
        grid=(1,),
        in_specs=[
            pl.BlockSpec((n_group, None, capacity, width), lambda step: (0, 1, 0, 0)),
            whole(far.shape),
            whole(sums.shape),
            whole((1, rank)),
            whole((slots, 1)),
            whole((1, slots)),
            whole(image.shape),
        ],
        out_specs=in_hbm(),
        scratch_shapes=[
            pltpu.VMEM((2 * rank, features), jnp.bfloat16),
            pltpu.VMEM((slots, features), jnp.bfloat16),
            pltpu.VMEM((slots, rank), jnp.bfloat16),
            pltpu.VMEM((1, slots), jnp.float32),
            pltpu.VMEM((slots, features), jnp.bfloat16),
            pltpu.SemaphoreType.DMA((slots // OWNER_BLOCK,)),
        ],
        compiler_params=pltpu.CompilerParams(vmem_limit_bytes=VMEM_BYTES),
        cost_estimate=owner_cost(slots, width),
        name="far_maps",
    )(
        near,
        far,
        sums,
        marginal[None, :],
        src_labels[:, None],
        tgt_labels[None, :],
        image,
    )


def labels_of(clusters, owner, capacity, spread):
    rows = clusters.shape[1]
    mine = clusters // spread == owner
    before = (jnp.arange(rows)[:, None] < jnp.arange(rows)[None, :]).astype(jnp.bfloat16)
    earlier = jnp.dot(mine.astype(jnp.bfloat16), before, preferred_element_type=jnp.float32)
    ranking = jnp.where(mine, earlier.astype(jnp.int32), -1)
    value = clusters - owner * spread + 1
    hit = ranking[:, None, :] == jnp.arange(capacity, dtype=jnp.int32)[None, :, None]
    return jnp.sum(jnp.where(hit, value[:, None, :], 0), axis=2).reshape(-1)


def exchange(rows):
    return lax.all_to_all(rows, GROUP, split_axis=0, concat_axis=0, tiled=True)


def per_device(
    src_points, tgt_points, src_factor, tgt_factor, inner_marginal, src_cluster, tgt_cluster
):
    n_src, n_rest = lax.axis_size("src"), lax.axis_size(REST)
    n_group = n_src * n_rest
    n_dev = 2 * n_group
    rows, features = src_points.shape
    rank = src_factor.shape[1]
    capacity = 2 * (2 * rows // n_dev)
    spread = 2 * CL_DEV
    me = lax.axis_index(ALL)
    my_half = lax.axis_index(HALF)
    owner = lax.axis_index(GROUP)

    near, raw = near_pack(
        tgt_cluster,
        src_cluster,
        tgt_points,
        tgt_factor,
        src_points,
        src_factor,
        n_group,
        capacity,
        spread,
    )
    near, me = lax.optimization_barrier((near, me))
    near = exchange(near)
    raw = lax.ppermute(raw, HALF, [(0, 1), (1, 0)])
    own, other = partial_sums(
        me,
        src_cluster,
        tgt_cluster,
        src_points,
        tgt_points,
        src_factor,
        tgt_factor,
        n_dev,
        2 * n_rest,
    )
    chain = Chain(own, other, n_src, 2 * n_rest)
    for digit in chain.plane[1:]:
        chain.scatter(digit)
    chain.x, raw = lax.optimization_barrier((chain.x, raw))
    for digit in chain.along:
        chain.swap(digit)
    far = far_pack(raw, n_group, capacity, spread)
    far, chain.x = lax.optimization_barrier((far, chain.x))
    far, near = lax.optimization_barrier((far, near))
    far = exchange(far)
    for digit in reversed(chain.plane):
        chain.gather(digit)
    sums = chain.x.reshape(n_dev, -1, rank)

    kept = 2 * features // n_dev
    table = sums[:, kept : kept + 2].astype(jnp.int32).reshape(n_src, 2, n_rest, 2, rows)
    near_table = lax.dynamic_index_in_dim(table, my_half, 1, keepdims=False)
    far_table = lax.dynamic_index_in_dim(table, 1 - my_half, 1, keepdims=False)
    near_table = near_table.reshape(n_group, 2, rows)
    far_table = far_table.reshape(n_group, 2, rows)
    src_labels = labels_of(near_table[:, 0], owner, capacity, spread)
    near_labels = labels_of(near_table[:, 1], owner, capacity, spread)
    far_labels = labels_of(far_table[:, 1], owner, capacity, spread)

    near = near.reshape(n_group, 2, capacity, features + rank)
    far = far.reshape(n_group, capacity, features + rank)
    image = near_maps(near, sums, inner_marginal, src_labels, near_labels, features)
    images = far_maps(near, far, sums, inner_marginal, src_labels, far_labels, image, features)
    returned = exchange(images)

    src_update, tgt_update = updates(
        src_points, tgt_points, src_factor, tgt_factor, inner_marginal, sums
    )
    slot = slot_row(src_cluster[None, :], n_group, capacity, spread, 0)
    back = slot.reshape(rows, 1) == jnp.arange(n_group * capacity, dtype=jnp.int32)[None, :]
    back = lax.optimization_barrier(back.astype(jnp.bfloat16))
    mapped = jnp.dot(back, returned, preferred_element_type=jnp.float32).astype(jnp.bfloat16)
    return (src_update, tgt_update, mapped)


def solution(mesh):
    n_src, n_tgt = mesh.shape["src"], mesh.shape["tgt"]
    halves = Mesh(mesh.devices.reshape(n_src, 2, n_tgt // 2), ALL)
    rows = P(ALL, None)
    return jax.shard_map(
        per_device,
        mesh=halves,
        in_specs=(rows, rows, rows, rows, P(), P(ALL), P(ALL)),
        out_specs=(rows, rows, rows),
        check_vma=False,
    )
```

```python
import functools

import jax
import jax.numpy as jnp
from jax import lax
from jax.experimental import pallas as pl
from jax.experimental.pallas import tpu as pltpu
from jax.sharding import Mesh
from jax.sharding import PartitionSpec as P

CL_DEV = 2

GAMMA = 2.0
TEMPER = 0.03
EPS = 1e-06

HALF, REST = "half", "rest"
ALL = ("src", HALF, REST)
GROUP = ("src", REST)
VMEM_BYTES = 48 * 1024 * 1024
PACK_VMEM_BYTES = 62 * 1024 * 1024
TABLE_ROWS = 8
BLOCK_ROWS = 16
OWNER_BLOCK = 256
LABEL_ROWS = 16


def contract_rows(left, right):
    return lax.dot_general(
        left, right, (((0,), (0,)), ((), ())), preferred_element_type=jnp.float32
    )


def contract_columns(left, right):
    return lax.dot_general(
        left, right, (((1,), (1,)), ((), ())), preferred_element_type=jnp.float32
    )


def mirror_step(points, total_round, factor, inner_marginal):
    gradient = -contract_columns(points, total_round) / inner_marginal
    row_scale = jnp.max(jnp.abs(gradient), axis=1, keepdims=True) + EPS
    tilted = factor.astype(jnp.float32) * jnp.exp(-GAMMA * gradient / row_scale)
    mean = jnp.mean(tilted, axis=1, keepdims=True)
    mean = jnp.where(mean > 0, mean, 1.0)
    return (tilted / mean).astype(jnp.bfloat16)


def inverse_norm(rows):
    return lax.rsqrt(jnp.sum(jnp.square(rows.astype(jnp.float32)), axis=1, keepdims=True) + EPS)


def blocks_of(n_dev, chunk, rank, features):
    kept = (chunk - TABLE_ROWS) // BLOCK_ROWS
    wide = features // rank
    return [
        (b // kept, b % kept * BLOCK_ROWS, b // wide * BLOCK_ROWS, b % wide * rank)
        for b in range(n_dev * kept)
    ]


def totals_of(sums_ref, total, features):
    n_dev, chunk, rank = sums_ref.shape
    for c, row, first, column in blocks_of(n_dev, chunk, rank, features):
        total[pl.ds(first, BLOCK_ROWS), pl.ds(column, rank)] = sums_ref[c, pl.ds(row, BLOCK_ROWS), :]


def whole(shape):
    return pl.BlockSpec(shape, lambda *_: (0,) * len(shape))


def in_hbm():
    return pl.BlockSpec(memory_space=pltpu.HBM)


def slot_row(cluster, n_group, capacity, spread, first):
    rows = cluster.shape[1]
    owners = cluster // spread
    onehot = owners == lax.broadcasted_iota(jnp.int32, (n_group, rows), 0)
    before = lax.broadcasted_iota(jnp.int32, (rows, rows), 0) < lax.broadcasted_iota(
        jnp.int32, (rows, rows), 1
    )
    earlier = jnp.dot(
        onehot.astype(jnp.bfloat16), before.astype(jnp.bfloat16), preferred_element_type=jnp.float32
    )
    ranking = jnp.sum(jnp.where(onehot, earlier, 0.0), axis=0, keepdims=True).astype(jnp.int32)
    return owners * capacity + ranking + first


def contract_kernel(n_dev, n_tgt, me_ref, src_cluster_ref, tgt_cluster_ref, *refs):
    hbm, (own_ref, other_ref), held, parts, in_sem = refs[:4], refs[4:6], refs[6:10], refs[10], refs[11]
    arrivals = [pltpu.make_async_copy(a, b, in_sem.at[i]) for i, (a, b) in enumerate(zip(hbm, held))]
    for copy in arrivals:
        copy.start()
    tgt_points, tgt_factor, src_points, src_factor = held
    _, _, _, chunk, rank = parts.shape
    kept = chunk - TABLE_ROWS
    me = me_ref[0]
    mine = (me // n_tgt) % 2
    row = lax.broadcasted_iota(jnp.int32, (TABLE_ROWS, rank), 0)
    table = jnp.where(row == 0, src_cluster_ref[...], jnp.where(row == 1, tgt_cluster_ref[...], 0))
    parts[:, :, :, kept:, :] = jnp.zeros(parts.shape[:3] + (TABLE_ROWS, rank), jnp.float32)
    parts[me // (2 * n_tgt), mine, me % n_tgt, kept:, :] = table.astype(jnp.float32)
    features = tgt_points.shape[1]
    blocks = blocks_of(n_dev, chunk, rank, features)
    for which, (points, factor) in enumerate(((tgt_points, tgt_factor), (src_points, src_factor))):
        arrivals[2 * which].wait()
        arrivals[2 * which + 1].wait()
        total = contract_rows(factor[...], points[...])
        for c, row, first, column in blocks:
            first -= which * rank
            if 0 <= first < rank:
                place = (c // (2 * n_tgt), c // n_tgt % 2, c % n_tgt)
                parts[(*place, pl.ds(row, BLOCK_ROWS))] = total[
                    first : first + BLOCK_ROWS, column : column + rank
                ]
    for i in range(parts.shape[0]):
        own_ref[i] = parts[i, mine]
        other_ref[i] = parts[i, 1 - mine].astype(jnp.bfloat16)


def partial_sums(
    me, src_cluster, tgt_cluster, src_points, tgt_points, src_factor, tgt_factor, n_dev, n_tgt
):
    rows, features = src_points.shape
    rank = src_factor.shape[1]
    chunk = 2 * features // n_dev + TABLE_ROWS
    shape = (n_dev // (2 * n_tgt), n_tgt, chunk, rank)
    vmem = pl.BlockSpec(memory_space=pltpu.VMEM)
    return pl.pallas_call(
        functools.partial(contract_kernel, n_dev, n_tgt),
        out_shape=(
            jax.ShapeDtypeStruct(shape, jnp.float32),
            jax.ShapeDtypeStruct(shape, jnp.bfloat16),
        ),
        in_specs=[pl.BlockSpec(memory_space=pltpu.SMEM)] + [vmem] * 2 + [in_hbm()] * 4,
        out_specs=(vmem, vmem),
        scratch_shapes=[
            pltpu.VMEM((rows, features), jnp.bfloat16),
            pltpu.VMEM((rows, rank), jnp.bfloat16),
            pltpu.VMEM((rows, features), jnp.bfloat16),
            pltpu.VMEM((rows, rank), jnp.bfloat16),
            pltpu.VMEM((n_dev // (2 * n_tgt), 2, n_tgt, chunk, rank), jnp.float32),
            pltpu.SemaphoreType.DMA((4,)),
        ],
        compiler_params=pltpu.CompilerParams(vmem_limit_bytes=PACK_VMEM_BYTES),
        cost_estimate=pl.CostEstimate(
            flops=4 * rows * features * rank,
            bytes_accessed=4 * rows * (features + rank) + 4 * n_dev * chunk * rank,
            transcendentals=0,
        ),
        name="partial_sums",
    )(me[None], src_cluster[None, :], tgt_cluster[None, :], tgt_points, tgt_factor, src_points, src_factor)


def near_pack_kernel(
    n_group,
    capacity,
    spread,
    tgt_cluster_ref,
    src_cluster_ref,
    tgt_points_hbm,
    tgt_factor_hbm,
    src_points_hbm,
    src_factor_hbm,
    packed_hbm,
    raw_hbm,
    tgt_points,
    tgt_factor,
    src_points,
    src_factor,
    packed,
    labels,
    in_sem,
    out_sem,
    raw_sem,
):
    hbm = (tgt_points_hbm, tgt_factor_hbm, src_points_hbm, src_factor_hbm)
    held = (tgt_points, tgt_factor, src_points, src_factor)
    arrivals = [pltpu.make_async_copy(a, b, in_sem.at[i]) for i, (a, b) in enumerate(zip(hbm, held))]
    for copy in arrivals:
        copy.start()
    rows, features = tgt_points.shape
    width = packed.shape[1]
    first = lax.broadcasted_iota(jnp.int32, (LABEL_ROWS, rows), 0) == 0
    labels[...] = jnp.zeros(labels.shape, jnp.bfloat16)
    labels[:, :rows] = jnp.where(first, tgt_cluster_ref[...], 0).astype(jnp.float32).astype(jnp.bfloat16)
    tgt_slot = slot_row(tgt_cluster_ref[...], n_group, 2 * capacity, spread, 0)
    src_slot = slot_row(src_cluster_ref[...], n_group, 2 * capacity, spread, capacity)
    for copy in arrivals:
        copy.wait()
    departures = [
        pltpu.make_async_copy(
            tgt_points, raw_hbm.at[pl.ds(0, rows), pl.ds(0, features)], raw_sem.at[0]
        ),
        pltpu.make_async_copy(
            tgt_factor, raw_hbm.at[pl.ds(0, rows), pl.ds(features, width - features)], raw_sem.at[1]
        ),
        pltpu.make_async_copy(labels, raw_hbm.at[pl.ds(rows, LABEL_ROWS)], raw_sem.at[2]),
    ]
    for copy in departures:
        copy.start()
    block = 256
    for part in range(packed.shape[0] // block):
        mine = pl.ds(part * block, block)
        index = lax.broadcasted_iota(jnp.int32, (block, rows), 0) + part * block
        tgt_place = (index == tgt_slot).astype(jnp.bfloat16)
        src_place = (index == src_slot).astype(jnp.bfloat16)
        packed[mine, :features] = (
            jnp.dot(tgt_place, tgt_points[...], preferred_element_type=jnp.float32)
            + jnp.dot(src_place, src_points[...], preferred_element_type=jnp.float32)
        ).astype(jnp.bfloat16)
        packed[mine, features:] = (
            jnp.dot(tgt_place, tgt_factor[...], preferred_element_type=jnp.float32)
            + jnp.dot(src_place, src_factor[...], preferred_element_type=jnp.float32)
        ).astype(jnp.bfloat16)
        departures.append(
            pltpu.make_async_copy(packed.at[mine], packed_hbm.at[mine], out_sem.at[part])
        )
        departures[-1].start()
    for copy in departures:
        copy.wait()


def near_pack(
    tgt_cluster, src_cluster, tgt_points, tgt_factor, src_points, src_factor, n_group, capacity, spread
):
    rows, features = tgt_points.shape
    rank = tgt_factor.shape[1]
    slots = 2 * n_group * capacity
    vmem = pl.BlockSpec(memory_space=pltpu.VMEM)
    held = [pltpu.VMEM((rows, features), jnp.bfloat16), pltpu.VMEM((rows, rank), jnp.bfloat16)]
    return pl.pallas_call(
        functools.partial(near_pack_kernel, n_group, capacity, spread),
        out_shape=(
            jax.ShapeDtypeStruct((slots, features + rank), jnp.bfloat16),
            jax.ShapeDtypeStruct((rows + LABEL_ROWS, features + rank), jnp.bfloat16),
        ),
        in_specs=[vmem] * 2 + [in_hbm()] * 4,
        out_specs=(in_hbm(), in_hbm()),
        scratch_shapes=held * 2
        + [
            pltpu.VMEM((slots, features + rank), jnp.bfloat16),
            pltpu.VMEM((LABEL_ROWS, features + rank), jnp.bfloat16),
            pltpu.SemaphoreType.DMA((4,)),
            pltpu.SemaphoreType.DMA((slots // 256,)),
            pltpu.SemaphoreType.DMA((3,)),
        ],
        compiler_params=pltpu.CompilerParams(vmem_limit_bytes=PACK_VMEM_BYTES),
        cost_estimate=pl.CostEstimate(
            flops=4 * slots * rows * (features + rank),
            bytes_accessed=2 * (slots + 3 * rows) * (features + rank),
            transcendentals=0,
        ),
        name="near_pack",
    )(tgt_cluster[None, :], src_cluster[None, :], tgt_points, tgt_factor, src_points, src_factor)


def far_pack_kernel(n_group, capacity, spread, raw_hbm, packed_hbm, raw, packed, in_sem, out_sem):
    rows = raw.shape[0] - LABEL_ROWS
    labels_in = pltpu.make_async_copy(
        raw_hbm.at[pl.ds(rows, LABEL_ROWS)], raw.at[pl.ds(rows, LABEL_ROWS)], in_sem.at[0]
    )
    rows_in = pltpu.make_async_copy(
        raw_hbm.at[pl.ds(0, rows)], raw.at[pl.ds(0, rows)], in_sem.at[1]
    )
    labels_in.start()
    rows_in.start()
    labels_in.wait()
    labels = raw[rows:, :rows].astype(jnp.float32)[:1].astype(jnp.int32)
    slot = slot_row(labels, n_group, capacity, spread, 0)
    rows_in.wait()
    block = 256
    departures = []
    for part in range(packed.shape[0] // block):
        mine = pl.ds(part * block, block)
        index = lax.broadcasted_iota(jnp.int32, (block, rows), 0) + part * block
        place = (index == slot).astype(jnp.bfloat16)
        packed[mine, :] = jnp.dot(
            place, raw[:rows, :], preferred_element_type=jnp.float32
        ).astype(jnp.bfloat16)
        departures.append(
            pltpu.make_async_copy(packed.at[mine], packed_hbm.at[mine], out_sem.at[part])
        )
        departures[-1].start()
    for copy in departures:
        copy.wait()


def far_pack(raw, n_group, capacity, spread):
    rows, width = raw.shape
    slots = n_group * capacity
    return pl.pallas_call(
        functools.partial(far_pack_kernel, n_group, capacity, spread),
        out_shape=jax.ShapeDtypeStruct((slots, width), jnp.bfloat16),
        in_specs=[in_hbm()],
        out_specs=in_hbm(),
        scratch_shapes=[
            pltpu.VMEM((rows, width), jnp.bfloat16),
            pltpu.VMEM((slots, width), jnp.bfloat16),
            pltpu.SemaphoreType.DMA((2,)),
            pltpu.SemaphoreType.DMA((slots // 256,)),
        ],
        compiler_params=pltpu.CompilerParams(vmem_limit_bytes=PACK_VMEM_BYTES),
        cost_estimate=pl.CostEstimate(
            flops=2 * slots * rows * width,
            bytes_accessed=2 * (slots + rows) * width,
            transcendentals=0,
        ),
        name="far_pack",
    )(raw)


def digits_of(size, stride):
    bits = size.bit_length() - 1
    found = []
    while bits:
        take = 1 if bits % 2 else 2
        found.append((stride, 1 << take))
        stride <<= take
        bits -= take
    return found


class Chain:
    def __init__(self, own, other, n_src, n_tgt):
        self.n_dev = n_src * n_tgt
        first = (n_tgt, 2)
        src, tgt = digits_of(n_src // 2, 2 * n_tgt), digits_of(n_tgt, 1)
        self.plane, self.along = [first] + src, tgt
        self.dims = src[::-1] + [first] + tgt[::-1]
        self.left = [d for d in self.dims if d != first]
        x = own + self.sent(other, n_tgt).astype(jnp.float32)
        self.x = x.reshape(tuple(radix for _, radix in self.left) + own.shape[2:])

    def sent(self, array, mask):
        return lax.ppermute(array, ALL, [(i, i ^ mask) for i in range(self.n_dev)])

    def scatter(self, digit):
        stride, radix = digit
        dim = self.left.index(digit)
        mine = (lax.axis_index(ALL) // stride) % radix
        total = lax.dynamic_index_in_dim(self.x, mine, dim, keepdims=False)
        for j in range(1, radix):
            piece = lax.dynamic_index_in_dim(self.x, mine ^ j, dim, keepdims=False)
            total = total + self.sent(piece.astype(jnp.bfloat16), j * stride).astype(jnp.float32)
        self.x = total
        self.left.remove(digit)

    def swap(self, digit):
        stride, radix = digit
        piece = self.x.astype(jnp.bfloat16)
        for j in range(1, radix):
            self.x = self.x + self.sent(piece, j * stride).astype(jnp.float32)

    def gather(self, digit):
        stride, radix = digit
        mine = (lax.axis_index(ALL) // stride) % radix
        x = self.x.astype(jnp.bfloat16)
        got = [x] + [self.sent(x, j * stride) for j in range(1, radix)]
        self.left = [d for d in self.dims if d in self.left or d == digit]
        self.x = jnp.stack(
            [lax.select_n(mine ^ d, *got) if radix > 2 else jnp.where(mine == d, *got) for d in range(radix)],
            axis=self.left.index(digit),
        )


def update_kernel(
    src_points_ref,
    tgt_points_ref,
    src_factor_ref,
    tgt_factor_ref,
    marginal_ref,
    sums_ref,
    src_ref,
    tgt_ref,
    total,
):
    totals_of(sums_ref, total, src_points_ref.shape[1])
    rank = src_ref.shape[1]
    marginal = marginal_ref[...]
    src_ref[...] = mirror_step(src_points_ref[...], total[:rank], src_factor_ref[...], marginal)
    tgt_ref[...] = mirror_step(tgt_points_ref[...], total[rank:], tgt_factor_ref[...], marginal)


def updates(src_points, tgt_points, src_factor, tgt_factor, marginal, sums):
    rows, features = src_points.shape
    rank = src_factor.shape[1]
    shape = jax.ShapeDtypeStruct(src_factor.shape, jnp.bfloat16)
    return pl.pallas_call(
        update_kernel,
        out_shape=(shape, shape),
        scratch_shapes=[pltpu.VMEM((2 * rank, features), jnp.bfloat16)],
        compiler_params=pltpu.CompilerParams(vmem_limit_bytes=VMEM_BYTES),
        cost_estimate=pl.CostEstimate(
            flops=4 * rows * features * rank,
            bytes_accessed=4 * rows * (features + 2 * rank),
            transcendentals=2 * rows * rank,
        ),
        name="mirror_updates",
    )(src_points, tgt_points, src_factor, tgt_factor, marginal[None, :], sums)


def seen_block(ref, part, block):
    piece = block // ref.shape[1]
    return ref[pl.ds(part * piece, piece)].reshape(block, ref.shape[2])


def owner_kernel(
    features,
    src_ref,
    near_ref,
    far_ref,
    sums_ref,
    marginal_ref,
    src_label_ref,
    tgt_label_ref,
    out_hbm,
    total,
    tgt_rows,
    tgt_update,
    tgt_inv,
    images,
    out_sem,
):
    totals_of(sums_ref, total, features)
    slots = images.shape[0]
    rank = tgt_update.shape[1]
    marginal = marginal_ref[...]
    block = OWNER_BLOCK
    for which, ref in enumerate((near_ref, far_ref)):
        for part in range(slots // block):
            mine = pl.ds(which * slots + part * block, block)
            both = seen_block(ref, part, block)
            rows = both[:, :features]
            tgt_rows[mine, :] = rows
            tgt_update[mine, :] = mirror_step(rows, total[rank:], both[:, features:], marginal)
            tgt_inv[:, mine] = inverse_norm(rows).reshape(1, block)

    departures = []
    for part in range(slots // block):
        mine = pl.ds(part * block, block)
        both = seen_block(src_ref, part, block)
        rows = both[:, :features]
        update = mirror_step(rows, total[:rank], both[:, features:], marginal)
        cosine = contract_columns(rows, tgt_rows[...]) * inverse_norm(rows) * tgt_inv[...]
        weight = contract_columns(update, tgt_update[...]) / rank
        label = src_label_ref[:, mine].reshape(block, 1)
        same = jnp.logical_and(label == tgt_label_ref[...], label > 0)
        kernel = jnp.where(same, weight * jnp.exp((cosine - 1.0) / TEMPER), 0.0)
        denominator = jnp.sum(kernel, axis=1, keepdims=True)
        denominator = jnp.where(denominator > 0, denominator, 1.0)
        transport = (kernel / denominator).astype(jnp.bfloat16)
        images[mine, :] = jnp.dot(
            transport, tgt_rows[...], preferred_element_type=jnp.float32
        ).astype(jnp.bfloat16)
        departures.append(
            pltpu.make_async_copy(images.at[mine], out_hbm.at[mine], out_sem.at[part])
        )
        departures[-1].start()
    for copy in departures:
        copy.wait()


def owner_maps(near, far, sums, marginal, src_labels, tgt_labels, features):
    n_group, capacity, width = far.shape
    slots = n_group * capacity
    rank = width - features
    return pl.pallas_call(
        functools.partial(owner_kernel, features),
        out_shape=jax.ShapeDtypeStruct((slots, features), jnp.bfloat16),
        grid=(1,),
        in_specs=[
            pl.BlockSpec((n_group, None, capacity, width), lambda step: (0, 1, 0, 0)),
            pl.BlockSpec((n_group, None, capacity, width), lambda step: (0, 0, 0, 0)),
            whole(far.shape),
            whole(sums.shape),
            whole((1, rank)),
            whole((1, slots)),
            whole((1, 2 * slots)),
        ],
        out_specs=in_hbm(),
        scratch_shapes=[
            pltpu.VMEM((2 * rank, features), jnp.bfloat16),
            pltpu.VMEM((2 * slots, features), jnp.bfloat16),
            pltpu.VMEM((2 * slots, rank), jnp.bfloat16),
            pltpu.VMEM((1, 2 * slots), jnp.float32),
            pltpu.VMEM((slots, features), jnp.bfloat16),
            pltpu.SemaphoreType.DMA((slots // OWNER_BLOCK,)),
        ],
        compiler_params=pltpu.CompilerParams(vmem_limit_bytes=VMEM_BYTES),
        cost_estimate=pl.CostEstimate(
            flops=2 * slots * features * (3 * rank + 4 * slots),
            bytes_accessed=8 * slots * width,
            transcendentals=2 * slots * slots,
        ),
        name="owner_maps",
    )(
        near,
        near,
        far,
        sums,
        marginal[None, :],
        src_labels[None, :],
        tgt_labels[None, :],
    )


def labels_of(clusters, owner, capacity, spread):
    rows = clusters.shape[1]
    mine = clusters // spread == owner
    before = (jnp.arange(rows)[:, None] < jnp.arange(rows)[None, :]).astype(jnp.bfloat16)
    earlier = jnp.dot(mine.astype(jnp.bfloat16), before, preferred_element_type=jnp.float32)
    ranking = jnp.where(mine, earlier.astype(jnp.int32), -1)
    value = clusters - owner * spread + 1
    hit = ranking[:, None, :] == jnp.arange(capacity, dtype=jnp.int32)[None, :, None]
    return jnp.sum(jnp.where(hit, value[:, None, :], 0), axis=2).reshape(-1)


def exchange(rows):
    return lax.all_to_all(rows, GROUP, split_axis=0, concat_axis=0, tiled=True)


def per_device(
    src_points, tgt_points, src_factor, tgt_factor, inner_marginal, src_cluster, tgt_cluster
):
    n_src, n_rest = lax.axis_size("src"), lax.axis_size(REST)
    n_group = n_src * n_rest
    n_dev = 2 * n_group
    rows, features = src_points.shape
    rank = src_factor.shape[1]
    capacity = 2 * (2 * rows // n_dev)
    spread = 2 * CL_DEV
    me = lax.axis_index(ALL)
    my_half = lax.axis_index(HALF)
    owner = lax.axis_index(GROUP)

    near, raw = near_pack(
        tgt_cluster,
        src_cluster,
        tgt_points,
        tgt_factor,
        src_points,
        src_factor,
        n_group,
        capacity,
        spread,
    )
    near, me = lax.optimization_barrier((near, me))
    near = exchange(near)
    raw = lax.ppermute(raw, HALF, [(0, 1), (1, 0)])
    own, other = partial_sums(
        me,
        src_cluster,
        tgt_cluster,
        src_points,
        tgt_points,
        src_factor,
        tgt_factor,
        n_dev,
        2 * n_rest,
    )
    chain = Chain(own, other, n_src, 2 * n_rest)
    for digit in chain.plane[1:]:
        chain.scatter(digit)
    for digit in chain.along:
        chain.swap(digit)
    far = far_pack(raw, n_group, capacity, spread)
    chain.x, _ = lax.optimization_barrier((chain.x, far))
    far = exchange(far)
    for digit in reversed(chain.plane):
        chain.gather(digit)
    sums = chain.x.reshape(n_dev, -1, rank)

    kept = 2 * features // n_dev
    table = sums[:, kept : kept + 2].astype(jnp.int32).reshape(n_src, 2, n_rest, 2, rows)
    near_table = lax.dynamic_index_in_dim(table, my_half, 1, keepdims=False)
    far_table = lax.dynamic_index_in_dim(table, 1 - my_half, 1, keepdims=False)
    near_table = near_table.reshape(n_group, 2, rows)
    far_table = far_table.reshape(n_group, 2, rows)
    src_labels = labels_of(near_table[:, 0], owner, capacity, spread)
    near_labels = labels_of(near_table[:, 1], owner, capacity, spread)
    far_labels = labels_of(far_table[:, 1], owner, capacity, spread)

    near = near.reshape(n_group, 2, capacity, features + rank)
    far = far.reshape(n_group, capacity, features + rank)
    tgt_labels = jnp.concatenate([near_labels, far_labels])
    images = owner_maps(near, far, sums, inner_marginal, src_labels, tgt_labels, features)
    returned = exchange(images)

    src_update, tgt_update = updates(
        src_points, tgt_points, src_factor, tgt_factor, inner_marginal, sums
    )
    slot = slot_row(src_cluster[None, :], n_group, capacity, spread, 0)
    back = slot.reshape(rows, 1) == jnp.arange(n_group * capacity, dtype=jnp.int32)[None, :]
    back = lax.optimization_barrier(back.astype(jnp.bfloat16))
    mapped = jnp.dot(back, returned, preferred_element_type=jnp.float32).astype(jnp.bfloat16)
    return (src_update, tgt_update, mapped)


def solution(mesh):
    n_src, n_tgt = mesh.shape["src"], mesh.shape["tgt"]
    halves = Mesh(mesh.devices.reshape(n_src, 2, n_tgt // 2), ALL)
    rows = P(ALL, None)
    return jax.shard_map(
        per_device,
        mesh=halves,
        in_specs=(rows, rows, rows, rows, P(), P(ALL), P(ALL)),
        out_specs=(rows, rows, rows),
        check_vma=False,
    )
```

```python
import functools

import jax
import jax.numpy as jnp
from jax import lax
from jax.experimental import pallas as pl
from jax.experimental.pallas import tpu as pltpu
from jax.sharding import Mesh
from jax.sharding import PartitionSpec as P

CL_DEV = 2

GAMMA = 2.0
TEMPER = 0.03
EPS = 1e-06

HALF, REST = "half", "rest"
ALL = ("src", HALF, REST)
GROUP = ("src", REST)
VMEM_BYTES = 48 * 1024 * 1024
PACK_VMEM_BYTES = 62 * 1024 * 1024
TABLE_ROWS = 8
BLOCK_ROWS = 16
OWNER_BLOCK = 256
LABEL_ROWS = 16


def contract_rows(left, right):
    return lax.dot_general(
        left, right, (((0,), (0,)), ((), ())), preferred_element_type=jnp.float32
    )


def contract_columns(left, right):
    return lax.dot_general(
        left, right, (((1,), (1,)), ((), ())), preferred_element_type=jnp.float32
    )


def mirror_step(points, total_round, factor, inner_marginal):
    gradient = -contract_columns(points, total_round) / inner_marginal
    row_scale = jnp.max(jnp.abs(gradient), axis=1, keepdims=True) + EPS
    tilted = factor.astype(jnp.float32) * jnp.exp(-GAMMA * gradient / row_scale)
    mean = jnp.mean(tilted, axis=1, keepdims=True)
    mean = jnp.where(mean > 0, mean, 1.0)
    return (tilted / mean).astype(jnp.bfloat16)


def inverse_norm(rows):
    return lax.rsqrt(jnp.sum(jnp.square(rows.astype(jnp.float32)), axis=1, keepdims=True) + EPS)


def blocks_of(n_dev, chunk, rank, features):
    kept = (chunk - TABLE_ROWS) // BLOCK_ROWS
    wide = features // rank
    return [
        (b // kept, b % kept * BLOCK_ROWS, b // wide * BLOCK_ROWS, b % wide * rank)
        for b in range(n_dev * kept)
    ]


def totals_of(sums_ref, total, features):
    n_dev, chunk, rank = sums_ref.shape
    for c, row, first, column in blocks_of(n_dev, chunk, rank, features):
        total[pl.ds(first, BLOCK_ROWS), pl.ds(column, rank)] = sums_ref[c, pl.ds(row, BLOCK_ROWS), :]


def whole(shape):
    return pl.BlockSpec(shape, lambda *_: (0,) * len(shape))


def in_hbm():
    return pl.BlockSpec(memory_space=pltpu.HBM)


def slot_row(cluster, n_group, capacity, spread, first):
    rows = cluster.shape[1]
    owners = cluster // spread
    onehot = owners == lax.broadcasted_iota(jnp.int32, (n_group, rows), 0)
    before = lax.broadcasted_iota(jnp.int32, (rows, rows), 0) < lax.broadcasted_iota(
        jnp.int32, (rows, rows), 1
    )
    earlier = jnp.dot(
        onehot.astype(jnp.bfloat16), before.astype(jnp.bfloat16), preferred_element_type=jnp.float32
    )
    ranking = jnp.sum(jnp.where(onehot, earlier, 0.0), axis=0, keepdims=True).astype(jnp.int32)
    return owners * capacity + ranking + first


def contract_kernel(n_dev, n_tgt, me_ref, src_cluster_ref, tgt_cluster_ref, *refs):
    hbm, (own_ref, other_ref), held, parts, in_sem = refs[:4], refs[4:6], refs[6:10], refs[10], refs[11]
    arrivals = [pltpu.make_async_copy(a, b, in_sem.at[i]) for i, (a, b) in enumerate(zip(hbm, held))]
    for copy in arrivals:
        copy.start()
    tgt_points, tgt_factor, src_points, src_factor = held
    _, _, _, chunk, rank = parts.shape
    kept = chunk - TABLE_ROWS
    me = me_ref[0]
    mine = (me // n_tgt) % 2
    row = lax.broadcasted_iota(jnp.int32, (TABLE_ROWS, rank), 0)
    table = jnp.where(row == 0, src_cluster_ref[...], jnp.where(row == 1, tgt_cluster_ref[...], 0))
    parts[:, :, :, kept:, :] = jnp.zeros(parts.shape[:3] + (TABLE_ROWS, rank), jnp.float32)
    parts[me // (2 * n_tgt), mine, me % n_tgt, kept:, :] = table.astype(jnp.float32)
    features = tgt_points.shape[1]
    blocks = blocks_of(n_dev, chunk, rank, features)
    for which, (points, factor) in enumerate(((tgt_points, tgt_factor), (src_points, src_factor))):
        arrivals[2 * which].wait()
        arrivals[2 * which + 1].wait()
        total = contract_rows(factor[...], points[...])
        for c, row, first, column in blocks:
            first -= which * rank
            if 0 <= first < rank:
                place = (c // (2 * n_tgt), c // n_tgt % 2, c % n_tgt)
                parts[(*place, pl.ds(row, BLOCK_ROWS))] = total[
                    first : first + BLOCK_ROWS, column : column + rank
                ]
    for i in range(parts.shape[0]):
        own_ref[i] = parts[i, mine]
        other_ref[i] = parts[i, 1 - mine].astype(jnp.bfloat16)


def partial_sums(
    me, src_cluster, tgt_cluster, src_points, tgt_points, src_factor, tgt_factor, n_dev, n_tgt
):
    rows, features = src_points.shape
    rank = src_factor.shape[1]
    chunk = 2 * features // n_dev + TABLE_ROWS
    shape = (n_dev // (2 * n_tgt), n_tgt, chunk, rank)
    vmem = pl.BlockSpec(memory_space=pltpu.VMEM)
    return pl.pallas_call(
        functools.partial(contract_kernel, n_dev, n_tgt),
        out_shape=(
            jax.ShapeDtypeStruct(shape, jnp.float32),
            jax.ShapeDtypeStruct(shape, jnp.bfloat16),
        ),
        in_specs=[pl.BlockSpec(memory_space=pltpu.SMEM)] + [vmem] * 2 + [in_hbm()] * 4,
        out_specs=(vmem, vmem),
        scratch_shapes=[
            pltpu.VMEM((rows, features), jnp.bfloat16),
            pltpu.VMEM((rows, rank), jnp.bfloat16),
            pltpu.VMEM((rows, features), jnp.bfloat16),
            pltpu.VMEM((rows, rank), jnp.bfloat16),
            pltpu.VMEM((n_dev // (2 * n_tgt), 2, n_tgt, chunk, rank), jnp.float32),
            pltpu.SemaphoreType.DMA((4,)),
        ],
        compiler_params=pltpu.CompilerParams(vmem_limit_bytes=PACK_VMEM_BYTES),
        cost_estimate=pl.CostEstimate(
            flops=4 * rows * features * rank,
            bytes_accessed=4 * rows * (features + rank) + 4 * n_dev * chunk * rank,
            transcendentals=0,
        ),
        name="partial_sums",
    )(me[None], src_cluster[None, :], tgt_cluster[None, :], tgt_points, tgt_factor, src_points, src_factor)


def near_pack_kernel(
    n_group,
    capacity,
    spread,
    tgt_cluster_ref,
    src_cluster_ref,
    tgt_points_hbm,
    tgt_factor_hbm,
    src_points_hbm,
    src_factor_hbm,
    packed_hbm,
    raw_hbm,
    tgt_points,
    tgt_factor,
    src_points,
    src_factor,
    packed,
    labels,
    in_sem,
    out_sem,
    raw_sem,
):
    hbm = (tgt_points_hbm, tgt_factor_hbm, src_points_hbm, src_factor_hbm)
    held = (tgt_points, tgt_factor, src_points, src_factor)
    arrivals = [pltpu.make_async_copy(a, b, in_sem.at[i]) for i, (a, b) in enumerate(zip(hbm, held))]
    for copy in arrivals:
        copy.start()
    rows, features = tgt_points.shape
    width = packed.shape[1]
    first = lax.broadcasted_iota(jnp.int32, (LABEL_ROWS, rows), 0) == 0
    labels[...] = jnp.zeros(labels.shape, jnp.bfloat16)
    labels[:, :rows] = jnp.where(first, tgt_cluster_ref[...], 0).astype(jnp.float32).astype(jnp.bfloat16)
    tgt_slot = slot_row(tgt_cluster_ref[...], n_group, 2 * capacity, spread, 0)
    src_slot = slot_row(src_cluster_ref[...], n_group, 2 * capacity, spread, capacity)
    for copy in arrivals:
        copy.wait()
    departures = [
        pltpu.make_async_copy(
            tgt_points, raw_hbm.at[pl.ds(0, rows), pl.ds(0, features)], raw_sem.at[0]
        ),
        pltpu.make_async_copy(
            tgt_factor, raw_hbm.at[pl.ds(0, rows), pl.ds(features, width - features)], raw_sem.at[1]
        ),
        pltpu.make_async_copy(labels, raw_hbm.at[pl.ds(rows, LABEL_ROWS)], raw_sem.at[2]),
    ]
    for copy in departures:
        copy.start()
    block = 256
    for part in range(packed.shape[0] // block):
        mine = pl.ds(part * block, block)
        index = lax.broadcasted_iota(jnp.int32, (block, rows), 0) + part * block
        tgt_place = (index == tgt_slot).astype(jnp.bfloat16)
        src_place = (index == src_slot).astype(jnp.bfloat16)
        packed[mine, :features] = (
            jnp.dot(tgt_place, tgt_points[...], preferred_element_type=jnp.float32)
            + jnp.dot(src_place, src_points[...], preferred_element_type=jnp.float32)
        ).astype(jnp.bfloat16)
        packed[mine, features:] = (
            jnp.dot(tgt_place, tgt_factor[...], preferred_element_type=jnp.float32)
            + jnp.dot(src_place, src_factor[...], preferred_element_type=jnp.float32)
        ).astype(jnp.bfloat16)
        departures.append(
            pltpu.make_async_copy(packed.at[mine], packed_hbm.at[mine], out_sem.at[part])
        )
        departures[-1].start()
    for copy in departures:
        copy.wait()


def near_pack(
    tgt_cluster, src_cluster, tgt_points, tgt_factor, src_points, src_factor, n_group, capacity, spread
):
    rows, features = tgt_points.shape
    rank = tgt_factor.shape[1]
    slots = 2 * n_group * capacity
    vmem = pl.BlockSpec(memory_space=pltpu.VMEM)
    held = [pltpu.VMEM((rows, features), jnp.bfloat16), pltpu.VMEM((rows, rank), jnp.bfloat16)]
    return pl.pallas_call(
        functools.partial(near_pack_kernel, n_group, capacity, spread),
        out_shape=(
            jax.ShapeDtypeStruct((slots, features + rank), jnp.bfloat16),
            jax.ShapeDtypeStruct((rows + LABEL_ROWS, features + rank), jnp.bfloat16),
        ),
        in_specs=[vmem] * 2 + [in_hbm()] * 4,
        out_specs=(in_hbm(), in_hbm()),
        scratch_shapes=held * 2
        + [
            pltpu.VMEM((slots, features + rank), jnp.bfloat16),
            pltpu.VMEM((LABEL_ROWS, features + rank), jnp.bfloat16),
            pltpu.SemaphoreType.DMA((4,)),
            pltpu.SemaphoreType.DMA((slots // 256,)),
            pltpu.SemaphoreType.DMA((3,)),
        ],
        compiler_params=pltpu.CompilerParams(vmem_limit_bytes=PACK_VMEM_BYTES),
        cost_estimate=pl.CostEstimate(
            flops=4 * slots * rows * (features + rank),
            bytes_accessed=2 * (slots + 3 * rows) * (features + rank),
            transcendentals=0,
        ),
        name="near_pack",
    )(tgt_cluster[None, :], src_cluster[None, :], tgt_points, tgt_factor, src_points, src_factor)


def far_pack_kernel(n_group, capacity, spread, raw_hbm, packed_hbm, raw, packed, in_sem, out_sem):
    rows = raw.shape[0] - LABEL_ROWS
    labels_in = pltpu.make_async_copy(
        raw_hbm.at[pl.ds(rows, LABEL_ROWS)], raw.at[pl.ds(rows, LABEL_ROWS)], in_sem.at[0]
    )
    rows_in = pltpu.make_async_copy(
        raw_hbm.at[pl.ds(0, rows)], raw.at[pl.ds(0, rows)], in_sem.at[1]
    )
    labels_in.start()
    rows_in.start()
    labels_in.wait()
    labels = raw[rows:, :rows].astype(jnp.float32)[:1].astype(jnp.int32)
    slot = slot_row(labels, n_group, capacity, spread, 0)
    rows_in.wait()
    block = 256
    departures = []
    for part in range(packed.shape[0] // block):
        mine = pl.ds(part * block, block)
        index = lax.broadcasted_iota(jnp.int32, (block, rows), 0) + part * block
        place = (index == slot).astype(jnp.bfloat16)
        packed[mine, :] = jnp.dot(
            place, raw[:rows, :], preferred_element_type=jnp.float32
        ).astype(jnp.bfloat16)
        departures.append(
            pltpu.make_async_copy(packed.at[mine], packed_hbm.at[mine], out_sem.at[part])
        )
        departures[-1].start()
    for copy in departures:
        copy.wait()


def far_pack(raw, n_group, capacity, spread):
    rows, width = raw.shape
    slots = n_group * capacity
    return pl.pallas_call(
        functools.partial(far_pack_kernel, n_group, capacity, spread),
        out_shape=jax.ShapeDtypeStruct((slots, width), jnp.bfloat16),
        in_specs=[in_hbm()],
        out_specs=in_hbm(),
        scratch_shapes=[
            pltpu.VMEM((rows, width), jnp.bfloat16),
            pltpu.VMEM((slots, width), jnp.bfloat16),
            pltpu.SemaphoreType.DMA((2,)),
            pltpu.SemaphoreType.DMA((slots // 256,)),
        ],
        compiler_params=pltpu.CompilerParams(vmem_limit_bytes=PACK_VMEM_BYTES),
        cost_estimate=pl.CostEstimate(
            flops=2 * slots * rows * width,
            bytes_accessed=2 * (slots + rows) * width,
            transcendentals=0,
        ),
        name="far_pack",
    )(raw)


def digits_of(size, stride):
    bits = size.bit_length() - 1
    found = []
    while bits:
        take = 1 if bits % 2 else 2
        found.append((stride, 1 << take))
        stride <<= take
        bits -= take
    return found


class Chain:
    def __init__(self, own, other, n_src, n_tgt):
        self.n_dev = n_src * n_tgt
        first = (n_tgt, 2)
        src, tgt = digits_of(n_src // 2, 2 * n_tgt), digits_of(n_tgt, 1)
        self.plane, self.along = [first] + src, tgt
        self.dims = src[::-1] + [first] + tgt[::-1]
        self.left = [d for d in self.dims if d != first]
        x = own + self.sent(other, n_tgt).astype(jnp.float32)
        self.x = x.reshape(tuple(radix for _, radix in self.left) + own.shape[2:])

    def sent(self, array, mask):
        return lax.ppermute(array, ALL, [(i, i ^ mask) for i in range(self.n_dev)])

    def scatter(self, digit):
        stride, radix = digit
        dim = self.left.index(digit)
        mine = (lax.axis_index(ALL) // stride) % radix
        total = lax.dynamic_index_in_dim(self.x, mine, dim, keepdims=False)
        for j in range(1, radix):
            piece = lax.dynamic_index_in_dim(self.x, mine ^ j, dim, keepdims=False)
            total = total + self.sent(piece.astype(jnp.bfloat16), j * stride).astype(jnp.float32)
        self.x = total
        self.left.remove(digit)

    def swap(self, digit):
        stride, radix = digit
        piece = self.x.astype(jnp.bfloat16)
        for j in range(1, radix):
            self.x = self.x + self.sent(piece, j * stride).astype(jnp.float32)

    def gather(self, digit):
        stride, radix = digit
        mine = (lax.axis_index(ALL) // stride) % radix
        x = self.x.astype(jnp.bfloat16)
        got = [x] + [self.sent(x, j * stride) for j in range(1, radix)]
        self.left = [d for d in self.dims if d in self.left or d == digit]
        self.x = jnp.stack(
            [lax.select_n(mine ^ d, *got) if radix > 2 else jnp.where(mine == d, *got) for d in range(radix)],
            axis=self.left.index(digit),
        )


def update_kernel(
    src_points_ref,
    tgt_points_ref,
    src_factor_ref,
    tgt_factor_ref,
    marginal_ref,
    sums_ref,
    src_ref,
    tgt_ref,
    total,
):
    totals_of(sums_ref, total, src_points_ref.shape[1])
    rank = src_ref.shape[1]
    marginal = marginal_ref[...]
    src_ref[...] = mirror_step(src_points_ref[...], total[:rank], src_factor_ref[...], marginal)
    tgt_ref[...] = mirror_step(tgt_points_ref[...], total[rank:], tgt_factor_ref[...], marginal)


def updates(src_points, tgt_points, src_factor, tgt_factor, marginal, sums):
    rows, features = src_points.shape
    rank = src_factor.shape[1]
    shape = jax.ShapeDtypeStruct(src_factor.shape, jnp.bfloat16)
    return pl.pallas_call(
        update_kernel,
        out_shape=(shape, shape),
        scratch_shapes=[pltpu.VMEM((2 * rank, features), jnp.bfloat16)],
        compiler_params=pltpu.CompilerParams(vmem_limit_bytes=VMEM_BYTES),
        cost_estimate=pl.CostEstimate(
            flops=4 * rows * features * rank,
            bytes_accessed=4 * rows * (features + 2 * rank),
            transcendentals=2 * rows * rank,
        ),
        name="mirror_updates",
    )(src_points, tgt_points, src_factor, tgt_factor, marginal[None, :], sums)


def seen_block(ref, part, block):
    piece = block // ref.shape[1]
    return ref[pl.ds(part * piece, piece)].reshape(block, ref.shape[2])


def owner_kernel(
    features,
    src_ref,
    near_ref,
    far_ref,
    sums_ref,
    marginal_ref,
    src_label_ref,
    tgt_label_ref,
    out_hbm,
    total,
    tgt_rows,
    tgt_update,
    tgt_inv,
    images,
    out_sem,
):
    totals_of(sums_ref, total, features)
    slots = images.shape[0]
    rank = tgt_update.shape[1]
    marginal = marginal_ref[...]
    block = OWNER_BLOCK
    for which, ref in enumerate((near_ref, far_ref)):
        for part in range(slots // block):
            mine = pl.ds(which * slots + part * block, block)
            both = seen_block(ref, part, block)
            rows = both[:, :features]
            tgt_rows[mine, :] = rows
            tgt_update[mine, :] = mirror_step(rows, total[rank:], both[:, features:], marginal)
            tgt_inv[:, mine] = inverse_norm(rows).reshape(1, block)

    departures = []
    for part in range(slots // block):
        mine = pl.ds(part * block, block)
        both = seen_block(src_ref, part, block)
        rows = both[:, :features]
        update = mirror_step(rows, total[:rank], both[:, features:], marginal)
        cosine = contract_columns(rows, tgt_rows[...]) * inverse_norm(rows) * tgt_inv[...]
        weight = contract_columns(update, tgt_update[...]) / rank
        label = src_label_ref[:, mine].reshape(block, 1)
        same = jnp.logical_and(label == tgt_label_ref[...], label > 0)
        kernel = jnp.where(same, weight * jnp.exp((cosine - 1.0) / TEMPER), 0.0)
        denominator = jnp.sum(kernel, axis=1, keepdims=True)
        denominator = jnp.where(denominator > 0, denominator, 1.0)
        transport = (kernel / denominator).astype(jnp.bfloat16)
        images[mine, :] = jnp.dot(
            transport, tgt_rows[...], preferred_element_type=jnp.float32
        ).astype(jnp.bfloat16)
        departures.append(
            pltpu.make_async_copy(images.at[mine], out_hbm.at[mine], out_sem.at[part])
        )
        departures[-1].start()
    for copy in departures:
        copy.wait()


def owner_maps(near, far, sums, marginal, src_labels, tgt_labels, features):
    n_group, capacity, width = far.shape
    slots = n_group * capacity
    rank = width - features
    return pl.pallas_call(
        functools.partial(owner_kernel, features),
        out_shape=jax.ShapeDtypeStruct((slots, features), jnp.bfloat16),
        grid=(1,),
        in_specs=[
            pl.BlockSpec((n_group, None, capacity, width), lambda step: (0, 1, 0, 0)),
            pl.BlockSpec((n_group, None, capacity, width), lambda step: (0, 0, 0, 0)),
            whole(far.shape),
            whole(sums.shape),
            whole((1, rank)),
            whole((1, slots)),
            whole((1, 2 * slots)),
        ],
        out_specs=in_hbm(),
        scratch_shapes=[
            pltpu.VMEM((2 * rank, features), jnp.bfloat16),
            pltpu.VMEM((2 * slots, features), jnp.bfloat16),
            pltpu.VMEM((2 * slots, rank), jnp.bfloat16),
            pltpu.VMEM((1, 2 * slots), jnp.float32),
            pltpu.VMEM((slots, features), jnp.bfloat16),
            pltpu.SemaphoreType.DMA((slots // OWNER_BLOCK,)),
        ],
        compiler_params=pltpu.CompilerParams(vmem_limit_bytes=VMEM_BYTES),
        cost_estimate=pl.CostEstimate(
            flops=2 * slots * features * (3 * rank + 4 * slots),
            bytes_accessed=8 * slots * width,
            transcendentals=2 * slots * slots,
        ),
        name="owner_maps",
    )(
        near,
        near,
        far,
        sums,
        marginal[None, :],
        src_labels[None, :],
        tgt_labels[None, :],
    )


def labels_of(clusters, owner, capacity, spread):
    rows = clusters.shape[1]
    mine = clusters // spread == owner
    before = (jnp.arange(rows)[:, None] < jnp.arange(rows)[None, :]).astype(jnp.bfloat16)
    earlier = jnp.dot(mine.astype(jnp.bfloat16), before, preferred_element_type=jnp.float32)
    ranking = jnp.where(mine, earlier.astype(jnp.int32), -1)
    value = clusters - owner * spread + 1
    hit = ranking[:, None, :] == jnp.arange(capacity, dtype=jnp.int32)[None, :, None]
    return jnp.sum(jnp.where(hit, value[:, None, :], 0), axis=2).reshape(-1)


def exchange(rows):
    return lax.all_to_all(rows, GROUP, split_axis=0, concat_axis=0, tiled=True)


def per_device(
    src_points, tgt_points, src_factor, tgt_factor, inner_marginal, src_cluster, tgt_cluster
):
    n_src, n_rest = lax.axis_size("src"), lax.axis_size(REST)
    n_group = n_src * n_rest
    n_dev = 2 * n_group
    rows, features = src_points.shape
    rank = src_factor.shape[1]
    capacity = 2 * (2 * rows // n_dev)
    spread = 2 * CL_DEV
    me = lax.axis_index(ALL)
    my_half = lax.axis_index(HALF)
    owner = lax.axis_index(GROUP)

    near, raw = near_pack(
        tgt_cluster,
        src_cluster,
        tgt_points,
        tgt_factor,
        src_points,
        src_factor,
        n_group,
        capacity,
        spread,
    )
    near, me = lax.optimization_barrier((near, me))
    near = exchange(near)
    raw = lax.ppermute(raw, HALF, [(0, 1), (1, 0)])
    own, other = partial_sums(
        me,
        src_cluster,
        tgt_cluster,
        src_points,
        tgt_points,
        src_factor,
        tgt_factor,
        n_dev,
        2 * n_rest,
    )
    chain = Chain(own, other, n_src, 2 * n_rest)
    for digit in chain.plane[1:]:
        chain.scatter(digit)
    for digit in chain.along:
        chain.swap(digit)
    far = far_pack(raw, n_group, capacity, spread)
    chain.x, _ = lax.optimization_barrier((chain.x, far))
    far, near = lax.optimization_barrier((far, near))
    far = exchange(far)
    for digit in reversed(chain.plane):
        chain.gather(digit)
    sums = chain.x.reshape(n_dev, -1, rank)

    kept = 2 * features // n_dev
    table = sums[:, kept : kept + 2].astype(jnp.int32).reshape(n_src, 2, n_rest, 2, rows)
    near_table = lax.dynamic_index_in_dim(table, my_half, 1, keepdims=False)
    far_table = lax.dynamic_index_in_dim(table, 1 - my_half, 1, keepdims=False)
    near_table = near_table.reshape(n_group, 2, rows)
    far_table = far_table.reshape(n_group, 2, rows)
    src_labels = labels_of(near_table[:, 0], owner, capacity, spread)
    near_labels = labels_of(near_table[:, 1], owner, capacity, spread)
    far_labels = labels_of(far_table[:, 1], owner, capacity, spread)

    near = near.reshape(n_group, 2, capacity, features + rank)
    far = far.reshape(n_group, capacity, features + rank)
    tgt_labels = jnp.concatenate([near_labels, far_labels])
    images = owner_maps(near, far, sums, inner_marginal, src_labels, tgt_labels, features)
    returned = exchange(images)

    src_update, tgt_update = updates(
        src_points, tgt_points, src_factor, tgt_factor, inner_marginal, sums
    )
    slot = slot_row(src_cluster[None, :], n_group, capacity, spread, 0)
    back = slot.reshape(rows, 1) == jnp.arange(n_group * capacity, dtype=jnp.int32)[None, :]
    back = lax.optimization_barrier(back.astype(jnp.bfloat16))
    mapped = jnp.dot(back, returned, preferred_element_type=jnp.float32).astype(jnp.bfloat16)
    return (src_update, tgt_update, mapped)


def solution(mesh):
    n_src, n_tgt = mesh.shape["src"], mesh.shape["tgt"]
    halves = Mesh(mesh.devices.reshape(n_src, 2, n_tgt // 2), ALL)
    rows = P(ALL, None)
    return jax.shard_map(
        per_device,
        mesh=halves,
        in_specs=(rows, rows, rows, rows, P(), P(ALL), P(ALL)),
        out_specs=(rows, rows, rows),
        check_vma=False,
    )
```

```python
import functools

import jax
import jax.numpy as jnp
from jax import lax
from jax.experimental import pallas as pl
from jax.experimental.pallas import tpu as pltpu
from jax.sharding import Mesh
from jax.sharding import PartitionSpec as P

CL_DEV = 2

GAMMA = 2.0
TEMPER = 0.03
EPS = 1e-06

HALF, REST = "half", "rest"
ALL = ("src", HALF, REST)
GROUP = ("src", REST)
VMEM_BYTES = 48 * 1024 * 1024
PACK_VMEM_BYTES = 62 * 1024 * 1024
TABLE_ROWS = 8
BLOCK_ROWS = 16
OWNER_BLOCK = 256
LABEL_ROWS = 16


def contract_rows(left, right):
    return lax.dot_general(
        left, right, (((0,), (0,)), ((), ())), preferred_element_type=jnp.float32
    )


def contract_columns(left, right):
    return lax.dot_general(
        left, right, (((1,), (1,)), ((), ())), preferred_element_type=jnp.float32
    )


def mirror_step(points, total_round, factor, inner_marginal):
    gradient = -contract_columns(points, total_round) / inner_marginal
    row_scale = jnp.max(jnp.abs(gradient), axis=1, keepdims=True) + EPS
    tilted = factor.astype(jnp.float32) * jnp.exp(-GAMMA * gradient / row_scale)
    mean = jnp.mean(tilted, axis=1, keepdims=True)
    mean = jnp.where(mean > 0, mean, 1.0)
    return (tilted / mean).astype(jnp.bfloat16)


def inverse_norm(rows):
    return lax.rsqrt(jnp.sum(jnp.square(rows.astype(jnp.float32)), axis=1, keepdims=True) + EPS)


def blocks_of(n_dev, chunk, rank, features):
    kept = (chunk - TABLE_ROWS) // BLOCK_ROWS
    wide = features // rank
    return [
        (b // kept, b % kept * BLOCK_ROWS, b // wide * BLOCK_ROWS, b % wide * rank)
        for b in range(n_dev * kept)
    ]


def totals_of(sums_ref, total, features):
    n_dev, chunk, rank = sums_ref.shape
    for c, row, first, column in blocks_of(n_dev, chunk, rank, features):
        total[pl.ds(first, BLOCK_ROWS), pl.ds(column, rank)] = sums_ref[c, pl.ds(row, BLOCK_ROWS), :]


def whole(shape):
    return pl.BlockSpec(shape, lambda *_: (0,) * len(shape))


def in_hbm():
    return pl.BlockSpec(memory_space=pltpu.HBM)


def slot_row(cluster, n_group, capacity, spread, first):
    rows = cluster.shape[1]
    owners = cluster // spread
    onehot = owners == lax.broadcasted_iota(jnp.int32, (n_group, rows), 0)
    before = lax.broadcasted_iota(jnp.int32, (rows, rows), 0) < lax.broadcasted_iota(
        jnp.int32, (rows, rows), 1
    )
    earlier = jnp.dot(
        onehot.astype(jnp.bfloat16), before.astype(jnp.bfloat16), preferred_element_type=jnp.float32
    )
    ranking = jnp.sum(jnp.where(onehot, earlier, 0.0), axis=0, keepdims=True).astype(jnp.int32)
    return owners * capacity + ranking + first


def contract_kernel(n_dev, n_tgt, me_ref, src_cluster_ref, tgt_cluster_ref, *refs):
    hbm, (own_ref, other_ref), held, parts, in_sem = refs[:4], refs[4:6], refs[6:10], refs[10], refs[11]
    arrivals = [pltpu.make_async_copy(a, b, in_sem.at[i]) for i, (a, b) in enumerate(zip(hbm, held))]
    for copy in arrivals:
        copy.start()
    tgt_points, tgt_factor, src_points, src_factor = held
    _, _, _, chunk, rank = parts.shape
    kept = chunk - TABLE_ROWS
    me = me_ref[0]
    mine = (me // n_tgt) % 2
    row = lax.broadcasted_iota(jnp.int32, (TABLE_ROWS, rank), 0)
    table = jnp.where(row == 0, src_cluster_ref[...], jnp.where(row == 1, tgt_cluster_ref[...], 0))
    parts[:, :, :, kept:, :] = jnp.zeros(parts.shape[:3] + (TABLE_ROWS, rank), jnp.float32)
    parts[me // (2 * n_tgt), mine, me % n_tgt, kept:, :] = table.astype(jnp.float32)
    features = tgt_points.shape[1]
    blocks = blocks_of(n_dev, chunk, rank, features)
    for which, (points, factor) in enumerate(((tgt_points, tgt_factor), (src_points, src_factor))):
        arrivals[2 * which].wait()
        arrivals[2 * which + 1].wait()
        total = contract_rows(factor[...], points[...])
        for c, row, first, column in blocks:
            first -= which * rank
            if 0 <= first < rank:
                place = (c // (2 * n_tgt), c // n_tgt % 2, c % n_tgt)
                parts[(*place, pl.ds(row, BLOCK_ROWS))] = total[
                    first : first + BLOCK_ROWS, column : column + rank
                ]
    for i in range(parts.shape[0]):
        own_ref[i] = parts[i, mine]
        other_ref[i] = parts[i, 1 - mine].astype(jnp.bfloat16)


def partial_sums(
    me, src_cluster, tgt_cluster, src_points, tgt_points, src_factor, tgt_factor, n_dev, n_tgt
):
    rows, features = src_points.shape
    rank = src_factor.shape[1]
    chunk = 2 * features // n_dev + TABLE_ROWS
    shape = (n_dev // (2 * n_tgt), n_tgt, chunk, rank)
    vmem = pl.BlockSpec(memory_space=pltpu.VMEM)
    return pl.pallas_call(
        functools.partial(contract_kernel, n_dev, n_tgt),
        out_shape=(
            jax.ShapeDtypeStruct(shape, jnp.float32),
            jax.ShapeDtypeStruct(shape, jnp.bfloat16),
        ),
        in_specs=[pl.BlockSpec(memory_space=pltpu.SMEM)] + [vmem] * 2 + [in_hbm()] * 4,
        out_specs=(vmem, vmem),
        scratch_shapes=[
            pltpu.VMEM((rows, features), jnp.bfloat16),
            pltpu.VMEM((rows, rank), jnp.bfloat16),
            pltpu.VMEM((rows, features), jnp.bfloat16),
            pltpu.VMEM((rows, rank), jnp.bfloat16),
            pltpu.VMEM((n_dev // (2 * n_tgt), 2, n_tgt, chunk, rank), jnp.float32),
            pltpu.SemaphoreType.DMA((4,)),
        ],
        compiler_params=pltpu.CompilerParams(vmem_limit_bytes=PACK_VMEM_BYTES),
        cost_estimate=pl.CostEstimate(
            flops=4 * rows * features * rank,
            bytes_accessed=4 * rows * (features + rank) + 4 * n_dev * chunk * rank,
            transcendentals=0,
        ),
        name="partial_sums",
    )(me[None], src_cluster[None, :], tgt_cluster[None, :], tgt_points, tgt_factor, src_points, src_factor)


def place_rows(kinds, packed, packed_hbm, out_sem):
    block = 256
    departures = []
    for part in range(packed.shape[0] // block):
        mine = pl.ds(part * block, block)
        total = None
        for slot, held in kinds:
            index = lax.broadcasted_iota(jnp.int32, (block, slot.shape[1]), 0) + part * block
            place = (index == slot).astype(jnp.bfloat16)
            rows = [
                jnp.dot(place, array, preferred_element_type=jnp.float32) for array in held
            ]
            total = rows if total is None else [a + b for a, b in zip(total, rows)]
        column = 0
        for rows in total:
            packed[mine, column : column + rows.shape[1]] = rows.astype(jnp.bfloat16)
            column += rows.shape[1]
        departures.append(
            pltpu.make_async_copy(packed.at[mine], packed_hbm.at[mine], out_sem.at[part])
        )
        departures[-1].start()
    return departures


def near_pack_kernel(
    n_group,
    capacity,
    spread,
    cluster_ref,
    points_hbm,
    factor_hbm,
    packed_hbm,
    raw_hbm,
    points,
    factor,
    packed,
    labels,
    in_sem,
    out_sem,
    raw_sem,
):
    arrivals = [
        pltpu.make_async_copy(points_hbm, points, in_sem.at[0]),
        pltpu.make_async_copy(factor_hbm, factor, in_sem.at[1]),
    ]
    for copy in arrivals:
        copy.start()
    rows, features = points.shape
    rank = factor.shape[1]
    first = lax.broadcasted_iota(jnp.int32, (LABEL_ROWS, rows), 0) == 0
    labels[...] = jnp.zeros(labels.shape, jnp.bfloat16)
    labels[:, :rows] = jnp.where(first, cluster_ref[...], 0).astype(jnp.float32).astype(jnp.bfloat16)
    slot = slot_row(cluster_ref[...], n_group, capacity, spread, 0)
    for copy in arrivals:
        copy.wait()
    departures = [
        pltpu.make_async_copy(
            points, raw_hbm.at[pl.ds(0, rows), pl.ds(0, features)], raw_sem.at[0]
        ),
        pltpu.make_async_copy(
            factor, raw_hbm.at[pl.ds(0, rows), pl.ds(features, rank)], raw_sem.at[1]
        ),
        pltpu.make_async_copy(labels, raw_hbm.at[pl.ds(rows, LABEL_ROWS)], raw_sem.at[2]),
    ]
    for copy in departures:
        copy.start()
    departures += place_rows([(slot, (points[...], factor[...]))], packed, packed_hbm, out_sem)
    for copy in departures:
        copy.wait()


def near_pack(cluster, points, factor, n_group, capacity, spread):
    rows, features = points.shape
    rank = factor.shape[1]
    width = features + rank
    slots = n_group * capacity
    return pl.pallas_call(
        functools.partial(near_pack_kernel, n_group, capacity, spread),
        out_shape=(
            jax.ShapeDtypeStruct((slots, width), jnp.bfloat16),
            jax.ShapeDtypeStruct((rows + LABEL_ROWS, width), jnp.bfloat16),
        ),
        in_specs=[pl.BlockSpec(memory_space=pltpu.VMEM), in_hbm(), in_hbm()],
        out_specs=(in_hbm(), in_hbm()),
        scratch_shapes=[
            pltpu.VMEM((rows, features), jnp.bfloat16),
            pltpu.VMEM((rows, rank), jnp.bfloat16),
            pltpu.VMEM((slots, width), jnp.bfloat16),
            pltpu.VMEM((LABEL_ROWS, width), jnp.bfloat16),
            pltpu.SemaphoreType.DMA((2,)),
            pltpu.SemaphoreType.DMA((slots // 256,)),
            pltpu.SemaphoreType.DMA((3,)),
        ],
        compiler_params=pltpu.CompilerParams(vmem_limit_bytes=PACK_VMEM_BYTES),
        cost_estimate=pl.CostEstimate(
            flops=2 * slots * rows * width,
            bytes_accessed=2 * (slots + 2 * rows) * width,
            transcendentals=0,
        ),
        name="near_pack",
    )(cluster[None, :], points, factor)


def far_pack_kernel(
    n_group,
    capacity,
    spread,
    cluster_ref,
    raw_hbm,
    points_hbm,
    factor_hbm,
    packed_hbm,
    raw,
    points,
    factor,
    packed,
    in_sem,
    out_sem,
):
    rows, features = points.shape
    arrivals = [
        pltpu.make_async_copy(raw_hbm, raw, in_sem.at[0]),
        pltpu.make_async_copy(points_hbm, points, in_sem.at[1]),
        pltpu.make_async_copy(factor_hbm, factor, in_sem.at[2]),
    ]
    for copy in arrivals:
        copy.start()
    src_slot = slot_row(cluster_ref[...], n_group, 2 * capacity, spread, capacity)
    arrivals[0].wait()
    labels = raw[rows:, :rows].astype(jnp.float32)[:1].astype(jnp.int32)
    tgt_slot = slot_row(labels, n_group, 2 * capacity, spread, 0)
    arrivals[1].wait()
    arrivals[2].wait()
    kinds = [
        (tgt_slot, (raw[:rows, :features], raw[:rows, features:])),
        (src_slot, (points[...], factor[...])),
    ]
    for copy in place_rows(kinds, packed, packed_hbm, out_sem):
        copy.wait()


def far_pack(raw, cluster, points, factor, n_group, capacity, spread):
    rows, features = points.shape
    width = raw.shape[1]
    slots = 2 * n_group * capacity
    return pl.pallas_call(
        functools.partial(far_pack_kernel, n_group, capacity, spread),
        out_shape=jax.ShapeDtypeStruct((slots, width), jnp.bfloat16),
        in_specs=[pl.BlockSpec(memory_space=pltpu.VMEM)] + [in_hbm()] * 3,
        out_specs=in_hbm(),
        scratch_shapes=[
            pltpu.VMEM(raw.shape, jnp.bfloat16),
            pltpu.VMEM(points.shape, jnp.bfloat16),
            pltpu.VMEM(factor.shape, jnp.bfloat16),
            pltpu.VMEM((slots, width), jnp.bfloat16),
            pltpu.SemaphoreType.DMA((3,)),
            pltpu.SemaphoreType.DMA((slots // 256,)),
        ],
        compiler_params=pltpu.CompilerParams(vmem_limit_bytes=PACK_VMEM_BYTES),
        cost_estimate=pl.CostEstimate(
            flops=4 * slots * rows * width,
            bytes_accessed=2 * (slots + 2 * rows) * width,
            transcendentals=0,
        ),
        name="far_pack",
    )(cluster[None, :], raw, points, factor)


def digits_of(size, stride):
    bits = size.bit_length() - 1
    found = []
    while bits:
        take = 1 if bits % 2 else 2
        found.append((stride, 1 << take))
        stride <<= take
        bits -= take
    return found


class Chain:
    def __init__(self, own, other, n_src, n_tgt):
        self.n_dev = n_src * n_tgt
        first = (n_tgt, 2)
        src, tgt = digits_of(n_src // 2, 2 * n_tgt), digits_of(n_tgt, 1)
        self.plane, self.along = [first] + src, tgt
        self.dims = src[::-1] + [first] + tgt[::-1]
        self.left = [d for d in self.dims if d != first]
        x = own + self.sent(other, n_tgt).astype(jnp.float32)
        self.x = x.reshape(tuple(radix for _, radix in self.left) + own.shape[2:])

    def sent(self, array, mask):
        return lax.ppermute(array, ALL, [(i, i ^ mask) for i in range(self.n_dev)])

    def scatter(self, digit):
        stride, radix = digit
        dim = self.left.index(digit)
        mine = (lax.axis_index(ALL) // stride) % radix
        total = lax.dynamic_index_in_dim(self.x, mine, dim, keepdims=False)
        for j in range(1, radix):
            piece = lax.dynamic_index_in_dim(self.x, mine ^ j, dim, keepdims=False)
            total = total + self.sent(piece.astype(jnp.bfloat16), j * stride).astype(jnp.float32)
        self.x = total
        self.left.remove(digit)

    def swap(self, digit):
        stride, radix = digit
        piece = self.x.astype(jnp.bfloat16)
        for j in range(1, radix):
            self.x = self.x + self.sent(piece, j * stride).astype(jnp.float32)

    def gather(self, digit):
        stride, radix = digit
        mine = (lax.axis_index(ALL) // stride) % radix
        x = self.x.astype(jnp.bfloat16)
        got = [x] + [self.sent(x, j * stride) for j in range(1, radix)]
        self.left = [d for d in self.dims if d in self.left or d == digit]
        self.x = jnp.stack(
            [lax.select_n(mine ^ d, *got) if radix > 2 else jnp.where(mine == d, *got) for d in range(radix)],
            axis=self.left.index(digit),
        )


def update_kernel(
    src_points_ref,
    tgt_points_ref,
    src_factor_ref,
    tgt_factor_ref,
    marginal_ref,
    sums_ref,
    src_ref,
    tgt_ref,
    total,
):
    totals_of(sums_ref, total, src_points_ref.shape[1])
    rank = src_ref.shape[1]
    marginal = marginal_ref[...]
    src_ref[...] = mirror_step(src_points_ref[...], total[:rank], src_factor_ref[...], marginal)
    tgt_ref[...] = mirror_step(tgt_points_ref[...], total[rank:], tgt_factor_ref[...], marginal)


def updates(src_points, tgt_points, src_factor, tgt_factor, marginal, sums):
    rows, features = src_points.shape
    rank = src_factor.shape[1]
    shape = jax.ShapeDtypeStruct(src_factor.shape, jnp.bfloat16)
    return pl.pallas_call(
        update_kernel,
        out_shape=(shape, shape),
        scratch_shapes=[pltpu.VMEM((2 * rank, features), jnp.bfloat16)],
        compiler_params=pltpu.CompilerParams(vmem_limit_bytes=VMEM_BYTES),
        cost_estimate=pl.CostEstimate(
            flops=4 * rows * features * rank,
            bytes_accessed=4 * rows * (features + 2 * rank),
            transcendentals=2 * rows * rank,
        ),
        name="mirror_updates",
    )(src_points, tgt_points, src_factor, tgt_factor, marginal[None, :], sums)


def seen_block(ref, part, block):
    piece = block // ref.shape[1]
    return ref[pl.ds(part * piece, piece)].reshape(block, ref.shape[2])


def owner_kernel(
    features,
    src_ref,
    near_ref,
    far_ref,
    sums_ref,
    marginal_ref,
    src_label_ref,
    tgt_label_ref,
    out_hbm,
    total,
    tgt_rows,
    tgt_update,
    tgt_inv,
    images,
    out_sem,
):
    totals_of(sums_ref, total, features)
    slots = images.shape[0]
    rank = tgt_update.shape[1]
    marginal = marginal_ref[...]
    block = OWNER_BLOCK
    for which, ref in enumerate((near_ref, far_ref)):
        for part in range(slots // block):
            mine = pl.ds(which * slots + part * block, block)
            both = seen_block(ref, part, block)
            rows = both[:, :features]
            tgt_rows[mine, :] = rows
            tgt_update[mine, :] = mirror_step(rows, total[rank:], both[:, features:], marginal)
            tgt_inv[:, mine] = inverse_norm(rows).reshape(1, block)

    departures = []
    for part in range(slots // block):
        mine = pl.ds(part * block, block)
        both = seen_block(src_ref, part, block)
        rows = both[:, :features]
        update = mirror_step(rows, total[:rank], both[:, features:], marginal)
        cosine = contract_columns(rows, tgt_rows[...]) * inverse_norm(rows) * tgt_inv[...]
        weight = contract_columns(update, tgt_update[...]) / rank
        label = src_label_ref[:, mine].reshape(block, 1)
        same = jnp.logical_and(label == tgt_label_ref[...], label > 0)
        kernel = jnp.where(same, weight * jnp.exp((cosine - 1.0) / TEMPER), 0.0)
        denominator = jnp.sum(kernel, axis=1, keepdims=True)
        denominator = jnp.where(denominator > 0, denominator, 1.0)
        transport = (kernel / denominator).astype(jnp.bfloat16)
        images[mine, :] = jnp.dot(
            transport, tgt_rows[...], preferred_element_type=jnp.float32
        ).astype(jnp.bfloat16)
        departures.append(
            pltpu.make_async_copy(images.at[mine], out_hbm.at[mine], out_sem.at[part])
        )
        departures[-1].start()
    for copy in departures:
        copy.wait()


def owner_maps(near, far, sums, marginal, src_labels, tgt_labels, features):
    n_group, capacity, width = near.shape
    slots = n_group * capacity
    rank = width - features
    return pl.pallas_call(
        functools.partial(owner_kernel, features),
        out_shape=jax.ShapeDtypeStruct((slots, features), jnp.bfloat16),
        grid=(1,),
        in_specs=[
            pl.BlockSpec((n_group, None, capacity, width), lambda step: (0, 1, 0, 0)),
            whole(near.shape),
            pl.BlockSpec((n_group, None, capacity, width), lambda step: (0, 0, 0, 0)),
            whole(sums.shape),
            whole((1, rank)),
            whole((1, slots)),
            whole((1, 2 * slots)),
        ],
        out_specs=in_hbm(),
        scratch_shapes=[
            pltpu.VMEM((2 * rank, features), jnp.bfloat16),
            pltpu.VMEM((2 * slots, features), jnp.bfloat16),
            pltpu.VMEM((2 * slots, rank), jnp.bfloat16),
            pltpu.VMEM((1, 2 * slots), jnp.float32),
            pltpu.VMEM((slots, features), jnp.bfloat16),
            pltpu.SemaphoreType.DMA((slots // OWNER_BLOCK,)),
        ],
        compiler_params=pltpu.CompilerParams(vmem_limit_bytes=VMEM_BYTES),
        cost_estimate=pl.CostEstimate(
            flops=2 * slots * features * (3 * rank + 4 * slots),
            bytes_accessed=8 * slots * width,
            transcendentals=2 * slots * slots,
        ),
        name="owner_maps",
    )(
        far,
        near,
        far,
        sums,
        marginal[None, :],
        src_labels[None, :],
        tgt_labels[None, :],
    )


def labels_of(clusters, owner, capacity, spread):
    rows = clusters.shape[1]
    mine = clusters // spread == owner
    before = (jnp.arange(rows)[:, None] < jnp.arange(rows)[None, :]).astype(jnp.bfloat16)
    earlier = jnp.dot(mine.astype(jnp.bfloat16), before, preferred_element_type=jnp.float32)
    ranking = jnp.where(mine, earlier.astype(jnp.int32), -1)
    value = clusters - owner * spread + 1
    hit = ranking[:, None, :] == jnp.arange(capacity, dtype=jnp.int32)[None, :, None]
    return jnp.sum(jnp.where(hit, value[:, None, :], 0), axis=2).reshape(-1)


def exchange(rows):
    return lax.all_to_all(rows, GROUP, split_axis=0, concat_axis=0, tiled=True)


def per_device(
    src_points, tgt_points, src_factor, tgt_factor, inner_marginal, src_cluster, tgt_cluster
):
    n_src, n_rest = lax.axis_size("src"), lax.axis_size(REST)
    n_group = n_src * n_rest
    n_dev = 2 * n_group
    rows, features = src_points.shape
    rank = src_factor.shape[1]
    capacity = 2 * (2 * rows // n_dev)
    spread = 2 * CL_DEV
    me = lax.axis_index(ALL)
    my_half = lax.axis_index(HALF)
    owner = lax.axis_index(GROUP)

    near, raw = near_pack(tgt_cluster, tgt_points, tgt_factor, n_group, capacity, spread)
    near, me = lax.optimization_barrier((near, me))
    near = exchange(near)
    raw = lax.ppermute(raw, HALF, [(0, 1), (1, 0)])
    own, other = partial_sums(
        me,
        src_cluster,
        tgt_cluster,
        src_points,
        tgt_points,
        src_factor,
        tgt_factor,
        n_dev,
        2 * n_rest,
    )
    chain = Chain(own, other, n_src, 2 * n_rest)
    for digit in chain.plane[1:]:
        chain.scatter(digit)
    for digit in chain.along:
        chain.swap(digit)
    far = far_pack(raw, src_cluster, src_points, src_factor, n_group, capacity, spread)
    chain.x, _ = lax.optimization_barrier((chain.x, far))
    far, near = lax.optimization_barrier((far, near))
    far = exchange(far)
    for digit in reversed(chain.plane):
        chain.gather(digit)
    sums = chain.x.reshape(n_dev, -1, rank)

    kept = 2 * features // n_dev
    table = sums[:, kept : kept + 2].astype(jnp.int32).reshape(n_src, 2, n_rest, 2, rows)
    near_table = lax.dynamic_index_in_dim(table, my_half, 1, keepdims=False)
    far_table = lax.dynamic_index_in_dim(table, 1 - my_half, 1, keepdims=False)
    near_table = near_table.reshape(n_group, 2, rows)
    far_table = far_table.reshape(n_group, 2, rows)
    src_labels = labels_of(near_table[:, 0], owner, capacity, spread)
    near_labels = labels_of(near_table[:, 1], owner, capacity, spread)
    far_labels = labels_of(far_table[:, 1], owner, capacity, spread)

    near = near.reshape(n_group, capacity, features + rank)
    far = far.reshape(n_group, 2, capacity, features + rank)
    tgt_labels = jnp.concatenate([near_labels, far_labels])
    images = owner_maps(near, far, sums, inner_marginal, src_labels, tgt_labels, features)
    returned = exchange(images)

    src_update, tgt_update = updates(
        src_points, tgt_points, src_factor, tgt_factor, inner_marginal, sums
    )
    slot = slot_row(src_cluster[None, :], n_group, capacity, spread, 0)
    back = slot.reshape(rows, 1) == jnp.arange(n_group * capacity, dtype=jnp.int32)[None, :]
    back = lax.optimization_barrier(back.astype(jnp.bfloat16))
    mapped = jnp.dot(back, returned, preferred_element_type=jnp.float32).astype(jnp.bfloat16)
    return (src_update, tgt_update, mapped)


def solution(mesh):
    n_src, n_tgt = mesh.shape["src"], mesh.shape["tgt"]
    halves = Mesh(mesh.devices.reshape(n_src, 2, n_tgt // 2), ALL)
    rows = P(ALL, None)
    return jax.shard_map(
        per_device,
        mesh=halves,
        in_specs=(rows, rows, rows, rows, P(), P(ALL), P(ALL)),
        out_specs=(rows, rows, rows),
        check_vma=False,
    )
```

```python
import functools

import jax
import jax.numpy as jnp
from jax import lax
from jax.experimental import pallas as pl
from jax.experimental.pallas import tpu as pltpu
from jax.sharding import Mesh
from jax.sharding import PartitionSpec as P

CL_DEV = 2

GAMMA = 2.0
TEMPER = 0.03
EPS = 1e-06

HALF, REST = "half", "rest"
ALL = ("src", HALF, REST)
GROUP = ("src", REST)
VMEM_BYTES = 48 * 1024 * 1024
PACK_VMEM_BYTES = 62 * 1024 * 1024
TABLE_ROWS = 8
BLOCK_ROWS = 16
OWNER_BLOCK = 256
LABEL_ROWS = 16


def contract_rows(left, right):
    return lax.dot_general(
        left, right, (((0,), (0,)), ((), ())), preferred_element_type=jnp.float32
    )


def contract_columns(left, right):
    return lax.dot_general(
        left, right, (((1,), (1,)), ((), ())), preferred_element_type=jnp.float32
    )


def mirror_step(points, total_round, factor, inner_marginal):
    gradient = -contract_columns(points, total_round) / inner_marginal
    row_scale = jnp.max(jnp.abs(gradient), axis=1, keepdims=True) + EPS
    tilted = factor.astype(jnp.float32) * jnp.exp(-GAMMA * gradient / row_scale)
    mean = jnp.mean(tilted, axis=1, keepdims=True)
    mean = jnp.where(mean > 0, mean, 1.0)
    return (tilted / mean).astype(jnp.bfloat16)


def inverse_norm(rows):
    return lax.rsqrt(jnp.sum(jnp.square(rows.astype(jnp.float32)), axis=1, keepdims=True) + EPS)


def blocks_of(n_dev, chunk, rank, features):
    kept = (chunk - TABLE_ROWS) // BLOCK_ROWS
    wide = features // rank
    return [
        (b // kept, b % kept * BLOCK_ROWS, b // wide * BLOCK_ROWS, b % wide * rank)
        for b in range(n_dev * kept)
    ]


def totals_of(sums_ref, total, features):
    n_dev, chunk, rank = sums_ref.shape
    for c, row, first, column in blocks_of(n_dev, chunk, rank, features):
        total[pl.ds(first, BLOCK_ROWS), pl.ds(column, rank)] = sums_ref[c, pl.ds(row, BLOCK_ROWS), :]


def whole(shape):
    return pl.BlockSpec(shape, lambda *_: (0,) * len(shape))


def in_hbm():
    return pl.BlockSpec(memory_space=pltpu.HBM)


def slot_row(cluster, n_group, capacity, spread, first):
    rows = cluster.shape[1]
    owners = cluster // spread
    onehot = owners == lax.broadcasted_iota(jnp.int32, (n_group, rows), 0)
    before = lax.broadcasted_iota(jnp.int32, (rows, rows), 0) < lax.broadcasted_iota(
        jnp.int32, (rows, rows), 1
    )
    earlier = jnp.dot(
        onehot.astype(jnp.bfloat16), before.astype(jnp.bfloat16), preferred_element_type=jnp.float32
    )
    ranking = jnp.sum(jnp.where(onehot, earlier, 0.0), axis=0, keepdims=True).astype(jnp.int32)
    return owners * capacity + ranking + first


def contract_kernel(n_dev, n_tgt, me_ref, src_cluster_ref, tgt_cluster_ref, *refs):
    hbm, (own_ref, other_ref), held, parts, in_sem = refs[:4], refs[4:6], refs[6:10], refs[10], refs[11]
    arrivals = [pltpu.make_async_copy(a, b, in_sem.at[i]) for i, (a, b) in enumerate(zip(hbm, held))]
    for copy in arrivals:
        copy.start()
    tgt_points, tgt_factor, src_points, src_factor = held
    _, _, _, chunk, rank = parts.shape
    kept = chunk - TABLE_ROWS
    me = me_ref[0]
    mine = (me // n_tgt) % 2
    row = lax.broadcasted_iota(jnp.int32, (TABLE_ROWS, rank), 0)
    table = jnp.where(row == 0, src_cluster_ref[...], jnp.where(row == 1, tgt_cluster_ref[...], 0))
    parts[:, :, :, kept:, :] = jnp.zeros(parts.shape[:3] + (TABLE_ROWS, rank), jnp.float32)
    parts[me // (2 * n_tgt), mine, me % n_tgt, kept:, :] = table.astype(jnp.float32)
    features = tgt_points.shape[1]
    blocks = blocks_of(n_dev, chunk, rank, features)
    for which, (points, factor) in enumerate(((tgt_points, tgt_factor), (src_points, src_factor))):
        arrivals[2 * which].wait()
        arrivals[2 * which + 1].wait()
        total = contract_rows(factor[...], points[...])
        for c, row, first, column in blocks:
            first -= which * rank
            if 0 <= first < rank:
                place = (c // (2 * n_tgt), c // n_tgt % 2, c % n_tgt)
                parts[(*place, pl.ds(row, BLOCK_ROWS))] = total[
                    first : first + BLOCK_ROWS, column : column + rank
                ]
    for i in range(parts.shape[0]):
        own_ref[i] = parts[i, mine]
        other_ref[i] = parts[i, 1 - mine].astype(jnp.bfloat16)


def partial_sums(
    me, src_cluster, tgt_cluster, src_points, tgt_points, src_factor, tgt_factor, n_dev, n_tgt
):
    rows, features = src_points.shape
    rank = src_factor.shape[1]
    chunk = 2 * features // n_dev + TABLE_ROWS
    shape = (n_dev // (2 * n_tgt), n_tgt, chunk, rank)
    vmem = pl.BlockSpec(memory_space=pltpu.VMEM)
    return pl.pallas_call(
        functools.partial(contract_kernel, n_dev, n_tgt),
        out_shape=(
            jax.ShapeDtypeStruct(shape, jnp.float32),
            jax.ShapeDtypeStruct(shape, jnp.bfloat16),
        ),
        in_specs=[pl.BlockSpec(memory_space=pltpu.SMEM)] + [vmem] * 2 + [in_hbm()] * 4,
        out_specs=(vmem, vmem),
        scratch_shapes=[
            pltpu.VMEM((rows, features), jnp.bfloat16),
            pltpu.VMEM((rows, rank), jnp.bfloat16),
            pltpu.VMEM((rows, features), jnp.bfloat16),
            pltpu.VMEM((rows, rank), jnp.bfloat16),
            pltpu.VMEM((n_dev // (2 * n_tgt), 2, n_tgt, chunk, rank), jnp.float32),
            pltpu.SemaphoreType.DMA((4,)),
        ],
        compiler_params=pltpu.CompilerParams(vmem_limit_bytes=PACK_VMEM_BYTES),
        cost_estimate=pl.CostEstimate(
            flops=4 * rows * features * rank,
            bytes_accessed=4 * rows * (features + rank) + 4 * n_dev * chunk * rank,
            transcendentals=0,
        ),
        name="partial_sums",
    )(me[None], src_cluster[None, :], tgt_cluster[None, :], tgt_points, tgt_factor, src_points, src_factor)


def place_rows(kinds, packed, packed_hbm, out_sem):
    block = 256
    departures = []
    for part in range(packed.shape[0] // block):
        mine = pl.ds(part * block, block)
        total = None
        for slot, held in kinds:
            index = lax.broadcasted_iota(jnp.int32, (block, slot.shape[1]), 0) + part * block
            place = (index == slot).astype(jnp.bfloat16)
            rows = [
                jnp.dot(place, array, preferred_element_type=jnp.float32) for array in held
            ]
            total = rows if total is None else [a + b for a, b in zip(total, rows)]
        column = 0
        for rows in total:
            packed[mine, column : column + rows.shape[1]] = rows.astype(jnp.bfloat16)
            column += rows.shape[1]
        departures.append(
            pltpu.make_async_copy(packed.at[mine], packed_hbm.at[mine], out_sem.at[part])
        )
        departures[-1].start()
    return departures


def near_pack_kernel(
    n_group,
    capacity,
    spread,
    cluster_ref,
    points_hbm,
    factor_hbm,
    packed_hbm,
    raw_hbm,
    points,
    factor,
    packed,
    labels,
    in_sem,
    out_sem,
    raw_sem,
):
    arrivals = [
        pltpu.make_async_copy(points_hbm, points, in_sem.at[0]),
        pltpu.make_async_copy(factor_hbm, factor, in_sem.at[1]),
    ]
    for copy in arrivals:
        copy.start()
    rows, features = points.shape
    rank = factor.shape[1]
    first = lax.broadcasted_iota(jnp.int32, (LABEL_ROWS, rows), 0) == 0
    labels[...] = jnp.zeros(labels.shape, jnp.bfloat16)
    labels[:, :rows] = jnp.where(first, cluster_ref[...], 0).astype(jnp.float32).astype(jnp.bfloat16)
    slot = slot_row(cluster_ref[...], n_group, capacity, spread, 0)
    for copy in arrivals:
        copy.wait()
    departures = [
        pltpu.make_async_copy(
            points, raw_hbm.at[pl.ds(0, rows), pl.ds(0, features)], raw_sem.at[0]
        ),
        pltpu.make_async_copy(
            factor, raw_hbm.at[pl.ds(0, rows), pl.ds(features, rank)], raw_sem.at[1]
        ),
        pltpu.make_async_copy(labels, raw_hbm.at[pl.ds(rows, LABEL_ROWS)], raw_sem.at[2]),
    ]
    for copy in departures:
        copy.start()
    departures += place_rows([(slot, (points[...], factor[...]))], packed, packed_hbm, out_sem)
    for copy in departures:
        copy.wait()


def near_pack(cluster, points, factor, n_group, capacity, spread):
    rows, features = points.shape
    rank = factor.shape[1]
    width = features + rank
    slots = n_group * capacity
    return pl.pallas_call(
        functools.partial(near_pack_kernel, n_group, capacity, spread),
        out_shape=(
            jax.ShapeDtypeStruct((slots, width), jnp.bfloat16),
            jax.ShapeDtypeStruct((rows + LABEL_ROWS, width), jnp.bfloat16),
        ),
        in_specs=[pl.BlockSpec(memory_space=pltpu.VMEM), in_hbm(), in_hbm()],
        out_specs=(in_hbm(), in_hbm()),
        scratch_shapes=[
            pltpu.VMEM((rows, features), jnp.bfloat16),
            pltpu.VMEM((rows, rank), jnp.bfloat16),
            pltpu.VMEM((slots, width), jnp.bfloat16),
            pltpu.VMEM((LABEL_ROWS, width), jnp.bfloat16),
            pltpu.SemaphoreType.DMA((2,)),
            pltpu.SemaphoreType.DMA((slots // 256,)),
            pltpu.SemaphoreType.DMA((3,)),
        ],
        compiler_params=pltpu.CompilerParams(vmem_limit_bytes=PACK_VMEM_BYTES),
        cost_estimate=pl.CostEstimate(
            flops=2 * slots * rows * width,
            bytes_accessed=2 * (slots + 2 * rows) * width,
            transcendentals=0,
        ),
        name="near_pack",
    )(cluster[None, :], points, factor)


def far_pack_kernel(
    n_group,
    capacity,
    spread,
    cluster_ref,
    raw_hbm,
    points_hbm,
    factor_hbm,
    packed_hbm,
    raw,
    points,
    factor,
    packed,
    in_sem,
    out_sem,
):
    rows, features = points.shape
    arrivals = [
        pltpu.make_async_copy(raw_hbm, raw, in_sem.at[0]),
        pltpu.make_async_copy(points_hbm, points, in_sem.at[1]),
        pltpu.make_async_copy(factor_hbm, factor, in_sem.at[2]),
    ]
    for copy in arrivals:
        copy.start()
    src_slot = slot_row(cluster_ref[...], n_group, 2 * capacity, spread, capacity)
    arrivals[0].wait()
    labels = raw[rows:, :rows].astype(jnp.float32)[:1].astype(jnp.int32)
    tgt_slot = slot_row(labels, n_group, 2 * capacity, spread, 0)
    arrivals[1].wait()
    arrivals[2].wait()
    kinds = [
        (tgt_slot, (raw[:rows, :features], raw[:rows, features:])),
        (src_slot, (points[...], factor[...])),
    ]
    for copy in place_rows(kinds, packed, packed_hbm, out_sem):
        copy.wait()


def far_pack(raw, cluster, points, factor, n_group, capacity, spread):
    rows, features = points.shape
    width = raw.shape[1]
    slots = 2 * n_group * capacity
    return pl.pallas_call(
        functools.partial(far_pack_kernel, n_group, capacity, spread),
        out_shape=jax.ShapeDtypeStruct((slots, width), jnp.bfloat16),
        in_specs=[pl.BlockSpec(memory_space=pltpu.VMEM)] + [in_hbm()] * 3,
        out_specs=in_hbm(),
        scratch_shapes=[
            pltpu.VMEM(raw.shape, jnp.bfloat16),
            pltpu.VMEM(points.shape, jnp.bfloat16),
            pltpu.VMEM(factor.shape, jnp.bfloat16),
            pltpu.VMEM((slots, width), jnp.bfloat16),
            pltpu.SemaphoreType.DMA((3,)),
            pltpu.SemaphoreType.DMA((slots // 256,)),
        ],
        compiler_params=pltpu.CompilerParams(vmem_limit_bytes=PACK_VMEM_BYTES),
        cost_estimate=pl.CostEstimate(
            flops=4 * slots * rows * width,
            bytes_accessed=2 * (slots + 2 * rows) * width,
            transcendentals=0,
        ),
        name="far_pack",
    )(cluster[None, :], raw, points, factor)


def digits_of(size, stride):
    bits = size.bit_length() - 1
    found = []
    while bits:
        take = 1 if bits % 2 else 2
        found.append((stride, 1 << take))
        stride <<= take
        bits -= take
    return found


class Chain:
    def __init__(self, own, other, n_src, n_tgt):
        self.n_dev = n_src * n_tgt
        first = (n_tgt, 2)
        src, tgt = digits_of(n_src // 2, 2 * n_tgt), digits_of(n_tgt, 1)
        self.plane, self.along = [first] + src, tgt
        self.dims = src[::-1] + [first] + tgt[::-1]
        self.left = [d for d in self.dims if d != first]
        x = own + self.sent(other, n_tgt).astype(jnp.float32)
        self.x = x.reshape(tuple(radix for _, radix in self.left) + own.shape[2:])

    def sent(self, array, mask):
        return lax.ppermute(array, ALL, [(i, i ^ mask) for i in range(self.n_dev)])

    def scatter(self, digit):
        stride, radix = digit
        dim = self.left.index(digit)
        mine = (lax.axis_index(ALL) // stride) % radix
        total = lax.dynamic_index_in_dim(self.x, mine, dim, keepdims=False)
        for j in range(1, radix):
            piece = lax.dynamic_index_in_dim(self.x, mine ^ j, dim, keepdims=False)
            total = total + self.sent(piece.astype(jnp.bfloat16), j * stride).astype(jnp.float32)
        self.x = total
        self.left.remove(digit)

    def swap(self, digit):
        stride, radix = digit
        piece = self.x.astype(jnp.bfloat16)
        for j in range(1, radix):
            self.x = self.x + self.sent(piece, j * stride).astype(jnp.float32)

    def gather(self, digit):
        stride, radix = digit
        mine = (lax.axis_index(ALL) // stride) % radix
        x = self.x.astype(jnp.bfloat16)
        got = [x] + [self.sent(x, j * stride) for j in range(1, radix)]
        self.left = [d for d in self.dims if d in self.left or d == digit]
        self.x = jnp.stack(
            [lax.select_n(mine ^ d, *got) if radix > 2 else jnp.where(mine == d, *got) for d in range(radix)],
            axis=self.left.index(digit),
        )


def update_kernel(
    src_points_ref,
    tgt_points_ref,
    src_factor_ref,
    tgt_factor_ref,
    marginal_ref,
    sums_ref,
    src_ref,
    tgt_ref,
    total,
):
    totals_of(sums_ref, total, src_points_ref.shape[1])
    rank = src_ref.shape[1]
    marginal = marginal_ref[...]
    src_ref[...] = mirror_step(src_points_ref[...], total[:rank], src_factor_ref[...], marginal)
    tgt_ref[...] = mirror_step(tgt_points_ref[...], total[rank:], tgt_factor_ref[...], marginal)


def updates(src_points, tgt_points, src_factor, tgt_factor, marginal, sums):
    rows, features = src_points.shape
    rank = src_factor.shape[1]
    shape = jax.ShapeDtypeStruct(src_factor.shape, jnp.bfloat16)
    return pl.pallas_call(
        update_kernel,
        out_shape=(shape, shape),
        scratch_shapes=[pltpu.VMEM((2 * rank, features), jnp.bfloat16)],
        compiler_params=pltpu.CompilerParams(vmem_limit_bytes=VMEM_BYTES),
        cost_estimate=pl.CostEstimate(
            flops=4 * rows * features * rank,
            bytes_accessed=4 * rows * (features + 2 * rank),
            transcendentals=2 * rows * rank,
        ),
        name="mirror_updates",
    )(src_points, tgt_points, src_factor, tgt_factor, marginal[None, :], sums)


def seen_block(ref, part, block):
    piece = block // ref.shape[1]
    return ref[pl.ds(part * piece, piece)].reshape(block, ref.shape[2])


def owner_kernel(
    features,
    src_ref,
    near_ref,
    far_ref,
    sums_ref,
    marginal_ref,
    src_label_ref,
    tgt_label_ref,
    out_hbm,
    total,
    tgt_rows,
    tgt_update,
    tgt_inv,
    images,
    out_sem,
):
    totals_of(sums_ref, total, features)
    slots = images.shape[0]
    rank = tgt_update.shape[1]
    marginal = marginal_ref[...]
    block = OWNER_BLOCK
    for which, ref in enumerate((near_ref, far_ref)):
        for part in range(slots // block):
            mine = pl.ds(which * slots + part * block, block)
            both = seen_block(ref, part, block)
            rows = both[:, :features]
            tgt_rows[mine, :] = rows
            tgt_update[mine, :] = mirror_step(rows, total[rank:], both[:, features:], marginal)
            tgt_inv[:, mine] = inverse_norm(rows).reshape(1, block)

    departures = []
    for part in range(slots // block):
        mine = pl.ds(part * block, block)
        both = seen_block(src_ref, part, block)
        rows = both[:, :features]
        update = mirror_step(rows, total[:rank], both[:, features:], marginal)
        cosine = contract_columns(rows, tgt_rows[...]) * inverse_norm(rows) * tgt_inv[...]
        weight = contract_columns(update, tgt_update[...]) / rank
        label = src_label_ref[:, mine].reshape(block, 1)
        same = jnp.logical_and(label == tgt_label_ref[...], label > 0)
        kernel = jnp.where(same, weight * jnp.exp((cosine - 1.0) / TEMPER), 0.0)
        denominator = jnp.sum(kernel, axis=1, keepdims=True)
        denominator = jnp.where(denominator > 0, denominator, 1.0)
        transport = (kernel / denominator).astype(jnp.bfloat16)
        images[mine, :] = jnp.dot(
            transport, tgt_rows[...], preferred_element_type=jnp.float32
        ).astype(jnp.bfloat16)
        departures.append(
            pltpu.make_async_copy(images.at[mine], out_hbm.at[mine], out_sem.at[part])
        )
        departures[-1].start()
    for copy in departures:
        copy.wait()


def owner_maps(near, far, sums, marginal, src_labels, tgt_labels, features):
    n_group, capacity, width = near.shape
    slots = n_group * capacity
    rank = width - features
    return pl.pallas_call(
        functools.partial(owner_kernel, features),
        out_shape=jax.ShapeDtypeStruct((slots, features), jnp.bfloat16),
        grid=(1,),
        in_specs=[
            pl.BlockSpec((n_group, None, capacity, width), lambda step: (0, 1, 0, 0)),
            whole(near.shape),
            pl.BlockSpec((n_group, None, capacity, width), lambda step: (0, 0, 0, 0)),
            whole(sums.shape),
            whole((1, rank)),
            whole((1, slots)),
            whole((1, 2 * slots)),
        ],
        out_specs=in_hbm(),
        scratch_shapes=[
            pltpu.VMEM((2 * rank, features), jnp.bfloat16),
            pltpu.VMEM((2 * slots, features), jnp.bfloat16),
            pltpu.VMEM((2 * slots, rank), jnp.bfloat16),
            pltpu.VMEM((1, 2 * slots), jnp.float32),
            pltpu.VMEM((slots, features), jnp.bfloat16),
            pltpu.SemaphoreType.DMA((slots // OWNER_BLOCK,)),
        ],
        compiler_params=pltpu.CompilerParams(vmem_limit_bytes=VMEM_BYTES),
        cost_estimate=pl.CostEstimate(
            flops=2 * slots * features * (3 * rank + 4 * slots),
            bytes_accessed=8 * slots * width,
            transcendentals=2 * slots * slots,
        ),
        name="owner_maps",
    )(
        far,
        near,
        far,
        sums,
        marginal[None, :],
        src_labels[None, :],
        tgt_labels[None, :],
    )


def labels_of(clusters, owner, capacity, spread):
    rows = clusters.shape[1]
    mine = clusters // spread == owner
    before = (jnp.arange(rows)[:, None] < jnp.arange(rows)[None, :]).astype(jnp.bfloat16)
    earlier = jnp.dot(mine.astype(jnp.bfloat16), before, preferred_element_type=jnp.float32)
    ranking = jnp.where(mine, earlier.astype(jnp.int32), -1)
    value = clusters - owner * spread + 1
    hit = ranking[:, None, :] == jnp.arange(capacity, dtype=jnp.int32)[None, :, None]
    return jnp.sum(jnp.where(hit, value[:, None, :], 0), axis=2).reshape(-1)


def exchange(rows):
    return lax.all_to_all(rows, GROUP, split_axis=0, concat_axis=0, tiled=True)


def per_device(
    src_points, tgt_points, src_factor, tgt_factor, inner_marginal, src_cluster, tgt_cluster
):
    n_src, n_rest = lax.axis_size("src"), lax.axis_size(REST)
    n_group = n_src * n_rest
    n_dev = 2 * n_group
    rows, features = src_points.shape
    rank = src_factor.shape[1]
    capacity = 2 * (2 * rows // n_dev)
    spread = 2 * CL_DEV
    me = lax.axis_index(ALL)
    my_half = lax.axis_index(HALF)
    owner = lax.axis_index(GROUP)

    near, raw = near_pack(tgt_cluster, tgt_points, tgt_factor, n_group, capacity, spread)
    near, me = lax.optimization_barrier((near, me))
    near = exchange(near)
    raw = lax.ppermute(raw, HALF, [(0, 1), (1, 0)])
    own, other = partial_sums(
        me,
        src_cluster,
        tgt_cluster,
        src_points,
        tgt_points,
        src_factor,
        tgt_factor,
        n_dev,
        2 * n_rest,
    )
    chain = Chain(own, other, n_src, 2 * n_rest)
    for digit in chain.plane[1:]:
        chain.scatter(digit)
    late_cluster, chain.x = lax.optimization_barrier((src_cluster, chain.x))
    for digit in chain.along:
        chain.swap(digit)
    far = far_pack(raw, late_cluster, src_points, src_factor, n_group, capacity, spread)
    far, near, chain.x = lax.optimization_barrier((far, near, chain.x))
    far = exchange(far)
    for digit in reversed(chain.plane):
        chain.gather(digit)
    sums = chain.x.reshape(n_dev, -1, rank)

    kept = 2 * features // n_dev
    table = sums[:, kept : kept + 2].astype(jnp.int32).reshape(n_src, 2, n_rest, 2, rows)
    near_table = lax.dynamic_index_in_dim(table, my_half, 1, keepdims=False)
    far_table = lax.dynamic_index_in_dim(table, 1 - my_half, 1, keepdims=False)
    near_table = near_table.reshape(n_group, 2, rows)
    far_table = far_table.reshape(n_group, 2, rows)
    src_labels = labels_of(near_table[:, 0], owner, capacity, spread)
    near_labels = labels_of(near_table[:, 1], owner, capacity, spread)
    far_labels = labels_of(far_table[:, 1], owner, capacity, spread)

    near = near.reshape(n_group, capacity, features + rank)
    far = far.reshape(n_group, 2, capacity, features + rank)
    tgt_labels = jnp.concatenate([near_labels, far_labels])
    images = owner_maps(near, far, sums, inner_marginal, src_labels, tgt_labels, features)
    returned = exchange(images)

    src_update, tgt_update = updates(
        src_points, tgt_points, src_factor, tgt_factor, inner_marginal, sums
    )
    slot = slot_row(src_cluster[None, :], n_group, capacity, spread, 0)
    back = slot.reshape(rows, 1) == jnp.arange(n_group * capacity, dtype=jnp.int32)[None, :]
    back = lax.optimization_barrier(back.astype(jnp.bfloat16))
    mapped = jnp.dot(back, returned, preferred_element_type=jnp.float32).astype(jnp.bfloat16)
    return (src_update, tgt_update, mapped)


def solution(mesh):
    n_src, n_tgt = mesh.shape["src"], mesh.shape["tgt"]
    halves = Mesh(mesh.devices.reshape(n_src, 2, n_tgt // 2), ALL)
    rows = P(ALL, None)
    return jax.shard_map(
        per_device,
        mesh=halves,
        in_specs=(rows, rows, rows, rows, P(), P(ALL), P(ALL)),
        out_specs=(rows, rows, rows),
        check_vma=False,
    )
```

```python
import functools

import jax
import jax.numpy as jnp
from jax import lax
from jax.experimental import pallas as pl
from jax.experimental.pallas import tpu as pltpu
from jax.sharding import Mesh
from jax.sharding import PartitionSpec as P

CL_DEV = 2

GAMMA = 2.0
TEMPER = 0.03
EPS = 1e-06

HALF, REST = "half", "rest"
ALL = ("src", HALF, REST)
GROUP = ("src", REST)
VMEM_BYTES = 48 * 1024 * 1024
PACK_VMEM_BYTES = 62 * 1024 * 1024
TABLE_ROWS = 8
BLOCK_ROWS = 16
OWNER_BLOCK = 256
LABEL_ROWS = 16


def contract_rows(left, right):
    return lax.dot_general(
        left, right, (((0,), (0,)), ((), ())), preferred_element_type=jnp.float32
    )


def contract_columns(left, right):
    return lax.dot_general(
        left, right, (((1,), (1,)), ((), ())), preferred_element_type=jnp.float32
    )


def mirror_step(points, total_round, factor, inner_marginal):
    gradient = -contract_columns(points, total_round) / inner_marginal
    row_scale = jnp.max(jnp.abs(gradient), axis=1, keepdims=True) + EPS
    tilted = factor.astype(jnp.float32) * jnp.exp(-GAMMA * gradient / row_scale)
    mean = jnp.mean(tilted, axis=1, keepdims=True)
    mean = jnp.where(mean > 0, mean, 1.0)
    return (tilted / mean).astype(jnp.bfloat16)


def inverse_norm(rows):
    return lax.rsqrt(jnp.sum(jnp.square(rows.astype(jnp.float32)), axis=1, keepdims=True) + EPS)


def blocks_of(n_dev, chunk, rank, features):
    kept = (chunk - TABLE_ROWS) // BLOCK_ROWS
    wide = features // rank
    return [
        (b // kept, b % kept * BLOCK_ROWS, b // wide * BLOCK_ROWS, b % wide * rank)
        for b in range(n_dev * kept)
    ]


def totals_of(sums_ref, total, features):
    n_dev, chunk, rank = sums_ref.shape
    for c, row, first, column in blocks_of(n_dev, chunk, rank, features):
        total[pl.ds(first, BLOCK_ROWS), pl.ds(column, rank)] = sums_ref[c, pl.ds(row, BLOCK_ROWS), :]


def whole(shape):
    return pl.BlockSpec(shape, lambda *_: (0,) * len(shape))


def in_hbm():
    return pl.BlockSpec(memory_space=pltpu.HBM)


def slot_row(cluster, n_group, capacity, spread, first):
    rows = cluster.shape[1]
    owners = cluster // spread
    onehot = owners == lax.broadcasted_iota(jnp.int32, (n_group, rows), 0)
    before = lax.broadcasted_iota(jnp.int32, (rows, rows), 0) < lax.broadcasted_iota(
        jnp.int32, (rows, rows), 1
    )
    earlier = jnp.dot(
        onehot.astype(jnp.bfloat16), before.astype(jnp.bfloat16), preferred_element_type=jnp.float32
    )
    ranking = jnp.sum(jnp.where(onehot, earlier, 0.0), axis=0, keepdims=True).astype(jnp.int32)
    return owners * capacity + ranking + first


def contract_kernel(n_dev, n_tgt, me_ref, src_cluster_ref, tgt_cluster_ref, *refs):
    hbm, (own_ref, other_ref), held, parts, in_sem = refs[:4], refs[4:6], refs[6:10], refs[10], refs[11]
    arrivals = [pltpu.make_async_copy(a, b, in_sem.at[i]) for i, (a, b) in enumerate(zip(hbm, held))]
    for copy in arrivals:
        copy.start()
    tgt_points, tgt_factor, src_points, src_factor = held
    _, _, _, chunk, rank = parts.shape
    kept = chunk - TABLE_ROWS
    me = me_ref[0]
    mine = (me // n_tgt) % 2
    row = lax.broadcasted_iota(jnp.int32, (TABLE_ROWS, rank), 0)
    table = jnp.where(row == 0, src_cluster_ref[...], jnp.where(row == 1, tgt_cluster_ref[...], 0))
    parts[:, :, :, kept:, :] = jnp.zeros(parts.shape[:3] + (TABLE_ROWS, rank), jnp.float32)
    parts[me // (2 * n_tgt), mine, me % n_tgt, kept:, :] = table.astype(jnp.float32)
    features = tgt_points.shape[1]
    blocks = blocks_of(n_dev, chunk, rank, features)
    for which, (points, factor) in enumerate(((tgt_points, tgt_factor), (src_points, src_factor))):
        arrivals[2 * which].wait()
        arrivals[2 * which + 1].wait()
        total = contract_rows(factor[...], points[...])
        for c, row, first, column in blocks:
            first -= which * rank
            if 0 <= first < rank:
                place = (c // (2 * n_tgt), c // n_tgt % 2, c % n_tgt)
                parts[(*place, pl.ds(row, BLOCK_ROWS))] = total[
                    first : first + BLOCK_ROWS, column : column + rank
                ]
    for i in range(parts.shape[0]):
        own_ref[i] = parts[i, mine]
        other_ref[i] = parts[i, 1 - mine].astype(jnp.bfloat16)


def partial_sums(
    me, src_cluster, tgt_cluster, src_points, tgt_points, src_factor, tgt_factor, n_dev, n_tgt
):
    rows, features = src_points.shape
    rank = src_factor.shape[1]
    chunk = 2 * features // n_dev + TABLE_ROWS
    shape = (n_dev // (2 * n_tgt), n_tgt, chunk, rank)
    vmem = pl.BlockSpec(memory_space=pltpu.VMEM)
    return pl.pallas_call(
        functools.partial(contract_kernel, n_dev, n_tgt),
        out_shape=(
            jax.ShapeDtypeStruct(shape, jnp.float32),
            jax.ShapeDtypeStruct(shape, jnp.bfloat16),
        ),
        in_specs=[pl.BlockSpec(memory_space=pltpu.SMEM)] + [vmem] * 2 + [in_hbm()] * 4,
        out_specs=(vmem, vmem),
        scratch_shapes=[
            pltpu.VMEM((rows, features), jnp.bfloat16),
            pltpu.VMEM((rows, rank), jnp.bfloat16),
            pltpu.VMEM((rows, features), jnp.bfloat16),
            pltpu.VMEM((rows, rank), jnp.bfloat16),
            pltpu.VMEM((n_dev // (2 * n_tgt), 2, n_tgt, chunk, rank), jnp.float32),
            pltpu.SemaphoreType.DMA((4,)),
        ],
        compiler_params=pltpu.CompilerParams(vmem_limit_bytes=PACK_VMEM_BYTES),
        cost_estimate=pl.CostEstimate(
            flops=4 * rows * features * rank,
            bytes_accessed=4 * rows * (features + rank) + 4 * n_dev * chunk * rank,
            transcendentals=0,
        ),
        name="partial_sums",
    )(me[None], src_cluster[None, :], tgt_cluster[None, :], tgt_points, tgt_factor, src_points, src_factor)


def place_rows(kinds, packed, packed_hbm, out_sem):
    block = 256
    departures = []
    for part in range(packed.shape[0] // block):
        mine = pl.ds(part * block, block)
        total = None
        for slot, held in kinds:
            index = lax.broadcasted_iota(jnp.int32, (block, slot.shape[1]), 0) + part * block
            place = (index == slot).astype(jnp.bfloat16)
            rows = [
                jnp.dot(place, array, preferred_element_type=jnp.float32) for array in held
            ]
            total = rows if total is None else [a + b for a, b in zip(total, rows)]
        column = 0
        for rows in total:
            packed[mine, column : column + rows.shape[1]] = rows.astype(jnp.bfloat16)
            column += rows.shape[1]
        departures.append(
            pltpu.make_async_copy(packed.at[mine], packed_hbm.at[mine], out_sem.at[part])
        )
        departures[-1].start()
    return departures


def near_pack_kernel(
    n_group,
    capacity,
    spread,
    cluster_ref,
    points_hbm,
    factor_hbm,
    packed_hbm,
    raw_hbm,
    points,
    factor,
    packed,
    labels,
    in_sem,
    out_sem,
    raw_sem,
):
    arrivals = [
        pltpu.make_async_copy(points_hbm, points, in_sem.at[0]),
        pltpu.make_async_copy(factor_hbm, factor, in_sem.at[1]),
    ]
    for copy in arrivals:
        copy.start()
    rows, features = points.shape
    rank = factor.shape[1]
    first = lax.broadcasted_iota(jnp.int32, (LABEL_ROWS, rows), 0) == 0
    labels[...] = jnp.zeros(labels.shape, jnp.bfloat16)
    labels[:, :rows] = jnp.where(first, cluster_ref[...], 0).astype(jnp.float32).astype(jnp.bfloat16)
    slot = slot_row(cluster_ref[...], n_group, capacity, spread, 0)
    for copy in arrivals:
        copy.wait()
    departures = [
        pltpu.make_async_copy(
            points, raw_hbm.at[pl.ds(0, rows), pl.ds(0, features)], raw_sem.at[0]
        ),
        pltpu.make_async_copy(
            factor, raw_hbm.at[pl.ds(0, rows), pl.ds(features, rank)], raw_sem.at[1]
        ),
        pltpu.make_async_copy(labels, raw_hbm.at[pl.ds(rows, LABEL_ROWS)], raw_sem.at[2]),
    ]
    for copy in departures:
        copy.start()
    departures += place_rows([(slot, (points[...], factor[...]))], packed, packed_hbm, out_sem)
    for copy in departures:
        copy.wait()


def near_pack(cluster, points, factor, n_group, capacity, spread):
    rows, features = points.shape
    rank = factor.shape[1]
    width = features + rank
    slots = n_group * capacity
    return pl.pallas_call(
        functools.partial(near_pack_kernel, n_group, capacity, spread),
        out_shape=(
            jax.ShapeDtypeStruct((slots, width), jnp.bfloat16),
            jax.ShapeDtypeStruct((rows + LABEL_ROWS, width), jnp.bfloat16),
        ),
        in_specs=[pl.BlockSpec(memory_space=pltpu.VMEM), in_hbm(), in_hbm()],
        out_specs=(in_hbm(), in_hbm()),
        scratch_shapes=[
            pltpu.VMEM((rows, features), jnp.bfloat16),
            pltpu.VMEM((rows, rank), jnp.bfloat16),
            pltpu.VMEM((slots, width), jnp.bfloat16),
            pltpu.VMEM((LABEL_ROWS, width), jnp.bfloat16),
            pltpu.SemaphoreType.DMA((2,)),
            pltpu.SemaphoreType.DMA((slots // 256,)),
            pltpu.SemaphoreType.DMA((3,)),
        ],
        compiler_params=pltpu.CompilerParams(vmem_limit_bytes=PACK_VMEM_BYTES),
        cost_estimate=pl.CostEstimate(
            flops=2 * slots * rows * width,
            bytes_accessed=2 * (slots + 2 * rows) * width,
            transcendentals=0,
        ),
        name="near_pack",
    )(cluster[None, :], points, factor)


def far_pack_kernel(
    n_group,
    capacity,
    spread,
    cluster_ref,
    raw_hbm,
    points_hbm,
    factor_hbm,
    packed_hbm,
    raw,
    points,
    factor,
    packed,
    in_sem,
    out_sem,
):
    rows, features = points.shape
    arrivals = [
        pltpu.make_async_copy(raw_hbm, raw, in_sem.at[0]),
        pltpu.make_async_copy(points_hbm, points, in_sem.at[1]),
        pltpu.make_async_copy(factor_hbm, factor, in_sem.at[2]),
    ]
    for copy in arrivals:
        copy.start()
    src_slot = slot_row(cluster_ref[...], n_group, 2 * capacity, spread, capacity)
    arrivals[0].wait()
    labels = raw[rows:, :rows].astype(jnp.float32)[:1].astype(jnp.int32)
    tgt_slot = slot_row(labels, n_group, 2 * capacity, spread, 0)
    arrivals[1].wait()
    arrivals[2].wait()
    kinds = [
        (tgt_slot, (raw[:rows, :features], raw[:rows, features:])),
        (src_slot, (points[...], factor[...])),
    ]
    for copy in place_rows(kinds, packed, packed_hbm, out_sem):
        copy.wait()


def far_pack(raw, cluster, points, factor, n_group, capacity, spread):
    rows, features = points.shape
    width = raw.shape[1]
    slots = 2 * n_group * capacity
    return pl.pallas_call(
        functools.partial(far_pack_kernel, n_group, capacity, spread),
        out_shape=jax.ShapeDtypeStruct((slots, width), jnp.bfloat16),
        in_specs=[pl.BlockSpec(memory_space=pltpu.VMEM)] + [in_hbm()] * 3,
        out_specs=in_hbm(),
        scratch_shapes=[
            pltpu.VMEM(raw.shape, jnp.bfloat16),
            pltpu.VMEM(points.shape, jnp.bfloat16),
            pltpu.VMEM(factor.shape, jnp.bfloat16),
            pltpu.VMEM((slots, width), jnp.bfloat16),
            pltpu.SemaphoreType.DMA((3,)),
            pltpu.SemaphoreType.DMA((slots // 256,)),
        ],
        compiler_params=pltpu.CompilerParams(vmem_limit_bytes=PACK_VMEM_BYTES),
        cost_estimate=pl.CostEstimate(
            flops=4 * slots * rows * width,
            bytes_accessed=2 * (slots + 2 * rows) * width,
            transcendentals=0,
        ),
        name="far_pack",
    )(cluster[None, :], raw, points, factor)


def digits_of(size, stride):
    bits = size.bit_length() - 1
    found = []
    while bits:
        take = 1 if bits % 2 else 2
        found.append((stride, 1 << take))
        stride <<= take
        bits -= take
    return found


class Chain:
    def __init__(self, own, other, n_src, n_tgt):
        self.n_dev = n_src * n_tgt
        first = (n_tgt, 2)
        src, tgt = digits_of(n_src // 2, 2 * n_tgt), digits_of(n_tgt, 1)
        self.plane, self.along = [first] + src, tgt
        self.dims = src[::-1] + [first] + tgt[::-1]
        self.left = [d for d in self.dims if d != first]
        x = own + self.sent(other, n_tgt).astype(jnp.float32)
        self.x = x.reshape(tuple(radix for _, radix in self.left) + own.shape[2:])

    def sent(self, array, mask):
        return lax.ppermute(array, ALL, [(i, i ^ mask) for i in range(self.n_dev)])

    def scatter(self, digit):
        stride, radix = digit
        dim = self.left.index(digit)
        mine = (lax.axis_index(ALL) // stride) % radix
        total = lax.dynamic_index_in_dim(self.x, mine, dim, keepdims=False)
        for j in range(1, radix):
            piece = lax.dynamic_index_in_dim(self.x, mine ^ j, dim, keepdims=False)
            total = total + self.sent(piece.astype(jnp.bfloat16), j * stride).astype(jnp.float32)
        self.x = total
        self.left.remove(digit)

    def gather(self, digit):
        stride, radix = digit
        mine = (lax.axis_index(ALL) // stride) % radix
        x = self.x.astype(jnp.bfloat16)
        got = [x] + [self.sent(x, j * stride) for j in range(1, radix)]
        self.left = [d for d in self.dims if d in self.left or d == digit]
        self.x = jnp.stack(
            [lax.select_n(mine ^ d, *got) if radix > 2 else jnp.where(mine == d, *got) for d in range(radix)],
            axis=self.left.index(digit),
        )


def update_kernel(
    src_points_ref,
    tgt_points_ref,
    src_factor_ref,
    tgt_factor_ref,
    marginal_ref,
    sums_ref,
    src_ref,
    tgt_ref,
    total,
):
    totals_of(sums_ref, total, src_points_ref.shape[1])
    rank = src_ref.shape[1]
    marginal = marginal_ref[...]
    src_ref[...] = mirror_step(src_points_ref[...], total[:rank], src_factor_ref[...], marginal)
    tgt_ref[...] = mirror_step(tgt_points_ref[...], total[rank:], tgt_factor_ref[...], marginal)


def updates(src_points, tgt_points, src_factor, tgt_factor, marginal, sums):
    rows, features = src_points.shape
    rank = src_factor.shape[1]
    shape = jax.ShapeDtypeStruct(src_factor.shape, jnp.bfloat16)
    return pl.pallas_call(
        update_kernel,
        out_shape=(shape, shape),
        scratch_shapes=[pltpu.VMEM((2 * rank, features), jnp.bfloat16)],
        compiler_params=pltpu.CompilerParams(vmem_limit_bytes=VMEM_BYTES),
        cost_estimate=pl.CostEstimate(
            flops=4 * rows * features * rank,
            bytes_accessed=4 * rows * (features + 2 * rank),
            transcendentals=2 * rows * rank,
        ),
        name="mirror_updates",
    )(src_points, tgt_points, src_factor, tgt_factor, marginal[None, :], sums)


def seen_block(ref, part, block):
    piece = block // ref.shape[1]
    return ref[pl.ds(part * piece, piece)].reshape(block, ref.shape[2])


def owner_kernel(
    features,
    src_ref,
    near_ref,
    far_ref,
    sums_ref,
    marginal_ref,
    src_label_ref,
    tgt_label_ref,
    out_hbm,
    total,
    tgt_rows,
    tgt_update,
    tgt_inv,
    images,
    out_sem,
):
    totals_of(sums_ref, total, features)
    slots = images.shape[0]
    rank = tgt_update.shape[1]
    marginal = marginal_ref[...]
    block = OWNER_BLOCK
    for which, ref in enumerate((near_ref, far_ref)):
        for part in range(slots // block):
            mine = pl.ds(which * slots + part * block, block)
            both = seen_block(ref, part, block)
            rows = both[:, :features]
            tgt_rows[mine, :] = rows
            tgt_update[mine, :] = mirror_step(rows, total[rank:], both[:, features:], marginal)
            tgt_inv[:, mine] = inverse_norm(rows).reshape(1, block)

    departures = []
    for part in range(slots // block):
        mine = pl.ds(part * block, block)
        both = seen_block(src_ref, part, block)
        rows = both[:, :features]
        update = mirror_step(rows, total[:rank], both[:, features:], marginal)
        cosine = contract_columns(rows, tgt_rows[...]) * inverse_norm(rows) * tgt_inv[...]
        weight = contract_columns(update, tgt_update[...]) / rank
        label = src_label_ref[:, mine].reshape(block, 1)
        same = jnp.logical_and(label == tgt_label_ref[...], label > 0)
        kernel = jnp.where(same, weight * jnp.exp((cosine - 1.0) / TEMPER), 0.0)
        denominator = jnp.sum(kernel, axis=1, keepdims=True)
        denominator = jnp.where(denominator > 0, denominator, 1.0)
        transport = (kernel / denominator).astype(jnp.bfloat16)
        images[mine, :] = jnp.dot(
            transport, tgt_rows[...], preferred_element_type=jnp.float32
        ).astype(jnp.bfloat16)
        departures.append(
            pltpu.make_async_copy(images.at[mine], out_hbm.at[mine], out_sem.at[part])
        )
        departures[-1].start()
    for copy in departures:
        copy.wait()


def owner_maps(near, far, sums, marginal, src_labels, tgt_labels, features):
    n_group, capacity, width = near.shape
    slots = n_group * capacity
    rank = width - features
    return pl.pallas_call(
        functools.partial(owner_kernel, features),
        out_shape=jax.ShapeDtypeStruct((slots, features), jnp.bfloat16),
        grid=(1,),
        in_specs=[
            pl.BlockSpec((n_group, None, capacity, width), lambda step: (0, 1, 0, 0)),
            whole(near.shape),
            pl.BlockSpec((n_group, None, capacity, width), lambda step: (0, 0, 0, 0)),
            whole(sums.shape),
            whole((1, rank)),
            whole((1, slots)),
            whole((1, 2 * slots)),
        ],
        out_specs=in_hbm(),
        scratch_shapes=[
            pltpu.VMEM((2 * rank, features), jnp.bfloat16),
            pltpu.VMEM((2 * slots, features), jnp.bfloat16),
            pltpu.VMEM((2 * slots, rank), jnp.bfloat16),
            pltpu.VMEM((1, 2 * slots), jnp.float32),
            pltpu.VMEM((slots, features), jnp.bfloat16),
            pltpu.SemaphoreType.DMA((slots // OWNER_BLOCK,)),
        ],
        compiler_params=pltpu.CompilerParams(vmem_limit_bytes=VMEM_BYTES),
        cost_estimate=pl.CostEstimate(
            flops=2 * slots * features * (3 * rank + 4 * slots),
            bytes_accessed=8 * slots * width,
            transcendentals=2 * slots * slots,
        ),
        name="owner_maps",
    )(
        far,
        near,
        far,
        sums,
        marginal[None, :],
        src_labels[None, :],
        tgt_labels[None, :],
    )


def labels_of(clusters, owner, capacity, spread):
    rows = clusters.shape[1]
    mine = clusters // spread == owner
    before = (jnp.arange(rows)[:, None] < jnp.arange(rows)[None, :]).astype(jnp.bfloat16)
    earlier = jnp.dot(mine.astype(jnp.bfloat16), before, preferred_element_type=jnp.float32)
    ranking = jnp.where(mine, earlier.astype(jnp.int32), -1)
    value = clusters - owner * spread + 1
    hit = ranking[:, None, :] == jnp.arange(capacity, dtype=jnp.int32)[None, :, None]
    return jnp.sum(jnp.where(hit, value[:, None, :], 0), axis=2).reshape(-1)


def exchange(rows):
    return lax.all_to_all(rows, GROUP, split_axis=0, concat_axis=0, tiled=True)


def per_device(
    src_points, tgt_points, src_factor, tgt_factor, inner_marginal, src_cluster, tgt_cluster
):
    n_src, n_rest = lax.axis_size("src"), lax.axis_size(REST)
    n_group = n_src * n_rest
    n_dev = 2 * n_group
    rows, features = src_points.shape
    rank = src_factor.shape[1]
    capacity = 2 * (2 * rows // n_dev)
    spread = 2 * CL_DEV
    me = lax.axis_index(ALL)
    my_half = lax.axis_index(HALF)
    owner = lax.axis_index(GROUP)

    near, raw = near_pack(tgt_cluster, tgt_points, tgt_factor, n_group, capacity, spread)
    near, me = lax.optimization_barrier((near, me))
    near = exchange(near)
    raw = lax.ppermute(raw, HALF, [(0, 1), (1, 0)])
    own, other = partial_sums(
        me,
        src_cluster,
        tgt_cluster,
        src_points,
        tgt_points,
        src_factor,
        tgt_factor,
        n_dev,
        2 * n_rest,
    )
    chain = Chain(own, other, n_src, 2 * n_rest)
    for digit in chain.plane[1:]:
        chain.scatter(digit)
    late_cluster, chain.x = lax.optimization_barrier((src_cluster, chain.x))
    for digit in chain.along:
        chain.scatter(digit)
    for digit in reversed(chain.along):
        chain.gather(digit)
    far = far_pack(raw, late_cluster, src_points, src_factor, n_group, capacity, spread)
    far, near, chain.x = lax.optimization_barrier((far, near, chain.x))
    far = exchange(far)
    for digit in reversed(chain.plane):
        chain.gather(digit)
    sums = chain.x.reshape(n_dev, -1, rank)

    kept = 2 * features // n_dev
    table = sums[:, kept : kept + 2].astype(jnp.int32).reshape(n_src, 2, n_rest, 2, rows)
    near_table = lax.dynamic_index_in_dim(table, my_half, 1, keepdims=False)
    far_table = lax.dynamic_index_in_dim(table, 1 - my_half, 1, keepdims=False)
    near_table = near_table.reshape(n_group, 2, rows)
    far_table = far_table.reshape(n_group, 2, rows)
    src_labels = labels_of(near_table[:, 0], owner, capacity, spread)
    near_labels = labels_of(near_table[:, 1], owner, capacity, spread)
    far_labels = labels_of(far_table[:, 1], owner, capacity, spread)

    near = near.reshape(n_group, capacity, features + rank)
    far = far.reshape(n_group, 2, capacity, features + rank)
    tgt_labels = jnp.concatenate([near_labels, far_labels])
    images = owner_maps(near, far, sums, inner_marginal, src_labels, tgt_labels, features)
    returned = exchange(images)

    src_update, tgt_update = updates(
        src_points, tgt_points, src_factor, tgt_factor, inner_marginal, sums
    )
    slot = slot_row(src_cluster[None, :], n_group, capacity, spread, 0)
    back = slot.reshape(rows, 1) == jnp.arange(n_group * capacity, dtype=jnp.int32)[None, :]
    back = lax.optimization_barrier(back.astype(jnp.bfloat16))
    mapped = jnp.dot(back, returned, preferred_element_type=jnp.float32).astype(jnp.bfloat16)
    return (src_update, tgt_update, mapped)


def solution(mesh):
    n_src, n_tgt = mesh.shape["src"], mesh.shape["tgt"]
    halves = Mesh(mesh.devices.reshape(n_src, 2, n_tgt // 2), ALL)
    rows = P(ALL, None)
    return jax.shard_map(
        per_device,
        mesh=halves,
        in_specs=(rows, rows, rows, rows, P(), P(ALL), P(ALL)),
        out_specs=(rows, rows, rows),
        check_vma=False,
    )
```

```python
import functools

import jax
import jax.numpy as jnp
from jax import lax
from jax.experimental import pallas as pl
from jax.experimental.pallas import tpu as pltpu
from jax.sharding import PartitionSpec as P

CL_DEV = 2

GAMMA = 2.0
TEMPER = 0.03
EPS = 1e-06

ALL = ("src", "tgt")
VMEM_BYTES = 48 * 1024 * 1024
PACK_VMEM_BYTES = 62 * 1024 * 1024
TABLE_ROWS = 8
BLOCK_ROWS = 16
OWNER_BLOCK = 256


def contract_rows(left, right):
    return lax.dot_general(
        left, right, (((0,), (0,)), ((), ())), preferred_element_type=jnp.float32
    )


def contract_columns(left, right):
    return lax.dot_general(
        left, right, (((1,), (1,)), ((), ())), preferred_element_type=jnp.float32
    )


def mirror_step(points, total_round, factor, inner_marginal):
    gradient = -contract_columns(points, total_round) / inner_marginal
    row_scale = jnp.max(jnp.abs(gradient), axis=1, keepdims=True) + EPS
    tilted = factor.astype(jnp.float32) * jnp.exp(-GAMMA * gradient / row_scale)
    mean = jnp.mean(tilted, axis=1, keepdims=True)
    mean = jnp.where(mean > 0, mean, 1.0)
    return (tilted / mean).astype(jnp.bfloat16)


def inverse_norm(rows):
    return lax.rsqrt(jnp.sum(jnp.square(rows.astype(jnp.float32)), axis=1, keepdims=True) + EPS)


def blocks_of(n_dev, chunk, rank, features):
    kept = (chunk - TABLE_ROWS) // BLOCK_ROWS
    wide = features // rank
    return [
        (b // kept, b % kept * BLOCK_ROWS, b // wide * BLOCK_ROWS, b % wide * rank)
        for b in range(n_dev * kept)
    ]


def totals_of(sums_ref, total, features):
    n_dev, chunk, rank = sums_ref.shape
    for c, row, first, column in blocks_of(n_dev, chunk, rank, features):
        total[pl.ds(first, BLOCK_ROWS), pl.ds(column, rank)] = sums_ref[c, pl.ds(row, BLOCK_ROWS), :]


def whole(shape):
    return pl.BlockSpec(shape, lambda *_: (0,) * len(shape))


def in_hbm():
    return pl.BlockSpec(memory_space=pltpu.HBM)


def slot_row(cluster, n_group, capacity, spread, first):
    rows = cluster.shape[1]
    owners = cluster // spread
    onehot = owners == lax.broadcasted_iota(jnp.int32, (n_group, rows), 0)
    before = lax.broadcasted_iota(jnp.int32, (rows, rows), 0) < lax.broadcasted_iota(
        jnp.int32, (rows, rows), 1
    )
    earlier = jnp.dot(
        onehot.astype(jnp.bfloat16), before.astype(jnp.bfloat16), preferred_element_type=jnp.float32
    )
    ranking = jnp.sum(jnp.where(onehot, earlier, 0.0), axis=0, keepdims=True).astype(jnp.int32)
    return owners * capacity + ranking + first


def contract_kernel(n_dev, n_tgt, me_ref, src_cluster_ref, tgt_cluster_ref, *refs):
    hbm, (own_ref, other_ref), held, parts, in_sem = refs[:4], refs[4:6], refs[6:10], refs[10], refs[11]
    arrivals = [pltpu.make_async_copy(a, b, in_sem.at[i]) for i, (a, b) in enumerate(zip(hbm, held))]
    for copy in arrivals:
        copy.start()
    tgt_points, tgt_factor, src_points, src_factor = held
    _, _, _, chunk, rank = parts.shape
    kept = chunk - TABLE_ROWS
    me = me_ref[0]
    mine = (me // n_tgt) % 2
    row = lax.broadcasted_iota(jnp.int32, (TABLE_ROWS, rank), 0)
    table = jnp.where(row == 0, src_cluster_ref[...], jnp.where(row == 1, tgt_cluster_ref[...], 0))
    parts[:, :, :, kept:, :] = jnp.zeros(parts.shape[:3] + (TABLE_ROWS, rank), jnp.float32)
    parts[me // (2 * n_tgt), mine, me % n_tgt, kept:, :] = table.astype(jnp.float32)
    features = tgt_points.shape[1]
    blocks = blocks_of(n_dev, chunk, rank, features)
    for which, (points, factor) in enumerate(((tgt_points, tgt_factor), (src_points, src_factor))):
        arrivals[2 * which].wait()
        arrivals[2 * which + 1].wait()
        total = contract_rows(factor[...], points[...])
        for c, row, first, column in blocks:
            first -= which * rank
            if 0 <= first < rank:
                place = (c // (2 * n_tgt), c // n_tgt % 2, c % n_tgt)
                parts[(*place, pl.ds(row, BLOCK_ROWS))] = total[
                    first : first + BLOCK_ROWS, column : column + rank
                ]
    for i in range(parts.shape[0]):
        own_ref[i] = parts[i, mine]
        other_ref[i] = parts[i, 1 - mine].astype(jnp.bfloat16)


def partial_sums(
    me, src_cluster, tgt_cluster, src_points, tgt_points, src_factor, tgt_factor, n_dev, n_tgt
):
    rows, features = src_points.shape
    rank = src_factor.shape[1]
    chunk = 2 * features // n_dev + TABLE_ROWS
    shape = (n_dev // (2 * n_tgt), n_tgt, chunk, rank)
    vmem = pl.BlockSpec(memory_space=pltpu.VMEM)
    return pl.pallas_call(
        functools.partial(contract_kernel, n_dev, n_tgt),
        out_shape=(
            jax.ShapeDtypeStruct(shape, jnp.float32),
            jax.ShapeDtypeStruct(shape, jnp.bfloat16),
        ),
        in_specs=[pl.BlockSpec(memory_space=pltpu.SMEM)] + [vmem] * 2 + [in_hbm()] * 4,
        out_specs=(vmem, vmem),
        scratch_shapes=[
            pltpu.VMEM((rows, features), jnp.bfloat16),
            pltpu.VMEM((rows, rank), jnp.bfloat16),
            pltpu.VMEM((rows, features), jnp.bfloat16),
            pltpu.VMEM((rows, rank), jnp.bfloat16),
            pltpu.VMEM((n_dev // (2 * n_tgt), 2, n_tgt, chunk, rank), jnp.float32),
            pltpu.SemaphoreType.DMA((4,)),
        ],
        compiler_params=pltpu.CompilerParams(vmem_limit_bytes=PACK_VMEM_BYTES),
        cost_estimate=pl.CostEstimate(
            flops=4 * rows * features * rank,
            bytes_accessed=4 * rows * (features + rank) + 4 * n_dev * chunk * rank,
            transcendentals=0,
        ),
        name="partial_sums",
    )(me[None], src_cluster[None, :], tgt_cluster[None, :], tgt_points, tgt_factor, src_points, src_factor)


def place_rows(kinds, packed, packed_hbm, out_sem):
    block = 256
    departures = []
    for part in range(packed.shape[0] // block):
        mine = pl.ds(part * block, block)
        total = None
        for slot, held in kinds:
            index = lax.broadcasted_iota(jnp.int32, (block, slot.shape[1]), 0) + part * block
            place = (index == slot).astype(jnp.bfloat16)
            rows = [
                jnp.dot(place, array, preferred_element_type=jnp.float32) for array in held
            ]
            total = rows if total is None else [a + b for a, b in zip(total, rows)]
        column = 0
        for rows in total:
            packed[mine, column : column + rows.shape[1]] = rows.astype(jnp.bfloat16)
            column += rows.shape[1]
        departures.append(
            pltpu.make_async_copy(packed.at[mine], packed_hbm.at[mine], out_sem.at[part])
        )
        departures[-1].start()
    return departures


def pack_kernel(
    n_dev,
    capacity,
    cluster_ref,
    points_hbm,
    factor_hbm,
    packed_hbm,
    points,
    factor,
    packed,
    in_sem,
    out_sem,
):
    arrivals = [
        pltpu.make_async_copy(points_hbm, points, in_sem.at[0]),
        pltpu.make_async_copy(factor_hbm, factor, in_sem.at[1]),
    ]
    for copy in arrivals:
        copy.start()
    slot = slot_row(cluster_ref[...], n_dev, capacity, CL_DEV, 0)
    for copy in arrivals:
        copy.wait()
    for copy in place_rows([(slot, (points[...], factor[...]))], packed, packed_hbm, out_sem):
        copy.wait()


def pack(cluster, points, factor, n_dev, capacity):
    rows, features = points.shape
    rank = factor.shape[1]
    width = features + rank
    slots = n_dev * capacity
    return pl.pallas_call(
        functools.partial(pack_kernel, n_dev, capacity),
        out_shape=jax.ShapeDtypeStruct((slots, width), jnp.bfloat16),
        in_specs=[pl.BlockSpec(memory_space=pltpu.VMEM), in_hbm(), in_hbm()],
        out_specs=in_hbm(),
        scratch_shapes=[
            pltpu.VMEM((rows, features), jnp.bfloat16),
            pltpu.VMEM((rows, rank), jnp.bfloat16),
            pltpu.VMEM((slots, width), jnp.bfloat16),
            pltpu.SemaphoreType.DMA((2,)),
            pltpu.SemaphoreType.DMA((slots // 256,)),
        ],
        compiler_params=pltpu.CompilerParams(vmem_limit_bytes=PACK_VMEM_BYTES),
        cost_estimate=pl.CostEstimate(
            flops=2 * slots * rows * width,
            bytes_accessed=2 * (slots + rows) * width,
            transcendentals=0,
        ),
        name="pack_rows",
    )(cluster[None, :], points, factor)


def digits_of(size, stride):
    bits = size.bit_length() - 1
    found = []
    while bits:
        take = 1 if bits % 2 else 2
        found.append((stride, 1 << take))
        stride <<= take
        bits -= take
    return found


class Chain:
    def __init__(self, own, other, n_src, n_tgt):
        self.n_dev = n_src * n_tgt
        first = (n_tgt, 2)
        src, tgt = digits_of(n_src // 2, 2 * n_tgt), digits_of(n_tgt, 1)
        self.plane, self.along = [first] + src, tgt
        self.dims = src[::-1] + [first] + tgt[::-1]
        self.left = [d for d in self.dims if d != first]
        x = own + self.sent(other, n_tgt).astype(jnp.float32)
        self.x = x.reshape(tuple(radix for _, radix in self.left) + own.shape[2:])

    def sent(self, array, mask):
        return lax.ppermute(array, ALL, [(i, i ^ mask) for i in range(self.n_dev)])

    def scatter(self, digit):
        stride, radix = digit
        dim = self.left.index(digit)
        mine = (lax.axis_index(ALL) // stride) % radix
        total = lax.dynamic_index_in_dim(self.x, mine, dim, keepdims=False)
        for j in range(1, radix):
            piece = lax.dynamic_index_in_dim(self.x, mine ^ j, dim, keepdims=False)
            total = total + self.sent(piece.astype(jnp.bfloat16), j * stride).astype(jnp.float32)
        self.x = total
        self.left.remove(digit)

    def swap(self, digit):
        stride, radix = digit
        piece = self.x.astype(jnp.bfloat16)
        for j in range(1, radix):
            self.x = self.x + self.sent(piece, j * stride).astype(jnp.float32)

    def gather(self, digit):
        stride, radix = digit
        mine = (lax.axis_index(ALL) // stride) % radix
        x = self.x.astype(jnp.bfloat16)
        got = [x] + [self.sent(x, j * stride) for j in range(1, radix)]
        self.left = [d for d in self.dims if d in self.left or d == digit]
        self.x = jnp.stack(
            [lax.select_n(mine ^ d, *got) if radix > 2 else jnp.where(mine == d, *got) for d in range(radix)],
            axis=self.left.index(digit),
        )


def update_kernel(
    src_points_ref,
    tgt_points_ref,
    src_factor_ref,
    tgt_factor_ref,
    marginal_ref,
    sums_ref,
    src_ref,
    tgt_ref,
    total,
):
    totals_of(sums_ref, total, src_points_ref.shape[1])
    rank = src_ref.shape[1]
    marginal = marginal_ref[...]
    src_ref[...] = mirror_step(src_points_ref[...], total[:rank], src_factor_ref[...], marginal)
    tgt_ref[...] = mirror_step(tgt_points_ref[...], total[rank:], tgt_factor_ref[...], marginal)


def updates(src_points, tgt_points, src_factor, tgt_factor, marginal, sums):
    rows, features = src_points.shape
    rank = src_factor.shape[1]
    shape = jax.ShapeDtypeStruct(src_factor.shape, jnp.bfloat16)
    return pl.pallas_call(
        update_kernel,
        out_shape=(shape, shape),
        scratch_shapes=[pltpu.VMEM((2 * rank, features), jnp.bfloat16)],
        compiler_params=pltpu.CompilerParams(vmem_limit_bytes=VMEM_BYTES),
        cost_estimate=pl.CostEstimate(
            flops=4 * rows * features * rank,
            bytes_accessed=4 * rows * (features + 2 * rank),
            transcendentals=2 * rows * rank,
        ),
        name="mirror_updates",
    )(src_points, tgt_points, src_factor, tgt_factor, marginal[None, :], sums)


def seen_block(ref, part, block):
    piece = block // ref.shape[1]
    return ref[pl.ds(part * piece, piece)].reshape(block, ref.shape[2])


def owner_kernel(
    features,
    src_ref,
    tgt_ref,
    sums_ref,
    marginal_ref,
    src_label_ref,
    tgt_label_ref,
    out_hbm,
    total,
    tgt_rows,
    tgt_update,
    tgt_inv,
    images,
    out_sem,
):
    totals_of(sums_ref, total, features)
    slots = images.shape[0]
    rank = tgt_update.shape[1]
    marginal = marginal_ref[...]
    block = OWNER_BLOCK
    for part in range(slots // block):
        mine = pl.ds(part * block, block)
        both = seen_block(tgt_ref, part, block)
        rows = both[:, :features]
        tgt_rows[mine, :] = rows
        tgt_update[mine, :] = mirror_step(rows, total[rank:], both[:, features:], marginal)
        tgt_inv[:, mine] = inverse_norm(rows).reshape(1, block)

    departures = []
    for part in range(slots // block):
        mine = pl.ds(part * block, block)
        both = seen_block(src_ref, part, block)
        rows = both[:, :features]
        update = mirror_step(rows, total[:rank], both[:, features:], marginal)
        cosine = contract_columns(rows, tgt_rows[...]) * inverse_norm(rows) * tgt_inv[...]
        weight = contract_columns(update, tgt_update[...]) / rank
        label = src_label_ref[:, mine].reshape(block, 1)
        same = jnp.logical_and(label == tgt_label_ref[...], label > 0)
        kernel = jnp.where(same, weight * jnp.exp((cosine - 1.0) / TEMPER), 0.0)
        denominator = jnp.sum(kernel, axis=1, keepdims=True)
        denominator = jnp.where(denominator > 0, denominator, 1.0)
        transport = (kernel / denominator).astype(jnp.bfloat16)
        images[mine, :] = jnp.dot(
            transport, tgt_rows[...], preferred_element_type=jnp.float32
        ).astype(jnp.bfloat16)
        departures.append(
            pltpu.make_async_copy(images.at[mine], out_hbm.at[mine], out_sem.at[part])
        )
        departures[-1].start()
    for copy in departures:
        copy.wait()


def owner_maps(src, tgt, sums, marginal, src_labels, tgt_labels, features):
    n_dev, capacity, width = src.shape
    slots = n_dev * capacity
    rank = width - features
    return pl.pallas_call(
        functools.partial(owner_kernel, features),
        out_shape=jax.ShapeDtypeStruct((slots, features), jnp.bfloat16),
        grid=(1,),
        in_specs=[
            whole(src.shape),
            whole(tgt.shape),
            whole(sums.shape),
            whole((1, rank)),
            whole((1, slots)),
            whole((1, slots)),
        ],
        out_specs=in_hbm(),
        scratch_shapes=[
            pltpu.VMEM((2 * rank, features), jnp.bfloat16),
            pltpu.VMEM((slots, features), jnp.bfloat16),
            pltpu.VMEM((slots, rank), jnp.bfloat16),
            pltpu.VMEM((1, slots), jnp.float32),
            pltpu.VMEM((slots, features), jnp.bfloat16),
            pltpu.SemaphoreType.DMA((slots // OWNER_BLOCK,)),
        ],
        compiler_params=pltpu.CompilerParams(vmem_limit_bytes=VMEM_BYTES),
        cost_estimate=pl.CostEstimate(
            flops=4 * slots * features * (rank + slots),
            bytes_accessed=6 * slots * width,
            transcendentals=slots * slots,
        ),
        name="owner_maps",
    )(src, tgt, sums, marginal[None, :], src_labels[None, :], tgt_labels[None, :])


def labels_of(clusters, owner, capacity, spread):
    rows = clusters.shape[1]
    mine = clusters // spread == owner
    before = (jnp.arange(rows)[:, None] < jnp.arange(rows)[None, :]).astype(jnp.bfloat16)
    earlier = jnp.dot(mine.astype(jnp.bfloat16), before, preferred_element_type=jnp.float32)
    ranking = jnp.where(mine, earlier.astype(jnp.int32), -1)
    value = clusters - owner * spread + 1
    hit = ranking[:, None, :] == jnp.arange(capacity, dtype=jnp.int32)[None, :, None]
    return jnp.sum(jnp.where(hit, value[:, None, :], 0), axis=2).reshape(-1)


def exchange(rows):
    return lax.all_to_all(rows, ALL, split_axis=0, concat_axis=0, tiled=True)


def per_device(
    src_points, tgt_points, src_factor, tgt_factor, inner_marginal, src_cluster, tgt_cluster
):
    n_src, n_tgt = lax.axis_size("src"), lax.axis_size("tgt")
    n_dev = n_src * n_tgt
    rows, features = src_points.shape
    rank = src_factor.shape[1]
    capacity = 2 * rows // n_dev
    owner = lax.axis_index(ALL)

    tgt = pack(tgt_cluster, tgt_points, tgt_factor, n_dev, capacity)
    tgt, me = lax.optimization_barrier((tgt, owner))
    tgt = exchange(tgt)
    own, other = partial_sums(
        me,
        src_cluster,
        tgt_cluster,
        src_points,
        tgt_points,
        src_factor,
        tgt_factor,
        n_dev,
        n_tgt,
    )
    chain = Chain(own, other, n_src, n_tgt)
    for digit in chain.plane[1:]:
        chain.scatter(digit)
    for digit in chain.along:
        chain.swap(digit)
    src = pack(src_cluster, src_points, src_factor, n_dev, capacity)
    src, tgt, chain.x = lax.optimization_barrier((src, tgt, chain.x))
    src = exchange(src)
    for digit in reversed(chain.plane):
        chain.gather(digit)
    sums = chain.x.reshape(n_dev, -1, rank)

    kept = 2 * features // n_dev
    table = sums[:, kept : kept + 2].astype(jnp.int32)
    src_labels = labels_of(table[:, 0], owner, capacity, CL_DEV)
    tgt_labels = labels_of(table[:, 1], owner, capacity, CL_DEV)

    shape = (n_dev, capacity, features + rank)
    images = owner_maps(
        src.reshape(shape), tgt.reshape(shape), sums, inner_marginal, src_labels, tgt_labels, features
    )
    returned = exchange(images)

    src_update, tgt_update = updates(
        src_points, tgt_points, src_factor, tgt_factor, inner_marginal, sums
    )
    slot = slot_row(src_cluster[None, :], n_dev, capacity, CL_DEV, 0)
    back = slot.reshape(rows, 1) == jnp.arange(n_dev * capacity, dtype=jnp.int32)[None, :]
    back = lax.optimization_barrier(back.astype(jnp.bfloat16))
    mapped = jnp.dot(back, returned, preferred_element_type=jnp.float32).astype(jnp.bfloat16)
    return (src_update, tgt_update, mapped)


def solution(mesh):
    rows = P(ALL, None)
    return jax.shard_map(
        per_device,
        mesh=mesh,
        in_specs=(rows, rows, rows, rows, P(), P(ALL), P(ALL)),
        out_specs=(rows, rows, rows),
        check_vma=False,
    )
```

```python
import functools

import jax
import jax.numpy as jnp
from jax import lax
from jax.experimental import pallas as pl
from jax.experimental.pallas import tpu as pltpu
from jax.sharding import PartitionSpec as P

CL_DEV = 2

GAMMA = 2.0
TEMPER = 0.03
EPS = 1e-06

ALL = ("src", "tgt")
VMEM_BYTES = 48 * 1024 * 1024
PACK_VMEM_BYTES = 62 * 1024 * 1024
TABLE_ROWS = 8
BLOCK_ROWS = 16
OWNER_BLOCK = 256


def contract_rows(left, right):
    return lax.dot_general(
        left, right, (((0,), (0,)), ((), ())), preferred_element_type=jnp.float32
    )


def contract_columns(left, right):
    return lax.dot_general(
        left, right, (((1,), (1,)), ((), ())), preferred_element_type=jnp.float32
    )


def mirror_step(points, total_round, factor, inner_marginal):
    gradient = contract_columns(points, total_round) * (-1.0 / inner_marginal)
    row_scale = jnp.max(jnp.abs(gradient), axis=1, keepdims=True) + EPS
    tilted = factor.astype(jnp.float32) * jnp.exp(gradient * (-GAMMA / row_scale))
    mean = jnp.mean(tilted, axis=1, keepdims=True)
    mean = jnp.where(mean > 0, mean, 1.0)
    return (tilted * (1.0 / mean)).astype(jnp.bfloat16)


def inverse_norm(rows):
    return lax.rsqrt(jnp.sum(jnp.square(rows.astype(jnp.float32)), axis=1, keepdims=True) + EPS)


def blocks_of(n_dev, chunk, rank, features):
    kept = (chunk - TABLE_ROWS) // BLOCK_ROWS
    wide = features // rank
    return [
        (b // kept, b % kept * BLOCK_ROWS, b // wide * BLOCK_ROWS, b % wide * rank)
        for b in range(n_dev * kept)
    ]


def totals_of(sums_ref, total, features):
    n_dev, chunk, rank = sums_ref.shape
    for c, row, first, column in blocks_of(n_dev, chunk, rank, features):
        total[pl.ds(first, BLOCK_ROWS), pl.ds(column, rank)] = sums_ref[c, pl.ds(row, BLOCK_ROWS), :]


def whole(shape):
    return pl.BlockSpec(shape, lambda *_: (0,) * len(shape))


def in_hbm():
    return pl.BlockSpec(memory_space=pltpu.HBM)


def slot_row(cluster, n_group, capacity, spread, first):
    rows = cluster.shape[1]
    owners = cluster // spread
    onehot = owners == lax.broadcasted_iota(jnp.int32, (n_group, rows), 0)
    before = lax.broadcasted_iota(jnp.int32, (rows, rows), 0) < lax.broadcasted_iota(
        jnp.int32, (rows, rows), 1
    )
    earlier = jnp.dot(
        onehot.astype(jnp.bfloat16), before.astype(jnp.bfloat16), preferred_element_type=jnp.float32
    )
    ranking = jnp.sum(jnp.where(onehot, earlier, 0.0), axis=0, keepdims=True).astype(jnp.int32)
    return owners * capacity + ranking + first


def contract_kernel(n_dev, n_tgt, me_ref, src_cluster_ref, tgt_cluster_ref, *refs):
    hbm, (own_ref, other_ref), held, parts, in_sem = refs[:4], refs[4:6], refs[6:10], refs[10], refs[11]
    arrivals = [pltpu.make_async_copy(a, b, in_sem.at[i]) for i, (a, b) in enumerate(zip(hbm, held))]
    for copy in arrivals:
        copy.start()
    tgt_points, tgt_factor, src_points, src_factor = held
    _, _, _, chunk, rank = parts.shape
    kept = chunk - TABLE_ROWS
    me = me_ref[0]
    mine = (me // n_tgt) % 2
    row = lax.broadcasted_iota(jnp.int32, (TABLE_ROWS, rank), 0)
    table = jnp.where(row == 0, src_cluster_ref[...], jnp.where(row == 1, tgt_cluster_ref[...], 0))
    parts[:, :, :, kept:, :] = jnp.zeros(parts.shape[:3] + (TABLE_ROWS, rank), jnp.float32)
    parts[me // (2 * n_tgt), mine, me % n_tgt, kept:, :] = table.astype(jnp.float32)
    features = tgt_points.shape[1]
    blocks = blocks_of(n_dev, chunk, rank, features)
    for which, (points, factor) in enumerate(((tgt_points, tgt_factor), (src_points, src_factor))):
        arrivals[2 * which].wait()
        arrivals[2 * which + 1].wait()
        total = contract_rows(factor[...], points[...])
        for c, row, first, column in blocks:
            first -= which * rank
            if 0 <= first < rank:
                place = (c // (2 * n_tgt), c // n_tgt % 2, c % n_tgt)
                parts[(*place, pl.ds(row, BLOCK_ROWS))] = total[
                    first : first + BLOCK_ROWS, column : column + rank
                ]
    for i in range(parts.shape[0]):
        own_ref[i] = parts[i, mine]
        other_ref[i] = parts[i, 1 - mine].astype(jnp.bfloat16)


def partial_sums(
    me, src_cluster, tgt_cluster, src_points, tgt_points, src_factor, tgt_factor, n_dev, n_tgt
):
    rows, features = src_points.shape
    rank = src_factor.shape[1]
    chunk = 2 * features // n_dev + TABLE_ROWS
    shape = (n_dev // (2 * n_tgt), n_tgt, chunk, rank)
    vmem = pl.BlockSpec(memory_space=pltpu.VMEM)
    return pl.pallas_call(
        functools.partial(contract_kernel, n_dev, n_tgt),
        out_shape=(
            jax.ShapeDtypeStruct(shape, jnp.float32),
            jax.ShapeDtypeStruct(shape, jnp.bfloat16),
        ),
        in_specs=[pl.BlockSpec(memory_space=pltpu.SMEM)] + [vmem] * 2 + [in_hbm()] * 4,
        out_specs=(vmem, vmem),
        scratch_shapes=[
            pltpu.VMEM((rows, features), jnp.bfloat16),
            pltpu.VMEM((rows, rank), jnp.bfloat16),
            pltpu.VMEM((rows, features), jnp.bfloat16),
            pltpu.VMEM((rows, rank), jnp.bfloat16),
            pltpu.VMEM((n_dev // (2 * n_tgt), 2, n_tgt, chunk, rank), jnp.float32),
            pltpu.SemaphoreType.DMA((4,)),
        ],
        compiler_params=pltpu.CompilerParams(vmem_limit_bytes=PACK_VMEM_BYTES),
        cost_estimate=pl.CostEstimate(
            flops=4 * rows * features * rank,
            bytes_accessed=4 * rows * (features + rank) + 4 * n_dev * chunk * rank,
            transcendentals=0,
        ),
        name="partial_sums",
    )(me[None], src_cluster[None, :], tgt_cluster[None, :], tgt_points, tgt_factor, src_points, src_factor)


def place_rows(kinds, packed, packed_hbm, out_sem):
    block = 256
    departures = []
    for part in range(packed.shape[0] // block):
        mine = pl.ds(part * block, block)
        total = None
        for slot, held in kinds:
            index = lax.broadcasted_iota(jnp.int32, (block, slot.shape[1]), 0) + part * block
            place = (index == slot).astype(jnp.bfloat16)
            rows = [
                jnp.dot(place, array, preferred_element_type=jnp.float32) for array in held
            ]
            total = rows if total is None else [a + b for a, b in zip(total, rows)]
        column = 0
        for rows in total:
            packed[mine, column : column + rows.shape[1]] = rows.astype(jnp.bfloat16)
            column += rows.shape[1]
        departures.append(
            pltpu.make_async_copy(packed.at[mine], packed_hbm.at[mine], out_sem.at[part])
        )
        departures[-1].start()
    return departures


def pack_kernel(
    n_dev,
    capacity,
    cluster_ref,
    points_hbm,
    factor_hbm,
    packed_hbm,
    points,
    factor,
    packed,
    in_sem,
    out_sem,
):
    arrivals = [
        pltpu.make_async_copy(points_hbm, points, in_sem.at[0]),
        pltpu.make_async_copy(factor_hbm, factor, in_sem.at[1]),
    ]
    for copy in arrivals:
        copy.start()
    slot = slot_row(cluster_ref[...], n_dev, capacity, CL_DEV, 0)
    for copy in arrivals:
        copy.wait()
    for copy in place_rows([(slot, (points[...], factor[...]))], packed, packed_hbm, out_sem):
        copy.wait()


def pack(cluster, points, factor, n_dev, capacity):
    rows, features = points.shape
    rank = factor.shape[1]
    width = features + rank
    slots = n_dev * capacity
    return pl.pallas_call(
        functools.partial(pack_kernel, n_dev, capacity),
        out_shape=jax.ShapeDtypeStruct((slots, width), jnp.bfloat16),
        in_specs=[pl.BlockSpec(memory_space=pltpu.VMEM), in_hbm(), in_hbm()],
        out_specs=in_hbm(),
        scratch_shapes=[
            pltpu.VMEM((rows, features), jnp.bfloat16),
            pltpu.VMEM((rows, rank), jnp.bfloat16),
            pltpu.VMEM((slots, width), jnp.bfloat16),
            pltpu.SemaphoreType.DMA((2,)),
            pltpu.SemaphoreType.DMA((slots // 256,)),
        ],
        compiler_params=pltpu.CompilerParams(vmem_limit_bytes=PACK_VMEM_BYTES),
        cost_estimate=pl.CostEstimate(
            flops=2 * slots * rows * width,
            bytes_accessed=2 * (slots + rows) * width,
            transcendentals=0,
        ),
        name="pack_rows",
    )(cluster[None, :], points, factor)


def digits_of(size, stride):
    bits = size.bit_length() - 1
    found = []
    while bits:
        take = 1 if bits % 2 else 2
        found.append((stride, 1 << take))
        stride <<= take
        bits -= take
    return found


class Chain:
    def __init__(self, own, other, n_src, n_tgt):
        self.n_dev = n_src * n_tgt
        first = (n_tgt, 2)
        src, tgt = digits_of(n_src // 2, 2 * n_tgt), digits_of(n_tgt, 1)
        self.plane, self.along = [first] + src, tgt
        self.dims = src[::-1] + [first] + tgt[::-1]
        self.left = [d for d in self.dims if d != first]
        x = own + self.sent(other, n_tgt).astype(jnp.float32)
        self.x = x.reshape(tuple(radix for _, radix in self.left) + own.shape[2:])

    def sent(self, array, mask):
        return lax.ppermute(array, ALL, [(i, i ^ mask) for i in range(self.n_dev)])

    def scatter(self, digit):
        stride, radix = digit
        dim = self.left.index(digit)
        mine = (lax.axis_index(ALL) // stride) % radix
        total = lax.dynamic_index_in_dim(self.x, mine, dim, keepdims=False)
        for j in range(1, radix):
            piece = lax.dynamic_index_in_dim(self.x, mine ^ j, dim, keepdims=False)
            total = total + self.sent(piece.astype(jnp.bfloat16), j * stride).astype(jnp.float32)
        self.x = total
        self.left.remove(digit)

    def gather(self, digit):
        stride, radix = digit
        mine = (lax.axis_index(ALL) // stride) % radix
        x = self.x.astype(jnp.bfloat16)
        got = [x] + [self.sent(x, j * stride) for j in range(1, radix)]
        self.left = [d for d in self.dims if d in self.left or d == digit]
        self.x = jnp.stack(
            [lax.select_n(mine ^ d, *got) if radix > 2 else jnp.where(mine == d, *got) for d in range(radix)],
            axis=self.left.index(digit),
        )


def update_kernel(
    src_points_ref,
    tgt_points_ref,
    src_factor_ref,
    tgt_factor_ref,
    marginal_ref,
    sums_ref,
    src_ref,
    tgt_ref,
    total,
):
    totals_of(sums_ref, total, src_points_ref.shape[1])
    rank = src_ref.shape[1]
    marginal = marginal_ref[...]
    src_ref[...] = mirror_step(src_points_ref[...], total[:rank], src_factor_ref[...], marginal)
    tgt_ref[...] = mirror_step(tgt_points_ref[...], total[rank:], tgt_factor_ref[...], marginal)


def updates(src_points, tgt_points, src_factor, tgt_factor, marginal, sums):
    rows, features = src_points.shape
    rank = src_factor.shape[1]
    shape = jax.ShapeDtypeStruct(src_factor.shape, jnp.bfloat16)
    return pl.pallas_call(
        update_kernel,
        out_shape=(shape, shape),
        scratch_shapes=[pltpu.VMEM((2 * rank, features), jnp.bfloat16)],
        compiler_params=pltpu.CompilerParams(vmem_limit_bytes=VMEM_BYTES),
        cost_estimate=pl.CostEstimate(
            flops=4 * rows * features * rank,
            bytes_accessed=4 * rows * (features + 2 * rank),
            transcendentals=2 * rows * rank,
        ),
        name="mirror_updates",
    )(src_points, tgt_points, src_factor, tgt_factor, marginal[None, :], sums)


def seen_block(ref, part, block):
    piece = block // ref.shape[1]
    return ref[pl.ds(part * piece, piece)].reshape(block, ref.shape[2])


def owner_kernel(
    features,
    src_ref,
    tgt_ref,
    sums_ref,
    marginal_ref,
    src_label_ref,
    tgt_label_ref,
    out_hbm,
    total,
    tgt_rows,
    tgt_update,
    tgt_inv,
    images,
    out_sem,
):
    totals_of(sums_ref, total, features)
    slots = images.shape[0]
    rank = tgt_update.shape[1]
    marginal = marginal_ref[...]
    block = OWNER_BLOCK
    for part in range(slots // block):
        mine = pl.ds(part * block, block)
        both = seen_block(tgt_ref, part, block)
        rows = both[:, :features]
        tgt_rows[mine, :] = rows
        tgt_update[mine, :] = mirror_step(rows, total[rank:], both[:, features:], marginal)
        tgt_inv[:, mine] = inverse_norm(rows).reshape(1, block)

    departures = []
    for part in range(slots // block):
        mine = pl.ds(part * block, block)
        both = seen_block(src_ref, part, block)
        rows = both[:, :features]
        update = mirror_step(rows, total[:rank], both[:, features:], marginal)
        cosine = contract_columns(rows, tgt_rows[...]) * inverse_norm(rows) * tgt_inv[...]
        weight = contract_columns(update, tgt_update[...]) * (1.0 / rank)
        label = src_label_ref[:, mine].reshape(block, 1)
        same = jnp.logical_and(label == tgt_label_ref[...], label > 0)
        kernel = jnp.where(same, weight * jnp.exp((cosine - 1.0) * (1.0 / TEMPER)), 0.0)
        denominator = jnp.sum(kernel, axis=1, keepdims=True)
        denominator = jnp.where(denominator > 0, denominator, 1.0)
        transport = (kernel * (1.0 / denominator)).astype(jnp.bfloat16)
        images[mine, :] = jnp.dot(
            transport, tgt_rows[...], preferred_element_type=jnp.float32
        ).astype(jnp.bfloat16)
        departures.append(
            pltpu.make_async_copy(images.at[mine], out_hbm.at[mine], out_sem.at[part])
        )
        departures[-1].start()
    for copy in departures:
        copy.wait()


def owner_maps(src, tgt, sums, marginal, src_labels, tgt_labels, features):
    n_dev, capacity, width = src.shape
    slots = n_dev * capacity
    rank = width - features
    return pl.pallas_call(
        functools.partial(owner_kernel, features),
        out_shape=jax.ShapeDtypeStruct((slots, features), jnp.bfloat16),
        grid=(1,),
        in_specs=[
            whole(src.shape),
            whole(tgt.shape),
            whole(sums.shape),
            whole((1, rank)),
            whole((1, slots)),
            whole((1, slots)),
        ],
        out_specs=in_hbm(),
        scratch_shapes=[
            pltpu.VMEM((2 * rank, features), jnp.bfloat16),
            pltpu.VMEM((slots, features), jnp.bfloat16),
            pltpu.VMEM((slots, rank), jnp.bfloat16),
            pltpu.VMEM((1, slots), jnp.float32),
            pltpu.VMEM((slots, features), jnp.bfloat16),
            pltpu.SemaphoreType.DMA((slots // OWNER_BLOCK,)),
        ],
        compiler_params=pltpu.CompilerParams(vmem_limit_bytes=VMEM_BYTES),
        cost_estimate=pl.CostEstimate(
            flops=4 * slots * features * (rank + slots),
            bytes_accessed=6 * slots * width,
            transcendentals=slots * slots,
        ),
        name="owner_maps",
    )(src, tgt, sums, marginal[None, :], src_labels[None, :], tgt_labels[None, :])


def labels_of(clusters, owner, capacity, spread):
    rows = clusters.shape[1]
    mine = clusters // spread == owner
    before = (jnp.arange(rows)[:, None] < jnp.arange(rows)[None, :]).astype(jnp.bfloat16)
    earlier = jnp.dot(mine.astype(jnp.bfloat16), before, preferred_element_type=jnp.float32)
    ranking = jnp.where(mine, earlier.astype(jnp.int32), -1)
    value = clusters - owner * spread + 1
    hit = ranking[:, None, :] == jnp.arange(capacity, dtype=jnp.int32)[None, :, None]
    return jnp.sum(jnp.where(hit, value[:, None, :], 0), axis=2).reshape(-1)


def exchange(rows):
    return lax.all_to_all(rows, ALL, split_axis=0, concat_axis=0, tiled=True)


def per_device(
    src_points, tgt_points, src_factor, tgt_factor, inner_marginal, src_cluster, tgt_cluster
):
    n_src, n_tgt = lax.axis_size("src"), lax.axis_size("tgt")
    n_dev = n_src * n_tgt
    rows, features = src_points.shape
    rank = src_factor.shape[1]
    capacity = 2 * rows // n_dev
    owner = lax.axis_index(ALL)

    tgt = pack(tgt_cluster, tgt_points, tgt_factor, n_dev, capacity)
    tgt, me = lax.optimization_barrier((tgt, owner))
    tgt = exchange(tgt)
    own, other = partial_sums(
        me,
        src_cluster,
        tgt_cluster,
        src_points,
        tgt_points,
        src_factor,
        tgt_factor,
        n_dev,
        n_tgt,
    )
    chain = Chain(own, other, n_src, n_tgt)
    for digit in chain.plane[1:]:
        chain.scatter(digit)
    for digit in chain.along:
        chain.scatter(digit)
    src = pack(src_cluster, src_points, src_factor, n_dev, capacity)
    src, tgt, chain.x = lax.optimization_barrier((src, tgt, chain.x))
    src = exchange(src)
    for digit in reversed(chain.plane + chain.along):
        chain.gather(digit)
    sums = chain.x.reshape(n_dev, -1, rank)

    kept = 2 * features // n_dev
    table = sums[:, kept : kept + 2].astype(jnp.int32)
    src_labels = labels_of(table[:, 0], owner, capacity, CL_DEV)
    tgt_labels = labels_of(table[:, 1], owner, capacity, CL_DEV)

    shape = (n_dev, capacity, features + rank)
    images = owner_maps(
        src.reshape(shape), tgt.reshape(shape), sums, inner_marginal, src_labels, tgt_labels, features
    )
    returned = exchange(images)

    src_update, tgt_update = updates(
        src_points, tgt_points, src_factor, tgt_factor, inner_marginal, sums
    )
    slot = slot_row(src_cluster[None, :], n_dev, capacity, CL_DEV, 0)
    back = slot.reshape(rows, 1) == jnp.arange(n_dev * capacity, dtype=jnp.int32)[None, :]
    back = lax.optimization_barrier(back.astype(jnp.bfloat16))
    mapped = jnp.dot(back, returned, preferred_element_type=jnp.float32).astype(jnp.bfloat16)
    return (src_update, tgt_update, mapped)


def solution(mesh):
    rows = P(ALL, None)
    return jax.shard_map(
        per_device,
        mesh=mesh,
        in_specs=(rows, rows, rows, rows, P(), P(ALL), P(ALL)),
        out_specs=(rows, rows, rows),
        check_vma=False,
    )
```

```python
import functools

import jax
import jax.numpy as jnp
from jax import lax
from jax.experimental import pallas as pl
from jax.experimental.pallas import tpu as pltpu
from jax.sharding import PartitionSpec as P

CL_DEV = 2

GAMMA = 2.0
TEMPER = 0.03
EPS = 1e-06

ALL = ("src", "tgt")
VMEM_BYTES = 48 * 1024 * 1024
PACK_VMEM_BYTES = 62 * 1024 * 1024
TABLE_ROWS = 8
BLOCK_ROWS = 16
OWNER_BLOCK = 256


def contract_rows(left, right):
    return lax.dot_general(
        left, right, (((0,), (0,)), ((), ())), preferred_element_type=jnp.float32
    )


def contract_columns(left, right):
    return lax.dot_general(
        left, right, (((1,), (1,)), ((), ())), preferred_element_type=jnp.float32
    )


def mirror_step(points, total_round, factor, inner_marginal):
    gradient = contract_columns(points, total_round) * (-1.0 / inner_marginal)
    row_scale = jnp.max(jnp.abs(gradient), axis=1, keepdims=True) + EPS
    tilted = factor.astype(jnp.float32) * jnp.exp(gradient * (-GAMMA / row_scale))
    mean = jnp.mean(tilted, axis=1, keepdims=True)
    mean = jnp.where(mean > 0, mean, 1.0)
    return (tilted * (1.0 / mean)).astype(jnp.bfloat16)


def inverse_norm(rows):
    return lax.rsqrt(jnp.sum(jnp.square(rows.astype(jnp.float32)), axis=1, keepdims=True) + EPS)


def blocks_of(n_dev, chunk, rank, features):
    kept = (chunk - TABLE_ROWS) // BLOCK_ROWS
    wide = features // rank
    return [
        (b // kept, b % kept * BLOCK_ROWS, b // wide * BLOCK_ROWS, b % wide * rank)
        for b in range(n_dev * kept)
    ]


def totals_of(sums_ref, total, features):
    n_dev, chunk, rank = sums_ref.shape
    for c, row, first, column in blocks_of(n_dev, chunk, rank, features):
        total[pl.ds(first, BLOCK_ROWS), pl.ds(column, rank)] = sums_ref[c, pl.ds(row, BLOCK_ROWS), :]


def whole(shape):
    return pl.BlockSpec(shape, lambda *_: (0,) * len(shape))


def in_hbm():
    return pl.BlockSpec(memory_space=pltpu.HBM)


def slot_row(cluster, n_group, capacity, spread, first):
    rows = cluster.shape[1]
    owners = cluster // spread
    onehot = owners == lax.broadcasted_iota(jnp.int32, (n_group, rows), 0)
    before = lax.broadcasted_iota(jnp.int32, (rows, rows), 0) < lax.broadcasted_iota(
        jnp.int32, (rows, rows), 1
    )
    earlier = jnp.dot(
        onehot.astype(jnp.bfloat16), before.astype(jnp.bfloat16), preferred_element_type=jnp.float32
    )
    ranking = jnp.sum(jnp.where(onehot, earlier, 0.0), axis=0, keepdims=True).astype(jnp.int32)
    return owners * capacity + ranking + first


def contract_kernel(n_dev, n_tgt, me_ref, src_cluster_ref, tgt_cluster_ref, *refs):
    hbm, (own_ref, other_ref), held, parts, in_sem = refs[:4], refs[4:6], refs[6:10], refs[10], refs[11]
    arrivals = [pltpu.make_async_copy(a, b, in_sem.at[i]) for i, (a, b) in enumerate(zip(hbm, held))]
    for copy in arrivals:
        copy.start()
    tgt_points, tgt_factor, src_points, src_factor = held
    _, _, _, chunk, rank = parts.shape
    kept = chunk - TABLE_ROWS
    me = me_ref[0]
    mine = (me // n_tgt) % 2
    row = lax.broadcasted_iota(jnp.int32, (TABLE_ROWS, rank), 0)
    table = jnp.where(row == 0, src_cluster_ref[...], jnp.where(row == 1, tgt_cluster_ref[...], 0))
    parts[:, :, :, kept:, :] = jnp.zeros(parts.shape[:3] + (TABLE_ROWS, rank), jnp.float32)
    parts[me // (2 * n_tgt), mine, me % n_tgt, kept:, :] = table.astype(jnp.float32)
    features = tgt_points.shape[1]
    blocks = blocks_of(n_dev, chunk, rank, features)
    for which, (points, factor) in enumerate(((tgt_points, tgt_factor), (src_points, src_factor))):
        arrivals[2 * which].wait()
        arrivals[2 * which + 1].wait()
        total = contract_rows(factor[...], points[...])
        for c, row, first, column in blocks:
            first -= which * rank
            if 0 <= first < rank:
                place = (c // (2 * n_tgt), c // n_tgt % 2, c % n_tgt)
                parts[(*place, pl.ds(row, BLOCK_ROWS))] = total[
                    first : first + BLOCK_ROWS, column : column + rank
                ]
    for i in range(parts.shape[0]):
        own_ref[i] = parts[i, mine]
        other_ref[i] = parts[i, 1 - mine].astype(jnp.bfloat16)


def partial_sums(
    me, src_cluster, tgt_cluster, src_points, tgt_points, src_factor, tgt_factor, n_dev, n_tgt
):
    rows, features = src_points.shape
    rank = src_factor.shape[1]
    chunk = 2 * features // n_dev + TABLE_ROWS
    shape = (n_dev // (2 * n_tgt), n_tgt, chunk, rank)
    vmem = pl.BlockSpec(memory_space=pltpu.VMEM)
    return pl.pallas_call(
        functools.partial(contract_kernel, n_dev, n_tgt),
        out_shape=(
            jax.ShapeDtypeStruct(shape, jnp.float32),
            jax.ShapeDtypeStruct(shape, jnp.bfloat16),
        ),
        in_specs=[pl.BlockSpec(memory_space=pltpu.SMEM)] + [vmem] * 2 + [in_hbm()] * 4,
        out_specs=(vmem, vmem),
        scratch_shapes=[
            pltpu.VMEM((rows, features), jnp.bfloat16),
            pltpu.VMEM((rows, rank), jnp.bfloat16),
            pltpu.VMEM((rows, features), jnp.bfloat16),
            pltpu.VMEM((rows, rank), jnp.bfloat16),
            pltpu.VMEM((n_dev // (2 * n_tgt), 2, n_tgt, chunk, rank), jnp.float32),
            pltpu.SemaphoreType.DMA((4,)),
        ],
        compiler_params=pltpu.CompilerParams(vmem_limit_bytes=PACK_VMEM_BYTES),
        cost_estimate=pl.CostEstimate(
            flops=4 * rows * features * rank,
            bytes_accessed=4 * rows * (features + rank) + 4 * n_dev * chunk * rank,
            transcendentals=0,
        ),
        name="partial_sums",
    )(me[None], src_cluster[None, :], tgt_cluster[None, :], tgt_points, tgt_factor, src_points, src_factor)


def place_rows(kinds, packed, packed_hbm, out_sem):
    block = 256
    departures = []
    for part in range(packed.shape[0] // block):
        mine = pl.ds(part * block, block)
        total = None
        for slot, held in kinds:
            index = lax.broadcasted_iota(jnp.int32, (block, slot.shape[1]), 0) + part * block
            place = (index == slot).astype(jnp.bfloat16)
            rows = [
                jnp.dot(place, array, preferred_element_type=jnp.float32) for array in held
            ]
            total = rows if total is None else [a + b for a, b in zip(total, rows)]
        column = 0
        for rows in total:
            packed[mine, column : column + rows.shape[1]] = rows.astype(jnp.bfloat16)
            column += rows.shape[1]
        departures.append(
            pltpu.make_async_copy(packed.at[mine], packed_hbm.at[mine], out_sem.at[part])
        )
        departures[-1].start()
    return departures


def pack_kernel(
    n_dev,
    capacity,
    cluster_ref,
    points_hbm,
    factor_hbm,
    packed_hbm,
    points,
    factor,
    packed,
    in_sem,
    out_sem,
):
    arrivals = [
        pltpu.make_async_copy(points_hbm, points, in_sem.at[0]),
        pltpu.make_async_copy(factor_hbm, factor, in_sem.at[1]),
    ]
    for copy in arrivals:
        copy.start()
    slot = slot_row(cluster_ref[...], n_dev, capacity, CL_DEV, 0)
    for copy in arrivals:
        copy.wait()
    for copy in place_rows([(slot, (points[...], factor[...]))], packed, packed_hbm, out_sem):
        copy.wait()


def pack(cluster, points, factor, n_dev, capacity):
    rows, features = points.shape
    rank = factor.shape[1]
    width = features + rank
    slots = n_dev * capacity
    return pl.pallas_call(
        functools.partial(pack_kernel, n_dev, capacity),
        out_shape=jax.ShapeDtypeStruct((slots, width), jnp.bfloat16),
        in_specs=[pl.BlockSpec(memory_space=pltpu.VMEM), in_hbm(), in_hbm()],
        out_specs=in_hbm(),
        scratch_shapes=[
            pltpu.VMEM((rows, features), jnp.bfloat16),
            pltpu.VMEM((rows, rank), jnp.bfloat16),
            pltpu.VMEM((slots, width), jnp.bfloat16),
            pltpu.SemaphoreType.DMA((2,)),
            pltpu.SemaphoreType.DMA((slots // 256,)),
        ],
        compiler_params=pltpu.CompilerParams(vmem_limit_bytes=PACK_VMEM_BYTES),
        cost_estimate=pl.CostEstimate(
            flops=2 * slots * rows * width,
            bytes_accessed=2 * (slots + rows) * width,
            transcendentals=0,
        ),
        name="pack_rows",
    )(cluster[None, :], points, factor)


def digits_of(size, stride):
    bits = size.bit_length() - 1
    found = []
    while bits:
        take = 1 if bits % 2 else 2
        found.append((stride, 1 << take))
        stride <<= take
        bits -= take
    return found


class Chain:
    def __init__(self, own, other, n_src, n_tgt):
        self.n_dev = n_src * n_tgt
        first = (n_tgt, 2)
        src, tgt = digits_of(n_src // 2, 2 * n_tgt), digits_of(n_tgt, 1)
        self.plane, self.along = [first] + src, tgt
        self.dims = src[::-1] + [first] + tgt[::-1]
        self.left = [d for d in self.dims if d != first]
        x = own + self.sent(other, n_tgt).astype(jnp.float32)
        self.x = x.reshape(tuple(radix for _, radix in self.left) + own.shape[2:])

    def sent(self, array, mask):
        return lax.ppermute(array, ALL, [(i, i ^ mask) for i in range(self.n_dev)])

    def scatter(self, digit):
        stride, radix = digit
        dim = self.left.index(digit)
        mine = (lax.axis_index(ALL) // stride) % radix
        total = lax.dynamic_index_in_dim(self.x, mine, dim, keepdims=False)
        for j in range(1, radix):
            piece = lax.dynamic_index_in_dim(self.x, mine ^ j, dim, keepdims=False)
            total = total + self.sent(piece.astype(jnp.bfloat16), j * stride).astype(jnp.float32)
        self.x = total
        self.left.remove(digit)

    def gather(self, digit):
        stride, radix = digit
        mine = (lax.axis_index(ALL) // stride) % radix
        x = self.x.astype(jnp.bfloat16)
        got = [x] + [self.sent(x, j * stride) for j in range(1, radix)]
        self.left = [d for d in self.dims if d in self.left or d == digit]
        self.x = jnp.stack(
            [lax.select_n(mine ^ d, *got) if radix > 2 else jnp.where(mine == d, *got) for d in range(radix)],
            axis=self.left.index(digit),
        )


def update_kernel(
    src_points_ref,
    tgt_points_ref,
    src_factor_ref,
    tgt_factor_ref,
    marginal_ref,
    sums_ref,
    src_ref,
    tgt_ref,
    total,
):
    totals_of(sums_ref, total, src_points_ref.shape[1])
    rank = src_ref.shape[1]
    marginal = marginal_ref[...]
    src_ref[...] = mirror_step(src_points_ref[...], total[:rank], src_factor_ref[...], marginal)
    tgt_ref[...] = mirror_step(tgt_points_ref[...], total[rank:], tgt_factor_ref[...], marginal)


def updates(src_points, tgt_points, src_factor, tgt_factor, marginal, sums):
    rows, features = src_points.shape
    rank = src_factor.shape[1]
    shape = jax.ShapeDtypeStruct(src_factor.shape, jnp.bfloat16)
    return pl.pallas_call(
        update_kernel,
        out_shape=(shape, shape),
        scratch_shapes=[pltpu.VMEM((2 * rank, features), jnp.bfloat16)],
        compiler_params=pltpu.CompilerParams(vmem_limit_bytes=VMEM_BYTES),
        cost_estimate=pl.CostEstimate(
            flops=4 * rows * features * rank,
            bytes_accessed=4 * rows * (features + 2 * rank),
            transcendentals=2 * rows * rank,
        ),
        name="mirror_updates",
    )(src_points, tgt_points, src_factor, tgt_factor, marginal[None, :], sums)


def seen_block(ref, part, block):
    piece = block // ref.shape[1]
    return ref[pl.ds(part * piece, piece)].reshape(block, ref.shape[2])


def owner_kernel(
    features,
    src_ref,
    tgt_ref,
    sums_ref,
    marginal_ref,
    src_label_ref,
    tgt_label_ref,
    out_hbm,
    total,
    tgt_rows,
    tgt_update,
    tgt_inv,
    images,
    out_sem,
):
    totals_of(sums_ref, total, features)
    slots = images.shape[0]
    rank = tgt_update.shape[1]
    marginal = marginal_ref[...]
    block = OWNER_BLOCK
    for part in range(slots // block):
        mine = pl.ds(part * block, block)
        both = seen_block(tgt_ref, part, block)
        rows = both[:, :features]
        tgt_rows[mine, :] = rows
        tgt_update[mine, :] = mirror_step(rows, total[rank:], both[:, features:], marginal)
        tgt_inv[:, mine] = inverse_norm(rows).reshape(1, block)

    departures = []
    for part in range(slots // block):
        mine = pl.ds(part * block, block)
        both = seen_block(src_ref, part, block)
        rows = both[:, :features]
        update = mirror_step(rows, total[:rank], both[:, features:], marginal)
        cosine = contract_columns(rows, tgt_rows[...]) * inverse_norm(rows) * tgt_inv[...]
        weight = contract_columns(update, tgt_update[...]) * (1.0 / rank)
        label = src_label_ref[:, mine].reshape(block, 1)
        same = jnp.logical_and(label == tgt_label_ref[...], label > 0)
        kernel = jnp.where(same, weight * jnp.exp((cosine - 1.0) * (1.0 / TEMPER)), 0.0)
        denominator = jnp.sum(kernel, axis=1, keepdims=True)
        denominator = jnp.where(denominator > 0, denominator, 1.0)
        transport = (kernel * (1.0 / denominator)).astype(jnp.bfloat16)
        images[mine, :] = jnp.dot(
            transport, tgt_rows[...], preferred_element_type=jnp.float32
        ).astype(jnp.bfloat16)
        departures.append(
            pltpu.make_async_copy(images.at[mine], out_hbm.at[mine], out_sem.at[part])
        )
        departures[-1].start()
    for copy in departures:
        copy.wait()


def owner_maps(src, tgt, sums, marginal, src_labels, tgt_labels, features):
    n_dev, capacity, width = src.shape
    slots = n_dev * capacity
    rank = width - features
    return pl.pallas_call(
        functools.partial(owner_kernel, features),
        out_shape=jax.ShapeDtypeStruct((slots, features), jnp.bfloat16),
        grid=(1,),
        in_specs=[
            whole(src.shape),
            whole(tgt.shape),
            whole(sums.shape),
            whole((1, rank)),
            whole((1, slots)),
            whole((1, slots)),
        ],
        out_specs=in_hbm(),
        scratch_shapes=[
            pltpu.VMEM((2 * rank, features), jnp.bfloat16),
            pltpu.VMEM((slots, features), jnp.bfloat16),
            pltpu.VMEM((slots, rank), jnp.bfloat16),
            pltpu.VMEM((1, slots), jnp.float32),
            pltpu.VMEM((slots, features), jnp.bfloat16),
            pltpu.SemaphoreType.DMA((slots // OWNER_BLOCK,)),
        ],
        compiler_params=pltpu.CompilerParams(vmem_limit_bytes=VMEM_BYTES),
        cost_estimate=pl.CostEstimate(
            flops=4 * slots * features * (rank + slots),
            bytes_accessed=6 * slots * width,
            transcendentals=slots * slots,
        ),
        name="owner_maps",
    )(src, tgt, sums, marginal[None, :], src_labels[None, :], tgt_labels[None, :])


def labels_of(clusters, owner, capacity, spread):
    rows = clusters.shape[1]
    mine = clusters // spread == owner
    before = (jnp.arange(rows)[:, None] < jnp.arange(rows)[None, :]).astype(jnp.bfloat16)
    earlier = jnp.dot(mine.astype(jnp.bfloat16), before, preferred_element_type=jnp.float32)
    ranking = jnp.where(mine, earlier.astype(jnp.int32), -1)
    value = clusters - owner * spread + 1
    hit = ranking[:, None, :] == jnp.arange(capacity, dtype=jnp.int32)[None, :, None]
    return jnp.sum(jnp.where(hit, value[:, None, :], 0), axis=2).reshape(-1)


def exchange(rows):
    return lax.all_to_all(rows, ALL, split_axis=0, concat_axis=0, tiled=True)


def per_device(
    src_points, tgt_points, src_factor, tgt_factor, inner_marginal, src_cluster, tgt_cluster
):
    n_src, n_tgt = lax.axis_size("src"), lax.axis_size("tgt")
    n_dev = n_src * n_tgt
    rows, features = src_points.shape
    rank = src_factor.shape[1]
    capacity = 2 * rows // n_dev
    owner = lax.axis_index(ALL)

    tgt = pack(tgt_cluster, tgt_points, tgt_factor, n_dev, capacity)
    tgt, me = lax.optimization_barrier((tgt, owner))
    tgt = exchange(tgt)
    own, other = partial_sums(
        me,
        src_cluster,
        tgt_cluster,
        src_points,
        tgt_points,
        src_factor,
        tgt_factor,
        n_dev,
        n_tgt,
    )
    chain = Chain(own, other, n_src, n_tgt)
    for digit in chain.plane[1:]:
        chain.scatter(digit)
    for digit in chain.along:
        chain.scatter(digit)
    src = pack(src_cluster, src_points, src_factor, n_dev, capacity)
    src, tgt, chain.x = lax.optimization_barrier((src, tgt, chain.x))
    src = exchange(src)
    for digit in reversed(chain.plane[1:] + chain.along):
        chain.gather(digit)
    src, chain.x = lax.optimization_barrier((src, chain.x))
    chain.gather(chain.plane[0])
    sums = chain.x.reshape(n_dev, -1, rank)

    kept = 2 * features // n_dev
    table = sums[:, kept : kept + 2].astype(jnp.int32)
    table = jnp.concatenate([table[:, 0], table[:, 1]])
    labels = labels_of(table, owner, capacity, CL_DEV)
    src_labels, tgt_labels = labels[: n_dev * capacity], labels[n_dev * capacity :]

    shape = (n_dev, capacity, features + rank)
    images = owner_maps(
        src.reshape(shape), tgt.reshape(shape), sums, inner_marginal, src_labels, tgt_labels, features
    )
    returned = exchange(images)

    src_update, tgt_update = updates(
        src_points, tgt_points, src_factor, tgt_factor, inner_marginal, sums
    )
    slot = slot_row(src_cluster[None, :], n_dev, capacity, CL_DEV, 0)
    back = slot.reshape(rows, 1) == jnp.arange(n_dev * capacity, dtype=jnp.int32)[None, :]
    back = lax.optimization_barrier(back.astype(jnp.bfloat16))
    mapped = jnp.dot(back, returned, preferred_element_type=jnp.float32).astype(jnp.bfloat16)
    return (src_update, tgt_update, mapped)


def solution(mesh):
    rows = P(ALL, None)
    return jax.shard_map(
        per_device,
        mesh=mesh,
        in_specs=(rows, rows, rows, rows, P(), P(ALL), P(ALL)),
        out_specs=(rows, rows, rows),
        check_vma=False,
    )
```

```python
import functools

import jax
import jax.numpy as jnp
from jax import lax
from jax.experimental import pallas as pl
from jax.experimental.pallas import tpu as pltpu
from jax.sharding import PartitionSpec as P

CL_DEV = 2

GAMMA = 2.0
TEMPER = 0.03
EPS = 1e-06

ALL = ("src", "tgt")
VMEM_BYTES = 48 * 1024 * 1024
PACK_VMEM_BYTES = 62 * 1024 * 1024
TABLE_ROWS = 8
BLOCK_ROWS = 16
OWNER_BLOCK = 256


def contract_rows(left, right):
    return lax.dot_general(
        left, right, (((0,), (0,)), ((), ())), preferred_element_type=jnp.float32
    )


def contract_columns(left, right):
    return lax.dot_general(
        left, right, (((1,), (1,)), ((), ())), preferred_element_type=jnp.float32
    )


def mirror_step(points, total_round, factor, inner_marginal):
    gradient = contract_columns(points, total_round) * (-1.0 / inner_marginal)
    row_scale = jnp.max(jnp.abs(gradient), axis=1, keepdims=True) + EPS
    tilted = factor.astype(jnp.float32) * jnp.exp(gradient * (-GAMMA / row_scale))
    mean = jnp.mean(tilted, axis=1, keepdims=True)
    mean = jnp.where(mean > 0, mean, 1.0)
    return (tilted * (1.0 / mean)).astype(jnp.bfloat16)


def inverse_norm(rows):
    return lax.rsqrt(jnp.sum(jnp.square(rows.astype(jnp.float32)), axis=1, keepdims=True) + EPS)


def blocks_of(n_dev, chunk, rank, features):
    kept = (chunk - TABLE_ROWS) // BLOCK_ROWS
    wide = features // rank
    return [
        (b // kept, b % kept * BLOCK_ROWS, b // wide * BLOCK_ROWS, b % wide * rank)
        for b in range(n_dev * kept)
    ]


def totals_of(sums_ref, total, features):
    n_dev, chunk, rank = sums_ref.shape
    for c, row, first, column in blocks_of(n_dev, chunk, rank, features):
        total[pl.ds(first, BLOCK_ROWS), pl.ds(column, rank)] = sums_ref[c, pl.ds(row, BLOCK_ROWS), :]


def whole(shape):
    return pl.BlockSpec(shape, lambda *_: (0,) * len(shape))


def in_hbm():
    return pl.BlockSpec(memory_space=pltpu.HBM)


def slot_row(cluster, n_group, capacity, spread, first):
    rows = cluster.shape[1]
    owners = cluster // spread
    onehot = owners == lax.broadcasted_iota(jnp.int32, (n_group, rows), 0)
    before = lax.broadcasted_iota(jnp.int32, (rows, rows), 0) < lax.broadcasted_iota(
        jnp.int32, (rows, rows), 1
    )
    earlier = jnp.dot(
        onehot.astype(jnp.bfloat16), before.astype(jnp.bfloat16), preferred_element_type=jnp.float32
    )
    ranking = jnp.sum(jnp.where(onehot, earlier, 0.0), axis=0, keepdims=True).astype(jnp.int32)
    return owners * capacity + ranking + first


def contract_kernel(n_dev, n_tgt, me_ref, src_cluster_ref, tgt_cluster_ref, *refs):
    hbm, (own_ref, other_ref), held, parts, in_sem = refs[:4], refs[4:6], refs[6:10], refs[10], refs[11]
    arrivals = [pltpu.make_async_copy(a, b, in_sem.at[i]) for i, (a, b) in enumerate(zip(hbm, held))]
    for copy in arrivals:
        copy.start()
    tgt_points, tgt_factor, src_points, src_factor = held
    _, _, _, chunk, rank = parts.shape
    kept = chunk - TABLE_ROWS
    me = me_ref[0]
    mine = (me // n_tgt) % 2
    row = lax.broadcasted_iota(jnp.int32, (TABLE_ROWS, rank), 0)
    table = jnp.where(row == 0, src_cluster_ref[...], jnp.where(row == 1, tgt_cluster_ref[...], 0))
    parts[:, :, :, kept:, :] = jnp.zeros(parts.shape[:3] + (TABLE_ROWS, rank), jnp.float32)
    parts[me // (2 * n_tgt), mine, me % n_tgt, kept:, :] = table.astype(jnp.float32)
    features = tgt_points.shape[1]
    blocks = blocks_of(n_dev, chunk, rank, features)
    for which, (points, factor) in enumerate(((tgt_points, tgt_factor), (src_points, src_factor))):
        arrivals[2 * which].wait()
        arrivals[2 * which + 1].wait()
        total = contract_rows(factor[...], points[...])
        for c, row, first, column in blocks:
            first -= which * rank
            if 0 <= first < rank:
                place = (c // (2 * n_tgt), c // n_tgt % 2, c % n_tgt)
                parts[(*place, pl.ds(row, BLOCK_ROWS))] = total[
                    first : first + BLOCK_ROWS, column : column + rank
                ]
    for i in range(parts.shape[0]):
        own_ref[i] = parts[i, mine]
        other_ref[i] = parts[i, 1 - mine].astype(jnp.bfloat16)


def partial_sums(
    me, src_cluster, tgt_cluster, src_points, tgt_points, src_factor, tgt_factor, n_dev, n_tgt
):
    rows, features = src_points.shape
    rank = src_factor.shape[1]
    chunk = 2 * features // n_dev + TABLE_ROWS
    shape = (n_dev // (2 * n_tgt), n_tgt, chunk, rank)
    vmem = pl.BlockSpec(memory_space=pltpu.VMEM)
    return pl.pallas_call(
        functools.partial(contract_kernel, n_dev, n_tgt),
        out_shape=(
            jax.ShapeDtypeStruct(shape, jnp.float32),
            jax.ShapeDtypeStruct(shape, jnp.bfloat16),
        ),
        in_specs=[pl.BlockSpec(memory_space=pltpu.SMEM)] + [vmem] * 2 + [in_hbm()] * 4,
        out_specs=(vmem, vmem),
        scratch_shapes=[
            pltpu.VMEM((rows, features), jnp.bfloat16),
            pltpu.VMEM((rows, rank), jnp.bfloat16),
            pltpu.VMEM((rows, features), jnp.bfloat16),
            pltpu.VMEM((rows, rank), jnp.bfloat16),
            pltpu.VMEM((n_dev // (2 * n_tgt), 2, n_tgt, chunk, rank), jnp.float32),
            pltpu.SemaphoreType.DMA((4,)),
        ],
        compiler_params=pltpu.CompilerParams(vmem_limit_bytes=PACK_VMEM_BYTES),
        cost_estimate=pl.CostEstimate(
            flops=4 * rows * features * rank,
            bytes_accessed=4 * rows * (features + rank) + 4 * n_dev * chunk * rank,
            transcendentals=0,
        ),
        name="partial_sums",
    )(me[None], src_cluster[None, :], tgt_cluster[None, :], tgt_points, tgt_factor, src_points, src_factor)


def place_rows(kinds, packed, packed_hbm, out_sem):
    block = 256
    departures = []
    for part in range(packed.shape[0] // block):
        mine = pl.ds(part * block, block)
        total = None
        for slot, held in kinds:
            index = lax.broadcasted_iota(jnp.int32, (block, slot.shape[1]), 0) + part * block
            place = (index == slot).astype(jnp.bfloat16)
            rows = [
                jnp.dot(place, array, preferred_element_type=jnp.float32) for array in held
            ]
            total = rows if total is None else [a + b for a, b in zip(total, rows)]
        column = 0
        for rows in total:
            packed[mine, column : column + rows.shape[1]] = rows.astype(jnp.bfloat16)
            column += rows.shape[1]
        departures.append(
            pltpu.make_async_copy(packed.at[mine], packed_hbm.at[mine], out_sem.at[part])
        )
        departures[-1].start()
    return departures


def pack_kernel(
    n_dev,
    capacity,
    cluster_ref,
    points_hbm,
    factor_hbm,
    packed_hbm,
    points,
    factor,
    packed,
    in_sem,
    out_sem,
):
    arrivals = [
        pltpu.make_async_copy(points_hbm, points, in_sem.at[0]),
        pltpu.make_async_copy(factor_hbm, factor, in_sem.at[1]),
    ]
    for copy in arrivals:
        copy.start()
    slot = slot_row(cluster_ref[...], n_dev, capacity, CL_DEV, 0)
    for copy in arrivals:
        copy.wait()
    for copy in place_rows([(slot, (points[...], factor[...]))], packed, packed_hbm, out_sem):
        copy.wait()


def pack(cluster, points, factor, n_dev, capacity):
    rows, features = points.shape
    rank = factor.shape[1]
    width = features + rank
    slots = n_dev * capacity
    return pl.pallas_call(
        functools.partial(pack_kernel, n_dev, capacity),
        out_shape=jax.ShapeDtypeStruct((slots, width), jnp.bfloat16),
        in_specs=[pl.BlockSpec(memory_space=pltpu.VMEM), in_hbm(), in_hbm()],
        out_specs=in_hbm(),
        scratch_shapes=[
            pltpu.VMEM((rows, features), jnp.bfloat16),
            pltpu.VMEM((rows, rank), jnp.bfloat16),
            pltpu.VMEM((slots, width), jnp.bfloat16),
            pltpu.SemaphoreType.DMA((2,)),
            pltpu.SemaphoreType.DMA((slots // 256,)),
        ],
        compiler_params=pltpu.CompilerParams(vmem_limit_bytes=PACK_VMEM_BYTES),
        cost_estimate=pl.CostEstimate(
            flops=2 * slots * rows * width,
            bytes_accessed=2 * (slots + rows) * width,
            transcendentals=0,
        ),
        name="pack_rows",
    )(cluster[None, :], points, factor)


def digits_of(size, stride):
    bits = size.bit_length() - 1
    found = []
    while bits:
        take = 1 if bits % 2 else 2
        found.append((stride, 1 << take))
        stride <<= take
        bits -= take
    return found


class Chain:
    def __init__(self, own, other, n_src, n_tgt):
        self.n_dev = n_src * n_tgt
        first = (n_tgt, 2)
        src, tgt = digits_of(n_src // 2, 2 * n_tgt), digits_of(n_tgt, 1)
        self.plane, self.along = [first] + src, tgt
        self.dims = src[::-1] + [first] + tgt[::-1]
        self.left = [d for d in self.dims if d != first]
        x = own + self.sent(other, n_tgt).astype(jnp.float32)
        self.x = x.reshape(tuple(radix for _, radix in self.left) + own.shape[2:])

    def sent(self, array, mask):
        return lax.ppermute(array, ALL, [(i, i ^ mask) for i in range(self.n_dev)])

    def scatter(self, digit):
        stride, radix = digit
        dim = self.left.index(digit)
        mine = (lax.axis_index(ALL) // stride) % radix
        total = lax.dynamic_index_in_dim(self.x, mine, dim, keepdims=False)
        for j in range(1, radix):
            piece = lax.dynamic_index_in_dim(self.x, mine ^ j, dim, keepdims=False)
            total = total + self.sent(piece.astype(jnp.bfloat16), j * stride).astype(jnp.float32)
        self.x = total
        self.left.remove(digit)

    def gather(self, digit):
        stride, radix = digit
        mine = (lax.axis_index(ALL) // stride) % radix
        x = self.x.astype(jnp.bfloat16)
        got = [x] + [self.sent(x, j * stride) for j in range(1, radix)]
        self.left = [d for d in self.dims if d in self.left or d == digit]
        self.x = jnp.stack(
            [lax.select_n(mine ^ d, *got) if radix > 2 else jnp.where(mine == d, *got) for d in range(radix)],
            axis=self.left.index(digit),
        )


def update_kernel(
    src_points_ref,
    tgt_points_ref,
    src_factor_ref,
    tgt_factor_ref,
    marginal_ref,
    sums_ref,
    src_ref,
    tgt_ref,
    total,
):
    totals_of(sums_ref, total, src_points_ref.shape[1])
    rank = src_ref.shape[1]
    marginal = marginal_ref[...]
    src_ref[...] = mirror_step(src_points_ref[...], total[:rank], src_factor_ref[...], marginal)
    tgt_ref[...] = mirror_step(tgt_points_ref[...], total[rank:], tgt_factor_ref[...], marginal)


def updates(src_points, tgt_points, src_factor, tgt_factor, marginal, sums):
    rows, features = src_points.shape
    rank = src_factor.shape[1]
    shape = jax.ShapeDtypeStruct(src_factor.shape, jnp.bfloat16)
    return pl.pallas_call(
        update_kernel,
        out_shape=(shape, shape),
        scratch_shapes=[pltpu.VMEM((2 * rank, features), jnp.bfloat16)],
        compiler_params=pltpu.CompilerParams(vmem_limit_bytes=VMEM_BYTES),
        cost_estimate=pl.CostEstimate(
            flops=4 * rows * features * rank,
            bytes_accessed=4 * rows * (features + 2 * rank),
            transcendentals=2 * rows * rank,
        ),
        name="mirror_updates",
    )(src_points, tgt_points, src_factor, tgt_factor, marginal[None, :], sums)


def seen_block(ref, part, block):
    piece = block // ref.shape[1]
    return ref[pl.ds(part * piece, piece)].reshape(block, ref.shape[2])


def target_kernel(
    features, tgt_ref, sums_ref, marginal_ref, rows_ref, update_ref, inv_ref, total_ref, total
):
    totals_of(sums_ref, total, features)
    rank = update_ref.shape[1]
    total_ref[...] = total[:rank]
    block = OWNER_BLOCK
    for part in range(rows_ref.shape[0] // block):
        mine = pl.ds(part * block, block)
        both = seen_block(tgt_ref, part, block)
        rows = both[:, :features]
        rows_ref[mine, :] = rows
        update_ref[mine, :] = mirror_step(
            rows, total[rank:], both[:, features:], marginal_ref[...]
        )
        inv_ref[:, mine] = inverse_norm(rows).reshape(1, block)


def prepare_targets(tgt, sums, marginal, features):
    n_dev, capacity, width = tgt.shape
    slots = n_dev * capacity
    rank = width - features
    vmem = pl.BlockSpec(memory_space=pltpu.VMEM)
    return pl.pallas_call(
        functools.partial(target_kernel, features),
        out_shape=(
            jax.ShapeDtypeStruct((slots, features), jnp.bfloat16),
            jax.ShapeDtypeStruct((slots, rank), jnp.bfloat16),
            jax.ShapeDtypeStruct((1, slots), jnp.float32),
            jax.ShapeDtypeStruct((rank, features), jnp.bfloat16),
        ),
        in_specs=[vmem] * 3,
        out_specs=(vmem,) * 4,
        scratch_shapes=[pltpu.VMEM((2 * rank, features), jnp.bfloat16)],
        compiler_params=pltpu.CompilerParams(vmem_limit_bytes=PACK_VMEM_BYTES),
        cost_estimate=pl.CostEstimate(
            flops=2 * slots * features * rank,
            bytes_accessed=4 * slots * width,
            transcendentals=slots * rank,
        ),
        name="prepare_targets",
    )(tgt, sums, marginal[None, :])


def owner_kernel(
    features,
    src_ref,
    rows_ref,
    update_ref,
    inv_ref,
    total_ref,
    marginal_ref,
    src_label_ref,
    tgt_label_ref,
    out_ref,
):
    block = out_ref.shape[0]
    rank = update_ref.shape[1]
    both = seen_block(src_ref, 0, block)
    rows = both[:, :features]
    update = mirror_step(rows, total_ref[...], both[:, features:], marginal_ref[...])
    cosine = contract_columns(rows, rows_ref[...]) * inverse_norm(rows) * inv_ref[...]
    weight = contract_columns(update, update_ref[...]) * (1.0 / rank)
    label = src_label_ref[...].reshape(block, 1)
    same = jnp.logical_and(label == tgt_label_ref[...], label > 0)
    kernel = jnp.where(same, weight * jnp.exp((cosine - 1.0) * (1.0 / TEMPER)), 0.0)
    denominator = jnp.sum(kernel, axis=1, keepdims=True)
    denominator = jnp.where(denominator > 0, denominator, 1.0)
    transport = (kernel * (1.0 / denominator)).astype(jnp.bfloat16)
    out_ref[...] = jnp.dot(
        transport, rows_ref[...], preferred_element_type=jnp.float32
    ).astype(jnp.bfloat16)


def owner_maps(src, targets, marginal, src_labels, tgt_labels, features):
    n_dev, capacity, width = src.shape
    slots = n_dev * capacity
    rank = width - features
    block = OWNER_BLOCK
    return pl.pallas_call(
        functools.partial(owner_kernel, features),
        out_shape=jax.ShapeDtypeStruct((slots, features), jnp.bfloat16),
        grid=(slots // block,),
        in_specs=[
            pl.BlockSpec((block // capacity, capacity, width), lambda part: (part, 0, 0)),
            *[whole(array.shape) for array in targets],
            whole((1, rank)),
            pl.BlockSpec((1, block), lambda part: (0, part)),
            whole((1, slots)),
        ],
        out_specs=pl.BlockSpec((block, features), lambda part: (part, 0)),
        compiler_params=pltpu.CompilerParams(vmem_limit_bytes=PACK_VMEM_BYTES),
        cost_estimate=pl.CostEstimate(
            flops=2 * slots * features * (rank + 2 * slots),
            bytes_accessed=6 * slots * width,
            transcendentals=slots * slots,
        ),
        name="owner_maps",
    )(src, *targets, marginal[None, :], src_labels[None, :], tgt_labels[None, :])


def labels_of(clusters, owner, capacity, spread):
    rows = clusters.shape[1]
    mine = clusters // spread == owner
    before = (jnp.arange(rows)[:, None] < jnp.arange(rows)[None, :]).astype(jnp.bfloat16)
    earlier = jnp.dot(mine.astype(jnp.bfloat16), before, preferred_element_type=jnp.float32)
    ranking = jnp.where(mine, earlier.astype(jnp.int32), -1)
    value = clusters - owner * spread + 1
    hit = ranking[:, None, :] == jnp.arange(capacity, dtype=jnp.int32)[None, :, None]
    return jnp.sum(jnp.where(hit, value[:, None, :], 0), axis=2).reshape(-1)


def exchange(rows):
    return lax.all_to_all(rows, ALL, split_axis=0, concat_axis=0, tiled=True)


def per_device(
    src_points, tgt_points, src_factor, tgt_factor, inner_marginal, src_cluster, tgt_cluster
):
    n_src, n_tgt = lax.axis_size("src"), lax.axis_size("tgt")
    n_dev = n_src * n_tgt
    rows, features = src_points.shape
    rank = src_factor.shape[1]
    capacity = 2 * rows // n_dev
    owner = lax.axis_index(ALL)

    tgt = pack(tgt_cluster, tgt_points, tgt_factor, n_dev, capacity)
    tgt, me = lax.optimization_barrier((tgt, owner))
    tgt = exchange(tgt)
    own, other = partial_sums(
        me,
        src_cluster,
        tgt_cluster,
        src_points,
        tgt_points,
        src_factor,
        tgt_factor,
        n_dev,
        n_tgt,
    )
    chain = Chain(own, other, n_src, n_tgt)
    for digit in chain.plane[1:]:
        chain.scatter(digit)
    for digit in chain.along:
        chain.scatter(digit)
    src = pack(src_cluster, src_points, src_factor, n_dev, capacity)
    src, tgt, chain.x = lax.optimization_barrier((src, tgt, chain.x))
    src = exchange(src)
    for digit in reversed(chain.plane + chain.along):
        chain.gather(digit)
    sums = chain.x.reshape(n_dev, -1, rank)

    kept = 2 * features // n_dev
    table = sums[:, kept : kept + 2].astype(jnp.int32)
    table = jnp.concatenate([table[:, 0], table[:, 1]])
    labels = labels_of(table, owner, capacity, CL_DEV)
    src_labels, tgt_labels = labels[: n_dev * capacity], labels[n_dev * capacity :]

    shape = (n_dev, capacity, features + rank)
    targets = prepare_targets(tgt.reshape(shape), sums, inner_marginal, features)
    images = owner_maps(src.reshape(shape), targets, inner_marginal, src_labels, tgt_labels, features)
    returned = exchange(images)

    src_update, tgt_update = updates(
        src_points, tgt_points, src_factor, tgt_factor, inner_marginal, sums
    )
    slot = slot_row(src_cluster[None, :], n_dev, capacity, CL_DEV, 0)
    back = slot.reshape(rows, 1) == jnp.arange(n_dev * capacity, dtype=jnp.int32)[None, :]
    back = lax.optimization_barrier(back.astype(jnp.bfloat16))
    mapped = jnp.dot(back, returned, preferred_element_type=jnp.float32).astype(jnp.bfloat16)
    return (src_update, tgt_update, mapped)


def solution(mesh):
    rows = P(ALL, None)
    return jax.shard_map(
        per_device,
        mesh=mesh,
        in_specs=(rows, rows, rows, rows, P(), P(ALL), P(ALL)),
        out_specs=(rows, rows, rows),
        check_vma=False,
    )
```

```python
import functools

import jax
import jax.numpy as jnp
from jax import lax
from jax.experimental import pallas as pl
from jax.experimental.pallas import tpu as pltpu
from jax.sharding import PartitionSpec as P

CL_DEV = 2

GAMMA = 2.0
TEMPER = 0.03
EPS = 1e-06

ALL = ("src", "tgt")
VMEM_BYTES = 48 * 1024 * 1024
PACK_VMEM_BYTES = 62 * 1024 * 1024
TABLE_ROWS = 8
BLOCK_ROWS = 16
OWNER_BLOCK = 256


def contract_rows(left, right):
    return lax.dot_general(
        left, right, (((0,), (0,)), ((), ())), preferred_element_type=jnp.float32
    )


def contract_columns(left, right):
    return lax.dot_general(
        left, right, (((1,), (1,)), ((), ())), preferred_element_type=jnp.float32
    )


def mirror_step(points, total_round, factor, inner_marginal):
    gradient = contract_columns(points, total_round) * (-1.0 / inner_marginal)
    row_scale = jnp.max(jnp.abs(gradient), axis=1, keepdims=True) + EPS
    tilted = factor.astype(jnp.float32) * jnp.exp(gradient * (-GAMMA / row_scale))
    mean = jnp.mean(tilted, axis=1, keepdims=True)
    mean = jnp.where(mean > 0, mean, 1.0)
    return (tilted * (1.0 / mean)).astype(jnp.bfloat16)


def inverse_norm(rows):
    return lax.rsqrt(jnp.sum(jnp.square(rows.astype(jnp.float32)), axis=1, keepdims=True) + EPS)


def blocks_of(n_dev, chunk, rank, features):
    kept = (chunk - TABLE_ROWS) // BLOCK_ROWS
    wide = features // rank
    return [
        (b // kept, b % kept * BLOCK_ROWS, b // wide * BLOCK_ROWS, b % wide * rank)
        for b in range(n_dev * kept)
    ]


def totals_of(sums_ref, total, features):
    n_dev, chunk, rank = sums_ref.shape
    for c, row, first, column in blocks_of(n_dev, chunk, rank, features):
        total[pl.ds(first, BLOCK_ROWS), pl.ds(column, rank)] = sums_ref[c, pl.ds(row, BLOCK_ROWS), :]


def whole(shape):
    return pl.BlockSpec(shape, lambda *_: (0,) * len(shape))


def in_hbm():
    return pl.BlockSpec(memory_space=pltpu.HBM)


def slot_row(cluster, n_group, capacity, spread, first):
    rows = cluster.shape[1]
    owners = cluster // spread
    onehot = owners == lax.broadcasted_iota(jnp.int32, (n_group, rows), 0)
    before = lax.broadcasted_iota(jnp.int32, (rows, rows), 0) < lax.broadcasted_iota(
        jnp.int32, (rows, rows), 1
    )
    earlier = jnp.dot(
        onehot.astype(jnp.bfloat16), before.astype(jnp.bfloat16), preferred_element_type=jnp.float32
    )
    ranking = jnp.sum(jnp.where(onehot, earlier, 0.0), axis=0, keepdims=True).astype(jnp.int32)
    return owners * capacity + ranking + first


def contract_kernel(n_dev, n_tgt, me_ref, src_cluster_ref, tgt_cluster_ref, *refs):
    hbm, (own_ref, other_ref), held, parts, in_sem = refs[:4], refs[4:6], refs[6:10], refs[10], refs[11]
    arrivals = [pltpu.make_async_copy(a, b, in_sem.at[i]) for i, (a, b) in enumerate(zip(hbm, held))]
    for copy in arrivals:
        copy.start()
    tgt_points, tgt_factor, src_points, src_factor = held
    _, _, _, chunk, rank = parts.shape
    kept = chunk - TABLE_ROWS
    me = me_ref[0]
    mine = (me // n_tgt) % 2
    row = lax.broadcasted_iota(jnp.int32, (TABLE_ROWS, rank), 0)
    table = jnp.where(row == 0, src_cluster_ref[...], jnp.where(row == 1, tgt_cluster_ref[...], 0))
    parts[:, :, :, kept:, :] = jnp.zeros(parts.shape[:3] + (TABLE_ROWS, rank), jnp.float32)
    parts[me // (2 * n_tgt), mine, me % n_tgt, kept:, :] = table.astype(jnp.float32)
    features = tgt_points.shape[1]
    blocks = blocks_of(n_dev, chunk, rank, features)
    for which, (points, factor) in enumerate(((tgt_points, tgt_factor), (src_points, src_factor))):
        arrivals[2 * which].wait()
        arrivals[2 * which + 1].wait()
        total = contract_rows(factor[...], points[...])
        for c, row, first, column in blocks:
            first -= which * rank
            if 0 <= first < rank:
                place = (c // (2 * n_tgt), c // n_tgt % 2, c % n_tgt)
                parts[(*place, pl.ds(row, BLOCK_ROWS))] = total[
                    first : first + BLOCK_ROWS, column : column + rank
                ]
    for i in range(parts.shape[0]):
        own_ref[i] = parts[i, mine]
        other_ref[i] = parts[i, 1 - mine].astype(jnp.bfloat16)


def partial_sums(
    me, src_cluster, tgt_cluster, src_points, tgt_points, src_factor, tgt_factor, n_dev, n_tgt
):
    rows, features = src_points.shape
    rank = src_factor.shape[1]
    chunk = 2 * features // n_dev + TABLE_ROWS
    shape = (n_dev // (2 * n_tgt), n_tgt, chunk, rank)
    vmem = pl.BlockSpec(memory_space=pltpu.VMEM)
    return pl.pallas_call(
        functools.partial(contract_kernel, n_dev, n_tgt),
        out_shape=(
            jax.ShapeDtypeStruct(shape, jnp.float32),
            jax.ShapeDtypeStruct(shape, jnp.bfloat16),
        ),
        in_specs=[pl.BlockSpec(memory_space=pltpu.SMEM)] + [vmem] * 2 + [in_hbm()] * 4,
        out_specs=(vmem, vmem),
        scratch_shapes=[
            pltpu.VMEM((rows, features), jnp.bfloat16),
            pltpu.VMEM((rows, rank), jnp.bfloat16),
            pltpu.VMEM((rows, features), jnp.bfloat16),
            pltpu.VMEM((rows, rank), jnp.bfloat16),
            pltpu.VMEM((n_dev // (2 * n_tgt), 2, n_tgt, chunk, rank), jnp.float32),
            pltpu.SemaphoreType.DMA((4,)),
        ],
        compiler_params=pltpu.CompilerParams(vmem_limit_bytes=PACK_VMEM_BYTES),
        cost_estimate=pl.CostEstimate(
            flops=4 * rows * features * rank,
            bytes_accessed=4 * rows * (features + rank) + 4 * n_dev * chunk * rank,
            transcendentals=0,
        ),
        name="partial_sums",
    )(me[None], src_cluster[None, :], tgt_cluster[None, :], tgt_points, tgt_factor, src_points, src_factor)


def place_rows(kinds, packed, packed_hbm, out_sem):
    block = 256
    departures = []
    for part in range(packed.shape[0] // block):
        mine = pl.ds(part * block, block)
        total = None
        for slot, held in kinds:
            index = lax.broadcasted_iota(jnp.int32, (block, slot.shape[1]), 0) + part * block
            place = (index == slot).astype(jnp.bfloat16)
            rows = [
                jnp.dot(place, array, preferred_element_type=jnp.float32) for array in held
            ]
            total = rows if total is None else [a + b for a, b in zip(total, rows)]
        column = 0
        for rows in total:
            packed[mine, column : column + rows.shape[1]] = rows.astype(jnp.bfloat16)
            column += rows.shape[1]
        departures.append(
            pltpu.make_async_copy(packed.at[mine], packed_hbm.at[mine], out_sem.at[part])
        )
        departures[-1].start()
    return departures


def pack_kernel(
    n_dev,
    capacity,
    cluster_ref,
    points_hbm,
    factor_hbm,
    packed_hbm,
    points,
    factor,
    packed,
    in_sem,
    out_sem,
):
    arrivals = [
        pltpu.make_async_copy(points_hbm, points, in_sem.at[0]),
        pltpu.make_async_copy(factor_hbm, factor, in_sem.at[1]),
    ]
    for copy in arrivals:
        copy.start()
    slot = slot_row(cluster_ref[...], n_dev, capacity, CL_DEV, 0)
    for copy in arrivals:
        copy.wait()
    for copy in place_rows([(slot, (points[...], factor[...]))], packed, packed_hbm, out_sem):
        copy.wait()


def pack(cluster, points, factor, n_dev, capacity):
    rows, features = points.shape
    rank = factor.shape[1]
    width = features + rank
    slots = n_dev * capacity
    return pl.pallas_call(
        functools.partial(pack_kernel, n_dev, capacity),
        out_shape=jax.ShapeDtypeStruct((slots, width), jnp.bfloat16),
        in_specs=[pl.BlockSpec(memory_space=pltpu.VMEM), in_hbm(), in_hbm()],
        out_specs=in_hbm(),
        scratch_shapes=[
            pltpu.VMEM((rows, features), jnp.bfloat16),
            pltpu.VMEM((rows, rank), jnp.bfloat16),
            pltpu.VMEM((slots, width), jnp.bfloat16),
            pltpu.SemaphoreType.DMA((2,)),
            pltpu.SemaphoreType.DMA((slots // 256,)),
        ],
        compiler_params=pltpu.CompilerParams(vmem_limit_bytes=PACK_VMEM_BYTES),
        cost_estimate=pl.CostEstimate(
            flops=2 * slots * rows * width,
            bytes_accessed=2 * (slots + rows) * width,
            transcendentals=0,
        ),
        name="pack_rows",
    )(cluster[None, :], points, factor)


def digits_of(size, stride):
    bits = size.bit_length() - 1
    found = []
    while bits:
        take = 1 if bits % 2 else 2
        found.append((stride, 1 << take))
        stride <<= take
        bits -= take
    return found


class Chain:
    def __init__(self, own, other, n_src, n_tgt):
        self.n_dev = n_src * n_tgt
        first = (n_tgt, 2)
        src, tgt = digits_of(n_src // 2, 2 * n_tgt), digits_of(n_tgt, 1)
        self.plane, self.along = [first] + src, tgt
        self.dims = src[::-1] + [first] + tgt[::-1]
        self.left = [d for d in self.dims if d != first]
        x = own + self.sent(other, n_tgt).astype(jnp.float32)
        self.x = x.reshape(tuple(radix for _, radix in self.left) + own.shape[2:])

    def sent(self, array, mask):
        return lax.ppermute(array, ALL, [(i, i ^ mask) for i in range(self.n_dev)])

    def scatter(self, digit):
        stride, radix = digit
        dim = self.left.index(digit)
        mine = (lax.axis_index(ALL) // stride) % radix
        total = lax.dynamic_index_in_dim(self.x, mine, dim, keepdims=False)
        for j in range(1, radix):
            piece = lax.dynamic_index_in_dim(self.x, mine ^ j, dim, keepdims=False)
            total = total + self.sent(piece.astype(jnp.bfloat16), j * stride).astype(jnp.float32)
        self.x = total
        self.left.remove(digit)

    def gather(self, digit):
        stride, radix = digit
        mine = (lax.axis_index(ALL) // stride) % radix
        x = self.x.astype(jnp.bfloat16)
        got = [x] + [self.sent(x, j * stride) for j in range(1, radix)]
        self.left = [d for d in self.dims if d in self.left or d == digit]
        self.x = jnp.stack(
            [lax.select_n(mine ^ d, *got) if radix > 2 else jnp.where(mine == d, *got) for d in range(radix)],
            axis=self.left.index(digit),
        )


def update_kernel(
    src_points_ref,
    tgt_points_ref,
    src_factor_ref,
    tgt_factor_ref,
    marginal_ref,
    sums_ref,
    src_ref,
    tgt_ref,
    total,
):
    totals_of(sums_ref, total, src_points_ref.shape[1])
    rank = src_ref.shape[1]
    marginal = marginal_ref[...]
    src_ref[...] = mirror_step(src_points_ref[...], total[:rank], src_factor_ref[...], marginal)
    tgt_ref[...] = mirror_step(tgt_points_ref[...], total[rank:], tgt_factor_ref[...], marginal)


def updates(src_points, tgt_points, src_factor, tgt_factor, marginal, sums):
    rows, features = src_points.shape
    rank = src_factor.shape[1]
    shape = jax.ShapeDtypeStruct(src_factor.shape, jnp.bfloat16)
    return pl.pallas_call(
        update_kernel,
        out_shape=(shape, shape),
        scratch_shapes=[pltpu.VMEM((2 * rank, features), jnp.bfloat16)],
        compiler_params=pltpu.CompilerParams(vmem_limit_bytes=VMEM_BYTES),
        cost_estimate=pl.CostEstimate(
            flops=4 * rows * features * rank,
            bytes_accessed=4 * rows * (features + 2 * rank),
            transcendentals=2 * rows * rank,
        ),
        name="mirror_updates",
    )(src_points, tgt_points, src_factor, tgt_factor, marginal[None, :], sums)


def seen_block(ref, part, block):
    piece = block // ref.shape[1]
    return ref[pl.ds(part * piece, piece)].reshape(block, ref.shape[2])


def target_kernel(
    features, tgt_ref, sums_ref, marginal_ref, rows_ref, update_ref, inv_ref, total_ref, total
):
    totals_of(sums_ref, total, features)
    rank = update_ref.shape[1]
    total_ref[...] = total[:rank]
    block = OWNER_BLOCK
    for part in range(rows_ref.shape[0] // block):
        mine = pl.ds(part * block, block)
        both = seen_block(tgt_ref, part, block)
        rows = both[:, :features]
        rows_ref[mine, :] = rows
        update_ref[mine, :] = mirror_step(
            rows, total[rank:], both[:, features:], marginal_ref[...]
        )
        inv_ref[:, mine] = inverse_norm(rows).reshape(1, block)


def prepare_targets(tgt, sums, marginal, features):
    n_dev, capacity, width = tgt.shape
    slots = n_dev * capacity
    rank = width - features
    vmem = pl.BlockSpec(memory_space=pltpu.VMEM)
    return pl.pallas_call(
        functools.partial(target_kernel, features),
        out_shape=(
            jax.ShapeDtypeStruct((slots, features), jnp.bfloat16),
            jax.ShapeDtypeStruct((slots, rank), jnp.bfloat16),
            jax.ShapeDtypeStruct((1, slots), jnp.float32),
            jax.ShapeDtypeStruct((rank, features), jnp.bfloat16),
        ),
        in_specs=[vmem] * 3,
        out_specs=(vmem,) * 4,
        scratch_shapes=[pltpu.VMEM((2 * rank, features), jnp.bfloat16)],
        compiler_params=pltpu.CompilerParams(vmem_limit_bytes=PACK_VMEM_BYTES),
        cost_estimate=pl.CostEstimate(
            flops=2 * slots * features * rank,
            bytes_accessed=4 * slots * width,
            transcendentals=slots * rank,
        ),
        name="prepare_targets",
    )(tgt, sums, marginal[None, :])


def owner_kernel(
    features,
    src_hbm,
    rows_hbm,
    update_hbm,
    total_hbm,
    inv_ref,
    marginal_ref,
    src_label_ref,
    tgt_label_ref,
    out_hbm,
    src,
    tgt_rows,
    tgt_update,
    total,
    images,
    src_sem,
    in_sem,
    out_sem,
):
    block = OWNER_BLOCK
    slots, rank = tgt_update.shape
    piece = block // src.shape[1]
    n_parts = slots // block
    sources = [
        pltpu.make_async_copy(
            src_hbm.at[pl.ds(part * piece, piece)], src.at[pl.ds(part * piece, piece)], src_sem.at[part]
        )
        for part in range(n_parts)
    ]
    total_in = pltpu.make_async_copy(total_hbm, total, in_sem.at[0])
    rows_in = pltpu.make_async_copy(rows_hbm, tgt_rows, in_sem.at[1])
    update_in = pltpu.make_async_copy(update_hbm, tgt_update, in_sem.at[2])
    for copy in (sources[0], total_in, rows_in, update_in, *sources[1:]):
        copy.start()
    marginal = marginal_ref[...]
    departures = []
    for part in range(n_parts):
        mine = pl.ds(part * block, block)
        sources[part].wait()
        both = seen_block(src, part, block)
        rows = both[:, :features]
        inverse = inverse_norm(rows)
        if part == 0:
            total_in.wait()
        update = mirror_step(rows, total[...], both[:, features:], marginal)
        if part == 0:
            rows_in.wait()
        cosine = contract_columns(rows, tgt_rows[...]) * inverse * inv_ref[...]
        if part == 0:
            update_in.wait()
        weight = contract_columns(update, tgt_update[...]) * (1.0 / rank)
        label = src_label_ref[:, mine].reshape(block, 1)
        same = jnp.logical_and(label == tgt_label_ref[...], label > 0)
        kernel = jnp.where(same, weight * jnp.exp((cosine - 1.0) * (1.0 / TEMPER)), 0.0)
        denominator = jnp.sum(kernel, axis=1, keepdims=True)
        denominator = jnp.where(denominator > 0, denominator, 1.0)
        transport = (kernel * (1.0 / denominator)).astype(jnp.bfloat16)
        images[mine, :] = jnp.dot(
            transport, tgt_rows[...], preferred_element_type=jnp.float32
        ).astype(jnp.bfloat16)
        departures.append(
            pltpu.make_async_copy(images.at[mine], out_hbm.at[mine], out_sem.at[part])
        )
        departures[-1].start()
    for copy in departures:
        copy.wait()


def owner_maps(src, targets, marginal, src_labels, tgt_labels, features):
    rows, update, inv, total = targets
    slots, rank = update.shape
    n_parts = slots // OWNER_BLOCK
    vmem = pl.BlockSpec(memory_space=pltpu.VMEM)
    return pl.pallas_call(
        functools.partial(owner_kernel, features),
        out_shape=jax.ShapeDtypeStruct((slots, features), jnp.bfloat16),
        in_specs=[in_hbm()] * 4 + [vmem] * 4,
        out_specs=in_hbm(),
        scratch_shapes=[
            pltpu.VMEM(src.shape, jnp.bfloat16),
            pltpu.VMEM(rows.shape, jnp.bfloat16),
            pltpu.VMEM(update.shape, jnp.bfloat16),
            pltpu.VMEM(total.shape, jnp.bfloat16),
            pltpu.VMEM((slots, features), jnp.bfloat16),
            pltpu.SemaphoreType.DMA((n_parts,)),
            pltpu.SemaphoreType.DMA((3,)),
            pltpu.SemaphoreType.DMA((n_parts,)),
        ],
        compiler_params=pltpu.CompilerParams(vmem_limit_bytes=PACK_VMEM_BYTES),
        cost_estimate=pl.CostEstimate(
            flops=2 * slots * features * (rank + 2 * slots),
            bytes_accessed=6 * slots * features,
            transcendentals=slots * slots,
        ),
        name="owner_maps",
    )(src, rows, update, total, inv, marginal[None, :], src_labels[None, :], tgt_labels[None, :])


def labels_of(clusters, owner, capacity, spread):
    rows = clusters.shape[1]
    mine = clusters // spread == owner
    before = (jnp.arange(rows)[:, None] < jnp.arange(rows)[None, :]).astype(jnp.bfloat16)
    earlier = jnp.dot(mine.astype(jnp.bfloat16), before, preferred_element_type=jnp.float32)
    ranking = jnp.where(mine, earlier.astype(jnp.int32), -1)
    value = clusters - owner * spread + 1
    hit = ranking[:, None, :] == jnp.arange(capacity, dtype=jnp.int32)[None, :, None]
    return jnp.sum(jnp.where(hit, value[:, None, :], 0), axis=2).reshape(-1)


def exchange(rows):
    return lax.all_to_all(rows, ALL, split_axis=0, concat_axis=0, tiled=True)


def per_device(
    src_points, tgt_points, src_factor, tgt_factor, inner_marginal, src_cluster, tgt_cluster
):
    n_src, n_tgt = lax.axis_size("src"), lax.axis_size("tgt")
    n_dev = n_src * n_tgt
    rows, features = src_points.shape
    rank = src_factor.shape[1]
    capacity = 2 * rows // n_dev
    owner = lax.axis_index(ALL)

    tgt = pack(tgt_cluster, tgt_points, tgt_factor, n_dev, capacity)
    tgt, me = lax.optimization_barrier((tgt, owner))
    tgt = exchange(tgt)
    own, other = partial_sums(
        me,
        src_cluster,
        tgt_cluster,
        src_points,
        tgt_points,
        src_factor,
        tgt_factor,
        n_dev,
        n_tgt,
    )
    chain = Chain(own, other, n_src, n_tgt)
    for digit in chain.plane[1:]:
        chain.scatter(digit)
    for digit in chain.along:
        chain.scatter(digit)
    src = pack(src_cluster, src_points, src_factor, n_dev, capacity)
    src, tgt, chain.x = lax.optimization_barrier((src, tgt, chain.x))
    src = exchange(src)
    for digit in reversed(chain.plane + chain.along):
        chain.gather(digit)
    sums = chain.x.reshape(n_dev, -1, rank)

    kept = 2 * features // n_dev
    table = sums[:, kept : kept + 2].astype(jnp.int32)
    table = jnp.concatenate([table[:, 0], table[:, 1]])
    labels = labels_of(table, owner, capacity, CL_DEV)
    src_labels, tgt_labels = labels[: n_dev * capacity], labels[n_dev * capacity :]

    shape = (n_dev, capacity, features + rank)
    targets = prepare_targets(tgt.reshape(shape), sums, inner_marginal, features)
    images = owner_maps(src.reshape(shape), targets, inner_marginal, src_labels, tgt_labels, features)
    returned = exchange(images)

    src_update, tgt_update = updates(
        src_points, tgt_points, src_factor, tgt_factor, inner_marginal, sums
    )
    slot = slot_row(src_cluster[None, :], n_dev, capacity, CL_DEV, 0)
    back = (jnp.arange(n_dev * capacity, dtype=jnp.int32)[:, None] == slot).astype(jnp.bfloat16)
    mapped = contract_rows(back, returned).astype(jnp.bfloat16)
    return (src_update, tgt_update, mapped)


def solution(mesh):
    rows = P(ALL, None)
    return jax.shard_map(
        per_device,
        mesh=mesh,
        in_specs=(rows, rows, rows, rows, P(), P(ALL), P(ALL)),
        out_specs=(rows, rows, rows),
        check_vma=False,
    )
```

```python
import functools

import jax
import jax.numpy as jnp
from jax import lax
from jax.experimental import pallas as pl
from jax.experimental.pallas import tpu as pltpu
from jax.sharding import PartitionSpec as P

CL_DEV = 2

GAMMA = 2.0
TEMPER = 0.03
EPS = 1e-06

ALL = ("src", "tgt")
VMEM_BYTES = 48 * 1024 * 1024
PACK_VMEM_BYTES = 62 * 1024 * 1024
TABLE_ROWS = 8
BLOCK_ROWS = 16
OWNER_BLOCK = 512


def contract_rows(left, right):
    return lax.dot_general(
        left, right, (((0,), (0,)), ((), ())), preferred_element_type=jnp.float32
    )


def contract_columns(left, right):
    return lax.dot_general(
        left, right, (((1,), (1,)), ((), ())), preferred_element_type=jnp.float32
    )


def mirror_step(points, total_round, factor, inner_marginal):
    gradient = contract_columns(points, total_round) * (-1.0 / inner_marginal)
    row_scale = jnp.max(jnp.abs(gradient), axis=1, keepdims=True) + EPS
    tilted = factor.astype(jnp.float32) * jnp.exp(gradient * (-GAMMA / row_scale))
    mean = jnp.mean(tilted, axis=1, keepdims=True)
    mean = jnp.where(mean > 0, mean, 1.0)
    return (tilted * (1.0 / mean)).astype(jnp.bfloat16)


def inverse_norm(rows):
    return lax.rsqrt(jnp.sum(jnp.square(rows.astype(jnp.float32)), axis=1, keepdims=True) + EPS)


def blocks_of(n_dev, chunk, rank, features):
    kept = (chunk - TABLE_ROWS) // BLOCK_ROWS
    wide = features // rank
    return [
        (b // kept, b % kept * BLOCK_ROWS, b // wide * BLOCK_ROWS, b % wide * rank)
        for b in range(n_dev * kept)
    ]


def totals_of(sums_ref, total, features):
    n_dev, chunk, rank = sums_ref.shape
    for c, row, first, column in blocks_of(n_dev, chunk, rank, features):
        total[pl.ds(first, BLOCK_ROWS), pl.ds(column, rank)] = sums_ref[c, pl.ds(row, BLOCK_ROWS), :]


def whole(shape):
    return pl.BlockSpec(shape, lambda *_: (0,) * len(shape))


def in_hbm():
    return pl.BlockSpec(memory_space=pltpu.HBM)


def slot_row(cluster, n_group, capacity, spread, first):
    rows = cluster.shape[1]
    owners = cluster // spread
    onehot = owners == lax.broadcasted_iota(jnp.int32, (n_group, rows), 0)
    before = lax.broadcasted_iota(jnp.int32, (rows, rows), 0) < lax.broadcasted_iota(
        jnp.int32, (rows, rows), 1
    )
    earlier = jnp.dot(
        onehot.astype(jnp.bfloat16), before.astype(jnp.bfloat16), preferred_element_type=jnp.float32
    )
    ranking = jnp.sum(jnp.where(onehot, earlier, 0.0), axis=0, keepdims=True).astype(jnp.int32)
    return owners * capacity + ranking + first


def contract_kernel(n_dev, n_tgt, me_ref, src_cluster_ref, tgt_cluster_ref, *refs):
    hbm, (own_ref, other_ref), held, parts, in_sem = refs[:4], refs[4:6], refs[6:10], refs[10], refs[11]
    arrivals = [pltpu.make_async_copy(a, b, in_sem.at[i]) for i, (a, b) in enumerate(zip(hbm, held))]
    for copy in arrivals:
        copy.start()
    tgt_points, tgt_factor, src_points, src_factor = held
    _, _, _, chunk, rank = parts.shape
    kept = chunk - TABLE_ROWS
    me = me_ref[0]
    mine = (me // n_tgt) % 2
    row = lax.broadcasted_iota(jnp.int32, (TABLE_ROWS, rank), 0)
    table = jnp.where(row == 0, src_cluster_ref[...], jnp.where(row == 1, tgt_cluster_ref[...], 0))
    parts[:, :, :, kept:, :] = jnp.zeros(parts.shape[:3] + (TABLE_ROWS, rank), jnp.float32)
    parts[me // (2 * n_tgt), mine, me % n_tgt, kept:, :] = table.astype(jnp.float32)
    features = tgt_points.shape[1]
    blocks = blocks_of(n_dev, chunk, rank, features)
    for which, (points, factor) in enumerate(((tgt_points, tgt_factor), (src_points, src_factor))):
        arrivals[2 * which].wait()
        arrivals[2 * which + 1].wait()
        total = contract_rows(factor[...], points[...])
        for c, row, first, column in blocks:
            first -= which * rank
            if 0 <= first < rank:
                place = (c // (2 * n_tgt), c // n_tgt % 2, c % n_tgt)
                parts[(*place, pl.ds(row, BLOCK_ROWS))] = total[
                    first : first + BLOCK_ROWS, column : column + rank
                ]
    for i in range(parts.shape[0]):
        own_ref[i] = parts[i, mine]
        other_ref[i] = parts[i, 1 - mine].astype(jnp.bfloat16)


def partial_sums(
    me, src_cluster, tgt_cluster, src_points, tgt_points, src_factor, tgt_factor, n_dev, n_tgt
):
    rows, features = src_points.shape
    rank = src_factor.shape[1]
    chunk = 2 * features // n_dev + TABLE_ROWS
    shape = (n_dev // (2 * n_tgt), n_tgt, chunk, rank)
    vmem = pl.BlockSpec(memory_space=pltpu.VMEM)
    return pl.pallas_call(
        functools.partial(contract_kernel, n_dev, n_tgt),
        out_shape=(
            jax.ShapeDtypeStruct(shape, jnp.float32),
            jax.ShapeDtypeStruct(shape, jnp.bfloat16),
        ),
        in_specs=[pl.BlockSpec(memory_space=pltpu.SMEM)] + [vmem] * 2 + [in_hbm()] * 4,
        out_specs=(vmem, vmem),
        scratch_shapes=[
            pltpu.VMEM((rows, features), jnp.bfloat16),
            pltpu.VMEM((rows, rank), jnp.bfloat16),
            pltpu.VMEM((rows, features), jnp.bfloat16),
            pltpu.VMEM((rows, rank), jnp.bfloat16),
            pltpu.VMEM((n_dev // (2 * n_tgt), 2, n_tgt, chunk, rank), jnp.float32),
            pltpu.SemaphoreType.DMA((4,)),
        ],
        compiler_params=pltpu.CompilerParams(vmem_limit_bytes=PACK_VMEM_BYTES),
        cost_estimate=pl.CostEstimate(
            flops=4 * rows * features * rank,
            bytes_accessed=4 * rows * (features + rank) + 4 * n_dev * chunk * rank,
            transcendentals=0,
        ),
        name="partial_sums",
    )(me[None], src_cluster[None, :], tgt_cluster[None, :], tgt_points, tgt_factor, src_points, src_factor)


def place_rows(kinds, packed, packed_hbm, out_sem):
    block = 256
    departures = []
    for part in range(packed.shape[0] // block):
        mine = pl.ds(part * block, block)
        total = None
        for slot, held in kinds:
            index = lax.broadcasted_iota(jnp.int32, (block, slot.shape[1]), 0) + part * block
            place = (index == slot).astype(jnp.bfloat16)
            rows = [
                jnp.dot(place, array, preferred_element_type=jnp.float32) for array in held
            ]
            total = rows if total is None else [a + b for a, b in zip(total, rows)]
        column = 0
        for rows in total:
            packed[mine, column : column + rows.shape[1]] = rows.astype(jnp.bfloat16)
            column += rows.shape[1]
        departures.append(
            pltpu.make_async_copy(packed.at[mine], packed_hbm.at[mine], out_sem.at[part])
        )
        departures[-1].start()
    return departures


def pack_kernel(
    n_dev,
    capacity,
    cluster_ref,
    points_hbm,
    factor_hbm,
    packed_hbm,
    points,
    factor,
    packed,
    in_sem,
    out_sem,
):
    arrivals = [
        pltpu.make_async_copy(points_hbm, points, in_sem.at[0]),
        pltpu.make_async_copy(factor_hbm, factor, in_sem.at[1]),
    ]
    for copy in arrivals:
        copy.start()
    slot = slot_row(cluster_ref[...], n_dev, capacity, CL_DEV, 0)
    for copy in arrivals:
        copy.wait()
    for copy in place_rows([(slot, (points[...], factor[...]))], packed, packed_hbm, out_sem):
        copy.wait()


def pack(cluster, points, factor, n_dev, capacity):
    rows, features = points.shape
    rank = factor.shape[1]
    width = features + rank
    slots = n_dev * capacity
    return pl.pallas_call(
        functools.partial(pack_kernel, n_dev, capacity),
        out_shape=jax.ShapeDtypeStruct((slots, width), jnp.bfloat16),
        in_specs=[pl.BlockSpec(memory_space=pltpu.VMEM), in_hbm(), in_hbm()],
        out_specs=in_hbm(),
        scratch_shapes=[
            pltpu.VMEM((rows, features), jnp.bfloat16),
            pltpu.VMEM((rows, rank), jnp.bfloat16),
            pltpu.VMEM((slots, width), jnp.bfloat16),
            pltpu.SemaphoreType.DMA((2,)),
            pltpu.SemaphoreType.DMA((slots // 256,)),
        ],
        compiler_params=pltpu.CompilerParams(vmem_limit_bytes=PACK_VMEM_BYTES),
        cost_estimate=pl.CostEstimate(
            flops=2 * slots * rows * width,
            bytes_accessed=2 * (slots + rows) * width,
            transcendentals=0,
        ),
        name="pack_rows",
    )(cluster[None, :], points, factor)


def digits_of(size, stride):
    bits = size.bit_length() - 1
    found = []
    while bits:
        take = 1 if bits % 2 else 2
        found.append((stride, 1 << take))
        stride <<= take
        bits -= take
    return found


class Chain:
    def __init__(self, own, other, n_src, n_tgt):
        self.n_dev = n_src * n_tgt
        first = (n_tgt, 2)
        src, tgt = digits_of(n_src // 2, 2 * n_tgt), digits_of(n_tgt, 1)
        self.plane, self.along = [first] + src, tgt
        self.dims = src[::-1] + [first] + tgt[::-1]
        self.left = [d for d in self.dims if d != first]
        x = own + self.sent(other, n_tgt).astype(jnp.float32)
        self.x = x.reshape(tuple(radix for _, radix in self.left) + own.shape[2:])

    def sent(self, array, mask):
        return lax.ppermute(array, ALL, [(i, i ^ mask) for i in range(self.n_dev)])

    def scatter(self, digit):
        stride, radix = digit
        dim = self.left.index(digit)
        mine = (lax.axis_index(ALL) // stride) % radix
        total = lax.dynamic_index_in_dim(self.x, mine, dim, keepdims=False)
        for j in range(1, radix):
            piece = lax.dynamic_index_in_dim(self.x, mine ^ j, dim, keepdims=False)
            total = total + self.sent(piece.astype(jnp.bfloat16), j * stride).astype(jnp.float32)
        self.x = total
        self.left.remove(digit)

    def gather(self, digit):
        stride, radix = digit
        mine = (lax.axis_index(ALL) // stride) % radix
        x = self.x.astype(jnp.bfloat16)
        got = [x] + [self.sent(x, j * stride) for j in range(1, radix)]
        self.left = [d for d in self.dims if d in self.left or d == digit]
        self.x = jnp.stack(
            [lax.select_n(mine ^ d, *got) if radix > 2 else jnp.where(mine == d, *got) for d in range(radix)],
            axis=self.left.index(digit),
        )


def update_kernel(
    src_points_ref,
    tgt_points_ref,
    src_factor_ref,
    tgt_factor_ref,
    marginal_ref,
    sums_ref,
    src_ref,
    tgt_ref,
    total,
):
    totals_of(sums_ref, total, src_points_ref.shape[1])
    rank = src_ref.shape[1]
    marginal = marginal_ref[...]
    src_ref[...] = mirror_step(src_points_ref[...], total[:rank], src_factor_ref[...], marginal)
    tgt_ref[...] = mirror_step(tgt_points_ref[...], total[rank:], tgt_factor_ref[...], marginal)


def updates(src_points, tgt_points, src_factor, tgt_factor, marginal, sums):
    rows, features = src_points.shape
    rank = src_factor.shape[1]
    shape = jax.ShapeDtypeStruct(src_factor.shape, jnp.bfloat16)
    return pl.pallas_call(
        update_kernel,
        out_shape=(shape, shape),
        scratch_shapes=[pltpu.VMEM((2 * rank, features), jnp.bfloat16)],
        compiler_params=pltpu.CompilerParams(vmem_limit_bytes=VMEM_BYTES),
        cost_estimate=pl.CostEstimate(
            flops=4 * rows * features * rank,
            bytes_accessed=4 * rows * (features + 2 * rank),
            transcendentals=2 * rows * rank,
        ),
        name="mirror_updates",
    )(src_points, tgt_points, src_factor, tgt_factor, marginal[None, :], sums)


def seen_block(ref, part, block):
    piece = block // ref.shape[1]
    return ref[pl.ds(part * piece, piece)].reshape(block, ref.shape[2])


def owner_kernel(
    features,
    src_ref,
    tgt_ref,
    sums_ref,
    marginal_ref,
    src_label_ref,
    tgt_label_ref,
    out_hbm,
    total,
    tgt_rows,
    tgt_update,
    tgt_inv,
    images,
    out_sem,
):
    totals_of(sums_ref, total, features)
    slots = images.shape[0]
    rank = tgt_update.shape[1]
    marginal = marginal_ref[...]
    block = OWNER_BLOCK
    for part in range(slots // block):
        mine = pl.ds(part * block, block)
        both = seen_block(tgt_ref, part, block)
        rows = both[:, :features]
        tgt_rows[mine, :] = rows
        tgt_update[mine, :] = mirror_step(rows, total[rank:], both[:, features:], marginal)
        tgt_inv[:, mine] = inverse_norm(rows).reshape(1, block)

    departures = []
    for part in range(slots // block):
        mine = pl.ds(part * block, block)
        both = seen_block(src_ref, part, block)
        rows = both[:, :features]
        update = mirror_step(rows, total[:rank], both[:, features:], marginal)
        cosine = contract_columns(rows, tgt_rows[...]) * inverse_norm(rows) * tgt_inv[...]
        weight = contract_columns(update, tgt_update[...]) * (1.0 / rank)
        label = src_label_ref[:, mine].reshape(block, 1)
        same = jnp.logical_and(label == tgt_label_ref[...], label > 0)
        kernel = jnp.where(same, weight * jnp.exp((cosine - 1.0) * (1.0 / TEMPER)), 0.0)
        denominator = jnp.sum(kernel, axis=1, keepdims=True)
        denominator = jnp.where(denominator > 0, denominator, 1.0)
        transport = (kernel * (1.0 / denominator)).astype(jnp.bfloat16)
        images[mine, :] = jnp.dot(
            transport, tgt_rows[...], preferred_element_type=jnp.float32
        ).astype(jnp.bfloat16)
        departures.append(
            pltpu.make_async_copy(images.at[mine], out_hbm.at[mine], out_sem.at[part])
        )
        departures[-1].start()
    for copy in departures:
        copy.wait()


def owner_maps(src, tgt, sums, marginal, src_labels, tgt_labels, features):
    n_dev, capacity, width = src.shape
    slots = n_dev * capacity
    rank = width - features
    return pl.pallas_call(
        functools.partial(owner_kernel, features),
        out_shape=jax.ShapeDtypeStruct((slots, features), jnp.bfloat16),
        grid=(1,),
        in_specs=[
            whole(src.shape),
            whole(tgt.shape),
            whole(sums.shape),
            whole((1, rank)),
            whole((1, slots)),
            whole((1, slots)),
        ],
        out_specs=in_hbm(),
        scratch_shapes=[
            pltpu.VMEM((2 * rank, features), jnp.bfloat16),
            pltpu.VMEM((slots, features), jnp.bfloat16),
            pltpu.VMEM((slots, rank), jnp.bfloat16),
            pltpu.VMEM((1, slots), jnp.float32),
            pltpu.VMEM((slots, features), jnp.bfloat16),
            pltpu.SemaphoreType.DMA((slots // OWNER_BLOCK,)),
        ],
        compiler_params=pltpu.CompilerParams(vmem_limit_bytes=VMEM_BYTES),
        cost_estimate=pl.CostEstimate(
            flops=4 * slots * features * (rank + slots),
            bytes_accessed=6 * slots * width,
            transcendentals=slots * slots,
        ),
        name="owner_maps",
    )(src, tgt, sums, marginal[None, :], src_labels[None, :], tgt_labels[None, :])


def labels_of(clusters, owner, capacity, spread):
    rows = clusters.shape[1]
    mine = clusters // spread == owner
    before = (jnp.arange(rows)[:, None] < jnp.arange(rows)[None, :]).astype(jnp.bfloat16)
    earlier = jnp.dot(mine.astype(jnp.bfloat16), before, preferred_element_type=jnp.float32)
    ranking = jnp.where(mine, earlier.astype(jnp.int32), -1)
    value = clusters - owner * spread + 1
    hit = ranking[:, None, :] == jnp.arange(capacity, dtype=jnp.int32)[None, :, None]
    return jnp.sum(jnp.where(hit, value[:, None, :], 0), axis=2).reshape(-1)


def exchange(rows):
    return lax.all_to_all(rows, ALL, split_axis=0, concat_axis=0, tiled=True)


def per_device(
    src_points, tgt_points, src_factor, tgt_factor, inner_marginal, src_cluster, tgt_cluster
):
    n_src, n_tgt = lax.axis_size("src"), lax.axis_size("tgt")
    n_dev = n_src * n_tgt
    rows, features = src_points.shape
    rank = src_factor.shape[1]
    capacity = 2 * rows // n_dev
    owner = lax.axis_index(ALL)

    tgt = pack(tgt_cluster, tgt_points, tgt_factor, n_dev, capacity)
    tgt, me = lax.optimization_barrier((tgt, owner))
    tgt = exchange(tgt)
    own, other = partial_sums(
        me,
        src_cluster,
        tgt_cluster,
        src_points,
        tgt_points,
        src_factor,
        tgt_factor,
        n_dev,
        n_tgt,
    )
    chain = Chain(own, other, n_src, n_tgt)
    for digit in chain.plane[1:]:
        chain.scatter(digit)
    for digit in chain.along:
        chain.scatter(digit)
    src = pack(src_cluster, src_points, src_factor, n_dev, capacity)
    src, tgt, chain.x = lax.optimization_barrier((src, tgt, chain.x))
    src = exchange(src)
    for digit in reversed(chain.plane + chain.along):
        chain.gather(digit)
    sums = chain.x.reshape(n_dev, -1, rank)

    kept = 2 * features // n_dev
    table = sums[:, kept : kept + 2].astype(jnp.int32)
    src_labels = labels_of(table[:, 0], owner, capacity, CL_DEV)
    tgt_labels = labels_of(table[:, 1], owner, capacity, CL_DEV)

    shape = (n_dev, capacity, features + rank)
    images = owner_maps(
        src.reshape(shape), tgt.reshape(shape), sums, inner_marginal, src_labels, tgt_labels, features
    )
    returned = exchange(images)

    src_update, tgt_update = updates(
        src_points, tgt_points, src_factor, tgt_factor, inner_marginal, sums
    )
    slot = slot_row(src_cluster[None, :], n_dev, capacity, CL_DEV, 0)
    back = (jnp.arange(n_dev * capacity, dtype=jnp.int32)[:, None] == slot).astype(jnp.bfloat16)
    mapped = contract_rows(back, returned).astype(jnp.bfloat16)
    return (src_update, tgt_update, mapped)


def solution(mesh):
    rows = P(ALL, None)
    return jax.shard_map(
        per_device,
        mesh=mesh,
        in_specs=(rows, rows, rows, rows, P(), P(ALL), P(ALL)),
        out_specs=(rows, rows, rows),
        check_vma=False,
    )
```

```python
import functools

import jax
import jax.numpy as jnp
from jax import lax
from jax.experimental import pallas as pl
from jax.experimental.pallas import tpu as pltpu
from jax.sharding import PartitionSpec as P

CL_DEV = 2

GAMMA = 2.0
TEMPER = 0.03
EPS = 1e-06

ALL = ("src", "tgt")
VMEM_BYTES = 48 * 1024 * 1024
PACK_VMEM_BYTES = 62 * 1024 * 1024
TABLE_ROWS = 8
BLOCK_ROWS = 16
OWNER_BLOCK = 512


def contract_rows(left, right):
    return lax.dot_general(
        left, right, (((0,), (0,)), ((), ())), preferred_element_type=jnp.float32
    )


def contract_columns(left, right):
    return lax.dot_general(
        left, right, (((1,), (1,)), ((), ())), preferred_element_type=jnp.float32
    )


def mirror_step(points, total_round, factor, inner_marginal):
    gradient = contract_columns(points, total_round) * (-1.0 / inner_marginal)
    row_scale = jnp.max(jnp.abs(gradient), axis=1, keepdims=True) + EPS
    tilted = factor.astype(jnp.float32) * jnp.exp(gradient * (-GAMMA / row_scale))
    mean = jnp.mean(tilted, axis=1, keepdims=True)
    mean = jnp.where(mean > 0, mean, 1.0)
    return (tilted * (1.0 / mean)).astype(jnp.bfloat16)


def inverse_norm(rows):
    return lax.rsqrt(jnp.sum(jnp.square(rows.astype(jnp.float32)), axis=1, keepdims=True) + EPS)


def blocks_of(n_dev, chunk, rank, features):
    kept = (chunk - TABLE_ROWS) // BLOCK_ROWS
    wide = features // rank
    return [
        (b // kept, b % kept * BLOCK_ROWS, b // wide * BLOCK_ROWS, b % wide * rank)
        for b in range(n_dev * kept)
    ]


def totals_of(sums_ref, total, features):
    n_dev, chunk, rank = sums_ref.shape
    for c, row, first, column in blocks_of(n_dev, chunk, rank, features):
        total[pl.ds(first, BLOCK_ROWS), pl.ds(column, rank)] = sums_ref[c, pl.ds(row, BLOCK_ROWS), :]


def whole(shape):
    return pl.BlockSpec(shape, lambda *_: (0,) * len(shape))


def in_hbm():
    return pl.BlockSpec(memory_space=pltpu.HBM)


def slot_row(cluster, n_group, capacity, spread, first):
    rows = cluster.shape[1]
    owners = cluster // spread
    onehot = owners == lax.broadcasted_iota(jnp.int32, (n_group, rows), 0)
    before = lax.broadcasted_iota(jnp.int32, (rows, rows), 0) < lax.broadcasted_iota(
        jnp.int32, (rows, rows), 1
    )
    earlier = jnp.dot(
        onehot.astype(jnp.bfloat16), before.astype(jnp.bfloat16), preferred_element_type=jnp.float32
    )
    ranking = jnp.sum(jnp.where(onehot, earlier, 0.0), axis=0, keepdims=True).astype(jnp.int32)
    return owners * capacity + ranking + first


def contract_kernel(n_dev, n_tgt, me_ref, src_cluster_ref, tgt_cluster_ref, *refs):
    hbm, (own_ref, other_ref), held, parts, in_sem = refs[:4], refs[4:6], refs[6:10], refs[10], refs[11]
    arrivals = [pltpu.make_async_copy(a, b, in_sem.at[i]) for i, (a, b) in enumerate(zip(hbm, held))]
    for copy in arrivals:
        copy.start()
    tgt_points, tgt_factor, src_points, src_factor = held
    _, _, _, chunk, rank = parts.shape
    kept = chunk - TABLE_ROWS
    me = me_ref[0]
    mine = (me // n_tgt) % 2
    row = lax.broadcasted_iota(jnp.int32, (TABLE_ROWS, rank), 0)
    table = jnp.where(row == 0, src_cluster_ref[...], jnp.where(row == 1, tgt_cluster_ref[...], 0))
    parts[:, :, :, kept:, :] = jnp.zeros(parts.shape[:3] + (TABLE_ROWS, rank), jnp.float32)
    parts[me // (2 * n_tgt), mine, me % n_tgt, kept:, :] = table.astype(jnp.float32)
    features = tgt_points.shape[1]
    blocks = blocks_of(n_dev, chunk, rank, features)
    for which, (points, factor) in enumerate(((tgt_points, tgt_factor), (src_points, src_factor))):
        arrivals[2 * which].wait()
        arrivals[2 * which + 1].wait()
        total = contract_rows(factor[...], points[...])
        for c, row, first, column in blocks:
            first -= which * rank
            if 0 <= first < rank:
                place = (c // (2 * n_tgt), c // n_tgt % 2, c % n_tgt)
                parts[(*place, pl.ds(row, BLOCK_ROWS))] = total[
                    first : first + BLOCK_ROWS, column : column + rank
                ]
    for i in range(parts.shape[0]):
        own_ref[i] = parts[i, mine]
        other_ref[i] = parts[i, 1 - mine].astype(jnp.bfloat16)


def partial_sums(
    me, src_cluster, tgt_cluster, src_points, tgt_points, src_factor, tgt_factor, n_dev, n_tgt
):
    rows, features = src_points.shape
    rank = src_factor.shape[1]
    chunk = 2 * features // n_dev + TABLE_ROWS
    shape = (n_dev // (2 * n_tgt), n_tgt, chunk, rank)
    vmem = pl.BlockSpec(memory_space=pltpu.VMEM)
    return pl.pallas_call(
        functools.partial(contract_kernel, n_dev, n_tgt),
        out_shape=(
            jax.ShapeDtypeStruct(shape, jnp.float32),
            jax.ShapeDtypeStruct(shape, jnp.bfloat16),
        ),
        in_specs=[pl.BlockSpec(memory_space=pltpu.SMEM)] + [vmem] * 2 + [in_hbm()] * 4,
        out_specs=(vmem, vmem),
        scratch_shapes=[
            pltpu.VMEM((rows, features), jnp.bfloat16),
            pltpu.VMEM((rows, rank), jnp.bfloat16),
            pltpu.VMEM((rows, features), jnp.bfloat16),
            pltpu.VMEM((rows, rank), jnp.bfloat16),
            pltpu.VMEM((n_dev // (2 * n_tgt), 2, n_tgt, chunk, rank), jnp.float32),
            pltpu.SemaphoreType.DMA((4,)),
        ],
        compiler_params=pltpu.CompilerParams(vmem_limit_bytes=PACK_VMEM_BYTES),
        cost_estimate=pl.CostEstimate(
            flops=4 * rows * features * rank,
            bytes_accessed=4 * rows * (features + rank) + 4 * n_dev * chunk * rank,
            transcendentals=0,
        ),
        name="partial_sums",
    )(me[None], src_cluster[None, :], tgt_cluster[None, :], tgt_points, tgt_factor, src_points, src_factor)


def place_rows(kinds, packed, packed_hbm, out_sem):
    block = 256
    departures = []
    for part in range(packed.shape[0] // block):
        mine = pl.ds(part * block, block)
        total = None
        for slot, held in kinds:
            index = lax.broadcasted_iota(jnp.int32, (block, slot.shape[1]), 0) + part * block
            place = (index == slot).astype(jnp.bfloat16)
            rows = [
                jnp.dot(place, array, preferred_element_type=jnp.float32) for array in held
            ]
            total = rows if total is None else [a + b for a, b in zip(total, rows)]
        column = 0
        for rows in total:
            packed[mine, column : column + rows.shape[1]] = rows.astype(jnp.bfloat16)
            column += rows.shape[1]
        departures.append(
            pltpu.make_async_copy(packed.at[mine], packed_hbm.at[mine], out_sem.at[part])
        )
        departures[-1].start()
    return departures


def pack_kernel(
    n_dev,
    capacity,
    cluster_ref,
    points_hbm,
    factor_hbm,
    packed_hbm,
    points,
    factor,
    packed,
    in_sem,
    out_sem,
):
    arrivals = [
        pltpu.make_async_copy(points_hbm, points, in_sem.at[0]),
        pltpu.make_async_copy(factor_hbm, factor, in_sem.at[1]),
    ]
    for copy in arrivals:
        copy.start()
    slot = slot_row(cluster_ref[...], n_dev, capacity, CL_DEV, 0)
    for copy in arrivals:
        copy.wait()
    for copy in place_rows([(slot, (points[...], factor[...]))], packed, packed_hbm, out_sem):
        copy.wait()


def pack(cluster, points, factor, n_dev, capacity):
    rows, features = points.shape
    rank = factor.shape[1]
    width = features + rank
    slots = n_dev * capacity
    return pl.pallas_call(
        functools.partial(pack_kernel, n_dev, capacity),
        out_shape=jax.ShapeDtypeStruct((slots, width), jnp.bfloat16),
        in_specs=[pl.BlockSpec(memory_space=pltpu.VMEM), in_hbm(), in_hbm()],
        out_specs=in_hbm(),
        scratch_shapes=[
            pltpu.VMEM((rows, features), jnp.bfloat16),
            pltpu.VMEM((rows, rank), jnp.bfloat16),
            pltpu.VMEM((slots, width), jnp.bfloat16),
            pltpu.SemaphoreType.DMA((2,)),
            pltpu.SemaphoreType.DMA((slots // 256,)),
        ],
        compiler_params=pltpu.CompilerParams(vmem_limit_bytes=PACK_VMEM_BYTES),
        cost_estimate=pl.CostEstimate(
            flops=2 * slots * rows * width,
            bytes_accessed=2 * (slots + rows) * width,
            transcendentals=0,
        ),
        name="pack_rows",
    )(cluster[None, :], points, factor)


def digits_of(size, stride):
    bits = size.bit_length() - 1
    found = []
    while bits:
        take = 1 if bits % 2 else 2
        found.append((stride, 1 << take))
        stride <<= take
        bits -= take
    return found


class Chain:
    def __init__(self, own, other, n_src, n_tgt):
        self.n_dev = n_src * n_tgt
        first = (n_tgt, 2)
        src, tgt = digits_of(n_src // 2, 2 * n_tgt), digits_of(n_tgt, 1)
        self.plane, self.along = [first] + src, tgt
        self.dims = src[::-1] + [first] + tgt[::-1]
        self.left = [d for d in self.dims if d != first]
        x = own + self.sent(other, n_tgt).astype(jnp.float32)
        self.x = x.reshape(tuple(radix for _, radix in self.left) + own.shape[2:])

    def sent(self, array, mask):
        return lax.ppermute(array, ALL, [(i, i ^ mask) for i in range(self.n_dev)])

    def scatter(self, digit):
        stride, radix = digit
        dim = self.left.index(digit)
        mine = (lax.axis_index(ALL) // stride) % radix
        total = lax.dynamic_index_in_dim(self.x, mine, dim, keepdims=False)
        for j in range(1, radix):
            piece = lax.dynamic_index_in_dim(self.x, mine ^ j, dim, keepdims=False)
            total = total + self.sent(piece.astype(jnp.bfloat16), j * stride).astype(jnp.float32)
        self.x = total
        self.left.remove(digit)

    def gather(self, digit):
        stride, radix = digit
        mine = (lax.axis_index(ALL) // stride) % radix
        x = self.x.astype(jnp.bfloat16)
        if radix == 4 and digit in self.plane:
            pair = jnp.stack([x, self.sent(x, stride)])
            other = self.sent(pair, 2 * stride)
            got = [pair[0], pair[1], other[0], other[1]]
        else:
            got = [x] + [self.sent(x, j * stride) for j in range(1, radix)]
        self.left = [d for d in self.dims if d in self.left or d == digit]
        self.x = jnp.stack(
            [lax.select_n(mine ^ d, *got) if radix > 2 else jnp.where(mine == d, *got) for d in range(radix)],
            axis=self.left.index(digit),
        )


def update_kernel(
    src_points_ref,
    tgt_points_ref,
    src_factor_ref,
    tgt_factor_ref,
    marginal_ref,
    sums_ref,
    src_ref,
    tgt_ref,
    total,
):
    totals_of(sums_ref, total, src_points_ref.shape[1])
    rank = src_ref.shape[1]
    marginal = marginal_ref[...]
    src_ref[...] = mirror_step(src_points_ref[...], total[:rank], src_factor_ref[...], marginal)
    tgt_ref[...] = mirror_step(tgt_points_ref[...], total[rank:], tgt_factor_ref[...], marginal)


def updates(src_points, tgt_points, src_factor, tgt_factor, marginal, sums):
    rows, features = src_points.shape
    rank = src_factor.shape[1]
    shape = jax.ShapeDtypeStruct(src_factor.shape, jnp.bfloat16)
    return pl.pallas_call(
        update_kernel,
        out_shape=(shape, shape),
        scratch_shapes=[pltpu.VMEM((2 * rank, features), jnp.bfloat16)],
        compiler_params=pltpu.CompilerParams(vmem_limit_bytes=VMEM_BYTES),
        cost_estimate=pl.CostEstimate(
            flops=4 * rows * features * rank,
            bytes_accessed=4 * rows * (features + 2 * rank),
            transcendentals=2 * rows * rank,
        ),
        name="mirror_updates",
    )(src_points, tgt_points, src_factor, tgt_factor, marginal[None, :], sums)


def seen_block(ref, part, block):
    piece = block // ref.shape[1]
    return ref[pl.ds(part * piece, piece)].reshape(block, ref.shape[2])


def owner_kernel(
    features,
    src_ref,
    tgt_ref,
    sums_ref,
    marginal_ref,
    src_label_ref,
    tgt_label_ref,
    out_hbm,
    total,
    tgt_rows,
    tgt_update,
    tgt_inv,
    images,
    out_sem,
):
    totals_of(sums_ref, total, features)
    slots = images.shape[0]
    rank = tgt_update.shape[1]
    marginal = marginal_ref[...]
    block = OWNER_BLOCK
    for part in range(slots // block):
        mine = pl.ds(part * block, block)
        both = seen_block(tgt_ref, part, block)
        rows = both[:, :features]
        tgt_rows[mine, :] = rows
        tgt_update[mine, :] = mirror_step(rows, total[rank:], both[:, features:], marginal)
        tgt_inv[:, mine] = inverse_norm(rows).reshape(1, block)

    departures = []
    for part in range(slots // block):
        mine = pl.ds(part * block, block)
        both = seen_block(src_ref, part, block)
        rows = both[:, :features]
        update = mirror_step(rows, total[:rank], both[:, features:], marginal)
        cosine = contract_columns(rows, tgt_rows[...]) * inverse_norm(rows) * tgt_inv[...]
        weight = contract_columns(update, tgt_update[...]) * (1.0 / rank)
        label = src_label_ref[:, mine].reshape(block, 1)
        same = jnp.logical_and(label == tgt_label_ref[...], label > 0)
        kernel = jnp.where(same, weight * jnp.exp((cosine - 1.0) * (1.0 / TEMPER)), 0.0)
        denominator = jnp.sum(kernel, axis=1, keepdims=True)
        denominator = jnp.where(denominator > 0, denominator, 1.0)
        transport = (kernel * (1.0 / denominator)).astype(jnp.bfloat16)
        images[mine, :] = jnp.dot(
            transport, tgt_rows[...], preferred_element_type=jnp.float32
        ).astype(jnp.bfloat16)
        departures.append(
            pltpu.make_async_copy(images.at[mine], out_hbm.at[mine], out_sem.at[part])
        )
        departures[-1].start()
    for copy in departures:
        copy.wait()


def owner_maps(src, tgt, sums, marginal, src_labels, tgt_labels, features):
    n_dev, capacity, width = src.shape
    slots = n_dev * capacity
    rank = width - features
    return pl.pallas_call(
        functools.partial(owner_kernel, features),
        out_shape=jax.ShapeDtypeStruct((slots, features), jnp.bfloat16),
        grid=(1,),
        in_specs=[
            whole(src.shape),
            whole(tgt.shape),
            whole(sums.shape),
            whole((1, rank)),
            whole((1, slots)),
            whole((1, slots)),
        ],
        out_specs=in_hbm(),
        scratch_shapes=[
            pltpu.VMEM((2 * rank, features), jnp.bfloat16),
            pltpu.VMEM((slots, features), jnp.bfloat16),
            pltpu.VMEM((slots, rank), jnp.bfloat16),
            pltpu.VMEM((1, slots), jnp.float32),
            pltpu.VMEM((slots, features), jnp.bfloat16),
            pltpu.SemaphoreType.DMA((slots // OWNER_BLOCK,)),
        ],
        compiler_params=pltpu.CompilerParams(vmem_limit_bytes=VMEM_BYTES),
        cost_estimate=pl.CostEstimate(
            flops=4 * slots * features * (rank + slots),
            bytes_accessed=6 * slots * width,
            transcendentals=slots * slots,
        ),
        name="owner_maps",
    )(src, tgt, sums, marginal[None, :], src_labels[None, :], tgt_labels[None, :])


def labels_of(clusters, owner, capacity, spread):
    rows = clusters.shape[1]
    mine = clusters // spread == owner
    before = (jnp.arange(rows)[:, None] < jnp.arange(rows)[None, :]).astype(jnp.bfloat16)
    earlier = jnp.dot(mine.astype(jnp.bfloat16), before, preferred_element_type=jnp.float32)
    ranking = jnp.where(mine, earlier.astype(jnp.int32), -1)
    value = clusters - owner * spread + 1
    hit = ranking[:, None, :] == jnp.arange(capacity, dtype=jnp.int32)[None, :, None]
    return jnp.sum(jnp.where(hit, value[:, None, :], 0), axis=2).reshape(-1)


def exchange(rows):
    return lax.all_to_all(rows, ALL, split_axis=0, concat_axis=0, tiled=True)


def per_device(
    src_points, tgt_points, src_factor, tgt_factor, inner_marginal, src_cluster, tgt_cluster
):
    n_src, n_tgt = lax.axis_size("src"), lax.axis_size("tgt")
    n_dev = n_src * n_tgt
    rows, features = src_points.shape
    rank = src_factor.shape[1]
    capacity = 2 * rows // n_dev
    owner = lax.axis_index(ALL)

    tgt = pack(tgt_cluster, tgt_points, tgt_factor, n_dev, capacity)
    tgt, me = lax.optimization_barrier((tgt, owner))
    tgt = exchange(tgt)
    own, other = partial_sums(
        me,
        src_cluster,
        tgt_cluster,
        src_points,
        tgt_points,
        src_factor,
        tgt_factor,
        n_dev,
        n_tgt,
    )
    chain = Chain(own, other, n_src, n_tgt)
    for digit in chain.plane[1:]:
        chain.scatter(digit)
    for digit in chain.along:
        chain.scatter(digit)
    src = pack(src_cluster, src_points, src_factor, n_dev, capacity)
    src, tgt, chain.x = lax.optimization_barrier((src, tgt, chain.x))
    src = exchange(src)
    for digit in reversed(chain.plane + chain.along):
        chain.gather(digit)
    sums = chain.x.reshape(n_dev, -1, rank)

    kept = 2 * features // n_dev
    table = sums[:, kept : kept + 2].astype(jnp.int32)
    src_labels = labels_of(table[:, 0], owner, capacity, CL_DEV)
    tgt_labels = labels_of(table[:, 1], owner, capacity, CL_DEV)

    shape = (n_dev, capacity, features + rank)
    images = owner_maps(
        src.reshape(shape), tgt.reshape(shape), sums, inner_marginal, src_labels, tgt_labels, features
    )
    returned = exchange(images)

    src_update, tgt_update = updates(
        src_points, tgt_points, src_factor, tgt_factor, inner_marginal, sums
    )
    slot = slot_row(src_cluster[None, :], n_dev, capacity, CL_DEV, 0)
    back = (jnp.arange(n_dev * capacity, dtype=jnp.int32)[:, None] == slot).astype(jnp.bfloat16)
    mapped = contract_rows(back, returned).astype(jnp.bfloat16)
    return (src_update, tgt_update, mapped)


def solution(mesh):
    rows = P(ALL, None)
    return jax.shard_map(
        per_device,
        mesh=mesh,
        in_specs=(rows, rows, rows, rows, P(), P(ALL), P(ALL)),
        out_specs=(rows, rows, rows),
        check_vma=False,
    )
```

```python
import functools

import jax
import jax.numpy as jnp
from jax import lax
from jax.experimental import pallas as pl
from jax.experimental.pallas import tpu as pltpu
from jax.sharding import PartitionSpec as P

CL_DEV = 2

GAMMA = 2.0
TEMPER = 0.03
EPS = 1e-06

ALL = ("src", "tgt")
VMEM_BYTES = 48 * 1024 * 1024
PACK_VMEM_BYTES = 62 * 1024 * 1024
TABLE_ROWS = 8
BLOCK_ROWS = 16
OWNER_BLOCK = 512


def contract_rows(left, right):
    return lax.dot_general(
        left, right, (((0,), (0,)), ((), ())), preferred_element_type=jnp.float32
    )


def contract_columns(left, right):
    return lax.dot_general(
        left, right, (((1,), (1,)), ((), ())), preferred_element_type=jnp.float32
    )


def mirror_step(points, total_round, factor, inner_marginal):
    gradient = contract_columns(points, total_round) * (-1.0 / inner_marginal)
    row_scale = jnp.max(jnp.abs(gradient), axis=1, keepdims=True) + EPS
    tilted = factor.astype(jnp.float32) * jnp.exp(gradient * (-GAMMA / row_scale))
    mean = jnp.mean(tilted, axis=1, keepdims=True)
    mean = jnp.where(mean > 0, mean, 1.0)
    return (tilted * (1.0 / mean)).astype(jnp.bfloat16)


def inverse_norm(rows):
    return lax.rsqrt(jnp.sum(jnp.square(rows.astype(jnp.float32)), axis=1, keepdims=True) + EPS)


def blocks_of(n_dev, chunk, rank, features):
    kept = (chunk - TABLE_ROWS) // BLOCK_ROWS
    wide = features // rank
    return [
        (b // kept, b % kept * BLOCK_ROWS, b // wide * BLOCK_ROWS, b % wide * rank)
        for b in range(n_dev * kept)
    ]


def totals_of(sums_ref, total, features):
    n_dev, chunk, rank = sums_ref.shape
    for c, row, first, column in blocks_of(n_dev, chunk, rank, features):
        total[pl.ds(first, BLOCK_ROWS), pl.ds(column, rank)] = sums_ref[c, pl.ds(row, BLOCK_ROWS), :]


def whole(shape):
    return pl.BlockSpec(shape, lambda *_: (0,) * len(shape))


def in_hbm():
    return pl.BlockSpec(memory_space=pltpu.HBM)


def slot_row(cluster, n_group, capacity, spread, first):
    rows = cluster.shape[1]
    owners = cluster // spread
    onehot = owners == lax.broadcasted_iota(jnp.int32, (n_group, rows), 0)
    before = lax.broadcasted_iota(jnp.int32, (rows, rows), 0) < lax.broadcasted_iota(
        jnp.int32, (rows, rows), 1
    )
    earlier = jnp.dot(
        onehot.astype(jnp.bfloat16), before.astype(jnp.bfloat16), preferred_element_type=jnp.float32
    )
    ranking = jnp.sum(jnp.where(onehot, earlier, 0.0), axis=0, keepdims=True).astype(jnp.int32)
    return owners * capacity + ranking + first


def contract_kernel(n_dev, n_tgt, me_ref, src_cluster_ref, tgt_cluster_ref, *refs):
    hbm, (own_ref, other_ref), held, parts, in_sem = refs[:4], refs[4:6], refs[6:10], refs[10], refs[11]
    arrivals = [pltpu.make_async_copy(a, b, in_sem.at[i]) for i, (a, b) in enumerate(zip(hbm, held))]
    for copy in arrivals:
        copy.start()
    tgt_points, tgt_factor, src_points, src_factor = held
    _, _, _, chunk, rank = parts.shape
    kept = chunk - TABLE_ROWS
    me = me_ref[0]
    mine = (me // n_tgt) % 2
    row = lax.broadcasted_iota(jnp.int32, (TABLE_ROWS, rank), 0)
    table = jnp.where(row == 0, src_cluster_ref[...], jnp.where(row == 1, tgt_cluster_ref[...], 0))
    parts[:, :, :, kept:, :] = jnp.zeros(parts.shape[:3] + (TABLE_ROWS, rank), jnp.float32)
    parts[me // (2 * n_tgt), mine, me % n_tgt, kept:, :] = table.astype(jnp.float32)
    features = tgt_points.shape[1]
    blocks = blocks_of(n_dev, chunk, rank, features)
    for which, (points, factor) in enumerate(((tgt_points, tgt_factor), (src_points, src_factor))):
        arrivals[2 * which].wait()
        arrivals[2 * which + 1].wait()
        total = contract_rows(factor[...], points[...])
        for c, row, first, column in blocks:
            first -= which * rank
            if 0 <= first < rank:
                place = (c // (2 * n_tgt), c // n_tgt % 2, c % n_tgt)
                parts[(*place, pl.ds(row, BLOCK_ROWS))] = total[
                    first : first + BLOCK_ROWS, column : column + rank
                ]
    for i in range(parts.shape[0]):
        own_ref[i] = parts[i, mine]
        other_ref[i] = parts[i, 1 - mine].astype(jnp.bfloat16)


def partial_sums(
    me, src_cluster, tgt_cluster, src_points, tgt_points, src_factor, tgt_factor, n_dev, n_tgt
):
    rows, features = src_points.shape
    rank = src_factor.shape[1]
    chunk = 2 * features // n_dev + TABLE_ROWS
    shape = (n_dev // (2 * n_tgt), n_tgt, chunk, rank)
    vmem = pl.BlockSpec(memory_space=pltpu.VMEM)
    return pl.pallas_call(
        functools.partial(contract_kernel, n_dev, n_tgt),
        out_shape=(
            jax.ShapeDtypeStruct(shape, jnp.float32),
            jax.ShapeDtypeStruct(shape, jnp.bfloat16),
        ),
        in_specs=[pl.BlockSpec(memory_space=pltpu.SMEM)] + [vmem] * 2 + [in_hbm()] * 4,
        out_specs=(vmem, vmem),
        scratch_shapes=[
            pltpu.VMEM((rows, features), jnp.bfloat16),
            pltpu.VMEM((rows, rank), jnp.bfloat16),
            pltpu.VMEM((rows, features), jnp.bfloat16),
            pltpu.VMEM((rows, rank), jnp.bfloat16),
            pltpu.VMEM((n_dev // (2 * n_tgt), 2, n_tgt, chunk, rank), jnp.float32),
            pltpu.SemaphoreType.DMA((4,)),
        ],
        compiler_params=pltpu.CompilerParams(vmem_limit_bytes=PACK_VMEM_BYTES),
        cost_estimate=pl.CostEstimate(
            flops=4 * rows * features * rank,
            bytes_accessed=4 * rows * (features + rank) + 4 * n_dev * chunk * rank,
            transcendentals=0,
        ),
        name="partial_sums",
    )(me[None], src_cluster[None, :], tgt_cluster[None, :], tgt_points, tgt_factor, src_points, src_factor)


def place_rows(kinds, packed, packed_hbm, out_sem):
    block = OWNER_BLOCK
    departures = []
    for part in range(packed.shape[0] // block):
        mine = pl.ds(part * block, block)
        total = None
        for slot, held in kinds:
            index = lax.broadcasted_iota(jnp.int32, (block, slot.shape[1]), 0) + part * block
            place = (index == slot).astype(jnp.bfloat16)
            rows = [
                jnp.dot(place, array, preferred_element_type=jnp.float32) for array in held
            ]
            total = rows if total is None else [a + b for a, b in zip(total, rows)]
        column = 0
        for rows in total:
            packed[mine, column : column + rows.shape[1]] = rows.astype(jnp.bfloat16)
            column += rows.shape[1]
        departures.append(
            pltpu.make_async_copy(packed.at[mine], packed_hbm.at[mine], out_sem.at[part])
        )
        departures[-1].start()
    return departures


def pack_kernel(
    n_dev,
    capacity,
    cluster_ref,
    points_hbm,
    factor_hbm,
    packed_hbm,
    points,
    factor,
    packed,
    in_sem,
    out_sem,
):
    arrivals = [
        pltpu.make_async_copy(points_hbm, points, in_sem.at[0]),
        pltpu.make_async_copy(factor_hbm, factor, in_sem.at[1]),
    ]
    for copy in arrivals:
        copy.start()
    slot = slot_row(cluster_ref[...], n_dev, capacity, CL_DEV, 0)
    for copy in arrivals:
        copy.wait()
    for copy in place_rows([(slot, (points[...], factor[...]))], packed, packed_hbm, out_sem):
        copy.wait()


def pack(cluster, points, factor, n_dev, capacity):
    rows, features = points.shape
    rank = factor.shape[1]
    width = features + rank
    slots = n_dev * capacity
    return pl.pallas_call(
        functools.partial(pack_kernel, n_dev, capacity),
        out_shape=jax.ShapeDtypeStruct((slots, width), jnp.bfloat16),
        in_specs=[pl.BlockSpec(memory_space=pltpu.VMEM), in_hbm(), in_hbm()],
        out_specs=in_hbm(),
        scratch_shapes=[
            pltpu.VMEM((rows, features), jnp.bfloat16),
            pltpu.VMEM((rows, rank), jnp.bfloat16),
            pltpu.VMEM((slots, width), jnp.bfloat16),
            pltpu.SemaphoreType.DMA((2,)),
            pltpu.SemaphoreType.DMA((slots // OWNER_BLOCK,)),
        ],
        compiler_params=pltpu.CompilerParams(vmem_limit_bytes=PACK_VMEM_BYTES),
        cost_estimate=pl.CostEstimate(
            flops=2 * slots * rows * width,
            bytes_accessed=2 * (slots + rows) * width,
            transcendentals=0,
        ),
        name="pack_rows",
    )(cluster[None, :], points, factor)


def digits_of(size, stride):
    bits = size.bit_length() - 1
    found = []
    while bits:
        take = 1 if bits % 2 else 2
        found.append((stride, 1 << take))
        stride <<= take
        bits -= take
    return found


class Chain:
    def __init__(self, own, other, n_src, n_tgt):
        self.n_dev = n_src * n_tgt
        first = (n_tgt, 2)
        src, tgt = digits_of(n_src // 2, 2 * n_tgt), digits_of(n_tgt, 1)
        self.plane, self.along = [first] + src, tgt
        self.dims = src[::-1] + [first] + tgt[::-1]
        self.left = [d for d in self.dims if d != first]
        x = own + self.sent(other, n_tgt).astype(jnp.float32)
        self.x = x.reshape(tuple(radix for _, radix in self.left) + own.shape[2:])

    def sent(self, array, mask):
        return lax.ppermute(array, ALL, [(i, i ^ mask) for i in range(self.n_dev)])

    def scatter(self, digit):
        stride, radix = digit
        dim = self.left.index(digit)
        mine = (lax.axis_index(ALL) // stride) % radix
        total = lax.dynamic_index_in_dim(self.x, mine, dim, keepdims=False)
        for j in range(1, radix):
            piece = lax.dynamic_index_in_dim(self.x, mine ^ j, dim, keepdims=False)
            total = total + self.sent(piece.astype(jnp.bfloat16), j * stride).astype(jnp.float32)
        self.x = total
        self.left.remove(digit)

    def gather(self, digit):
        stride, radix = digit
        mine = (lax.axis_index(ALL) // stride) % radix
        x = self.x.astype(jnp.bfloat16)
        got = [x] + [self.sent(x, j * stride) for j in range(1, radix)]
        self.left = [d for d in self.dims if d in self.left or d == digit]
        self.x = jnp.stack(
            [lax.select_n(mine ^ d, *got) if radix > 2 else jnp.where(mine == d, *got) for d in range(radix)],
            axis=self.left.index(digit),
        )


def update_kernel(
    src_points_ref,
    tgt_points_ref,
    src_factor_ref,
    tgt_factor_ref,
    marginal_ref,
    sums_ref,
    src_ref,
    tgt_ref,
    total,
):
    totals_of(sums_ref, total, src_points_ref.shape[1])
    rank = src_ref.shape[1]
    marginal = marginal_ref[...]
    src_ref[...] = mirror_step(src_points_ref[...], total[:rank], src_factor_ref[...], marginal)
    tgt_ref[...] = mirror_step(tgt_points_ref[...], total[rank:], tgt_factor_ref[...], marginal)


def updates(src_points, tgt_points, src_factor, tgt_factor, marginal, sums):
    rows, features = src_points.shape
    rank = src_factor.shape[1]
    shape = jax.ShapeDtypeStruct(src_factor.shape, jnp.bfloat16)
    return pl.pallas_call(
        update_kernel,
        out_shape=(shape, shape),
        scratch_shapes=[pltpu.VMEM((2 * rank, features), jnp.bfloat16)],
        compiler_params=pltpu.CompilerParams(vmem_limit_bytes=VMEM_BYTES),
        cost_estimate=pl.CostEstimate(
            flops=4 * rows * features * rank,
            bytes_accessed=4 * rows * (features + 2 * rank),
            transcendentals=2 * rows * rank,
        ),
        name="mirror_updates",
    )(src_points, tgt_points, src_factor, tgt_factor, marginal[None, :], sums)


def seen_block(ref, part, block):
    piece = block // ref.shape[1]
    return ref[pl.ds(part * piece, piece)].reshape(block, ref.shape[2])


def owner_kernel(
    features,
    src_ref,
    tgt_ref,
    sums_ref,
    marginal_ref,
    src_label_ref,
    tgt_label_ref,
    out_hbm,
    total,
    tgt_rows,
    tgt_update,
    tgt_inv,
    images,
    out_sem,
):
    totals_of(sums_ref, total, features)
    slots = images.shape[0]
    rank = tgt_update.shape[1]
    marginal = marginal_ref[...]
    block = OWNER_BLOCK
    for part in range(slots // block):
        mine = pl.ds(part * block, block)
        both = seen_block(tgt_ref, part, block)
        rows = both[:, :features]
        tgt_rows[mine, :] = rows
        tgt_update[mine, :] = mirror_step(rows, total[rank:], both[:, features:], marginal)
        tgt_inv[:, mine] = inverse_norm(rows).reshape(1, block)

    departures = []
    for part in range(slots // block):
        mine = pl.ds(part * block, block)
        both = seen_block(src_ref, part, block)
        rows = both[:, :features]
        update = mirror_step(rows, total[:rank], both[:, features:], marginal)
        cosine = contract_columns(rows, tgt_rows[...]) * inverse_norm(rows) * tgt_inv[...]
        weight = contract_columns(update, tgt_update[...]) * (1.0 / rank)
        label = src_label_ref[:, mine].reshape(block, 1)
        same = jnp.logical_and(label == tgt_label_ref[...], label > 0)
        kernel = jnp.where(same, weight * jnp.exp((cosine - 1.0) * (1.0 / TEMPER)), 0.0)
        denominator = jnp.sum(kernel, axis=1, keepdims=True)
        denominator = jnp.where(denominator > 0, denominator, 1.0)
        transport = (kernel * (1.0 / denominator)).astype(jnp.bfloat16)
        images[mine, :] = jnp.dot(
            transport, tgt_rows[...], preferred_element_type=jnp.float32
        ).astype(jnp.bfloat16)
        departures.append(
            pltpu.make_async_copy(images.at[mine], out_hbm.at[mine], out_sem.at[part])
        )
        departures[-1].start()
    for copy in departures:
        copy.wait()


def owner_maps(src, tgt, sums, marginal, src_labels, tgt_labels, features):
    n_dev, capacity, width = src.shape
    slots = n_dev * capacity
    rank = width - features
    return pl.pallas_call(
        functools.partial(owner_kernel, features),
        out_shape=jax.ShapeDtypeStruct((slots, features), jnp.bfloat16),
        grid=(1,),
        in_specs=[
            whole(src.shape),
            whole(tgt.shape),
            whole(sums.shape),
            whole((1, rank)),
            whole((1, slots)),
            whole((1, slots)),
        ],
        out_specs=in_hbm(),
        scratch_shapes=[
            pltpu.VMEM((2 * rank, features), jnp.bfloat16),
            pltpu.VMEM((slots, features), jnp.bfloat16),
            pltpu.VMEM((slots, rank), jnp.bfloat16),
            pltpu.VMEM((1, slots), jnp.float32),
            pltpu.VMEM((slots, features), jnp.bfloat16),
            pltpu.SemaphoreType.DMA((slots // OWNER_BLOCK,)),
        ],
        compiler_params=pltpu.CompilerParams(vmem_limit_bytes=VMEM_BYTES),
        cost_estimate=pl.CostEstimate(
            flops=4 * slots * features * (rank + slots),
            bytes_accessed=6 * slots * width,
            transcendentals=slots * slots,
        ),
        name="owner_maps",
    )(src, tgt, sums, marginal[None, :], src_labels[None, :], tgt_labels[None, :])


def labels_of(clusters, owner, capacity, spread):
    rows = clusters.shape[1]
    mine = clusters // spread == owner
    before = (jnp.arange(rows)[:, None] < jnp.arange(rows)[None, :]).astype(jnp.bfloat16)
    earlier = jnp.dot(mine.astype(jnp.bfloat16), before, preferred_element_type=jnp.float32)
    ranking = jnp.where(mine, earlier.astype(jnp.int32), -1)
    value = clusters - owner * spread + 1
    hit = ranking[:, None, :] == jnp.arange(capacity, dtype=jnp.int32)[None, :, None]
    return jnp.sum(jnp.where(hit, value[:, None, :], 0), axis=2).reshape(-1)


def exchange(rows):
    return lax.all_to_all(rows, ALL, split_axis=0, concat_axis=0, tiled=True)


def per_device(
    src_points, tgt_points, src_factor, tgt_factor, inner_marginal, src_cluster, tgt_cluster
):
    n_src, n_tgt = lax.axis_size("src"), lax.axis_size("tgt")
    n_dev = n_src * n_tgt
    rows, features = src_points.shape
    rank = src_factor.shape[1]
    capacity = 2 * rows // n_dev
    owner = lax.axis_index(ALL)

    tgt = pack(tgt_cluster, tgt_points, tgt_factor, n_dev, capacity)
    tgt, me = lax.optimization_barrier((tgt, owner))
    tgt = exchange(tgt)
    own, other = partial_sums(
        me,
        src_cluster,
        tgt_cluster,
        src_points,
        tgt_points,
        src_factor,
        tgt_factor,
        n_dev,
        n_tgt,
    )
    chain = Chain(own, other, n_src, n_tgt)
    for digit in chain.plane[1:]:
        chain.scatter(digit)
    for digit in chain.along:
        chain.scatter(digit)
    src = pack(src_cluster, src_points, src_factor, n_dev, capacity)
    src, tgt, chain.x = lax.optimization_barrier((src, tgt, chain.x))
    src = exchange(src)
    for digit in reversed(chain.plane + chain.along):
        chain.gather(digit)
    sums = chain.x.reshape(n_dev, -1, rank)

    kept = 2 * features // n_dev
    table = sums[:, kept : kept + 2].astype(jnp.int32)
    src_labels = labels_of(table[:, 0], owner, capacity, CL_DEV)
    tgt_labels = labels_of(table[:, 1], owner, capacity, CL_DEV)

    shape = (n_dev, capacity, features + rank)
    images = owner_maps(
        src.reshape(shape), tgt.reshape(shape), sums, inner_marginal, src_labels, tgt_labels, features
    )
    returned = exchange(images)

    src_update, tgt_update = updates(
        src_points, tgt_points, src_factor, tgt_factor, inner_marginal, sums
    )
    slot = slot_row(src_cluster[None, :], n_dev, capacity, CL_DEV, 0)
    back = (jnp.arange(n_dev * capacity, dtype=jnp.int32)[:, None] == slot).astype(jnp.bfloat16)
    mapped = contract_rows(back, returned).astype(jnp.bfloat16)
    return (src_update, tgt_update, mapped)


def solution(mesh):
    rows = P(ALL, None)
    return jax.shard_map(
        per_device,
        mesh=mesh,
        in_specs=(rows, rows, rows, rows, P(), P(ALL), P(ALL)),
        out_specs=(rows, rows, rows),
        check_vma=False,
    )
```
